32 devices in a mesh: dp: 4 (over y, core), seq: 8 (over z, x).
Axes of the slice: x: 2, y: 2, z: 4, core: 2. Of those that a mesh axis runs over, the one named last changes fastest.
Arguments:
- token_ids: int32 [4, 1024], P('dp', 'seq'), may hold values from 0 to 255
- cotangent: bfloat16 [4, 1024, 768], P('dp', 'seq'), may hold values from -6 to 6
- table: bfloat16 [256, 768], replicated, may hold values from -12 to 12
- w_query: bfloat16 [768, 768], replicated, may hold values from -2 to 2
- w_key: bfloat16 [768, 768], replicated, may hold values from -2 to 2
- w_value: bfloat16 [768, 768], replicated, may hold values from -0.21875 to 0.21875
- w_out: bfloat16 [768, 768], replicated, may hold values from -0.21875 to 0.21875
- window: int32 [12], replicated, may hold values from 64 to 512, as said below
Outputs:
- grad_input: bfloat16 [4, 1024, 768], P('dp', 'seq')
- weight_grads: float32 [3072, 768], P('seq')
The draws below stay inside these ranges and needn't reach their ends.
Inputs may be any that keep to these rules, and one draw needn't show every extreme that they name: Some head's window is exactly 512.
All inputs are finite; a program needn't handle non-finite values.
Results may differ from the reference program's by a relative error of at most 0.025.
Values may be sent and summed in bfloat16 or wider, within the bound.
No kernel may reach another device: no remote copies, remote signals or barrier semaphores. Data moves between devices by JAX's collectives and lax.ppermute only.
A program may use at most 128 MiB of HBM per device.

```python
import math
import jax
import jax.numpy as jnp
import numpy as np
from jax import lax

D = 768
HEADS = 12
HEAD_DIM = 64
VOCAB = 256
WINDOW = 512
SEQ = 1024
SEQS = 4


def draw_table(key, part):
    normal_part = jax.random.normal(jax.random.fold_in(key, 11), (VOCAB, D), jnp.float32)
    base_values = normal_part
    log_scale = jax.random.uniform(jax.random.fold_in(key, 12), (VOCAB, 1), jnp.float32, jnp.log(0.3), jnp.log(3.0))
    return jnp.clip(base_values * jnp.exp(log_scale), -12.0, 12.0).astype(jnp.bfloat16)


def paired_weight(key, which):
    own_part = jax.random.normal(jax.random.fold_in(key, 22 + which), (D, D), jnp.float32)
    mixed = own_part
    return jnp.clip(mixed * D ** (-0.5), -2.0, 2.0)


def draw_w_query(key, part):
    return paired_weight(key, 0).astype(jnp.bfloat16)


def draw_w_key(key, part):
    return paired_weight(key, 1).astype(jnp.bfloat16)


def draw_window(key, part):
    widths = jax.random.randint(jax.random.fold_in(key, 31), (HEADS,), WINDOW // 8, WINDOW + 1)
    chosen = jax.random.randint(jax.random.fold_in(key, 32), (), 0, HEADS)
    return jnp.where(jnp.arange(HEADS, dtype=jnp.int32) == chosen, WINDOW, widths).astype(jnp.int32)


def set_ends(result, rng, low, largest):
    longest = result.shape.index(max(result.shape))
    spots = []
    for shift in (0, 1):
        where = [jax.random.randint(jax.random.fold_in(rng, axis), (), 0, length) for axis, length in enumerate(result.shape)]
        where[longest] = (where[longest] + shift) % result.shape[longest]
        spots.append(tuple(where))
    return result.at[spots[0]].set(low).at[spots[1]].set(largest)


def level_of(key, dims, split, least, top_value):
    def one(dim, blocks):
        steps = jax.random.uniform(jax.random.fold_in(jax.random.fold_in(key, 6), dim), (blocks,), jnp.float32, least / len(split), top_value / len(split))
        return jnp.repeat(jnp.exp(steps), dims[dim] // blocks).reshape((-1,) + (1,) * (len(dims) - dim - 1))

    loudness = one(*split[0])
    for cut in split[1:]:
        loudness = loudness * one(*cut)
    return loudness


def rank_table(count, lean):
    weights = [(1 << 20) // math.isqrt(rank ** lean) + 1 for rank in range(1, count + 1)]
    width = 1 + sum(weights) // (1 << 30)
    return np.cumsum(np.array([max(1, weight // width) for weight in weights]))


def skewed_ids(own_key, dims, number_of, lean):
    grid = rank_table(number_of, lean)
    ticket = jax.random.randint(jax.random.fold_in(own_key, 1), dims, 0, int(grid[number_of - 1]))
    standing = jnp.searchsorted(jnp.asarray(grid, jnp.int32), ticket, side="right")
    return jax.random.permutation(jax.random.fold_in(own_key, 2), number_of)[standing].astype(jnp.int32)


def scatter_about(stream_key, shape, scale, most, cuts=(), kind=jnp.bfloat16):
    values = scale * jax.random.normal(stream_key, shape, jnp.float32)
    if cuts:
        values = values * level_of(stream_key, shape, cuts, -0.22, 0.18)
    return jnp.clip(values, -most, most).astype(kind)


def setup_inputs(seed: int = 0) -> dict:
    keys = jax.random.split(jax.random.key(seed), 9)
    token_ids = set_ends(skewed_ids(keys[0], (SEQS, SEQ), VOCAB, 2), jax.random.fold_in(keys[0], 3), 0, VOCAB - 1).astype(jnp.int32)
    cotangent = scatter_about(keys[1], (SEQS, SEQ, D), 1.0, 6.0, ((0, 4), (1, 8)))
    table = draw_table(jax.random.fold_in(keys[8], 71), 0)
    w_query = draw_w_query(jax.random.fold_in(keys[8], 71), 0)
    w_key = draw_w_key(jax.random.fold_in(keys[8], 71), 0)
    w_value = scatter_about(keys[5], (D, D), D ** -0.5, 0.21875)
    w_out = scatter_about(keys[6], (D, D), D ** -0.5, 0.21875)
    window = draw_window(jax.random.fold_in(keys[8], 71), 0)
    return {"token_ids": token_ids, "cotangent": cotangent, "table": table, "w_query": w_query, "w_key": w_key, "w_value": w_value, "w_out": w_out, "window": window}


EPSILON = 1e-05

def rotate(values, positions):
    row_count = values.shape[0]
    shaped = values.reshape(row_count, -1, HEAD_DIM)
    middle = HEAD_DIM // 2
    frequency = 10000.0 ** (-2.0 * jnp.arange(middle, dtype=jnp.float32) / HEAD_DIM)
    angles = positions.astype(jnp.float32)[:, None] * frequency[None, :]
    cosine = jnp.cos(angles)[:, None, :]
    sine_part = jnp.sin(angles)[:, None, :]
    former = shaped[..., :middle]
    latter = shaped[..., middle:]
    turned = jnp.concatenate([former * cosine - latter * sine_part, latter * cosine + former * sine_part], axis=-1)
    return turned.reshape(row_count, -1)

def unrotate(values, positions):
    row_count = values.shape[0]
    shaped = values.reshape(row_count, -1, HEAD_DIM)
    middle = HEAD_DIM // 2
    frequency = 10000.0 ** (-2.0 * jnp.arange(middle, dtype=jnp.float32) / HEAD_DIM)
    angles = positions.astype(jnp.float32)[:, None] * frequency[None, :]
    cosine = jnp.cos(angles)[:, None, :]
    sine_part = jnp.sin(angles)[:, None, :]
    former = shaped[..., :middle]
    latter = shaped[..., middle:]
    turned = jnp.concatenate([former * cosine + latter * sine_part, latter * cosine - former * sine_part], axis=-1)
    return turned.reshape(row_count, -1)

def tdot(left, right):
    return lax.dot_general(left, right, (((0,), (0,)), ((), ())), preferred_element_type=jnp.float32)

def ndot(left, right):
    return lax.dot_general(left, right, (((1,), (1,)), ((), ())), preferred_element_type=jnp.float32)

def reference(token_ids, cotangent, table, w_query, w_key, w_value, w_out, window):
    score_scale = HEAD_DIM ** (-0.5)
    block_rows = min(512, SEQ)
    block_count = SEQ // block_rows
    positions = jnp.arange(SEQ, dtype=jnp.int32)

    def one_sequence(pair):
        byte_ids, grad_out = pair
        embedded = table[byte_ids]
        widened = embedded.astype(jnp.float32)
        inv_rms = lax.rsqrt(lax.optimization_barrier(jnp.mean(widened * widened, axis=1, keepdims=True)) + EPSILON)
        normed = (widened * inv_rms).astype(jnp.bfloat16)
        query = rotate(jnp.dot(normed, w_query, preferred_element_type=jnp.float32), positions).astype(jnp.bfloat16)
        key_rows = rotate(jnp.dot(normed, w_key, preferred_element_type=jnp.float32), positions).astype(jnp.bfloat16)
        value_rows = jnp.dot(normed, w_value, preferred_element_type=jnp.float32).astype(jnp.bfloat16)
        grad_att = ndot(grad_out, w_out).astype(jnp.bfloat16)
        padding = jnp.zeros((WINDOW, D), jnp.bfloat16)
        key_pad = jnp.concatenate([padding, key_rows], axis=0)
        value_pad = jnp.concatenate([padding, value_rows], axis=0)

        def one_block(carry, block_index):
            grad_keys, grad_values = carry
            start = (block_index * block_rows).astype(jnp.int32)
            span_rows = WINDOW + block_rows
            query_heads = lax.dynamic_slice_in_dim(query, start, block_rows, 0).astype(jnp.float32).reshape(block_rows, HEADS, HEAD_DIM)
            key_heads = lax.dynamic_slice_in_dim(key_pad, start, span_rows, 0).astype(jnp.float32).reshape(span_rows, HEADS, HEAD_DIM)
            value_heads = lax.dynamic_slice_in_dim(value_pad, start, span_rows, 0).astype(jnp.float32).reshape(span_rows, HEADS, HEAD_DIM)
            grad_heads = lax.dynamic_slice_in_dim(grad_att, start, block_rows, 0).astype(jnp.float32).reshape(block_rows, HEADS, HEAD_DIM)
            query_pos = start + jnp.arange(block_rows, dtype=jnp.int32)
            key_pos = start - WINDOW + jnp.arange(span_rows, dtype=jnp.int32)
            distance = query_pos[:, None] - key_pos[None, :]
            allowed = (distance[None] >= 0) & (distance[None] < window[:, None, None]) & (key_pos[None, None, :] >= 0)
            scores = jnp.einsum('qhd,khd->hqk', query_heads, key_heads) * score_scale
            masked = jnp.where(allowed, scores, -1e+30)
            row_max = lax.optimization_barrier(jnp.max(masked, axis=-1, keepdims=True))
            weights = jnp.where(allowed, jnp.exp(masked - row_max), 0.0)
            probs = weights / lax.optimization_barrier(jnp.sum(weights, axis=-1, keepdims=True))
            probs_b = probs.astype(jnp.bfloat16)
            probs_wide = probs_b.astype(jnp.float32)
            attended = jnp.einsum('hqk,khd->qhd', probs_wide, value_heads).astype(jnp.bfloat16).reshape(block_rows, D)
            grad_probs = jnp.einsum('qhd,khd->hqk', grad_heads, value_heads)
            row_term = lax.optimization_barrier(jnp.sum(probs * grad_probs, axis=-1, keepdims=True))
            grad_scores = (probs * (grad_probs - row_term) * score_scale).astype(jnp.bfloat16).astype(jnp.float32)
            grad_query = jnp.einsum('hqk,khd->qhd', grad_scores, key_heads).reshape(block_rows, D)
            part_keys = jnp.einsum('hqk,qhd->khd', grad_scores, query_heads).reshape(span_rows, D)
            part_values = jnp.einsum('hqk,qhd->khd', probs_wide, grad_heads).reshape(span_rows, D)
            slab_keys = lax.dynamic_slice_in_dim(grad_keys, start, span_rows, 0) + part_keys
            slab_values = lax.dynamic_slice_in_dim(grad_values, start, span_rows, 0) + part_values
            grad_keys = lax.dynamic_update_slice_in_dim(grad_keys, slab_keys, start, 0)
            grad_values = lax.dynamic_update_slice_in_dim(grad_values, slab_values, start, 0)
            return ((grad_keys, grad_values), (attended, grad_query))
        empty = jnp.zeros((SEQ + WINDOW, D), jnp.float32)
        (grad_keys, grad_values), (attended, grad_query) = lax.scan(one_block, (empty, empty), jnp.arange(block_count, dtype=jnp.int32))
        attended = attended.reshape(SEQ, D)
        grad_query = grad_query.reshape(SEQ, D)
        grad_q_lin = unrotate(grad_query, positions).astype(jnp.bfloat16)
        grad_k_lin = unrotate(grad_keys[WINDOW:], positions).astype(jnp.bfloat16)
        grad_v_lin = grad_values[WINDOW:].astype(jnp.bfloat16)
        grad_normed = ndot(grad_q_lin, w_query) + ndot(grad_k_lin, w_key) + ndot(grad_v_lin, w_value)
        scaled = widened * inv_rms
        grad_input = (inv_rms * (grad_normed - scaled * lax.optimization_barrier(jnp.mean(grad_normed * scaled, axis=1, keepdims=True)))).astype(jnp.bfloat16)
        term = jnp.concatenate([tdot(normed, grad_q_lin), tdot(normed, grad_k_lin), tdot(normed, grad_v_lin), tdot(attended, grad_out)], axis=0)
        return (grad_input, term)

    def accumulate(total, pair):
        grad_input, term = one_sequence(pair)
        return (total + term, grad_input)
    weight_grads, grad_input = lax.scan(accumulate, jnp.zeros((4 * D, D), jnp.float32), (token_ids, cotangent))
    return (grad_input, weight_grads)
```

```python
import functools

import jax
import jax.numpy as jnp
from jax import lax
from jax.experimental import pallas as pl
from jax.experimental.pallas import tpu as pltpu
from jax.sharding import PartitionSpec as P

HEADS = 12
HEAD_DIM = 64
WINDOW = 512


EPSILON = 1e-05


def shifted(block, axis, distance):
    devices = range(lax.axis_size(axis))
    route = [(i - distance, i) for i in devices if i - distance in devices]
    return lax.ppermute(block, axis, route)


def rotate(values, positions):
    row_count = values.shape[0]
    shaped = values.reshape(row_count, -1, HEAD_DIM)
    middle = HEAD_DIM // 2
    frequency = 10000.0 ** (-2.0 * jnp.arange(middle, dtype=jnp.float32) / HEAD_DIM)
    angles = positions.astype(jnp.float32)[:, None] * frequency[None, :]
    cosine = jnp.cos(angles)[:, None, :]
    sine_part = jnp.sin(angles)[:, None, :]
    former = shaped[..., :middle]
    latter = shaped[..., middle:]
    turned = jnp.concatenate(
        [former * cosine - latter * sine_part, latter * cosine + former * sine_part], axis=-1
    )
    return turned.reshape(row_count, -1)


def unrotate(values, positions):
    row_count = values.shape[0]
    shaped = values.reshape(row_count, -1, HEAD_DIM)
    middle = HEAD_DIM // 2
    frequency = 10000.0 ** (-2.0 * jnp.arange(middle, dtype=jnp.float32) / HEAD_DIM)
    angles = positions.astype(jnp.float32)[:, None] * frequency[None, :]
    cosine = jnp.cos(angles)[:, None, :]
    sine_part = jnp.sin(angles)[:, None, :]
    former = shaped[..., :middle]
    latter = shaped[..., middle:]
    turned = jnp.concatenate(
        [former * cosine + latter * sine_part, latter * cosine - former * sine_part], axis=-1
    )
    return turned.reshape(row_count, -1)


def tdot(left, right):
    return lax.dot_general(
        left, right, (((0,), (0,)), ((), ())), preferred_element_type=jnp.float32
    )


def ndot(left, right):
    return lax.dot_general(
        left, right, (((1,), (1,)), ((), ())), preferred_element_type=jnp.float32
    )


def embed_rows(byte_ids, table):
    onehot = (byte_ids[:, None] == jnp.arange(table.shape[0], dtype=jnp.int32)[None, :]).astype(
        jnp.bfloat16
    )
    return jnp.dot(onehot, table, preferred_element_type=jnp.float32).astype(jnp.bfloat16)


def normalize(embedded):
    widened = embedded.astype(jnp.float32)
    inv_rms = lax.rsqrt(jnp.mean(widened * widened, axis=1, keepdims=True) + EPSILON)
    return (widened, inv_rms, (widened * inv_rms).astype(jnp.bfloat16))


def keys_values(normed, positions, w_key, w_value):
    key_rows = rotate(jnp.dot(normed, w_key, preferred_element_type=jnp.float32), positions).astype(
        jnp.bfloat16
    )
    value_rows = jnp.dot(normed, w_value, preferred_element_type=jnp.float32).astype(jnp.bfloat16)
    return (key_rows, value_rows)


def head_group(
    query_heads, key_heads, value_heads, grad_heads, group_window, own_pos, key_pos, score_scale
):
    distance = own_pos[:, None] - key_pos[None, :]
    allowed = (
        (distance[None] >= 0)
        & (distance[None] < group_window[:, None, None])
        & (key_pos[None, None, :] >= 0)
    )
    scores = (
        jnp.einsum("qhd,khd->hqk", query_heads, key_heads, preferred_element_type=jnp.float32)
        * score_scale
    )
    masked = jnp.where(allowed, scores, -1e30)
    row_max = jnp.max(masked, axis=-1, keepdims=True)
    weights = jnp.where(allowed, jnp.exp(masked - row_max), 0.0)
    probs = weights / jnp.sum(weights, axis=-1, keepdims=True)
    probs_b = probs.astype(jnp.bfloat16)
    attended = jnp.einsum(
        "hqk,khd->qhd", probs_b, value_heads, preferred_element_type=jnp.float32
    ).astype(jnp.bfloat16)
    grad_probs = jnp.einsum(
        "qhd,khd->hqk", grad_heads, value_heads, preferred_element_type=jnp.float32
    )
    row_term = jnp.sum(probs * grad_probs, axis=-1, keepdims=True)
    grad_scores = (probs * (grad_probs - row_term) * score_scale).astype(jnp.bfloat16)
    grad_query = jnp.einsum(
        "hqk,khd->qhd", grad_scores, key_heads, preferred_element_type=jnp.float32
    )
    grad_key = jnp.einsum(
        "hqk,qhd->khd", grad_scores, query_heads, preferred_element_type=jnp.float32
    )
    grad_value = jnp.einsum("hqk,qhd->khd", probs_b, grad_heads, preferred_element_type=jnp.float32)
    return (attended, grad_query, grad_key, grad_value)


def general_device(token_ids, cotangent, table, w_query, w_key, w_value, w_out, window):
    local_ids = token_ids[0]
    grad_out = cotangent[0]
    length = local_ids.shape[0]
    features = table.shape[1]
    tail_rows = min(length, WINDOW)
    reach_devs = -(-WINDOW // length)
    halo_rows = reach_devs * tail_rows
    offset = lax.axis_index("seq") * length
    own_pos = offset + jnp.arange(length, dtype=jnp.int32)
    halo_pos = offset - halo_rows + jnp.arange(halo_rows, dtype=jnp.int32)
    score_scale = HEAD_DIM ** (-0.5)
    embedded = embed_rows(local_ids, table)
    widened, inv_rms, normed = normalize(embedded)
    query = rotate(jnp.dot(normed, w_query, preferred_element_type=jnp.float32), own_pos).astype(
        jnp.bfloat16
    )
    key_own, value_own = keys_values(normed, own_pos, w_key, w_value)
    key_pieces = []
    value_pieces = []
    for hop_index in range(reach_devs):
        far_keys, far_values = shifted((key_own, value_own), "seq", hop_index + 1)
        key_pieces.insert(0, far_keys)
        value_pieces.insert(0, far_values)
    key_halo = jnp.concatenate(key_pieces, axis=0)
    value_halo = jnp.concatenate(value_pieces, axis=0)
    span_rows = halo_rows + length
    key_all = jnp.concatenate([key_halo, key_own], axis=0)
    value_all = jnp.concatenate([value_halo, value_own], axis=0)
    key_pos = jnp.concatenate([halo_pos, own_pos], axis=0)
    query_heads = query.reshape(length, HEADS, HEAD_DIM)
    key_heads = key_all.reshape(span_rows, HEADS, HEAD_DIM)
    value_heads = value_all.reshape(span_rows, HEADS, HEAD_DIM)
    grad_att = ndot(grad_out, w_out).astype(jnp.bfloat16)
    grad_heads = grad_att.reshape(length, HEADS, HEAD_DIM)
    group_size = 4
    attended_parts = []
    query_parts = []
    key_parts = []
    value_parts = []
    for group_index in range(HEADS // group_size):
        lower = group_index * group_size
        upper = lower + group_size
        outputs = head_group(
            query_heads[:, lower:upper],
            key_heads[:, lower:upper],
            value_heads[:, lower:upper],
            grad_heads[:, lower:upper],
            window[lower:upper],
            own_pos,
            key_pos,
            score_scale,
        )
        attended_parts.append(outputs[0])
        query_parts.append(outputs[1])
        key_parts.append(outputs[2])
        value_parts.append(outputs[3])
    attended = jnp.concatenate(attended_parts, axis=1).reshape(length, features)
    grad_query = jnp.concatenate(query_parts, axis=1).reshape(length, features)
    grad_key = jnp.concatenate(key_parts, axis=1).reshape(span_rows, features)
    grad_value = jnp.concatenate(value_parts, axis=1).reshape(span_rows, features)
    tail_keys = grad_key[:halo_rows].reshape(reach_devs, tail_rows, features)
    tail_values = grad_value[:halo_rows].reshape(reach_devs, tail_rows, features)
    back_keys = jnp.zeros((tail_rows, features), jnp.float32)
    back_values = jnp.zeros((tail_rows, features), jnp.float32)
    for hop_index in range(reach_devs):
        got_keys, got_values = shifted(
            (tail_keys[reach_devs - 1 - hop_index], tail_values[reach_devs - 1 - hop_index]),
            "seq",
            -(hop_index + 1),
        )
        back_keys = back_keys + got_keys
        back_values = back_values + got_values
    own_keys = grad_key[halo_rows:]
    own_values = grad_value[halo_rows:]
    own_keys = jnp.concatenate([own_keys[: length - tail_rows], own_keys + back_keys], axis=0)
    own_values = jnp.concatenate(
        [own_values[: length - tail_rows], own_values + back_values], axis=0
    )
    grad_q_lin = unrotate(grad_query, own_pos).astype(jnp.bfloat16)
    grad_k_lin = unrotate(own_keys, own_pos).astype(jnp.bfloat16)
    grad_v_lin = own_values.astype(jnp.bfloat16)
    grad_normed = ndot(grad_q_lin, w_query) + ndot(grad_k_lin, w_key) + ndot(grad_v_lin, w_value)
    scaled = widened * inv_rms
    grad_input = (
        inv_rms * (grad_normed - scaled * jnp.mean(grad_normed * scaled, axis=1, keepdims=True))
    ).astype(jnp.bfloat16)
    term = jnp.concatenate(
        [
            tdot(normed, grad_q_lin),
            tdot(normed, grad_k_lin),
            tdot(normed, grad_v_lin),
            tdot(attended, grad_out),
        ],
        axis=0,
    )
    shares = lax.psum_scatter(term.astype(jnp.bfloat16), "seq", scatter_dimension=0, tiled=True)
    weight_grads = lax.psum(shares, "dp").astype(jnp.float32)
    return (grad_input[None], weight_grads)


GROUPS = 4
GROUP_HEADS = HEADS // GROUPS
GROUP_COLS = GROUP_HEADS * HEAD_DIM
TILE = 256
TOKEN_ROWS = 16
HALF = HEAD_DIM // 2
VMEM_BYTES = 48 * 1024 * 1024


def key_span(query_tile):
    first = max(0, query_tile - WINDOW // TILE)
    return (first * TILE, (query_tile - first + 1) * TILE)


def normed_table(table_ref):
    widened = table_ref[...].astype(jnp.float32)
    inv_rms = lax.rsqrt(jnp.mean(widened * widened, axis=1, keepdims=True) + EPSILON)
    return (widened * inv_rms).astype(jnp.bfloat16)


def onehot_columns(tokens, vocab):
    rows = lax.broadcasted_iota(jnp.int32, (vocab, tokens.shape[1]), 0)
    return (rows == tokens).astype(jnp.float32).astype(jnp.bfloat16)


def send_kernel(tokens_ref, cotangent_ref, out_weights_ref, early_ref, late_ref):
    cotangent = cotangent_ref[...]
    grad_att = ndot(out_weights_ref[...], cotangent).astype(jnp.bfloat16)
    block = tokens_ref.shape[1]
    tokens = jnp.broadcast_to(tokens_ref[...].astype(jnp.float32), (TOKEN_ROWS, block)).astype(
        jnp.bfloat16
    )
    columns = late_ref.shape[2]
    for target in range(2 * GROUPS):
        group, side = divmod(target, 2)
        early_ref[target, :GROUP_COLS, :] = grad_att[
            group * GROUP_COLS : (group + 1) * GROUP_COLS
        ]
        early_ref[target, GROUP_COLS:, :] = tokens
        late_ref[target] = cotangent[:, side * columns : (side + 1) * columns]


def attention_kernel(
    meta_ref,
    early_ref,
    table_ref,
    weights_ref,
    cosine_ref,
    sine_ref,
    rows_ref,
    sums_ref,
    attended_ref,
    query_key_ref,
    zero_query_ref,
    key_t_ref,
    value_ref,
    value_t_ref,
    grad_att_ref,
    onehot_ref,
    grad_query_ref,
    grad_key_ref,
    grad_value_ref,
):
    head = pl.program_id(0)
    blocks, _, block = early_ref.shape
    length = blocks * block
    vocab = table_ref.shape[0]
    half_vocab = vocab // 2
    cosine = cosine_ref[...]
    sine_part = sine_ref[...]
    blank = jnp.zeros((HEAD_DIM, length), jnp.float32)

    @pl.when(head == 0)
    def _():
        normed = normed_table(table_ref)
        lookup = jnp.dot(normed, weights_ref[...], preferred_element_type=jnp.float32).T
        upper = lookup.astype(jnp.bfloat16)
        lower = (lookup - upper.astype(jnp.float32)).astype(jnp.bfloat16)
        for source in range(blocks):
            lanes = slice(source * block, (source + 1) * block)
            tokens = early_ref[source, GROUP_COLS : GROUP_COLS + TOKEN_ROWS, :]
            tokens = tokens.astype(jnp.float32)[:1].astype(jnp.int32)
            onehot_ref[:, lanes] = onehot_columns(tokens, vocab)
            grad_att_ref[:, :, lanes] = early_ref[source, :GROUP_COLS, :].reshape(
                GROUP_HEADS, HEAD_DIM, block
            )
        onehot = onehot_ref[...]

        def chosen(start):
            rows = slice(start, start + HEAD_DIM)
            return jnp.dot(upper[rows], onehot, preferred_element_type=jnp.float32) + jnp.dot(
                lower[rows], onehot, preferred_element_type=jnp.float32
            )

        def turned(columns):
            former = columns[:HALF]
            latter = columns[HALF:]
            return jnp.concatenate(
                [former * cosine - latter * sine_part, latter * cosine + former * sine_part], axis=0
            )

        for index in range(GROUP_HEADS):
            query = turned(chosen(index * HEAD_DIM)) * HEAD_DIM ** (-0.5)
            keys = turned(chosen(GROUP_COLS + index * HEAD_DIM))
            values = chosen(2 * GROUP_COLS + index * HEAD_DIM)
            query_key_ref[index] = jnp.concatenate([query, keys], axis=0).T.astype(jnp.bfloat16)
            value_ref[index] = jnp.concatenate([values, blank], axis=0).T.astype(jnp.bfloat16)
            zero_query_ref[index] = jnp.concatenate([blank, query], axis=0).astype(jnp.bfloat16)
            key_t_ref[index] = keys.astype(jnp.bfloat16)
            value_t_ref[index] = values.astype(jnp.bfloat16)

    width = meta_ref[head]
    grad_att = grad_att_ref[head]
    wide_grad = grad_att.astype(jnp.float32)
    grad_blank = jnp.concatenate([wide_grad, blank], axis=0).astype(jnp.bfloat16)
    blank_grad = jnp.concatenate([blank, wide_grad], axis=0).T.astype(jnp.bfloat16)
    grad_key_ref[...] = jnp.zeros_like(grad_key_ref)
    grad_value_ref[...] = jnp.zeros_like(grad_value_ref)
    distance = lax.broadcasted_iota(jnp.int32, (TILE, TILE), 1) - lax.broadcasted_iota(
        jnp.int32, (TILE, TILE), 0
    )
    for query_tile in range(length // TILE):
        first, count = key_span(query_tile)
        columns = slice(query_tile * TILE, (query_tile + 1) * TILE)
        scores = jnp.dot(
            query_key_ref[head, first : first + count, :],
            zero_query_ref[head, :, columns],
            preferred_element_type=jnp.float32,
        )
        masked = []
        for key_tile in range(count // TILE):
            offset = query_tile * TILE - first - key_tile * TILE
            allowed = distance < width - offset
            if offset == 0:
                allowed = allowed & (distance >= 0)
            part = scores[key_tile * TILE : (key_tile + 1) * TILE]
            masked.append(jnp.where(allowed, part, -1e30))
        masked = jnp.concatenate(masked, axis=0)
        row_max = jnp.max(masked, axis=0, keepdims=True)
        weights = jnp.exp(masked - row_max)
        probs = weights * (1.0 / jnp.sum(weights, axis=0, keepdims=True))
        rounded = probs.astype(jnp.bfloat16)
        attended = jnp.dot(
            value_t_ref[head, :, first : first + count], rounded, preferred_element_type=jnp.float32
        )
        attended_ref[pl.ds(pl.multiple_of(head * HEAD_DIM, HEAD_DIM), HEAD_DIM), columns] = (
            attended.astype(jnp.bfloat16)
        )
        row_term = jnp.sum(attended * wide_grad[:, columns], axis=0, keepdims=True)
        grad_probs = jnp.dot(
            value_ref[head, first : first + count, :],
            grad_blank[:, columns],
            preferred_element_type=jnp.float32,
        )
        grad_scores = (probs * (grad_probs - row_term)).astype(jnp.bfloat16)
        grad_query_ref[:, columns] = jnp.dot(
            key_t_ref[head, :, first : first + count],
            grad_scores,
            preferred_element_type=jnp.float32,
        )
        grad_key_ref[first : first + count, :] += jnp.dot(
            grad_scores, query_key_ref[head, columns, :], preferred_element_type=jnp.float32
        )
        grad_value_ref[first : first + count, :] += jnp.dot(
            rounded, blank_grad[columns, :], preferred_element_type=jnp.float32
        )

    def turned_back(columns):
        former = columns[:HALF]
        latter = columns[HALF:]
        return jnp.concatenate(
            [former * cosine + latter * sine_part, latter * cosine - former * sine_part], axis=0
        )

    lanes = lax.broadcasted_iota(jnp.int32, grad_key_ref.shape, 1)
    both = jnp.where(lanes < HEAD_DIM, grad_key_ref[...], grad_value_ref[...]).T
    grads = jnp.concatenate(
        [
            turned_back(grad_query_ref[...] * HEAD_DIM ** (-0.5)),
            turned_back(both[:HEAD_DIM]),
            both[HEAD_DIM:],
        ],
        axis=0,
    ).astype(jnp.bfloat16)
    sums = ndot(grads, onehot_ref[...]).astype(jnp.bfloat16)
    for matrix in range(3):
        rows = slice(matrix * HEAD_DIM, (matrix + 1) * HEAD_DIM)
        place = pl.ds(
            pl.multiple_of(matrix * GROUP_COLS + head * HEAD_DIM, HEAD_DIM), HEAD_DIM
        )
        for core in range(2):
            lane = core * half_vocab
            sums_ref[core, place, :] = sums[rows, lane : lane + half_vocab]
        for target in range(GROUPS):
            start = target * 2 * block
            even = grads[rows, start : start + block]
            odd = grads[rows, start + block : start + 2 * block]
            rows_ref[target, place, :] = jnp.where(meta_ref[GROUP_HEADS] == 0, even, odd)


def out_kernel(attended_ref, cotangent_ref, out_ref):
    total = jnp.dot(attended_ref[...], cotangent_ref[...], preferred_element_type=jnp.float32)
    rows = total.shape[0] // 2
    lanes = out_ref.shape[2]
    for core in range(2):
        for chunk in range(total.shape[1] // lanes):
            out_ref[core, chunk * rows : (chunk + 1) * rows, :] = total[
                core * rows : (core + 1) * rows, chunk * lanes : (chunk + 1) * lanes
            ].astype(jnp.bfloat16)


def gather_kernel(meta_ref, kept_ref, kept_out_ref, s1, s2, s3, n0, n1, f0, f1, pieces_ref):
    group = meta_ref[GROUP_HEADS + 1]
    rows = GROUP_COLS

    @pl.when(group < 3)
    def _():
        own = pl.multiple_of(group * rows, rows)
        pieces_ref[pl.ds(own, rows), :] = kept_ref[pl.ds(own, rows), :]
        for turn, got in ((1, s1), (2, s2), (3, s3)):
            source = lax.rem(group - turn + GROUPS, GROUPS)
            pieces_ref[pl.ds(pl.multiple_of(source * rows, rows), rows), :] = got[...]
        tail = pieces_ref.shape[0] - GROUPS * rows
        pieces_ref[GROUPS * rows :, :] = jnp.zeros((tail, kept_ref.shape[1]), jnp.bfloat16)

    @pl.when(group == 3)
    def _():
        size = kept_out_ref.shape[0]
        own = meta_ref[GROUP_HEADS] == 1
        pieces_ref[0:size, :] = n0[...]
        pieces_ref[size : 2 * size, :] = f0[...]
        pieces_ref[2 * size : 3 * size, :] = jnp.where(own, kept_out_ref[...], n1[...])
        pieces_ref[3 * size :, :] = f1[...]


def input_kernel(tokens_ref, table_ref, query_ref, key_ref, value_ref, rows_ref, out_ref):
    widened = table_ref[...].astype(jnp.float32)
    vocab = table_ref.shape[0]
    onehot = onehot_columns(tokens_ref[...], vocab)
    embedded = tdot(onehot, table_ref[...])
    inv_rms = lax.rsqrt(jnp.mean(embedded * embedded, axis=1, keepdims=True) + EPSILON)
    grad_normed = None
    for matrix, weights in enumerate((query_ref, key_ref, value_ref)):
        columns = jnp.concatenate(
            [
                rows_ref[group, matrix * GROUP_COLS : (matrix + 1) * GROUP_COLS, :]
                for group in range(GROUPS)
            ],
            axis=0,
        )
        part = ndot(columns.astype(jnp.float32).T.astype(jnp.bfloat16), weights[...])
        grad_normed = part if grad_normed is None else grad_normed + part
    scaled = embedded * inv_rms
    out_ref[...] = (
        inv_rms * (grad_normed - scaled * jnp.mean(grad_normed * scaled, axis=1, keepdims=True))
    ).astype(jnp.bfloat16)


def weight_kernel(meta_ref, table_ref, mine_ref, other_ref, out_ref):
    side_rows = out_ref.shape[0]
    half_vocab = mine_ref.shape[1]
    first_core = meta_ref[GROUP_HEADS + 2] == 0

    @pl.when(meta_ref[GROUP_HEADS + 1] < 3)
    def _():
        normed = normed_table(table_ref)
        first = normed[:, :side_rows]
        second = normed[:, side_rows:]
        taken = jnp.where(meta_ref[GROUP_HEADS] == 0, first, second)
        upper = jnp.where(first_core, taken[:half_vocab], taken[half_vocab:])
        lower = jnp.where(first_core, taken[half_vocab:], taken[:half_vocab])
        total = None
        for part, sums_ref in ((upper, mine_ref), (lower, other_ref)):
            term = lax.dot_general(
                part,
                sums_ref[: GROUPS * GROUP_COLS, :],
                (((0,), (1,)), ((), ())),
                preferred_element_type=jnp.float32,
            )
            total = term if total is None else total + term
        out_ref[...] = total

    @pl.when(meta_ref[GROUP_HEADS + 1] == 3)
    def _():
        rows = GROUP_COLS // 2
        side = meta_ref[GROUP_HEADS]
        for core in range(2):
            for half in range(2):
                for plane in range(2):
                    for chunk in range(3):
                        place = ((2 * half + plane) * 3 + chunk) * rows
                        here = mine_ref[place : place + rows, :]
                        there = other_ref[place : place + rows, :]
                        value = jnp.where(first_core == (core == 0), here, there)
                        row = half * GROUP_COLS + core * rows
                        column = jnp.where(side == 0, plane, 1 - plane) * 3 + chunk
                        lanes = pl.ds(
                            pl.multiple_of(column * half_vocab, half_vocab), half_vocab
                        )
                        out_ref[row : row + rows, lanes] = value.astype(jnp.float32)


def whole(shape):
    return pl.BlockSpec(shape, lambda *_: (0,) * len(shape))


def kernel_call(body, steps, operands, in_specs, outs, out_specs, scratch, flops, moved):
    return pl.pallas_call(
        body,
        grid=(steps,),
        in_specs=[pl.BlockSpec(memory_space=pltpu.SMEM)] + in_specs
        if operands[0].ndim == 1
        else in_specs,
        out_specs=out_specs,
        out_shape=outs,
        scratch_shapes=scratch,
        compiler_params=pltpu.CompilerParams(
            dimension_semantics=("arbitrary",), vmem_limit_bytes=VMEM_BYTES
        ),
        cost_estimate=pl.CostEstimate(flops=flops, bytes_accessed=moved, transcendentals=0),
    )(*operands)


def swapped(block, axis, bit):
    route = [(i, i ^ bit) for i in range(lax.axis_size(axis))]
    return lax.ppermute(block, axis, route)


def grouped_device(token_ids, cotangent, table, w_query, w_key, w_value, w_out, window):
    place = lax.axis_index("seq")
    core = lax.axis_index("dp") % 2
    group = place // 2
    side = place % 2
    block = token_ids.shape[1]
    features = table.shape[1]
    vocab = table.shape[0]
    blocks = lax.axis_size("seq")
    length = block * blocks
    early, late = kernel_call(
        send_kernel,
        1,
        (token_ids, cotangent[0], w_out),
        [whole(token_ids.shape), whole((block, features)), whole(w_out.shape)],
        [
            jax.ShapeDtypeStruct((blocks, GROUP_COLS + TOKEN_ROWS, block), jnp.bfloat16),
            jax.ShapeDtypeStruct((blocks, block, features // 2), jnp.bfloat16),
        ],
        [
            whole((blocks, GROUP_COLS + TOKEN_ROWS, block)),
            whole((blocks, block, features // 2)),
        ],
        [],
        2 * 10**8,
        3 * 10**6,
    )
    early = lax.all_to_all(early, "seq", split_axis=0, concat_axis=0, tiled=True)
    late = lax.all_to_all(late, "seq", split_axis=0, concat_axis=0, tiled=True)
    start = group * GROUP_COLS
    weights = jnp.concatenate(
        [lax.dynamic_slice_in_dim(w, start, GROUP_COLS, 1) for w in (w_query, w_key, w_value)],
        axis=1,
    )
    meta = jnp.concatenate(
        [
            lax.dynamic_slice_in_dim(window, group * GROUP_HEADS, GROUP_HEADS, 0),
            jnp.stack([side, group, core]).astype(jnp.int32),
        ]
    )
    frequency = 10000.0 ** (-2.0 * jnp.arange(HALF, dtype=jnp.float32) / HEAD_DIM)
    angles = frequency[:, None] * jnp.arange(length, dtype=jnp.int32).astype(jnp.float32)[None, :]
    cosine = jnp.cos(angles)
    sine_part = jnp.sin(angles)
    heads_shape = (GROUP_HEADS, HEAD_DIM, length)
    rows_shape = (GROUP_HEADS, length, 2 * HEAD_DIM)
    rows_out = (GROUPS, 3 * GROUP_COLS, block)
    sums_out = (2, 3 * GROUP_COLS, vocab // 2)
    rows, sums, attended = kernel_call(
        attention_kernel,
        GROUP_HEADS,
        (meta, early, table, weights, cosine, sine_part),
        [
            whole(early.shape),
            whole(table.shape),
            whole(weights.shape),
            whole(cosine.shape),
            whole(sine_part.shape),
        ],
        [
            jax.ShapeDtypeStruct(rows_out, jnp.bfloat16),
            jax.ShapeDtypeStruct(sums_out, jnp.bfloat16),
            jax.ShapeDtypeStruct((GROUP_COLS, length), jnp.bfloat16),
        ],
        [whole(rows_out), whole(sums_out), whole((GROUP_COLS, length))],
        [
            pltpu.VMEM(rows_shape, jnp.bfloat16),
            pltpu.VMEM((GROUP_HEADS, 2 * HEAD_DIM, length), jnp.bfloat16),
            pltpu.VMEM(heads_shape, jnp.bfloat16),
            pltpu.VMEM(rows_shape, jnp.bfloat16),
            pltpu.VMEM(heads_shape, jnp.bfloat16),
            pltpu.VMEM(heads_shape, jnp.bfloat16),
            pltpu.VMEM((vocab, length), jnp.bfloat16),
            pltpu.VMEM((HEAD_DIM, length), jnp.float32),
            pltpu.VMEM((length, 2 * HEAD_DIM), jnp.float32),
            pltpu.VMEM((length, 2 * HEAD_DIM), jnp.float32),
        ],
        8 * 10**9,
        8 * 10**6,
    )
    late = late.reshape(length, features // 2)
    out_shape = (2, 3 * GROUP_COLS // 2, 128)
    out_sums = kernel_call(
        out_kernel,
        1,
        (attended, late),
        [whole(attended.shape), whole(late.shape)],
        jax.ShapeDtypeStruct(out_shape, jnp.bfloat16),
        whole(out_shape),
        [],
        3 * 10**8,
        2 * 10**6,
    )

    def over_dp(halves):
        kept = lax.dynamic_index_in_dim(halves, core, 0, keepdims=False)
        given = lax.dynamic_index_in_dim(halves, 1 - core, 0, keepdims=False)
        kept = kept + swapped(given, "dp", 1)
        return kept + swapped(kept, "dp", 2)

    kept = over_dp(sums)
    kept_out = over_dp(out_sums)
    planes = [[2 * z + x for z in range(GROUPS)] for x in range(2)]
    got_rows = lax.all_to_all(
        rows, "seq", split_axis=0, concat_axis=0, axis_index_groups=planes, tiled=True
    )
    grad_input = kernel_call(
        input_kernel,
        1,
        (token_ids, table, w_query, w_key, w_value, got_rows),
        [
            whole(token_ids.shape),
            whole(table.shape),
            whole(w_query.shape),
            whole(w_key.shape),
            whole(w_value.shape),
            whole(got_rows.shape),
        ],
        jax.ShapeDtypeStruct((block, features), jnp.bfloat16),
        whole((block, features)),
        [],
        10**9,
        5 * 10**6,
    )
    got = []
    for turn in range(1, GROUPS):
        route = [
            (2 * z + x, 2 * ((z + turn) % GROUPS) + x)
            for z in range(GROUPS)
            for x in range(2)
            if (z + turn) % GROUPS != 3
        ]
        target = jnp.minimum((group + turn) % GROUPS, 2)
        piece = lax.dynamic_slice_in_dim(kept, target * GROUP_COLS, GROUP_COLS, 0)
        got.append(lax.ppermute(piece, "seq", route))
    for other in range(2):
        for half in range(2):
            route = [(2 * (2 * x + half) + (x ^ other), 6 + x) for x in range(2)]
            route = [(s, t) for s, t in route if s != t]
            got.append(lax.ppermute(kept_out, "seq", route))
    pieces = kernel_call(
        gather_kernel,
        1,
        (meta, kept, kept_out, *got),
        [whole(kept.shape), whole(kept_out.shape)] + [whole(piece.shape) for piece in got],
        jax.ShapeDtypeStruct((4 * kept_out.shape[0], kept.shape[1]), jnp.bfloat16),
        whole((4 * kept_out.shape[0], kept.shape[1])),
        [],
        10**6,
        10**6,
    )
    others = swapped(pieces, "dp", 1)
    weight_grads = kernel_call(
        weight_kernel,
        1,
        (meta, table, pieces, others),
        [whole(table.shape), whole(pieces.shape), whole(others.shape)],
        jax.ShapeDtypeStruct((features // 2, features), jnp.float32),
        whole((features // 2, features)),
        [],
        10**9,
        5 * 10**6,
    )
    return (grad_input[None], weight_grads)


def on_device(token_ids, cotangent, table, w_query, w_key, w_value, w_out, window):
    fits = (
        lax.axis_size("seq") == 2 * GROUPS
        and lax.axis_size("dp") == 4
        and token_ids.shape == (1, 128)
        and table.shape == (256, HEADS * HEAD_DIM)
    )
    plan = grouped_device if fits else general_device
    return plan(token_ids, cotangent, table, w_query, w_key, w_value, w_out, window)


def solution(mesh):
    return jax.shard_map(
        on_device,
        mesh=mesh,
        in_specs=(P("dp", "seq"), P("dp", "seq", None), P(), P(), P(), P(), P(), P()),
        out_specs=(P("dp", "seq", None), P("seq", None)),
        check_vma=False,
    )
```

```python
import functools

import jax
import jax.numpy as jnp
from jax import lax
from jax.experimental import pallas as pl
from jax.experimental.pallas import tpu as pltpu
from jax.sharding import PartitionSpec as P

HEADS = 12
HEAD_DIM = 64
WINDOW = 512


EPSILON = 1e-05


def shifted(block, axis, distance):
    devices = range(lax.axis_size(axis))
    route = [(i - distance, i) for i in devices if i - distance in devices]
    return lax.ppermute(block, axis, route)


def rotate(values, positions):
    row_count = values.shape[0]
    shaped = values.reshape(row_count, -1, HEAD_DIM)
    middle = HEAD_DIM // 2
    frequency = 10000.0 ** (-2.0 * jnp.arange(middle, dtype=jnp.float32) / HEAD_DIM)
    angles = positions.astype(jnp.float32)[:, None] * frequency[None, :]
    cosine = jnp.cos(angles)[:, None, :]
    sine_part = jnp.sin(angles)[:, None, :]
    former = shaped[..., :middle]
    latter = shaped[..., middle:]
    turned = jnp.concatenate(
        [former * cosine - latter * sine_part, latter * cosine + former * sine_part], axis=-1
    )
    return turned.reshape(row_count, -1)


def unrotate(values, positions):
    row_count = values.shape[0]
    shaped = values.reshape(row_count, -1, HEAD_DIM)
    middle = HEAD_DIM // 2
    frequency = 10000.0 ** (-2.0 * jnp.arange(middle, dtype=jnp.float32) / HEAD_DIM)
    angles = positions.astype(jnp.float32)[:, None] * frequency[None, :]
    cosine = jnp.cos(angles)[:, None, :]
    sine_part = jnp.sin(angles)[:, None, :]
    former = shaped[..., :middle]
    latter = shaped[..., middle:]
    turned = jnp.concatenate(
        [former * cosine + latter * sine_part, latter * cosine - former * sine_part], axis=-1
    )
    return turned.reshape(row_count, -1)


def tdot(left, right):
    return lax.dot_general(
        left, right, (((0,), (0,)), ((), ())), preferred_element_type=jnp.float32
    )


def ndot(left, right):
    return lax.dot_general(
        left, right, (((1,), (1,)), ((), ())), preferred_element_type=jnp.float32
    )


def embed_rows(byte_ids, table):
    onehot = (byte_ids[:, None] == jnp.arange(table.shape[0], dtype=jnp.int32)[None, :]).astype(
        jnp.bfloat16
    )
    return jnp.dot(onehot, table, preferred_element_type=jnp.float32).astype(jnp.bfloat16)


def normalize(embedded):
    widened = embedded.astype(jnp.float32)
    inv_rms = lax.rsqrt(jnp.mean(widened * widened, axis=1, keepdims=True) + EPSILON)
    return (widened, inv_rms, (widened * inv_rms).astype(jnp.bfloat16))


def keys_values(normed, positions, w_key, w_value):
    key_rows = rotate(jnp.dot(normed, w_key, preferred_element_type=jnp.float32), positions).astype(
        jnp.bfloat16
    )
    value_rows = jnp.dot(normed, w_value, preferred_element_type=jnp.float32).astype(jnp.bfloat16)
    return (key_rows, value_rows)


def head_group(
    query_heads, key_heads, value_heads, grad_heads, group_window, own_pos, key_pos, score_scale
):
    distance = own_pos[:, None] - key_pos[None, :]
    allowed = (
        (distance[None] >= 0)
        & (distance[None] < group_window[:, None, None])
        & (key_pos[None, None, :] >= 0)
    )
    scores = (
        jnp.einsum("qhd,khd->hqk", query_heads, key_heads, preferred_element_type=jnp.float32)
        * score_scale
    )
    masked = jnp.where(allowed, scores, -1e30)
    row_max = jnp.max(masked, axis=-1, keepdims=True)
    weights = jnp.where(allowed, jnp.exp(masked - row_max), 0.0)
    probs = weights / jnp.sum(weights, axis=-1, keepdims=True)
    probs_b = probs.astype(jnp.bfloat16)
    attended = jnp.einsum(
        "hqk,khd->qhd", probs_b, value_heads, preferred_element_type=jnp.float32
    ).astype(jnp.bfloat16)
    grad_probs = jnp.einsum(
        "qhd,khd->hqk", grad_heads, value_heads, preferred_element_type=jnp.float32
    )
    row_term = jnp.sum(probs * grad_probs, axis=-1, keepdims=True)
    grad_scores = (probs * (grad_probs - row_term) * score_scale).astype(jnp.bfloat16)
    grad_query = jnp.einsum(
        "hqk,khd->qhd", grad_scores, key_heads, preferred_element_type=jnp.float32
    )
    grad_key = jnp.einsum(
        "hqk,qhd->khd", grad_scores, query_heads, preferred_element_type=jnp.float32
    )
    grad_value = jnp.einsum("hqk,qhd->khd", probs_b, grad_heads, preferred_element_type=jnp.float32)
    return (attended, grad_query, grad_key, grad_value)


def general_device(token_ids, cotangent, table, w_query, w_key, w_value, w_out, window):
    local_ids = token_ids[0]
    grad_out = cotangent[0]
    length = local_ids.shape[0]
    features = table.shape[1]
    tail_rows = min(length, WINDOW)
    reach_devs = -(-WINDOW // length)
    halo_rows = reach_devs * tail_rows
    offset = lax.axis_index("seq") * length
    own_pos = offset + jnp.arange(length, dtype=jnp.int32)
    halo_pos = offset - halo_rows + jnp.arange(halo_rows, dtype=jnp.int32)
    score_scale = HEAD_DIM ** (-0.5)
    embedded = embed_rows(local_ids, table)
    widened, inv_rms, normed = normalize(embedded)
    query = rotate(jnp.dot(normed, w_query, preferred_element_type=jnp.float32), own_pos).astype(
        jnp.bfloat16
    )
    key_own, value_own = keys_values(normed, own_pos, w_key, w_value)
    key_pieces = []
    value_pieces = []
    for hop_index in range(reach_devs):
        far_keys, far_values = shifted((key_own, value_own), "seq", hop_index + 1)
        key_pieces.insert(0, far_keys)
        value_pieces.insert(0, far_values)
    key_halo = jnp.concatenate(key_pieces, axis=0)
    value_halo = jnp.concatenate(value_pieces, axis=0)
    span_rows = halo_rows + length
    key_all = jnp.concatenate([key_halo, key_own], axis=0)
    value_all = jnp.concatenate([value_halo, value_own], axis=0)
    key_pos = jnp.concatenate([halo_pos, own_pos], axis=0)
    query_heads = query.reshape(length, HEADS, HEAD_DIM)
    key_heads = key_all.reshape(span_rows, HEADS, HEAD_DIM)
    value_heads = value_all.reshape(span_rows, HEADS, HEAD_DIM)
    grad_att = ndot(grad_out, w_out).astype(jnp.bfloat16)
    grad_heads = grad_att.reshape(length, HEADS, HEAD_DIM)
    group_size = 4
    attended_parts = []
    query_parts = []
    key_parts = []
    value_parts = []
    for group_index in range(HEADS // group_size):
        lower = group_index * group_size
        upper = lower + group_size
        outputs = head_group(
            query_heads[:, lower:upper],
            key_heads[:, lower:upper],
            value_heads[:, lower:upper],
            grad_heads[:, lower:upper],
            window[lower:upper],
            own_pos,
            key_pos,
            score_scale,
        )
        attended_parts.append(outputs[0])
        query_parts.append(outputs[1])
        key_parts.append(outputs[2])
        value_parts.append(outputs[3])
    attended = jnp.concatenate(attended_parts, axis=1).reshape(length, features)
    grad_query = jnp.concatenate(query_parts, axis=1).reshape(length, features)
    grad_key = jnp.concatenate(key_parts, axis=1).reshape(span_rows, features)
    grad_value = jnp.concatenate(value_parts, axis=1).reshape(span_rows, features)
    tail_keys = grad_key[:halo_rows].reshape(reach_devs, tail_rows, features)
    tail_values = grad_value[:halo_rows].reshape(reach_devs, tail_rows, features)
    back_keys = jnp.zeros((tail_rows, features), jnp.float32)
    back_values = jnp.zeros((tail_rows, features), jnp.float32)
    for hop_index in range(reach_devs):
        got_keys, got_values = shifted(
            (tail_keys[reach_devs - 1 - hop_index], tail_values[reach_devs - 1 - hop_index]),
            "seq",
            -(hop_index + 1),
        )
        back_keys = back_keys + got_keys
        back_values = back_values + got_values
    own_keys = grad_key[halo_rows:]
    own_values = grad_value[halo_rows:]
    own_keys = jnp.concatenate([own_keys[: length - tail_rows], own_keys + back_keys], axis=0)
    own_values = jnp.concatenate(
        [own_values[: length - tail_rows], own_values + back_values], axis=0
    )
    grad_q_lin = unrotate(grad_query, own_pos).astype(jnp.bfloat16)
    grad_k_lin = unrotate(own_keys, own_pos).astype(jnp.bfloat16)
    grad_v_lin = own_values.astype(jnp.bfloat16)
    grad_normed = ndot(grad_q_lin, w_query) + ndot(grad_k_lin, w_key) + ndot(grad_v_lin, w_value)
    scaled = widened * inv_rms
    grad_input = (
        inv_rms * (grad_normed - scaled * jnp.mean(grad_normed * scaled, axis=1, keepdims=True))
    ).astype(jnp.bfloat16)
    term = jnp.concatenate(
        [
            tdot(normed, grad_q_lin),
            tdot(normed, grad_k_lin),
            tdot(normed, grad_v_lin),
            tdot(attended, grad_out),
        ],
        axis=0,
    )
    shares = lax.psum_scatter(term.astype(jnp.bfloat16), "seq", scatter_dimension=0, tiled=True)
    weight_grads = lax.psum(shares, "dp").astype(jnp.float32)
    return (grad_input[None], weight_grads)


GROUPS = 4
GROUP_HEADS = HEADS // GROUPS
GROUP_COLS = GROUP_HEADS * HEAD_DIM
TILE = 256
TOKEN_ROWS = 16
HALF = HEAD_DIM // 2
VMEM_BYTES = 48 * 1024 * 1024


def key_span(query_tile):
    first = max(0, query_tile - WINDOW // TILE)
    return (first * TILE, (query_tile - first + 1) * TILE)


def probs_row(query_tile):
    return sum(key_span(earlier)[1] for earlier in range(query_tile))


def normed_table(table_ref):
    widened = table_ref[...].astype(jnp.float32)
    inv_rms = lax.rsqrt(jnp.mean(widened * widened, axis=1, keepdims=True) + EPSILON)
    return (widened * inv_rms).astype(jnp.bfloat16)


def onehot_columns(tokens, vocab):
    rows = lax.broadcasted_iota(jnp.int32, (vocab, tokens.shape[1]), 0)
    return (rows == tokens).astype(jnp.float32).astype(jnp.bfloat16)


def send_kernel(cotangent_ref, out_weights_ref, early_ref, late_ref):
    cotangent = cotangent_ref[...]
    grad_att = ndot(out_weights_ref[...], cotangent).astype(jnp.bfloat16)
    columns = late_ref.shape[2]
    for target in range(2 * GROUPS):
        group, side = divmod(target, 2)
        early_ref[target] = grad_att[group * GROUP_COLS : (group + 1) * GROUP_COLS]
        late_ref[target] = cotangent[:, side * columns : (side + 1) * columns]


def forward_kernel(
    meta_ref,
    tokens_ref,
    table_ref,
    weights_ref,
    cosine_ref,
    sine_ref,
    probs_ref,
    attended_ref,
    query_key_ref,
    key_t_ref,
    value_ref,
    zero_query_ref,
    value_t_ref,
    onehot_ref,
):
    head = pl.program_id(0)
    blocks, block = tokens_ref.shape
    length = blocks * block
    vocab = table_ref.shape[0]

    @pl.when(head == 0)
    def _():
        normed = normed_table(table_ref)
        lookup = jnp.dot(normed, weights_ref[...], preferred_element_type=jnp.float32).T
        upper = lookup.astype(jnp.bfloat16)
        lower = (lookup - upper.astype(jnp.float32)).astype(jnp.bfloat16)
        for source in range(blocks):
            onehot_ref[:, source * block : (source + 1) * block] = onehot_columns(
                tokens_ref[source : source + 1, :], vocab
            )
        onehot = onehot_ref[...]
        cosine = cosine_ref[...]
        sine_part = sine_ref[...]
        blank = jnp.zeros((HEAD_DIM, length), jnp.float32)

        def chosen(start):
            rows = slice(start, start + HEAD_DIM)
            return jnp.dot(upper[rows], onehot, preferred_element_type=jnp.float32) + jnp.dot(
                lower[rows], onehot, preferred_element_type=jnp.float32
            )

        def turned(columns):
            former = columns[:HALF]
            latter = columns[HALF:]
            return jnp.concatenate(
                [former * cosine - latter * sine_part, latter * cosine + former * sine_part], axis=0
            )

        for index in range(GROUP_HEADS):
            query = turned(chosen(index * HEAD_DIM)) * HEAD_DIM ** (-0.5)
            keys = turned(chosen(GROUP_COLS + index * HEAD_DIM))
            values = chosen(2 * GROUP_COLS + index * HEAD_DIM)
            query_key_ref[index] = jnp.concatenate([query, keys], axis=0).T.astype(jnp.bfloat16)
            value_ref[index] = jnp.concatenate([values, blank], axis=0).T.astype(jnp.bfloat16)
            zero_query_ref[index] = jnp.concatenate([blank, query], axis=0).astype(jnp.bfloat16)
            key_t_ref[index] = keys.astype(jnp.bfloat16)
            value_t_ref[index] = values.astype(jnp.bfloat16)

    width = meta_ref[head]
    distance = lax.broadcasted_iota(jnp.int32, (TILE, TILE), 1) - lax.broadcasted_iota(
        jnp.int32, (TILE, TILE), 0
    )
    for query_tile in range(length // TILE):
        first, count = key_span(query_tile)
        columns = slice(query_tile * TILE, (query_tile + 1) * TILE)
        scores = jnp.dot(
            query_key_ref[head, first : first + count, :],
            zero_query_ref[head, :, columns],
            preferred_element_type=jnp.float32,
        )
        masked = []
        for key_tile in range(count // TILE):
            offset = query_tile * TILE - first - key_tile * TILE
            allowed = distance < width - offset
            if offset == 0:
                allowed = allowed & (distance >= 0)
            part = scores[key_tile * TILE : (key_tile + 1) * TILE]
            masked.append(jnp.where(allowed, part, -1e30))
        masked = jnp.concatenate(masked, axis=0)
        row_max = jnp.max(masked, axis=0, keepdims=True)
        weights = jnp.exp(masked - row_max)
        probs = (weights * (1.0 / jnp.sum(weights, axis=0, keepdims=True))).astype(jnp.bfloat16)
        base = probs_row(query_tile)
        probs_ref[0, base : base + count, :] = probs
        attended_ref[head, :, columns] = jnp.dot(
            value_t_ref[head, :, first : first + count], probs, preferred_element_type=jnp.float32
        )


def backward_kernel(
    meta_ref,
    tokens_ref,
    early_ref,
    cosine_ref,
    sine_ref,
    probs_ref,
    attended_ref,
    query_key_ref,
    key_t_ref,
    value_ref,
    rows_ref,
    sums_ref,
    grad_att_ref,
    onehot_ref,
    grad_query_ref,
    grad_key_ref,
    grad_value_ref,
):
    head = pl.program_id(0)
    blocks, block = tokens_ref.shape
    length = blocks * block
    vocab = onehot_ref.shape[0]
    half_vocab = vocab // 2

    @pl.when(head == 0)
    def _():
        for source in range(blocks):
            lanes = slice(source * block, (source + 1) * block)
            onehot_ref[:, lanes] = onehot_columns(tokens_ref[source : source + 1, :], vocab)
            grad_att_ref[:, :, lanes] = early_ref[source].reshape(GROUP_HEADS, HEAD_DIM, block)

    wide_grad = grad_att_ref[head].astype(jnp.float32)
    blank = jnp.zeros((HEAD_DIM, length), jnp.float32)
    grad_blank = jnp.concatenate([wide_grad, blank], axis=0).astype(jnp.bfloat16)
    blank_grad = jnp.concatenate([blank, wide_grad], axis=0).T.astype(jnp.bfloat16)
    row_term = jnp.sum(attended_ref[head] * wide_grad, axis=0, keepdims=True)
    grad_key_ref[...] = jnp.zeros_like(grad_key_ref)
    grad_value_ref[...] = jnp.zeros_like(grad_value_ref)
    for query_tile in range(length // TILE):
        first, count = key_span(query_tile)
        columns = slice(query_tile * TILE, (query_tile + 1) * TILE)
        base = probs_row(query_tile)
        probs = probs_ref[0, base : base + count, :]
        grad_probs = jnp.dot(
            value_ref[head, first : first + count, :],
            grad_blank[:, columns],
            preferred_element_type=jnp.float32,
        )
        grad_scores = (probs.astype(jnp.float32) * (grad_probs - row_term[:, columns])).astype(
            jnp.bfloat16
        )
        grad_query_ref[:, columns] = jnp.dot(
            key_t_ref[head, :, first : first + count],
            grad_scores,
            preferred_element_type=jnp.float32,
        )
        grad_key_ref[first : first + count, :] += jnp.dot(
            grad_scores, query_key_ref[head, columns, :], preferred_element_type=jnp.float32
        )
        grad_value_ref[first : first + count, :] += jnp.dot(
            probs, blank_grad[columns, :], preferred_element_type=jnp.float32
        )
    cosine = cosine_ref[...]
    sine_part = sine_ref[...]

    def turned_back(columns):
        former = columns[:HALF]
        latter = columns[HALF:]
        return jnp.concatenate(
            [former * cosine + latter * sine_part, latter * cosine - former * sine_part], axis=0
        )

    lanes = lax.broadcasted_iota(jnp.int32, grad_key_ref.shape, 1)
    both = jnp.where(lanes < HEAD_DIM, grad_key_ref[...], grad_value_ref[...]).T
    grads = jnp.concatenate(
        [
            turned_back(grad_query_ref[...] * HEAD_DIM ** (-0.5)),
            turned_back(both[:HEAD_DIM]),
            both[HEAD_DIM:],
        ],
        axis=0,
    ).astype(jnp.bfloat16)
    sums = ndot(grads, onehot_ref[...]).astype(jnp.bfloat16)
    for matrix in range(3):
        rows = slice(matrix * HEAD_DIM, (matrix + 1) * HEAD_DIM)
        place = pl.ds(
            pl.multiple_of(matrix * GROUP_COLS + head * HEAD_DIM, HEAD_DIM), HEAD_DIM
        )
        for core in range(2):
            lane = core * half_vocab
            sums_ref[core, place, :] = sums[rows, lane : lane + half_vocab]
        for target in range(GROUPS):
            start = target * 2 * block
            even = grads[rows, start : start + block]
            odd = grads[rows, start + block : start + 2 * block]
            rows_ref[target, place, :] = jnp.where(meta_ref[GROUP_HEADS] == 0, even, odd)


def out_kernel(attended_ref, cotangent_ref, out_ref):
    attended = attended_ref[...].reshape(GROUP_COLS, -1).astype(jnp.bfloat16)
    total = jnp.dot(attended, cotangent_ref[...], preferred_element_type=jnp.float32)
    rows = total.shape[0] // 2
    lanes = out_ref.shape[2]
    for core in range(2):
        for chunk in range(total.shape[1] // lanes):
            out_ref[core, chunk * rows : (chunk + 1) * rows, :] = total[
                core * rows : (core + 1) * rows, chunk * lanes : (chunk + 1) * lanes
            ].astype(jnp.bfloat16)


def gather_kernel(meta_ref, kept_ref, s1, s2, s3, kept_out_ref, o2, o1, o0, mine_ref, other_ref):
    group = meta_ref[GROUP_HEADS + 1]
    rows = GROUP_COLS

    @pl.when(group < 3)
    def _():
        own = pl.multiple_of(group * rows, rows)
        mine_ref[pl.ds(own, rows), :] = kept_ref[pl.ds(own, rows), :]
        for turn, got in ((1, s1), (2, s2), (3, s3)):
            source = lax.rem(group - turn + GROUPS, GROUPS)
            mine_ref[pl.ds(pl.multiple_of(source * rows, rows), rows), :] = got[...]
        other_ref[...] = jnp.zeros_like(other_ref)

    @pl.when(group == 3)
    def _():
        size = kept_out_ref.shape[0]
        first = meta_ref[GROUP_HEADS] == 0
        mine_ref[0:size, :] = jnp.where(first, o0[...], o2[...])
        mine_ref[size : 2 * size, :] = jnp.where(first, o1[...], kept_out_ref[...])
        mine_ref[2 * size :, :] = jnp.zeros((GROUPS * rows - 2 * size, o0.shape[1]), jnp.bfloat16)
        other_ref[0:size, :] = jnp.where(first, o2[...], o0[...])
        other_ref[size:, :] = jnp.where(first, kept_out_ref[...], o1[...])


def input_kernel(
    meta_ref,
    tokens_ref,
    table_ref,
    query_ref,
    key_ref,
    value_ref,
    own_ref,
    first_ref,
    second_ref,
    third_ref,
    out_ref,
    columns_ref,
):
    group = meta_ref[GROUP_HEADS + 1]
    for turn, got in enumerate((own_ref, first_ref, second_ref, third_ref)):
        source = lax.rem(group - turn + GROUPS, GROUPS)
        for matrix in range(3):
            columns_ref[
                matrix, pl.ds(pl.multiple_of(source * GROUP_COLS, GROUP_COLS), GROUP_COLS), :
            ] = got[matrix * GROUP_COLS : (matrix + 1) * GROUP_COLS, :]
    onehot = onehot_columns(tokens_ref[...], table_ref.shape[0])
    embedded = tdot(onehot, table_ref[...])
    inv_rms = lax.rsqrt(jnp.mean(embedded * embedded, axis=1, keepdims=True) + EPSILON)
    grad_normed = None
    for matrix, weights in enumerate((query_ref, key_ref, value_ref)):
        columns = columns_ref[matrix].astype(jnp.float32).T.astype(jnp.bfloat16)
        part = ndot(columns, weights[...])
        grad_normed = part if grad_normed is None else grad_normed + part
    scaled = embedded * inv_rms
    out_ref[...] = (
        inv_rms * (grad_normed - scaled * jnp.mean(grad_normed * scaled, axis=1, keepdims=True))
    ).astype(jnp.bfloat16)


def weight_kernel(meta_ref, table_ref, mine_ref, other_ref, near_ref, far_ref, out_ref):
    side_rows = out_ref.shape[0]
    half_vocab = mine_ref.shape[1]
    first_core = meta_ref[GROUP_HEADS + 2] == 0

    @pl.when(meta_ref[GROUP_HEADS + 1] < 3)
    def _():
        normed = normed_table(table_ref)
        first = normed[:, :side_rows]
        second = normed[:, side_rows:]
        taken = jnp.where(meta_ref[GROUP_HEADS] == 0, first, second)
        upper = jnp.where(first_core, taken[:half_vocab], taken[half_vocab:])
        lower = jnp.where(first_core, taken[half_vocab:], taken[:half_vocab])
        total = None
        for part, sums_ref in ((upper, mine_ref), (lower, other_ref)):
            term = lax.dot_general(
                part,
                sums_ref[...],
                (((0,), (1,)), ((), ())),
                preferred_element_type=jnp.float32,
            )
            total = term if total is None else total + term
        out_ref[...] = total

    @pl.when(meta_ref[GROUP_HEADS + 1] == 3)
    def _():
        rows = GROUP_COLS // 2
        first_side = meta_ref[GROUP_HEADS] == 0
        for half in range(2):
            for chunk in range(3):
                place = slice((half * 3 + chunk) * rows, (half * 3 + chunk + 1) * rows)
                for core in range(2):
                    same = first_core == (core == 0)
                    own = jnp.where(same, mine_ref[place, :], other_ref[place, :])
                    crossed = jnp.where(same, near_ref[place, :], far_ref[place, :])
                    row = half * GROUP_COLS + core * rows
                    for side in range(2):
                        value = jnp.where(first_side == (side == 0), own, crossed)
                        start = (side * 3 + chunk) * half_vocab
                        out_ref[row : row + rows, start : start + half_vocab] = value.astype(
                            jnp.float32
                        )


def whole(shape):
    return pl.BlockSpec(shape, lambda *_: (0,) * len(shape))


def kernel_call(body, steps, operands, in_specs, outs, out_specs, scratch, flops, moved):
    return pl.pallas_call(
        body,
        grid=(steps,),
        in_specs=[pl.BlockSpec(memory_space=pltpu.SMEM)] + in_specs
        if operands[0].ndim == 1
        else in_specs,
        out_specs=out_specs,
        out_shape=outs,
        scratch_shapes=scratch,
        compiler_params=pltpu.CompilerParams(
            dimension_semantics=("arbitrary",), vmem_limit_bytes=VMEM_BYTES
        ),
        cost_estimate=pl.CostEstimate(flops=flops, bytes_accessed=moved, transcendentals=0),
    )(*operands)


def swapped(block, axis, bit):
    route = [(i, i ^ bit) for i in range(lax.axis_size(axis))]
    return lax.ppermute(block, axis, route)


def grouped_device(token_ids, cotangent, table, w_query, w_key, w_value, w_out, window):
    place = lax.axis_index("seq")
    core = lax.axis_index("dp") % 2
    group = place // 2
    side = place % 2
    block = token_ids.shape[1]
    features = table.shape[1]
    vocab = table.shape[0]
    blocks = lax.axis_size("seq")
    length = block * blocks
    tokens = lax.all_to_all(
        jnp.broadcast_to(token_ids, (blocks, block)), "seq", split_axis=0, concat_axis=0, tiled=True
    )
    early_shape = (blocks, GROUP_COLS, block)
    late_shape = (blocks, block, features // 2)
    early, late = kernel_call(
        send_kernel,
        1,
        (cotangent[0], w_out),
        [whole((block, features)), whole(w_out.shape)],
        [
            jax.ShapeDtypeStruct(early_shape, jnp.bfloat16),
            jax.ShapeDtypeStruct(late_shape, jnp.bfloat16),
        ],
        [whole(early_shape), whole(late_shape)],
        [],
        2 * 10**8,
        3 * 10**6,
    )
    early = lax.all_to_all(early, "seq", split_axis=0, concat_axis=0, tiled=True)
    late = lax.all_to_all(late, "seq", split_axis=0, concat_axis=0, tiled=True)
    start = group * GROUP_COLS
    weights = jnp.concatenate(
        [lax.dynamic_slice_in_dim(w, start, GROUP_COLS, 1) for w in (w_query, w_key, w_value)],
        axis=1,
    )
    meta = jnp.concatenate(
        [
            lax.dynamic_slice_in_dim(window, group * GROUP_HEADS, GROUP_HEADS, 0),
            jnp.stack([side, group, core]).astype(jnp.int32),
        ]
    )
    frequency = 10000.0 ** (-2.0 * jnp.arange(HALF, dtype=jnp.float32) / HEAD_DIM)
    angles = frequency[:, None] * jnp.arange(length, dtype=jnp.int32).astype(jnp.float32)[None, :]
    cosine = jnp.cos(angles)
    sine_part = jnp.sin(angles)
    heads_shape = (GROUP_HEADS, HEAD_DIM, length)
    rows_shape = (GROUP_HEADS, length, 2 * HEAD_DIM)
    probs_shape = (GROUP_HEADS, probs_row(length // TILE), TILE)
    probs_spec = pl.BlockSpec((1,) + probs_shape[1:], lambda h: (h, 0, 0))
    rows_out = (GROUPS, 3 * GROUP_COLS, block)
    sums_out = (2, 3 * GROUP_COLS, vocab // 2)
    probs, attended, query_key, key_t, value_rows = kernel_call(
        forward_kernel,
        GROUP_HEADS,
        (meta, tokens, table, weights, cosine, sine_part),
        [
            whole(tokens.shape),
            whole(table.shape),
            whole(weights.shape),
            whole(cosine.shape),
            whole(sine_part.shape),
        ],
        [
            jax.ShapeDtypeStruct(probs_shape, jnp.bfloat16),
            jax.ShapeDtypeStruct(heads_shape, jnp.float32),
            jax.ShapeDtypeStruct(rows_shape, jnp.bfloat16),
            jax.ShapeDtypeStruct(heads_shape, jnp.bfloat16),
            jax.ShapeDtypeStruct(rows_shape, jnp.bfloat16),
        ],
        [probs_spec, whole(heads_shape), whole(rows_shape), whole(heads_shape), whole(rows_shape)],
        [
            pltpu.VMEM((GROUP_HEADS, 2 * HEAD_DIM, length), jnp.bfloat16),
            pltpu.VMEM(heads_shape, jnp.bfloat16),
            pltpu.VMEM((vocab, length), jnp.bfloat16),
        ],
        4 * 10**9,
        8 * 10**6,
    )
    rows, sums = kernel_call(
        backward_kernel,
        GROUP_HEADS,
        (
            meta,
            tokens,
            early,
            cosine,
            sine_part,
            probs,
            attended,
            query_key,
            key_t,
            value_rows,
        ),
        [
            whole(tokens.shape),
            whole(early.shape),
            whole(cosine.shape),
            whole(sine_part.shape),
            probs_spec,
            whole(heads_shape),
            whole(rows_shape),
            whole(heads_shape),
            whole(rows_shape),
        ],
        [
            jax.ShapeDtypeStruct(rows_out, jnp.bfloat16),
            jax.ShapeDtypeStruct(sums_out, jnp.bfloat16),
        ],
        [whole(rows_out), whole(sums_out)],
        [
            pltpu.VMEM(heads_shape, jnp.bfloat16),
            pltpu.VMEM((vocab, length), jnp.bfloat16),
            pltpu.VMEM((HEAD_DIM, length), jnp.float32),
            pltpu.VMEM((length, 2 * HEAD_DIM), jnp.float32),
            pltpu.VMEM((length, 2 * HEAD_DIM), jnp.float32),
        ],
        4 * 10**9,
        8 * 10**6,
    )
    late = late.reshape(length, features // 2)
    out_shape = (2, 3 * GROUP_COLS // 2, 128)
    out_sums = kernel_call(
        out_kernel,
        1,
        (attended, late),
        [whole(attended.shape), whole(late.shape)],
        jax.ShapeDtypeStruct(out_shape, jnp.bfloat16),
        whole(out_shape),
        [],
        3 * 10**8,
        2 * 10**6,
    )

    def over_dp(halves):
        kept = lax.dynamic_index_in_dim(halves, core, 0, keepdims=False)
        given = lax.dynamic_index_in_dim(halves, 1 - core, 0, keepdims=False)
        kept = kept + swapped(given, "dp", 1)
        return kept + swapped(kept, "dp", 2)

    def turned_round(block, turn, goes):
        route = [
            (2 * z + x, 2 * ((z + turn) % GROUPS) + x)
            for z in range(GROUPS)
            for x in range(2)
            if goes((z + turn) % GROUPS)
        ]
        return lax.ppermute(block, "seq", route)

    turns = range(1, GROUPS)
    got_rows = [
        turned_round(
            lax.dynamic_index_in_dim(rows, (group + turn) % GROUPS, 0, keepdims=False),
            turn,
            lambda target: True,
        )
        for turn in turns
    ]
    own_rows = lax.dynamic_index_in_dim(rows, group, 0, keepdims=False)
    kept = over_dp(sums)
    kept_out = over_dp(out_sums)
    got = []
    for turn in turns:
        target = jnp.minimum((group + turn) % GROUPS, 2)
        piece = lax.dynamic_slice_in_dim(kept, target * GROUP_COLS, GROUP_COLS, 0)
        got.append(turned_round(piece, turn, lambda target: target != 3))
    got_out = [turned_round(kept_out, turn, lambda target: target == 3) for turn in turns]
    grad_input = kernel_call(
        input_kernel,
        1,
        (meta, token_ids, table, w_query, w_key, w_value, own_rows, *got_rows),
        [
            whole(token_ids.shape),
            whole(table.shape),
            whole(w_query.shape),
            whole(w_key.shape),
            whole(w_value.shape),
        ]
        + [whole(own_rows.shape)] * GROUPS,
        jax.ShapeDtypeStruct((block, features), jnp.bfloat16),
        whole((block, features)),
        [pltpu.VMEM((3, features, block), jnp.bfloat16)],
        10**9,
        5 * 10**6,
    )
    mine_shape = (GROUPS * GROUP_COLS, vocab // 2)
    other_shape = (2 * kept_out.shape[0], vocab // 2)
    mine, other = kernel_call(
        gather_kernel,
        1,
        (meta, kept, *got, kept_out, *got_out),
        [whole(piece.shape) for piece in (kept, *got, kept_out, *got_out)],
        [
            jax.ShapeDtypeStruct(mine_shape, jnp.bfloat16),
            jax.ShapeDtypeStruct(other_shape, jnp.bfloat16),
        ],
        [whole(mine_shape), whole(other_shape)],
        [],
        10**6,
        10**6,
    )
    sequences = lax.axis_size("dp")
    last = blocks - 2
    near = lax.ppermute(other, "seq", [(last, last + 1), (last + 1, last)])
    far = lax.ppermute(
        other,
        ("dp", "seq"),
        [
            (blocks * d + last + x, blocks * (d ^ 1) + last + 1 - x)
            for d in range(sequences)
            for x in range(2)
        ],
    )
    paired = swapped(mine, "dp", 1)
    weight_grads = kernel_call(
        weight_kernel,
        1,
        (meta, table, mine, paired, near, far),
        [
            whole(table.shape),
            whole(mine_shape),
            whole(mine_shape),
            whole(other_shape),
            whole(other_shape),
        ],
        jax.ShapeDtypeStruct((features // 2, features), jnp.float32),
        whole((features // 2, features)),
        [],
        10**9,
        5 * 10**6,
    )
    return (grad_input[None], weight_grads)


def on_device(token_ids, cotangent, table, w_query, w_key, w_value, w_out, window):
    fits = (
        lax.axis_size("seq") == 2 * GROUPS
        and lax.axis_size("dp") == 4
        and token_ids.shape == (1, 128)
        and table.shape == (256, HEADS * HEAD_DIM)
    )
    plan = grouped_device if fits else general_device
    return plan(token_ids, cotangent, table, w_query, w_key, w_value, w_out, window)


def solution(mesh):
    return jax.shard_map(
        on_device,
        mesh=mesh,
        in_specs=(P("dp", "seq"), P("dp", "seq", None), P(), P(), P(), P(), P(), P()),
        out_specs=(P("dp", "seq", None), P("seq", None)),
        check_vma=False,
    )
```

```python
import jax
import jax.numpy as jnp
import numpy as np
from jax import lax
from jax.experimental import pallas as pl
from jax.experimental.pallas import tpu as pltpu
from jax.sharding import PartitionSpec as P

HEADS = 12
HEAD_DIM = 64
WINDOW = 512


EPSILON = 1e-05


def shifted(block, axis, distance):
    devices = range(lax.axis_size(axis))
    route = [(i - distance, i) for i in devices if i - distance in devices]
    return lax.ppermute(block, axis, route)


def rotate(values, positions):
    row_count = values.shape[0]
    shaped = values.reshape(row_count, -1, HEAD_DIM)
    middle = HEAD_DIM // 2
    frequency = 10000.0 ** (-2.0 * jnp.arange(middle, dtype=jnp.float32) / HEAD_DIM)
    angles = positions.astype(jnp.float32)[:, None] * frequency[None, :]
    cosine = jnp.cos(angles)[:, None, :]
    sine_part = jnp.sin(angles)[:, None, :]
    former = shaped[..., :middle]
    latter = shaped[..., middle:]
    turned = jnp.concatenate(
        [former * cosine - latter * sine_part, latter * cosine + former * sine_part], axis=-1
    )
    return turned.reshape(row_count, -1)


def unrotate(values, positions):
    row_count = values.shape[0]
    shaped = values.reshape(row_count, -1, HEAD_DIM)
    middle = HEAD_DIM // 2
    frequency = 10000.0 ** (-2.0 * jnp.arange(middle, dtype=jnp.float32) / HEAD_DIM)
    angles = positions.astype(jnp.float32)[:, None] * frequency[None, :]
    cosine = jnp.cos(angles)[:, None, :]
    sine_part = jnp.sin(angles)[:, None, :]
    former = shaped[..., :middle]
    latter = shaped[..., middle:]
    turned = jnp.concatenate(
        [former * cosine + latter * sine_part, latter * cosine - former * sine_part], axis=-1
    )
    return turned.reshape(row_count, -1)


def tdot(left, right):
    return lax.dot_general(
        left, right, (((0,), (0,)), ((), ())), preferred_element_type=jnp.float32
    )


def ndot(left, right):
    return lax.dot_general(
        left, right, (((1,), (1,)), ((), ())), preferred_element_type=jnp.float32
    )


def embed_rows(byte_ids, table):
    onehot = (byte_ids[:, None] == jnp.arange(table.shape[0], dtype=jnp.int32)[None, :]).astype(
        jnp.bfloat16
    )
    return jnp.dot(onehot, table, preferred_element_type=jnp.float32).astype(jnp.bfloat16)


def normalize(embedded):
    widened = embedded.astype(jnp.float32)
    inv_rms = lax.rsqrt(jnp.mean(widened * widened, axis=1, keepdims=True) + EPSILON)
    return (widened, inv_rms, (widened * inv_rms).astype(jnp.bfloat16))


def keys_values(normed, positions, w_key, w_value):
    key_rows = rotate(jnp.dot(normed, w_key, preferred_element_type=jnp.float32), positions).astype(
        jnp.bfloat16
    )
    value_rows = jnp.dot(normed, w_value, preferred_element_type=jnp.float32).astype(jnp.bfloat16)
    return (key_rows, value_rows)


def head_group(
    query_heads, key_heads, value_heads, grad_heads, group_window, own_pos, key_pos, score_scale
):
    distance = own_pos[:, None] - key_pos[None, :]
    allowed = (
        (distance[None] >= 0)
        & (distance[None] < group_window[:, None, None])
        & (key_pos[None, None, :] >= 0)
    )
    scores = (
        jnp.einsum("qhd,khd->hqk", query_heads, key_heads, preferred_element_type=jnp.float32)
        * score_scale
    )
    masked = jnp.where(allowed, scores, -1e30)
    row_max = jnp.max(masked, axis=-1, keepdims=True)
    weights = jnp.where(allowed, jnp.exp(masked - row_max), 0.0)
    probs = weights / jnp.sum(weights, axis=-1, keepdims=True)
    probs_b = probs.astype(jnp.bfloat16)
    attended = jnp.einsum(
        "hqk,khd->qhd", probs_b, value_heads, preferred_element_type=jnp.float32
    ).astype(jnp.bfloat16)
    grad_probs = jnp.einsum(
        "qhd,khd->hqk", grad_heads, value_heads, preferred_element_type=jnp.float32
    )
    row_term = jnp.sum(probs * grad_probs, axis=-1, keepdims=True)
    grad_scores = (probs * (grad_probs - row_term) * score_scale).astype(jnp.bfloat16)
    grad_query = jnp.einsum(
        "hqk,khd->qhd", grad_scores, key_heads, preferred_element_type=jnp.float32
    )
    grad_key = jnp.einsum(
        "hqk,qhd->khd", grad_scores, query_heads, preferred_element_type=jnp.float32
    )
    grad_value = jnp.einsum("hqk,qhd->khd", probs_b, grad_heads, preferred_element_type=jnp.float32)
    return (attended, grad_query, grad_key, grad_value)


def general_device(token_ids, cotangent, table, w_query, w_key, w_value, w_out, window):
    local_ids = token_ids[0]
    grad_out = cotangent[0]
    length = local_ids.shape[0]
    features = table.shape[1]
    tail_rows = min(length, WINDOW)
    reach_devs = -(-WINDOW // length)
    halo_rows = reach_devs * tail_rows
    offset = lax.axis_index("seq") * length
    own_pos = offset + jnp.arange(length, dtype=jnp.int32)
    halo_pos = offset - halo_rows + jnp.arange(halo_rows, dtype=jnp.int32)
    score_scale = HEAD_DIM ** (-0.5)
    embedded = embed_rows(local_ids, table)
    widened, inv_rms, normed = normalize(embedded)
    query = rotate(jnp.dot(normed, w_query, preferred_element_type=jnp.float32), own_pos).astype(
        jnp.bfloat16
    )
    key_own, value_own = keys_values(normed, own_pos, w_key, w_value)
    key_pieces = []
    value_pieces = []
    for hop_index in range(reach_devs):
        far_keys, far_values = shifted((key_own, value_own), "seq", hop_index + 1)
        key_pieces.insert(0, far_keys)
        value_pieces.insert(0, far_values)
    key_halo = jnp.concatenate(key_pieces, axis=0)
    value_halo = jnp.concatenate(value_pieces, axis=0)
    span_rows = halo_rows + length
    key_all = jnp.concatenate([key_halo, key_own], axis=0)
    value_all = jnp.concatenate([value_halo, value_own], axis=0)
    key_pos = jnp.concatenate([halo_pos, own_pos], axis=0)
    query_heads = query.reshape(length, HEADS, HEAD_DIM)
    key_heads = key_all.reshape(span_rows, HEADS, HEAD_DIM)
    value_heads = value_all.reshape(span_rows, HEADS, HEAD_DIM)
    grad_att = ndot(grad_out, w_out).astype(jnp.bfloat16)
    grad_heads = grad_att.reshape(length, HEADS, HEAD_DIM)
    group_size = 4
    attended_parts = []
    query_parts = []
    key_parts = []
    value_parts = []
    for group_index in range(HEADS // group_size):
        lower = group_index * group_size
        upper = lower + group_size
        outputs = head_group(
            query_heads[:, lower:upper],
            key_heads[:, lower:upper],
            value_heads[:, lower:upper],
            grad_heads[:, lower:upper],
            window[lower:upper],
            own_pos,
            key_pos,
            score_scale,
        )
        attended_parts.append(outputs[0])
        query_parts.append(outputs[1])
        key_parts.append(outputs[2])
        value_parts.append(outputs[3])
    attended = jnp.concatenate(attended_parts, axis=1).reshape(length, features)
    grad_query = jnp.concatenate(query_parts, axis=1).reshape(length, features)
    grad_key = jnp.concatenate(key_parts, axis=1).reshape(span_rows, features)
    grad_value = jnp.concatenate(value_parts, axis=1).reshape(span_rows, features)
    tail_keys = grad_key[:halo_rows].reshape(reach_devs, tail_rows, features)
    tail_values = grad_value[:halo_rows].reshape(reach_devs, tail_rows, features)
    back_keys = jnp.zeros((tail_rows, features), jnp.float32)
    back_values = jnp.zeros((tail_rows, features), jnp.float32)
    for hop_index in range(reach_devs):
        got_keys, got_values = shifted(
            (tail_keys[reach_devs - 1 - hop_index], tail_values[reach_devs - 1 - hop_index]),
            "seq",
            -(hop_index + 1),
        )
        back_keys = back_keys + got_keys
        back_values = back_values + got_values
    own_keys = grad_key[halo_rows:]
    own_values = grad_value[halo_rows:]
    own_keys = jnp.concatenate([own_keys[: length - tail_rows], own_keys + back_keys], axis=0)
    own_values = jnp.concatenate(
        [own_values[: length - tail_rows], own_values + back_values], axis=0
    )
    grad_q_lin = unrotate(grad_query, own_pos).astype(jnp.bfloat16)
    grad_k_lin = unrotate(own_keys, own_pos).astype(jnp.bfloat16)
    grad_v_lin = own_values.astype(jnp.bfloat16)
    grad_normed = ndot(grad_q_lin, w_query) + ndot(grad_k_lin, w_key) + ndot(grad_v_lin, w_value)
    scaled = widened * inv_rms
    grad_input = (
        inv_rms * (grad_normed - scaled * jnp.mean(grad_normed * scaled, axis=1, keepdims=True))
    ).astype(jnp.bfloat16)
    term = jnp.concatenate(
        [
            tdot(normed, grad_q_lin),
            tdot(normed, grad_k_lin),
            tdot(normed, grad_v_lin),
            tdot(attended, grad_out),
        ],
        axis=0,
    )
    shares = lax.psum_scatter(term.astype(jnp.bfloat16), "seq", scatter_dimension=0, tiled=True)
    weight_grads = lax.psum(shares, "dp").astype(jnp.float32)
    return (grad_input[None], weight_grads)


GROUPS = 4
GROUP_HEADS = HEADS // GROUPS
GROUP_COLS = GROUP_HEADS * HEAD_DIM
TILE = 256
TOKEN_ROWS = 16
HALF = HEAD_DIM // 2
VMEM_BYTES = 48 * 1024 * 1024


def key_span(query_tile):
    first = max(0, query_tile - WINDOW // TILE)
    return (first * TILE, (query_tile - first + 1) * TILE)


def normed_table(table_ref):
    widened = table_ref[...].astype(jnp.float32)
    inv_rms = lax.rsqrt(jnp.mean(widened * widened, axis=1, keepdims=True) + EPSILON)
    return (widened * inv_rms).astype(jnp.bfloat16)


def onehot_columns(tokens, vocab):
    rows = lax.broadcasted_iota(jnp.int32, (vocab, tokens.shape[1]), 0)
    return (rows == tokens).astype(jnp.float32).astype(jnp.bfloat16)


def send_kernel(tokens_ref, cotangent_ref, out_weights_ref, early_ref):
    grad_att = ndot(out_weights_ref[...], cotangent_ref[...]).astype(jnp.bfloat16)
    block = tokens_ref.shape[1]
    tokens = jnp.broadcast_to(tokens_ref[...].astype(jnp.float32), (TOKEN_ROWS, block)).astype(
        jnp.bfloat16
    )
    for target in range(2 * GROUPS):
        group = target // 2
        early_ref[target, :GROUP_COLS, :] = grad_att[
            group * GROUP_COLS : (group + 1) * GROUP_COLS
        ]
        early_ref[target, GROUP_COLS:, :] = tokens


def prepare_kernel(
    meta_ref,
    cotangent_ref,
    table_ref,
    query_ref,
    key_ref,
    value_ref,
    late_ref,
    lookup_ref,
    normed_ref,
    columns_ref,
):
    columns = late_ref.shape[2]
    for target in range(2 * GROUPS):
        side = target % 2
        late_ref[target] = cotangent_ref[:, side * columns : (side + 1) * columns]
    normed = normed_table(table_ref)
    half = normed.shape[1] // 2
    normed_ref[...] = jnp.where(meta_ref[GROUP_HEADS] == 0, normed[:, :half], normed[:, half:])
    place = pl.ds(pl.multiple_of(meta_ref[GROUP_HEADS + 1] * GROUP_COLS, GROUP_COLS), GROUP_COLS)
    for matrix, weights_ref in enumerate((query_ref, key_ref, value_ref)):
        columns_ref[...] = jnp.dot(
            normed, weights_ref[...], preferred_element_type=jnp.float32
        ).T
        mine = columns_ref[place, :]
        upper = mine.astype(jnp.bfloat16)
        rows = slice(matrix * GROUP_COLS, (matrix + 1) * GROUP_COLS)
        lookup_ref[0, rows, :] = upper
        lookup_ref[1, rows, :] = (mine - upper.astype(jnp.float32)).astype(jnp.bfloat16)


def attention_kernel(
    meta_ref,
    early_ref,
    lookup_ref,
    cosine_ref,
    sine_ref,
    rows_ref,
    sums_ref,
    attended_ref,
    query_key_ref,
    zero_query_ref,
    key_t_ref,
    value_ref,
    value_t_ref,
    grad_att_ref,
    onehot_ref,
    grad_query_ref,
    grad_key_ref,
    grad_value_ref,
):
    head = pl.program_id(0)
    blocks, _, block = early_ref.shape
    length = blocks * block
    vocab = lookup_ref.shape[2]
    half_vocab = vocab // 2
    cosine = cosine_ref[...]
    sine_part = sine_ref[...]
    blank = jnp.zeros((HEAD_DIM, length), jnp.float32)

    @pl.when(head == 0)
    def _():
        for source in range(blocks):
            lanes = slice(source * block, (source + 1) * block)
            tokens = early_ref[source, GROUP_COLS : GROUP_COLS + TOKEN_ROWS, :]
            tokens = tokens.astype(jnp.float32)[:1].astype(jnp.int32)
            onehot_ref[:, lanes] = onehot_columns(tokens, vocab)
            grad_att_ref[:, :, lanes] = early_ref[source, :GROUP_COLS, :].reshape(
                GROUP_HEADS, HEAD_DIM, block
            )
        onehot = onehot_ref[...]

        def chosen(start):
            rows = slice(start, start + HEAD_DIM)
            return jnp.dot(
                lookup_ref[0, rows, :], onehot, preferred_element_type=jnp.float32
            ) + jnp.dot(lookup_ref[1, rows, :], onehot, preferred_element_type=jnp.float32)

        def turned(columns):
            former = columns[:HALF]
            latter = columns[HALF:]
            return jnp.concatenate(
                [former * cosine - latter * sine_part, latter * cosine + former * sine_part], axis=0
            )

        for index in range(GROUP_HEADS):
            query = turned(chosen(index * HEAD_DIM)) * HEAD_DIM ** (-0.5)
            keys = turned(chosen(GROUP_COLS + index * HEAD_DIM))
            values = chosen(2 * GROUP_COLS + index * HEAD_DIM)
            query_key_ref[index] = jnp.concatenate([query, keys], axis=0).T.astype(jnp.bfloat16)
            value_ref[index] = jnp.concatenate([values, blank], axis=0).T.astype(jnp.bfloat16)
            zero_query_ref[index] = jnp.concatenate([blank, query], axis=0).astype(jnp.bfloat16)
            key_t_ref[index] = keys.astype(jnp.bfloat16)
            value_t_ref[index] = values.astype(jnp.bfloat16)

    width = meta_ref[head]
    grad_att = grad_att_ref[head]
    wide_grad = grad_att.astype(jnp.float32)
    grad_blank = jnp.concatenate([wide_grad, blank], axis=0).astype(jnp.bfloat16)
    blank_grad = jnp.concatenate([blank, wide_grad], axis=0).T.astype(jnp.bfloat16)
    grad_key_ref[...] = jnp.zeros_like(grad_key_ref)
    grad_value_ref[...] = jnp.zeros_like(grad_value_ref)
    distance = lax.broadcasted_iota(jnp.int32, (TILE, TILE), 1) - lax.broadcasted_iota(
        jnp.int32, (TILE, TILE), 0
    )
    for query_tile in range(length // TILE):
        first, count = key_span(query_tile)
        columns = slice(query_tile * TILE, (query_tile + 1) * TILE)
        scores = jnp.dot(
            query_key_ref[head, first : first + count, :],
            zero_query_ref[head, :, columns],
            preferred_element_type=jnp.float32,
        )
        masked = []
        for key_tile in range(count // TILE):
            offset = query_tile * TILE - first - key_tile * TILE
            allowed = distance < width - offset
            if offset == 0:
                allowed = allowed & (distance >= 0)
            part = scores[key_tile * TILE : (key_tile + 1) * TILE]
            masked.append(jnp.where(allowed, part, -1e30))
        masked = jnp.concatenate(masked, axis=0)
        row_max = jnp.max(masked, axis=0, keepdims=True)
        weights = jnp.exp(masked - row_max)
        probs = weights * (1.0 / jnp.sum(weights, axis=0, keepdims=True))
        rounded = probs.astype(jnp.bfloat16)
        attended = jnp.dot(
            value_t_ref[head, :, first : first + count], rounded, preferred_element_type=jnp.float32
        )
        attended_ref[pl.ds(pl.multiple_of(head * HEAD_DIM, HEAD_DIM), HEAD_DIM), columns] = (
            attended.astype(jnp.bfloat16)
        )
        row_term = jnp.sum(attended * wide_grad[:, columns], axis=0, keepdims=True)
        grad_probs = jnp.dot(
            value_ref[head, first : first + count, :],
            grad_blank[:, columns],
            preferred_element_type=jnp.float32,
        )
        grad_scores = (probs * (grad_probs - row_term)).astype(jnp.bfloat16)
        grad_query_ref[:, columns] = jnp.dot(
            key_t_ref[head, :, first : first + count],
            grad_scores,
            preferred_element_type=jnp.float32,
        )
        grad_key_ref[first : first + count, :] += jnp.dot(
            grad_scores, query_key_ref[head, columns, :], preferred_element_type=jnp.float32
        )
        grad_value_ref[first : first + count, :] += jnp.dot(
            rounded, blank_grad[columns, :], preferred_element_type=jnp.float32
        )

    def turned_back(columns):
        former = columns[:HALF]
        latter = columns[HALF:]
        return jnp.concatenate(
            [former * cosine + latter * sine_part, latter * cosine - former * sine_part], axis=0
        )

    lanes = lax.broadcasted_iota(jnp.int32, grad_key_ref.shape, 1)
    both = jnp.where(lanes < HEAD_DIM, grad_key_ref[...], grad_value_ref[...]).T
    grads = jnp.concatenate(
        [
            turned_back(grad_query_ref[...] * HEAD_DIM ** (-0.5)),
            turned_back(both[:HEAD_DIM]),
            both[HEAD_DIM:],
        ],
        axis=0,
    ).astype(jnp.bfloat16)
    sums = ndot(grads, onehot_ref[...]).astype(jnp.bfloat16)
    for matrix in range(3):
        rows = slice(matrix * HEAD_DIM, (matrix + 1) * HEAD_DIM)
        place = pl.ds(
            pl.multiple_of(matrix * GROUP_COLS + head * HEAD_DIM, HEAD_DIM), HEAD_DIM
        )
        for core in range(2):
            lane = core * half_vocab
            sums_ref[core, place, :] = sums[rows, lane : lane + half_vocab]
        for target in range(GROUPS):
            start = target * 2 * block
            even = grads[rows, start : start + block]
            odd = grads[rows, start + block : start + 2 * block]
            rows_ref[target, place, :] = jnp.where(meta_ref[GROUP_HEADS] == 0, even, odd)


def out_kernel(meta_ref, attended_ref, cotangent_ref, sums_ref, keep_ref, give_ref):
    total = jnp.dot(attended_ref[...], cotangent_ref[...], preferred_element_type=jnp.float32)
    rows = total.shape[0] // 2
    base = sums_ref.shape[1]
    lanes = keep_ref.shape[1]
    first = meta_ref[GROUP_HEADS + 2] == 0
    keep_ref[:base, :] = jnp.where(first, sums_ref[0], sums_ref[1])
    give_ref[:base, :] = jnp.where(first, sums_ref[1], sums_ref[0])
    for chunk in range(total.shape[1] // lanes):
        part = total[:, chunk * lanes : (chunk + 1) * lanes]
        place = slice(base + chunk * rows, base + (chunk + 1) * rows)
        keep_ref[place, :] = jnp.where(first, part[:rows], part[rows:]).astype(jnp.bfloat16)
        give_ref[place, :] = jnp.where(first, part[rows:], part[:rows]).astype(jnp.bfloat16)


def combine_kernel(here_ref, there_ref, after_ref, out_ref):
    del after_ref
    rows = GROUP_COLS
    size = out_ref.shape[1]
    blank = jnp.zeros((size - rows, out_ref.shape[2]), jnp.bfloat16)
    for matrix in range(3):
        place = slice(matrix * rows, (matrix + 1) * rows)
        out_ref[matrix, :rows, :] = here_ref[place, :] + there_ref[place, :]
        out_ref[matrix, rows:, :] = blank
    out_ref[3] = here_ref[3 * rows :, :] + there_ref[3 * rows :, :]


def gather_kernel(meta_ref, got_ref, mine_ref, other_ref):
    rows = GROUP_COLS
    size = got_ref.shape[1]

    @pl.when(meta_ref[GROUP_HEADS + 1] < 3)
    def _():
        for group in range(GROUPS):
            mine_ref[group * rows : (group + 1) * rows, :] = got_ref[group, :rows, :]
        other_ref[...] = jnp.zeros_like(other_ref)

    @pl.when(meta_ref[GROUP_HEADS + 1] == 3)
    def _():
        first = meta_ref[GROUP_HEADS] == 0
        for part in range(2):
            place = slice(part * size, (part + 1) * size)
            mine_ref[place, :] = jnp.where(first, got_ref[part], got_ref[2 + part])
            other_ref[place, :] = jnp.where(first, got_ref[2 + part], got_ref[part])
        tail = mine_ref.shape[0] - 2 * size
        mine_ref[2 * size :, :] = jnp.zeros((tail, mine_ref.shape[1]), jnp.bfloat16)


def input_kernel(tokens_ref, table_ref, query_ref, key_ref, value_ref, rows_ref, out_ref):
    vocab = table_ref.shape[0]
    onehot = onehot_columns(tokens_ref[...], vocab)
    embedded = tdot(onehot, table_ref[...])
    inv_rms = lax.rsqrt(jnp.mean(embedded * embedded, axis=1, keepdims=True) + EPSILON)
    grad_normed = None
    for matrix, weights in enumerate((query_ref, key_ref, value_ref)):
        columns = jnp.concatenate(
            [
                rows_ref[group, matrix * GROUP_COLS : (matrix + 1) * GROUP_COLS, :]
                for group in range(GROUPS)
            ],
            axis=0,
        )
        part = ndot(columns.astype(jnp.float32).T.astype(jnp.bfloat16), weights[...])
        grad_normed = part if grad_normed is None else grad_normed + part
    scaled = embedded * inv_rms
    out_ref[...] = (
        inv_rms * (grad_normed - scaled * jnp.mean(grad_normed * scaled, axis=1, keepdims=True))
    ).astype(jnp.bfloat16)


def weight_kernel(meta_ref, normed_ref, mine_ref, other_ref, near_ref, far_ref, out_ref):
    half_vocab = mine_ref.shape[1]
    first_core = meta_ref[GROUP_HEADS + 2] == 0

    @pl.when(meta_ref[GROUP_HEADS + 1] < 3)
    def _():
        first = normed_ref[:half_vocab, :]
        second = normed_ref[half_vocab:, :]
        upper = jnp.where(first_core, first, second)
        lower = jnp.where(first_core, second, first)
        total = None
        for part, sums_ref in ((upper, mine_ref), (lower, other_ref)):
            term = lax.dot_general(
                part,
                sums_ref[...],
                (((0,), (1,)), ((), ())),
                preferred_element_type=jnp.float32,
            )
            total = term if total is None else total + term
        out_ref[...] = total

    @pl.when(meta_ref[GROUP_HEADS + 1] == 3)
    def _():
        rows = GROUP_COLS // 2
        first_side = meta_ref[GROUP_HEADS] == 0
        for half in range(2):
            for chunk in range(3):
                place = slice((half * 3 + chunk) * rows, (half * 3 + chunk + 1) * rows)
                for core in range(2):
                    same = first_core == (core == 0)
                    own = jnp.where(same, mine_ref[place, :], other_ref[place, :])
                    crossed = jnp.where(same, near_ref[place, :], far_ref[place, :])
                    row = half * GROUP_COLS + core * rows
                    for side in range(2):
                        value = jnp.where(first_side == (side == 0), own, crossed)
                        start = (side * 3 + chunk) * half_vocab
                        out_ref[row : row + rows, start : start + half_vocab] = value.astype(
                            jnp.float32
                        )


def whole(shape):
    return pl.BlockSpec(shape, lambda *_: (0,) * len(shape))


def swapped(block, axis, bit):
    route = [(i, i ^ bit) for i in range(lax.axis_size(axis))]
    return lax.ppermute(block, axis, route)


def rope_table(length):
    frequency = (10000.0 ** (-2.0 * np.arange(HALF, dtype=np.float32) / HEAD_DIM)).astype(np.float32)
    angles = frequency[:, None] * np.arange(length, dtype=np.float32)[None, :]
    angles = angles.astype(np.float64)
    return (
        jnp.asarray(np.cos(angles).astype(np.float32)),
        jnp.asarray(np.sin(angles).astype(np.float32)),
    )


def grouped_device(token_ids, cotangent, table, w_query, w_key, w_value, w_out, window):
    place = lax.axis_index("seq")
    core = lax.axis_index("dp") % 2
    group = place // 2
    side = place % 2
    block = token_ids.shape[1]
    features = table.shape[1]
    vocab = table.shape[0]
    blocks = lax.axis_size("seq")
    length = block * blocks
    grad_out = cotangent[0]
    meta = jnp.concatenate(
        [
            lax.dynamic_slice_in_dim(window, group * GROUP_HEADS, GROUP_HEADS, 0),
            jnp.stack([side, group, core]).astype(jnp.int32),
        ]
    )
    cosine, sine_part = rope_table(length)

    def call(body, operands, outs, scratch=(), steps=1, flops=10**8, moved=10**6, loose=0):
        spaces = [whole(operand.shape) for operand in operands]
        for index in range(loose):
            spaces[-1 - index] = pl.BlockSpec(memory_space=pl.ANY)
        if operands[0].ndim == 1:
            spaces[0] = pl.BlockSpec(memory_space=pltpu.SMEM)
        return pl.pallas_call(
            body,
            grid=(steps,),
            in_specs=spaces,
            out_specs=[whole(shape) for shape, _ in outs],
            out_shape=[jax.ShapeDtypeStruct(shape, dtype) for shape, dtype in outs],
            scratch_shapes=list(scratch),
            compiler_params=pltpu.CompilerParams(
                dimension_semantics=("arbitrary",), vmem_limit_bytes=VMEM_BYTES
            ),
            cost_estimate=pl.CostEstimate(flops=flops, bytes_accessed=moved, transcendentals=0),
        )(*operands)

    half = jnp.bfloat16
    (early,) = call(
        send_kernel,
        (token_ids, grad_out, w_out),
        [((blocks, GROUP_COLS + TOKEN_ROWS, block), half)],
    )
    early = lax.all_to_all(early, "seq", split_axis=0, concat_axis=0, tiled=True)
    late, lookup, normed = call(
        prepare_kernel,
        (meta, grad_out, table, w_query, w_key, w_value),
        [
            ((blocks, block, features // 2), half),
            ((2, 3 * GROUP_COLS, vocab), half),
            ((vocab, features // 2), half),
        ],
        [pltpu.VMEM((features, vocab), jnp.float32)],
        flops=10**9,
        moved=5 * 10**6,
    )
    late = lax.all_to_all(late, "seq", split_axis=0, concat_axis=0, tiled=True)
    heads_shape = (GROUP_HEADS, HEAD_DIM, length)
    rows_shape = (GROUP_HEADS, length, 2 * HEAD_DIM)
    rows, sums, attended = call(
        attention_kernel,
        (meta, early, lookup, cosine, sine_part),
        [
            ((GROUPS, 3 * GROUP_COLS, block), half),
            ((2, 3 * GROUP_COLS, vocab // 2), half),
            ((GROUP_COLS, length), half),
        ],
        [
            pltpu.VMEM(rows_shape, half),
            pltpu.VMEM((GROUP_HEADS, 2 * HEAD_DIM, length), half),
            pltpu.VMEM(heads_shape, half),
            pltpu.VMEM(rows_shape, half),
            pltpu.VMEM(heads_shape, half),
            pltpu.VMEM(heads_shape, half),
            pltpu.VMEM((vocab, length), half),
            pltpu.VMEM((HEAD_DIM, length), jnp.float32),
            pltpu.VMEM((length, 2 * HEAD_DIM), jnp.float32),
            pltpu.VMEM((length, 2 * HEAD_DIM), jnp.float32),
        ],
        steps=GROUP_HEADS,
        flops=8 * 10**9,
        moved=8 * 10**6,
    )
    planes = [[2 * z + x for z in range(GROUPS)] for x in range(2)]

    def over_plane(chunks):
        return lax.all_to_all(
            chunks, "seq", split_axis=0, concat_axis=0, axis_index_groups=planes, tiled=True
        )

    got_rows = over_plane(rows)
    lanes = vocab // 2
    out_rows = 3 * GROUP_COLS // 2
    packed = 3 * GROUP_COLS + out_rows
    keep, give = call(
        out_kernel,
        (meta, attended, late.reshape(length, features // 2), sums),
        [((packed, lanes), half)] * 2,
    )
    here = keep + swapped(give, "dp", 1)
    there = swapped(here, "dp", 2)
    (chunks,) = call(
        combine_kernel, (here, there, got_rows), [((GROUPS, out_rows, lanes), half)], loose=1
    )
    mine, other = call(
        gather_kernel,
        (meta, over_plane(chunks)),
        [((GROUPS * GROUP_COLS, lanes), half), ((2 * out_rows, lanes), half)],
    )
    (grad_input,) = call(
        input_kernel,
        (token_ids, table, w_query, w_key, w_value, got_rows),
        [((block, features), half)],
        flops=10**9,
        moved=5 * 10**6,
    )
    last = blocks - 2
    paired = swapped(mine, "dp", 1)
    near = lax.ppermute(other, "seq", [(last, last + 1), (last + 1, last)])
    far = lax.ppermute(
        other,
        ("dp", "seq"),
        [
            (blocks * d + last + x, blocks * (d ^ 1) + last + 1 - x)
            for d in range(lax.axis_size("dp"))
            for x in range(2)
        ],
    )
    (weight_grads,) = call(
        weight_kernel,
        (meta, normed, mine, paired, near, far),
        [((features // 2, features), jnp.float32)],
        flops=10**9,
        moved=5 * 10**6,
    )
    return (grad_input[None], weight_grads)


def on_device(token_ids, cotangent, table, w_query, w_key, w_value, w_out, window):
    fits = (
        lax.axis_size("seq") == 2 * GROUPS
        and lax.axis_size("dp") == 4
        and token_ids.shape == (1, 128)
        and table.shape == (256, HEADS * HEAD_DIM)
    )
    plan = grouped_device if fits else general_device
    return plan(token_ids, cotangent, table, w_query, w_key, w_value, w_out, window)


def solution(mesh):
    return jax.shard_map(
        on_device,
        mesh=mesh,
        in_specs=(P("dp", "seq"), P("dp", "seq", None), P(), P(), P(), P(), P(), P()),
        out_specs=(P("dp", "seq", None), P("seq", None)),
        check_vma=False,
    )
```

```python
import jax
import jax.numpy as jnp
import numpy as np
from jax import lax
from jax.experimental import pallas as pl
from jax.experimental.pallas import tpu as pltpu
from jax.sharding import PartitionSpec as P

HEADS = 12
HEAD_DIM = 64
WINDOW = 512


EPSILON = 1e-05


def shifted(block, axis, distance):
    devices = range(lax.axis_size(axis))
    route = [(i - distance, i) for i in devices if i - distance in devices]
    return lax.ppermute(block, axis, route)


def rotate(values, positions):
    row_count = values.shape[0]
    shaped = values.reshape(row_count, -1, HEAD_DIM)
    middle = HEAD_DIM // 2
    frequency = 10000.0 ** (-2.0 * jnp.arange(middle, dtype=jnp.float32) / HEAD_DIM)
    angles = positions.astype(jnp.float32)[:, None] * frequency[None, :]
    cosine = jnp.cos(angles)[:, None, :]
    sine_part = jnp.sin(angles)[:, None, :]
    former = shaped[..., :middle]
    latter = shaped[..., middle:]
    turned = jnp.concatenate(
        [former * cosine - latter * sine_part, latter * cosine + former * sine_part], axis=-1
    )
    return turned.reshape(row_count, -1)


def unrotate(values, positions):
    row_count = values.shape[0]
    shaped = values.reshape(row_count, -1, HEAD_DIM)
    middle = HEAD_DIM // 2
    frequency = 10000.0 ** (-2.0 * jnp.arange(middle, dtype=jnp.float32) / HEAD_DIM)
    angles = positions.astype(jnp.float32)[:, None] * frequency[None, :]
    cosine = jnp.cos(angles)[:, None, :]
    sine_part = jnp.sin(angles)[:, None, :]
    former = shaped[..., :middle]
    latter = shaped[..., middle:]
    turned = jnp.concatenate(
        [former * cosine + latter * sine_part, latter * cosine - former * sine_part], axis=-1
    )
    return turned.reshape(row_count, -1)


def tdot(left, right):
    return lax.dot_general(
        left, right, (((0,), (0,)), ((), ())), preferred_element_type=jnp.float32
    )


def ndot(left, right):
    return lax.dot_general(
        left, right, (((1,), (1,)), ((), ())), preferred_element_type=jnp.float32
    )


def embed_rows(byte_ids, table):
    onehot = (byte_ids[:, None] == jnp.arange(table.shape[0], dtype=jnp.int32)[None, :]).astype(
        jnp.bfloat16
    )
    return jnp.dot(onehot, table, preferred_element_type=jnp.float32).astype(jnp.bfloat16)


def normalize(embedded):
    widened = embedded.astype(jnp.float32)
    inv_rms = lax.rsqrt(jnp.mean(widened * widened, axis=1, keepdims=True) + EPSILON)
    return (widened, inv_rms, (widened * inv_rms).astype(jnp.bfloat16))


def keys_values(normed, positions, w_key, w_value):
    key_rows = rotate(jnp.dot(normed, w_key, preferred_element_type=jnp.float32), positions).astype(
        jnp.bfloat16
    )
    value_rows = jnp.dot(normed, w_value, preferred_element_type=jnp.float32).astype(jnp.bfloat16)
    return (key_rows, value_rows)


def head_group(
    query_heads, key_heads, value_heads, grad_heads, group_window, own_pos, key_pos, score_scale
):
    distance = own_pos[:, None] - key_pos[None, :]
    allowed = (
        (distance[None] >= 0)
        & (distance[None] < group_window[:, None, None])
        & (key_pos[None, None, :] >= 0)
    )
    scores = (
        jnp.einsum("qhd,khd->hqk", query_heads, key_heads, preferred_element_type=jnp.float32)
        * score_scale
    )
    masked = jnp.where(allowed, scores, -1e30)
    row_max = jnp.max(masked, axis=-1, keepdims=True)
    weights = jnp.where(allowed, jnp.exp(masked - row_max), 0.0)
    probs = weights / jnp.sum(weights, axis=-1, keepdims=True)
    probs_b = probs.astype(jnp.bfloat16)
    attended = jnp.einsum(
        "hqk,khd->qhd", probs_b, value_heads, preferred_element_type=jnp.float32
    ).astype(jnp.bfloat16)
    grad_probs = jnp.einsum(
        "qhd,khd->hqk", grad_heads, value_heads, preferred_element_type=jnp.float32
    )
    row_term = jnp.sum(probs * grad_probs, axis=-1, keepdims=True)
    grad_scores = (probs * (grad_probs - row_term) * score_scale).astype(jnp.bfloat16)
    grad_query = jnp.einsum(
        "hqk,khd->qhd", grad_scores, key_heads, preferred_element_type=jnp.float32
    )
    grad_key = jnp.einsum(
        "hqk,qhd->khd", grad_scores, query_heads, preferred_element_type=jnp.float32
    )
    grad_value = jnp.einsum("hqk,qhd->khd", probs_b, grad_heads, preferred_element_type=jnp.float32)
    return (attended, grad_query, grad_key, grad_value)


def general_device(token_ids, cotangent, table, w_query, w_key, w_value, w_out, window):
    local_ids = token_ids[0]
    grad_out = cotangent[0]
    length = local_ids.shape[0]
    features = table.shape[1]
    tail_rows = min(length, WINDOW)
    reach_devs = -(-WINDOW // length)
    halo_rows = reach_devs * tail_rows
    offset = lax.axis_index("seq") * length
    own_pos = offset + jnp.arange(length, dtype=jnp.int32)
    halo_pos = offset - halo_rows + jnp.arange(halo_rows, dtype=jnp.int32)
    score_scale = HEAD_DIM ** (-0.5)
    embedded = embed_rows(local_ids, table)
    widened, inv_rms, normed = normalize(embedded)
    query = rotate(jnp.dot(normed, w_query, preferred_element_type=jnp.float32), own_pos).astype(
        jnp.bfloat16
    )
    key_own, value_own = keys_values(normed, own_pos, w_key, w_value)
    key_pieces = []
    value_pieces = []
    for hop_index in range(reach_devs):
        far_keys, far_values = shifted((key_own, value_own), "seq", hop_index + 1)
        key_pieces.insert(0, far_keys)
        value_pieces.insert(0, far_values)
    key_halo = jnp.concatenate(key_pieces, axis=0)
    value_halo = jnp.concatenate(value_pieces, axis=0)
    span_rows = halo_rows + length
    key_all = jnp.concatenate([key_halo, key_own], axis=0)
    value_all = jnp.concatenate([value_halo, value_own], axis=0)
    key_pos = jnp.concatenate([halo_pos, own_pos], axis=0)
    query_heads = query.reshape(length, HEADS, HEAD_DIM)
    key_heads = key_all.reshape(span_rows, HEADS, HEAD_DIM)
    value_heads = value_all.reshape(span_rows, HEADS, HEAD_DIM)
    grad_att = ndot(grad_out, w_out).astype(jnp.bfloat16)
    grad_heads = grad_att.reshape(length, HEADS, HEAD_DIM)
    group_size = 4
    attended_parts = []
    query_parts = []
    key_parts = []
    value_parts = []
    for group_index in range(HEADS // group_size):
        lower = group_index * group_size
        upper = lower + group_size
        outputs = head_group(
            query_heads[:, lower:upper],
            key_heads[:, lower:upper],
            value_heads[:, lower:upper],
            grad_heads[:, lower:upper],
            window[lower:upper],
            own_pos,
            key_pos,
            score_scale,
        )
        attended_parts.append(outputs[0])
        query_parts.append(outputs[1])
        key_parts.append(outputs[2])
        value_parts.append(outputs[3])
    attended = jnp.concatenate(attended_parts, axis=1).reshape(length, features)
    grad_query = jnp.concatenate(query_parts, axis=1).reshape(length, features)
    grad_key = jnp.concatenate(key_parts, axis=1).reshape(span_rows, features)
    grad_value = jnp.concatenate(value_parts, axis=1).reshape(span_rows, features)
    tail_keys = grad_key[:halo_rows].reshape(reach_devs, tail_rows, features)
    tail_values = grad_value[:halo_rows].reshape(reach_devs, tail_rows, features)
    back_keys = jnp.zeros((tail_rows, features), jnp.float32)
    back_values = jnp.zeros((tail_rows, features), jnp.float32)
    for hop_index in range(reach_devs):
        got_keys, got_values = shifted(
            (tail_keys[reach_devs - 1 - hop_index], tail_values[reach_devs - 1 - hop_index]),
            "seq",
            -(hop_index + 1),
        )
        back_keys = back_keys + got_keys
        back_values = back_values + got_values
    own_keys = grad_key[halo_rows:]
    own_values = grad_value[halo_rows:]
    own_keys = jnp.concatenate([own_keys[: length - tail_rows], own_keys + back_keys], axis=0)
    own_values = jnp.concatenate(
        [own_values[: length - tail_rows], own_values + back_values], axis=0
    )
    grad_q_lin = unrotate(grad_query, own_pos).astype(jnp.bfloat16)
    grad_k_lin = unrotate(own_keys, own_pos).astype(jnp.bfloat16)
    grad_v_lin = own_values.astype(jnp.bfloat16)
    grad_normed = ndot(grad_q_lin, w_query) + ndot(grad_k_lin, w_key) + ndot(grad_v_lin, w_value)
    scaled = widened * inv_rms
    grad_input = (
        inv_rms * (grad_normed - scaled * jnp.mean(grad_normed * scaled, axis=1, keepdims=True))
    ).astype(jnp.bfloat16)
    term = jnp.concatenate(
        [
            tdot(normed, grad_q_lin),
            tdot(normed, grad_k_lin),
            tdot(normed, grad_v_lin),
            tdot(attended, grad_out),
        ],
        axis=0,
    )
    shares = lax.psum_scatter(term.astype(jnp.bfloat16), "seq", scatter_dimension=0, tiled=True)
    weight_grads = lax.psum(shares, "dp").astype(jnp.float32)
    return (grad_input[None], weight_grads)


GROUPS = 4
GROUP_HEADS = HEADS // GROUPS
GROUP_COLS = GROUP_HEADS * HEAD_DIM
TILE = 256
TOKEN_ROWS = 16
HALF = HEAD_DIM // 2
VMEM_BYTES = 48 * 1024 * 1024


def key_span(query_tile):
    first = max(0, query_tile - WINDOW // TILE)
    return (first * TILE, (query_tile - first + 1) * TILE)


def normed_table(table_ref):
    widened = table_ref[...].astype(jnp.float32)
    inv_rms = lax.rsqrt(jnp.mean(widened * widened, axis=1, keepdims=True) + EPSILON)
    return (widened * inv_rms).astype(jnp.bfloat16)


def onehot_columns(tokens, vocab):
    rows = lax.broadcasted_iota(jnp.int32, (vocab, tokens.shape[1]), 0)
    return (rows == tokens).astype(jnp.float32).astype(jnp.bfloat16)


def send_kernel(meta_ref, tokens_ref, cotangent_ref, out_weights_ref, *out_refs):
    early_refs, grads_ref = out_refs[:-1], out_refs[-1]
    grad_att = ndot(out_weights_ref[...], cotangent_ref[...]).astype(jnp.bfloat16)
    grads_ref[...] = grad_att
    block = tokens_ref.shape[1]
    tokens = jnp.broadcast_to(tokens_ref[...].astype(jnp.float32), (TOKEN_ROWS, block)).astype(
        jnp.bfloat16
    )
    for turn, early_ref in enumerate(early_refs):
        group = meta_ref[GROUP_HEADS + 1] ^ turn
        place = pl.ds(pl.multiple_of(group * GROUP_COLS, GROUP_COLS), GROUP_COLS)
        early_ref[:GROUP_COLS, :] = grads_ref[place, :]
        early_ref[GROUP_COLS:, :] = tokens


def prepare_kernel(
    meta_ref,
    cotangent_ref,
    table_ref,
    query_ref,
    key_ref,
    value_ref,
    keep_ref,
    give_ref,
    lookup_ref,
    normed_ref,
    columns_ref,
):
    first = meta_ref[GROUP_HEADS] == 0
    columns = keep_ref.shape[1]
    left = cotangent_ref[:, :columns]
    right = cotangent_ref[:, columns:]
    keep_ref[...] = jnp.where(first, left, right)
    give_ref[...] = jnp.where(first, right, left)
    normed = normed_table(table_ref)
    normed_ref[...] = jnp.where(first, normed[:, :columns], normed[:, columns:])
    place = pl.ds(pl.multiple_of(meta_ref[GROUP_HEADS + 1] * GROUP_COLS, GROUP_COLS), GROUP_COLS)
    for matrix, weights_ref in enumerate((query_ref, key_ref, value_ref)):
        columns_ref[...] = jnp.dot(
            normed, weights_ref[...], preferred_element_type=jnp.float32
        ).T
        mine = columns_ref[place, :]
        upper = mine.astype(jnp.bfloat16)
        rows = slice(matrix * GROUP_COLS, (matrix + 1) * GROUP_COLS)
        lookup_ref[0, rows, :] = upper
        lookup_ref[1, rows, :] = (mine - upper.astype(jnp.float32)).astype(jnp.bfloat16)


def pair_kernel(meta_ref, keep_ref, got_ref, out_ref):
    first = meta_ref[GROUP_HEADS] == 0
    rows = keep_ref.shape[0]
    out_ref[:rows, :] = jnp.where(first, keep_ref[...], got_ref[...])
    out_ref[rows:, :] = jnp.where(first, got_ref[...], keep_ref[...])


def attention_kernel(
    meta_ref,
    lookup_ref,
    cosine_ref,
    sine_ref,
    *rest,
):
    early_refs = rest[: 2 * GROUPS]
    attention_body(meta_ref, lookup_ref, cosine_ref, sine_ref, early_refs, *rest[2 * GROUPS :])


def attention_body(
    meta_ref,
    lookup_ref,
    cosine_ref,
    sine_ref,
    early_refs,
    rows_ref,
    sums_ref,
    attended_ref,
    query_key_ref,
    zero_query_ref,
    key_t_ref,
    value_ref,
    value_t_ref,
    grad_att_ref,
    onehot_ref,
    grad_query_ref,
    grad_key_ref,
    grad_value_ref,
):
    head = pl.program_id(0)
    block = early_refs[0].shape[1]
    length = len(early_refs) * block
    vocab = lookup_ref.shape[2]
    half_vocab = vocab // 2
    cosine = cosine_ref[...]
    sine_part = sine_ref[...]
    blank = jnp.zeros((HEAD_DIM, length), jnp.float32)

    @pl.when(head == 0)
    def _():
        own = 2 * meta_ref[GROUP_HEADS + 1] + meta_ref[GROUP_HEADS]
        for turn, early_ref in enumerate(early_refs):
            lanes = pl.ds(pl.multiple_of((own ^ turn) * block, block), block)
            tokens = early_ref[GROUP_COLS : GROUP_COLS + TOKEN_ROWS, :]
            tokens = tokens.astype(jnp.float32)[:1].astype(jnp.int32)
            onehot_ref[:, lanes] = onehot_columns(tokens, vocab)
            grad_att_ref[:, :, lanes] = early_ref[:GROUP_COLS, :].reshape(
                GROUP_HEADS, HEAD_DIM, block
            )
        onehot = onehot_ref[...]

        def chosen(start):
            rows = slice(start, start + HEAD_DIM)
            return jnp.dot(
                lookup_ref[0, rows, :], onehot, preferred_element_type=jnp.float32
            ) + jnp.dot(lookup_ref[1, rows, :], onehot, preferred_element_type=jnp.float32)

        def turned(columns):
            former = columns[:HALF]
            latter = columns[HALF:]
            return jnp.concatenate(
                [former * cosine - latter * sine_part, latter * cosine + former * sine_part], axis=0
            )

        for index in range(GROUP_HEADS):
            query = turned(chosen(index * HEAD_DIM)) * HEAD_DIM ** (-0.5)
            keys = turned(chosen(GROUP_COLS + index * HEAD_DIM))
            values = chosen(2 * GROUP_COLS + index * HEAD_DIM)
            query_key_ref[index] = jnp.concatenate([query, keys], axis=0).T.astype(jnp.bfloat16)
            value_ref[index] = jnp.concatenate([values, blank], axis=0).T.astype(jnp.bfloat16)
            zero_query_ref[index] = jnp.concatenate([blank, query], axis=0).astype(jnp.bfloat16)
            key_t_ref[index] = keys.astype(jnp.bfloat16)
            value_t_ref[index] = values.astype(jnp.bfloat16)

    width = meta_ref[head]
    grad_att = grad_att_ref[head]
    wide_grad = grad_att.astype(jnp.float32)
    grad_blank = jnp.concatenate([wide_grad, blank], axis=0).astype(jnp.bfloat16)
    blank_grad = jnp.concatenate([blank, wide_grad], axis=0).T.astype(jnp.bfloat16)
    grad_key_ref[...] = jnp.zeros_like(grad_key_ref)
    grad_value_ref[...] = jnp.zeros_like(grad_value_ref)
    distance = lax.broadcasted_iota(jnp.int32, (TILE, TILE), 1) - lax.broadcasted_iota(
        jnp.int32, (TILE, TILE), 0
    )
    for query_tile in range(length // TILE):
        first, count = key_span(query_tile)
        columns = slice(query_tile * TILE, (query_tile + 1) * TILE)
        scores = jnp.dot(
            query_key_ref[head, first : first + count, :],
            zero_query_ref[head, :, columns],
            preferred_element_type=jnp.float32,
        )
        masked = []
        for key_tile in range(count // TILE):
            offset = query_tile * TILE - first - key_tile * TILE
            allowed = distance < width - offset
            if offset == 0:
                allowed = allowed & (distance >= 0)
            part = scores[key_tile * TILE : (key_tile + 1) * TILE]
            masked.append(jnp.where(allowed, part, -1e30))
        masked = jnp.concatenate(masked, axis=0)
        row_max = jnp.max(masked, axis=0, keepdims=True)
        weights = jnp.exp(masked - row_max)
        probs = weights * (1.0 / jnp.sum(weights, axis=0, keepdims=True))
        rounded = probs.astype(jnp.bfloat16)
        attended = jnp.dot(
            value_t_ref[head, :, first : first + count], rounded, preferred_element_type=jnp.float32
        )
        attended_ref[pl.ds(pl.multiple_of(head * HEAD_DIM, HEAD_DIM), HEAD_DIM), columns] = (
            attended.astype(jnp.bfloat16)
        )
        row_term = jnp.sum(attended * wide_grad[:, columns], axis=0, keepdims=True)
        grad_probs = jnp.dot(
            value_ref[head, first : first + count, :],
            grad_blank[:, columns],
            preferred_element_type=jnp.float32,
        )
        grad_scores = (probs * (grad_probs - row_term)).astype(jnp.bfloat16)
        grad_query_ref[:, columns] = jnp.dot(
            key_t_ref[head, :, first : first + count],
            grad_scores,
            preferred_element_type=jnp.float32,
        )
        grad_key_ref[first : first + count, :] += jnp.dot(
            grad_scores, query_key_ref[head, columns, :], preferred_element_type=jnp.float32
        )
        grad_value_ref[first : first + count, :] += jnp.dot(
            rounded, blank_grad[columns, :], preferred_element_type=jnp.float32
        )

    def turned_back(columns):
        former = columns[:HALF]
        latter = columns[HALF:]
        return jnp.concatenate(
            [former * cosine + latter * sine_part, latter * cosine - former * sine_part], axis=0
        )

    lanes = lax.broadcasted_iota(jnp.int32, grad_key_ref.shape, 1)
    both = jnp.where(lanes < HEAD_DIM, grad_key_ref[...], grad_value_ref[...]).T
    grads = jnp.concatenate(
        [
            turned_back(grad_query_ref[...] * HEAD_DIM ** (-0.5)),
            turned_back(both[:HEAD_DIM]),
            both[HEAD_DIM:],
        ],
        axis=0,
    ).astype(jnp.bfloat16)
    sums = ndot(grads, onehot_ref[...]).astype(jnp.bfloat16)
    for matrix in range(3):
        rows = slice(matrix * HEAD_DIM, (matrix + 1) * HEAD_DIM)
        place = pl.ds(
            pl.multiple_of(matrix * GROUP_COLS + head * HEAD_DIM, HEAD_DIM), HEAD_DIM
        )
        for core in range(2):
            lane = core * half_vocab
            sums_ref[core, place, :] = sums[rows, lane : lane + half_vocab]
        for target in range(GROUPS):
            start = target * 2 * block
            even = grads[rows, start : start + block]
            odd = grads[rows, start + block : start + 2 * block]
            rows_ref[target, place, :] = jnp.where(meta_ref[GROUP_HEADS] == 0, even, odd)


def out_kernel(
    meta_ref, attended_ref, c0_ref, c1_ref, c2_ref, c3_ref, sums_ref, keep_ref, give_ref
):
    span = c0_ref.shape[0]
    total = None
    for turn, rows_ref in enumerate((c0_ref, c1_ref, c2_ref, c3_ref)):
        source = meta_ref[GROUP_HEADS + 1] ^ turn
        part = jnp.dot(
            attended_ref[:, pl.ds(pl.multiple_of(source * span, span), span)],
            rows_ref[...],
            preferred_element_type=jnp.float32,
        )
        total = part if total is None else total + part
    rows = total.shape[0] // 2
    base = sums_ref.shape[1]
    lanes = keep_ref.shape[1]
    first = meta_ref[GROUP_HEADS + 2] == 0
    keep_ref[:base, :] = jnp.where(first, sums_ref[0], sums_ref[1])
    give_ref[:base, :] = jnp.where(first, sums_ref[1], sums_ref[0])
    for chunk in range(total.shape[1] // lanes):
        part = total[:, chunk * lanes : (chunk + 1) * lanes]
        place = slice(base + chunk * rows, base + (chunk + 1) * rows)
        keep_ref[place, :] = jnp.where(first, part[:rows], part[rows:]).astype(jnp.bfloat16)
        give_ref[place, :] = jnp.where(first, part[rows:], part[:rows]).astype(jnp.bfloat16)


def combine_kernel(meta_ref, here_ref, there_ref, after_ref, out_ref, *piece_refs):
    del after_ref
    rows = GROUP_COLS
    out_ref[...] = here_ref[3 * rows :, :] + there_ref[3 * rows :, :]
    for turn, piece_ref in enumerate(piece_refs):
        target = jnp.minimum(meta_ref[GROUP_HEADS + 1] ^ turn, 2)
        place = pl.ds(pl.multiple_of(target * rows, rows), rows)
        piece_ref[...] = here_ref[place, :] + there_ref[place, :]


def gather_kernel(meta_ref, s0, s1, s2, s3, own_ref, o0, o1, o2, o3, mine_ref):
    rows = GROUP_COLS
    group = meta_ref[GROUP_HEADS + 1]

    @pl.when(group < 3)
    def _():
        for turn, got in enumerate((s0, s1, s2, s3)):
            source = group ^ turn
            mine_ref[pl.ds(pl.multiple_of(source * rows, rows), rows), :] = got[...]
        tail = mine_ref.shape[0] - GROUPS * rows
        mine_ref[GROUPS * rows :, :] = jnp.zeros((tail, mine_ref.shape[1]), jnp.bfloat16)

    @pl.when(group == 3)
    def _():
        size = own_ref.shape[0]
        own = meta_ref[GROUP_HEADS] == 1
        mine_ref[0:size, :] = o0[...]
        mine_ref[size : 2 * size, :] = o1[...]
        mine_ref[2 * size : 3 * size, :] = jnp.where(own, own_ref[...], o2[...])
        mine_ref[3 * size :, :] = o3[...]


def input_kernel(tokens_ref, table_ref, query_ref, key_ref, value_ref, rows_ref, out_ref):
    vocab = table_ref.shape[0]
    onehot = onehot_columns(tokens_ref[...], vocab)
    embedded = tdot(onehot, table_ref[...])
    inv_rms = lax.rsqrt(jnp.mean(embedded * embedded, axis=1, keepdims=True) + EPSILON)
    grad_normed = None
    for matrix, weights in enumerate((query_ref, key_ref, value_ref)):
        columns = jnp.concatenate(
            [
                rows_ref[group, matrix * GROUP_COLS : (matrix + 1) * GROUP_COLS, :]
                for group in range(GROUPS)
            ],
            axis=0,
        )
        part = ndot(columns.astype(jnp.float32).T.astype(jnp.bfloat16), weights[...])
        grad_normed = part if grad_normed is None else grad_normed + part
    scaled = embedded * inv_rms
    out_ref[...] = (
        inv_rms * (grad_normed - scaled * jnp.mean(grad_normed * scaled, axis=1, keepdims=True))
    ).astype(jnp.bfloat16)


def weight_kernel(meta_ref, normed_ref, mine_ref, other_ref, out_ref):
    half_vocab = mine_ref.shape[1]
    first_core = meta_ref[GROUP_HEADS + 2] == 0

    @pl.when(meta_ref[GROUP_HEADS + 1] < 3)
    def _():
        first = normed_ref[:half_vocab, :]
        second = normed_ref[half_vocab:, :]
        upper = jnp.where(first_core, first, second)
        lower = jnp.where(first_core, second, first)
        total = None
        for part, sums_ref in ((upper, mine_ref), (lower, other_ref)):
            term = lax.dot_general(
                part,
                sums_ref[: GROUPS * GROUP_COLS, :],
                (((0,), (1,)), ((), ())),
                preferred_element_type=jnp.float32,
            )
            total = term if total is None else total + term
        out_ref[...] = total

    @pl.when(meta_ref[GROUP_HEADS + 1] == 3)
    def _():
        rows = GROUP_COLS // 2
        first_side = meta_ref[GROUP_HEADS] == 0
        for half in range(2):
            for chunk in range(3):
                for core in range(2):
                    same = first_core == (core == 0)
                    planes = []
                    for plane in range(2):
                        start = ((2 * half + plane) * 3 + chunk) * rows
                        place = slice(start, start + rows)
                        planes.append(jnp.where(same, mine_ref[place, :], other_ref[place, :]))
                    row = half * GROUP_COLS + core * rows
                    for side in range(2):
                        value = jnp.where(first_side, planes[side], planes[1 - side])
                        start = (side * 3 + chunk) * half_vocab
                        out_ref[row : row + rows, start : start + half_vocab] = value.astype(
                            jnp.float32
                        )


def whole(shape):
    return pl.BlockSpec(shape, lambda *_: (0,) * len(shape))


def swapped(block, axis, bit):
    route = [(i, i ^ bit) for i in range(lax.axis_size(axis))]
    return lax.ppermute(block, axis, route)


def rope_table(length):
    frequency = (10000.0 ** (-2.0 * np.arange(HALF, dtype=np.float32) / HEAD_DIM)).astype(np.float32)
    angles = frequency[:, None] * np.arange(length, dtype=np.float32)[None, :]
    angles = angles.astype(np.float64)
    return (
        jnp.asarray(np.cos(angles).astype(np.float32)),
        jnp.asarray(np.sin(angles).astype(np.float32)),
    )


def grouped_device(token_ids, cotangent, table, w_query, w_key, w_value, w_out, window):
    place = lax.axis_index("seq")
    core = lax.axis_index("dp") % 2
    group = place // 2
    side = place % 2
    block = token_ids.shape[1]
    features = table.shape[1]
    vocab = table.shape[0]
    blocks = lax.axis_size("seq")
    length = block * blocks
    grad_out = cotangent[0]
    meta = jnp.concatenate(
        [
            lax.dynamic_slice_in_dim(window, group * GROUP_HEADS, GROUP_HEADS, 0),
            jnp.stack([side, group, core]).astype(jnp.int32),
        ]
    )
    cosine, sine_part = rope_table(length)

    def call(
        body, operands, outs, scratch=(), steps=1, flops=10**8, moved=10**6, loose=0, grant=VMEM_BYTES
    ):
        spaces = [whole(operand.shape) for operand in operands]
        for index in range(loose):
            spaces[-1 - index] = pl.BlockSpec(memory_space=pl.ANY)
        if operands[0].ndim == 1:
            spaces[0] = pl.BlockSpec(memory_space=pltpu.SMEM)
        return pl.pallas_call(
            body,
            grid=(steps,),
            in_specs=spaces,
            out_specs=[whole(shape) for shape, _ in outs],
            out_shape=[jax.ShapeDtypeStruct(shape, dtype) for shape, dtype in outs],
            scratch_shapes=list(scratch),
            compiler_params=pltpu.CompilerParams(
                dimension_semantics=("arbitrary",), vmem_limit_bytes=grant
            ),
            cost_estimate=pl.CostEstimate(flops=flops, bytes_accessed=moved, transcendentals=0),
        )(*operands)

    half = jnp.bfloat16
    sent = call(
        send_kernel,
        (meta, token_ids, grad_out, w_out),
        [((GROUP_COLS + TOKEN_ROWS, block), half)] * GROUPS,
        [pltpu.VMEM((features, block), half)],
        grant=60 * 1024 * 1024,
    )
    early = [sent[0]] + [None] * (blocks - 1)
    for turn in (4, 6, 5, 7, 2, 3, 1):
        early[turn] = swapped(sent[turn // 2], "seq", turn)
    keep, give, lookup, normed = call(
        prepare_kernel,
        (meta, grad_out, table, w_query, w_key, w_value),
        [
            ((block, features // 2), half),
            ((block, features // 2), half),
            ((2, 3 * GROUP_COLS, vocab), half),
            ((vocab, features // 2), half),
        ],
        [pltpu.VMEM((features, vocab), jnp.float32)],
        flops=10**9,
        moved=5 * 10**6,
    )
    (late,) = call(
        pair_kernel, (meta, keep, swapped(give, "seq", 1)), [((2 * block, features // 2), half)]
    )
    lates = [late] + [swapped(late, "seq", 2 * turn) for turn in range(1, GROUPS)]
    heads_shape = (GROUP_HEADS, HEAD_DIM, length)
    rows_shape = (GROUP_HEADS, length, 2 * HEAD_DIM)
    rows, sums, attended = call(
        attention_kernel,
        (meta, lookup, cosine, sine_part, *early),
        [
            ((GROUPS, 3 * GROUP_COLS, block), half),
            ((2, 3 * GROUP_COLS, vocab // 2), half),
            ((GROUP_COLS, length), half),
        ],
        [
            pltpu.VMEM(rows_shape, half),
            pltpu.VMEM((GROUP_HEADS, 2 * HEAD_DIM, length), half),
            pltpu.VMEM(heads_shape, half),
            pltpu.VMEM(rows_shape, half),
            pltpu.VMEM(heads_shape, half),
            pltpu.VMEM(heads_shape, half),
            pltpu.VMEM((vocab, length), half),
            pltpu.VMEM((HEAD_DIM, length), jnp.float32),
            pltpu.VMEM((length, 2 * HEAD_DIM), jnp.float32),
            pltpu.VMEM((length, 2 * HEAD_DIM), jnp.float32),
        ],
        steps=GROUP_HEADS,
        flops=8 * 10**9,
        moved=8 * 10**6,
    )
    planes = [[2 * z + x for z in range(GROUPS)] for x in range(2)]

    def over_plane(chunks):
        return lax.all_to_all(
            chunks, "seq", split_axis=0, concat_axis=0, axis_index_groups=planes, tiled=True
        )

    got_rows = over_plane(rows)
    lanes = vocab // 2
    out_rows = 3 * GROUP_COLS // 2
    packed = 3 * GROUP_COLS + out_rows
    keep, give = call(
        out_kernel,
        (meta, attended, *lates, sums),
        [((packed, lanes), half)] * 2,
    )
    here = keep + swapped(give, "dp", 1)
    there = swapped(here, "dp", 2)
    kept_out, *pieces = call(
        combine_kernel,
        (meta, here, there, got_rows),
        [((out_rows, lanes), half)] + [((GROUP_COLS, lanes), half)] * GROUPS,
        loose=1,
    )
    got = [pieces[0]]
    for turn in range(1, GROUPS):
        route = [(i, i ^ (2 * turn)) for i in range(blocks) if (i ^ (2 * turn)) < blocks - 2]
        got.append(lax.ppermute(pieces[turn], "seq", route))
    got_out = []
    for part in range(2):
        for other in range(2):
            route = [(2 * (2 * x + part) + (x ^ other), blocks - 2 + x) for x in range(2)]
            route = [(s, t) for s, t in route if s != t]
            got_out.append(lax.ppermute(kept_out, "seq", route))
    (mine,) = call(
        gather_kernel, (meta, *got, kept_out, *got_out), [((4 * out_rows, lanes), half)]
    )
    (grad_input,) = call(
        input_kernel,
        (token_ids, table, w_query, w_key, w_value, got_rows),
        [((block, features), half)],
        flops=10**9,
        moved=5 * 10**6,
    )
    (weight_grads,) = call(
        weight_kernel,
        (meta, normed, mine, swapped(mine, "dp", 1)),
        [((features // 2, features), jnp.float32)],
        flops=10**9,
        moved=5 * 10**6,
    )
    return (grad_input[None], weight_grads)


def on_device(token_ids, cotangent, table, w_query, w_key, w_value, w_out, window):
    fits = (
        lax.axis_size("seq") == 2 * GROUPS
        and lax.axis_size("dp") == 4
        and token_ids.shape == (1, 128)
        and table.shape == (256, HEADS * HEAD_DIM)
    )
    plan = grouped_device if fits else general_device
    return plan(token_ids, cotangent, table, w_query, w_key, w_value, w_out, window)


def solution(mesh):
    return jax.shard_map(
        on_device,
        mesh=mesh,
        in_specs=(P("dp", "seq"), P("dp", "seq", None), P(), P(), P(), P(), P(), P()),
        out_specs=(P("dp", "seq", None), P("seq", None)),
        check_vma=False,
    )
```

```python
import jax
import jax.numpy as jnp
import numpy as np
from jax import lax
from jax.experimental import pallas as pl
from jax.experimental.pallas import tpu as pltpu
from jax.sharding import PartitionSpec as P

HEADS = 12
HEAD_DIM = 64
WINDOW = 512


EPSILON = 1e-05


def shifted(block, axis, distance):
    devices = range(lax.axis_size(axis))
    route = [(i - distance, i) for i in devices if i - distance in devices]
    return lax.ppermute(block, axis, route)


def rotate(values, positions):
    row_count = values.shape[0]
    shaped = values.reshape(row_count, -1, HEAD_DIM)
    middle = HEAD_DIM // 2
    frequency = 10000.0 ** (-2.0 * jnp.arange(middle, dtype=jnp.float32) / HEAD_DIM)
    angles = positions.astype(jnp.float32)[:, None] * frequency[None, :]
    cosine = jnp.cos(angles)[:, None, :]
    sine_part = jnp.sin(angles)[:, None, :]
    former = shaped[..., :middle]
    latter = shaped[..., middle:]
    turned = jnp.concatenate(
        [former * cosine - latter * sine_part, latter * cosine + former * sine_part], axis=-1
    )
    return turned.reshape(row_count, -1)


def unrotate(values, positions):
    row_count = values.shape[0]
    shaped = values.reshape(row_count, -1, HEAD_DIM)
    middle = HEAD_DIM // 2
    frequency = 10000.0 ** (-2.0 * jnp.arange(middle, dtype=jnp.float32) / HEAD_DIM)
    angles = positions.astype(jnp.float32)[:, None] * frequency[None, :]
    cosine = jnp.cos(angles)[:, None, :]
    sine_part = jnp.sin(angles)[:, None, :]
    former = shaped[..., :middle]
    latter = shaped[..., middle:]
    turned = jnp.concatenate(
        [former * cosine + latter * sine_part, latter * cosine - former * sine_part], axis=-1
    )
    return turned.reshape(row_count, -1)


def tdot(left, right):
    return lax.dot_general(
        left, right, (((0,), (0,)), ((), ())), preferred_element_type=jnp.float32
    )


def ndot(left, right):
    return lax.dot_general(
        left, right, (((1,), (1,)), ((), ())), preferred_element_type=jnp.float32
    )


def embed_rows(byte_ids, table):
    onehot = (byte_ids[:, None] == jnp.arange(table.shape[0], dtype=jnp.int32)[None, :]).astype(
        jnp.bfloat16
    )
    return jnp.dot(onehot, table, preferred_element_type=jnp.float32).astype(jnp.bfloat16)


def normalize(embedded):
    widened = embedded.astype(jnp.float32)
    inv_rms = lax.rsqrt(jnp.mean(widened * widened, axis=1, keepdims=True) + EPSILON)
    return (widened, inv_rms, (widened * inv_rms).astype(jnp.bfloat16))


def keys_values(normed, positions, w_key, w_value):
    key_rows = rotate(jnp.dot(normed, w_key, preferred_element_type=jnp.float32), positions).astype(
        jnp.bfloat16
    )
    value_rows = jnp.dot(normed, w_value, preferred_element_type=jnp.float32).astype(jnp.bfloat16)
    return (key_rows, value_rows)


def head_group(
    query_heads, key_heads, value_heads, grad_heads, group_window, own_pos, key_pos, score_scale
):
    distance = own_pos[:, None] - key_pos[None, :]
    allowed = (
        (distance[None] >= 0)
        & (distance[None] < group_window[:, None, None])
        & (key_pos[None, None, :] >= 0)
    )
    scores = (
        jnp.einsum("qhd,khd->hqk", query_heads, key_heads, preferred_element_type=jnp.float32)
        * score_scale
    )
    masked = jnp.where(allowed, scores, -1e30)
    row_max = jnp.max(masked, axis=-1, keepdims=True)
    weights = jnp.where(allowed, jnp.exp(masked - row_max), 0.0)
    probs = weights / jnp.sum(weights, axis=-1, keepdims=True)
    probs_b = probs.astype(jnp.bfloat16)
    attended = jnp.einsum(
        "hqk,khd->qhd", probs_b, value_heads, preferred_element_type=jnp.float32
    ).astype(jnp.bfloat16)
    grad_probs = jnp.einsum(
        "qhd,khd->hqk", grad_heads, value_heads, preferred_element_type=jnp.float32
    )
    row_term = jnp.sum(probs * grad_probs, axis=-1, keepdims=True)
    grad_scores = (probs * (grad_probs - row_term) * score_scale).astype(jnp.bfloat16)
    grad_query = jnp.einsum(
        "hqk,khd->qhd", grad_scores, key_heads, preferred_element_type=jnp.float32
    )
    grad_key = jnp.einsum(
        "hqk,qhd->khd", grad_scores, query_heads, preferred_element_type=jnp.float32
    )
    grad_value = jnp.einsum("hqk,qhd->khd", probs_b, grad_heads, preferred_element_type=jnp.float32)
    return (attended, grad_query, grad_key, grad_value)


def general_device(token_ids, cotangent, table, w_query, w_key, w_value, w_out, window):
    local_ids = token_ids[0]
    grad_out = cotangent[0]
    length = local_ids.shape[0]
    features = table.shape[1]
    tail_rows = min(length, WINDOW)
    reach_devs = -(-WINDOW // length)
    halo_rows = reach_devs * tail_rows
    offset = lax.axis_index("seq") * length
    own_pos = offset + jnp.arange(length, dtype=jnp.int32)
    halo_pos = offset - halo_rows + jnp.arange(halo_rows, dtype=jnp.int32)
    score_scale = HEAD_DIM ** (-0.5)
    embedded = embed_rows(local_ids, table)
    widened, inv_rms, normed = normalize(embedded)
    query = rotate(jnp.dot(normed, w_query, preferred_element_type=jnp.float32), own_pos).astype(
        jnp.bfloat16
    )
    key_own, value_own = keys_values(normed, own_pos, w_key, w_value)
    key_pieces = []
    value_pieces = []
    for hop_index in range(reach_devs):
        far_keys, far_values = shifted((key_own, value_own), "seq", hop_index + 1)
        key_pieces.insert(0, far_keys)
        value_pieces.insert(0, far_values)
    key_halo = jnp.concatenate(key_pieces, axis=0)
    value_halo = jnp.concatenate(value_pieces, axis=0)
    span_rows = halo_rows + length
    key_all = jnp.concatenate([key_halo, key_own], axis=0)
    value_all = jnp.concatenate([value_halo, value_own], axis=0)
    key_pos = jnp.concatenate([halo_pos, own_pos], axis=0)
    query_heads = query.reshape(length, HEADS, HEAD_DIM)
    key_heads = key_all.reshape(span_rows, HEADS, HEAD_DIM)
    value_heads = value_all.reshape(span_rows, HEADS, HEAD_DIM)
    grad_att = ndot(grad_out, w_out).astype(jnp.bfloat16)
    grad_heads = grad_att.reshape(length, HEADS, HEAD_DIM)
    group_size = 4
    attended_parts = []
    query_parts = []
    key_parts = []
    value_parts = []
    for group_index in range(HEADS // group_size):
        lower = group_index * group_size
        upper = lower + group_size
        outputs = head_group(
            query_heads[:, lower:upper],
            key_heads[:, lower:upper],
            value_heads[:, lower:upper],
            grad_heads[:, lower:upper],
            window[lower:upper],
            own_pos,
            key_pos,
            score_scale,
        )
        attended_parts.append(outputs[0])
        query_parts.append(outputs[1])
        key_parts.append(outputs[2])
        value_parts.append(outputs[3])
    attended = jnp.concatenate(attended_parts, axis=1).reshape(length, features)
    grad_query = jnp.concatenate(query_parts, axis=1).reshape(length, features)
    grad_key = jnp.concatenate(key_parts, axis=1).reshape(span_rows, features)
    grad_value = jnp.concatenate(value_parts, axis=1).reshape(span_rows, features)
    tail_keys = grad_key[:halo_rows].reshape(reach_devs, tail_rows, features)
    tail_values = grad_value[:halo_rows].reshape(reach_devs, tail_rows, features)
    back_keys = jnp.zeros((tail_rows, features), jnp.float32)
    back_values = jnp.zeros((tail_rows, features), jnp.float32)
    for hop_index in range(reach_devs):
        got_keys, got_values = shifted(
            (tail_keys[reach_devs - 1 - hop_index], tail_values[reach_devs - 1 - hop_index]),
            "seq",
            -(hop_index + 1),
        )
        back_keys = back_keys + got_keys
        back_values = back_values + got_values
    own_keys = grad_key[halo_rows:]
    own_values = grad_value[halo_rows:]
    own_keys = jnp.concatenate([own_keys[: length - tail_rows], own_keys + back_keys], axis=0)
    own_values = jnp.concatenate(
        [own_values[: length - tail_rows], own_values + back_values], axis=0
    )
    grad_q_lin = unrotate(grad_query, own_pos).astype(jnp.bfloat16)
    grad_k_lin = unrotate(own_keys, own_pos).astype(jnp.bfloat16)
    grad_v_lin = own_values.astype(jnp.bfloat16)
    grad_normed = ndot(grad_q_lin, w_query) + ndot(grad_k_lin, w_key) + ndot(grad_v_lin, w_value)
    scaled = widened * inv_rms
    grad_input = (
        inv_rms * (grad_normed - scaled * jnp.mean(grad_normed * scaled, axis=1, keepdims=True))
    ).astype(jnp.bfloat16)
    term = jnp.concatenate(
        [
            tdot(normed, grad_q_lin),
            tdot(normed, grad_k_lin),
            tdot(normed, grad_v_lin),
            tdot(attended, grad_out),
        ],
        axis=0,
    )
    shares = lax.psum_scatter(term.astype(jnp.bfloat16), "seq", scatter_dimension=0, tiled=True)
    weight_grads = lax.psum(shares, "dp").astype(jnp.float32)
    return (grad_input[None], weight_grads)


GROUPS = 4
GROUP_HEADS = HEADS // GROUPS
GROUP_COLS = GROUP_HEADS * HEAD_DIM
TILE = 256
TOKEN_ROWS = 16
HALF = HEAD_DIM // 2
VMEM_BYTES = 48 * 1024 * 1024


def key_span(query_tile):
    first = max(0, query_tile - WINDOW // TILE)
    return (first * TILE, (query_tile - first + 1) * TILE)


def normed_table(table_ref):
    widened = table_ref[...].astype(jnp.float32)
    inv_rms = lax.rsqrt(jnp.mean(widened * widened, axis=1, keepdims=True) + EPSILON)
    return (widened * inv_rms).astype(jnp.bfloat16)


def onehot_columns(tokens, vocab):
    rows = lax.broadcasted_iota(jnp.int32, (vocab, tokens.shape[1]), 0)
    return (rows == tokens).astype(jnp.float32).astype(jnp.bfloat16)


def send_kernel(meta_ref, tokens_ref, cotangent_ref, out_weights_ref, *out_refs):
    early_refs, grads_ref = out_refs[:-1], out_refs[-1]
    grad_att = ndot(out_weights_ref[...], cotangent_ref[...]).astype(jnp.bfloat16)
    grads_ref[...] = grad_att
    block = tokens_ref.shape[1]
    tokens = jnp.broadcast_to(tokens_ref[...].astype(jnp.float32), (TOKEN_ROWS, block)).astype(
        jnp.bfloat16
    )
    for turn, early_ref in enumerate(early_refs):
        group = meta_ref[GROUP_HEADS + 1] ^ turn
        place = pl.ds(pl.multiple_of(group * GROUP_COLS, GROUP_COLS), GROUP_COLS)
        early_ref[:GROUP_COLS, :] = grads_ref[place, :]
        early_ref[GROUP_COLS:, :] = tokens


def prepare_kernel(
    meta_ref,
    cotangent_ref,
    table_ref,
    query_ref,
    key_ref,
    value_ref,
    late_ref,
    lookup_ref,
    normed_ref,
    columns_ref,
):
    columns = late_ref.shape[2]
    for target in range(2 * GROUPS):
        side = target % 2
        late_ref[target] = cotangent_ref[:, side * columns : (side + 1) * columns]
    normed = normed_table(table_ref)
    half = normed.shape[1] // 2
    normed_ref[...] = jnp.where(meta_ref[GROUP_HEADS] == 0, normed[:, :half], normed[:, half:])
    place = pl.ds(pl.multiple_of(meta_ref[GROUP_HEADS + 1] * GROUP_COLS, GROUP_COLS), GROUP_COLS)
    for matrix, weights_ref in enumerate((query_ref, key_ref, value_ref)):
        columns_ref[...] = jnp.dot(
            normed, weights_ref[...], preferred_element_type=jnp.float32
        ).T
        mine = columns_ref[place, :]
        upper = mine.astype(jnp.bfloat16)
        rows = slice(matrix * GROUP_COLS, (matrix + 1) * GROUP_COLS)
        lookup_ref[0, rows, :] = upper
        lookup_ref[1, rows, :] = (mine - upper.astype(jnp.float32)).astype(jnp.bfloat16)


def attention_kernel(
    meta_ref,
    lookup_ref,
    cosine_ref,
    sine_ref,
    *rest,
):
    early_refs = rest[: 2 * GROUPS]
    attention_body(meta_ref, lookup_ref, cosine_ref, sine_ref, early_refs, *rest[2 * GROUPS :])


def attention_body(
    meta_ref,
    lookup_ref,
    cosine_ref,
    sine_ref,
    early_refs,
    rows_ref,
    sums_ref,
    attended_ref,
    query_key_ref,
    zero_query_ref,
    key_t_ref,
    value_t_ref,
    grad_att_ref,
    onehot_ref,
    grad_query_ref,
    both_ref,
    value_grad_ref,
    probs_ref,
    scores_ref,
):
    head = pl.program_id(0)
    block = early_refs[0].shape[1]
    length = len(early_refs) * block
    vocab = lookup_ref.shape[2]
    half_vocab = vocab // 2
    half = jnp.bfloat16
    cosine = cosine_ref[...]
    sine_part = sine_ref[...]
    blank = jnp.zeros((HEAD_DIM, length), half)

    @pl.when(head == 0)
    def _():
        own = 2 * meta_ref[GROUP_HEADS + 1] + meta_ref[GROUP_HEADS]
        for turn, early_ref in enumerate(early_refs):
            lanes = pl.ds(pl.multiple_of((own ^ turn) * block, block), block)
            tokens = early_ref[GROUP_COLS : GROUP_COLS + TOKEN_ROWS, :]
            tokens = tokens.astype(jnp.float32)[:1].astype(jnp.int32)
            onehot_ref[:, lanes] = onehot_columns(tokens, vocab)
            grad_att_ref[:, :, lanes] = early_ref[:GROUP_COLS, :].reshape(
                GROUP_HEADS, HEAD_DIM, block
            )
        onehot = onehot_ref[...]

        def chosen(start):
            rows = slice(start, start + HEAD_DIM)
            return jnp.dot(
                lookup_ref[0, rows, :], onehot, preferred_element_type=jnp.float32
            ) + jnp.dot(lookup_ref[1, rows, :], onehot, preferred_element_type=jnp.float32)

        def turned(columns):
            former = columns[:HALF]
            latter = columns[HALF:]
            return jnp.concatenate(
                [former * cosine - latter * sine_part, latter * cosine + former * sine_part], axis=0
            )

        for index in range(GROUP_HEADS):
            query = (turned(chosen(index * HEAD_DIM)) * HEAD_DIM ** (-0.5)).astype(half)
            keys = turned(chosen(GROUP_COLS + index * HEAD_DIM)).astype(half)
            values = chosen(2 * GROUP_COLS + index * HEAD_DIM).astype(half)
            query_key_ref[index] = jnp.concatenate([query, keys], axis=0).T
            zero_query_ref[index] = jnp.concatenate([blank, query], axis=0)
            key_t_ref[index] = keys
            value_t_ref[index] = values

    width = meta_ref[head]
    grad_att = grad_att_ref[head]
    wide_grad = grad_att.astype(jnp.float32)
    grad_blank = jnp.concatenate([grad_att, blank], axis=0)
    value_grad_ref[...] = jnp.concatenate([value_t_ref[head], grad_att], axis=0).T
    distance = lax.broadcasted_iota(jnp.int32, (TILE, TILE), 1) - lax.broadcasted_iota(
        jnp.int32, (TILE, TILE), 0
    )
    for query_tile in range(length // TILE):
        first, count = key_span(query_tile)
        columns = slice(query_tile * TILE, (query_tile + 1) * TILE)
        scores = jnp.dot(
            query_key_ref[head, first : first + count, :],
            zero_query_ref[head, :, columns],
            preferred_element_type=jnp.float32,
        )
        masked = []
        for key_tile in range(count // TILE):
            offset = query_tile * TILE - first - key_tile * TILE
            allowed = distance < width - offset
            if offset == 0:
                allowed = allowed & (distance >= 0)
            part = scores[key_tile * TILE : (key_tile + 1) * TILE]
            masked.append(jnp.where(allowed, part, -1e30))
        masked = jnp.concatenate(masked, axis=0)
        row_max = jnp.max(masked, axis=0, keepdims=True)
        weights = jnp.exp(masked - row_max)
        probs = weights * (1.0 / jnp.sum(weights, axis=0, keepdims=True))
        rounded = probs.astype(half)
        probs_ref[first : first + count, columns] = rounded
        attended = jnp.dot(
            value_t_ref[head, :, first : first + count], rounded, preferred_element_type=jnp.float32
        )
        attended_ref[pl.ds(pl.multiple_of(head * HEAD_DIM, HEAD_DIM), HEAD_DIM), columns] = (
            attended.astype(jnp.bfloat16)
        )
        row_term = jnp.sum(attended * wide_grad[:, columns], axis=0, keepdims=True)
        grad_probs = jnp.dot(
            value_grad_ref[first : first + count, :],
            grad_blank[:, columns],
            preferred_element_type=jnp.float32,
        )
        grad_scores = (probs * (grad_probs - row_term)).astype(jnp.bfloat16)
        grad_query_ref[:, columns] = jnp.dot(
            key_t_ref[head, :, first : first + count],
            grad_scores,
            preferred_element_type=jnp.float32,
        )
        scores_ref[first : first + count, columns] = grad_scores
    lanes = lax.broadcasted_iota(jnp.int32, (TILE, 2 * HEAD_DIM), 1)
    for key_tile in range(length // TILE):
        start = key_tile * TILE
        stop = min(length, start + TILE + WINDOW)
        grad_key = jnp.dot(
            scores_ref[start : start + TILE, start:stop],
            query_key_ref[head, start:stop, :],
            preferred_element_type=jnp.float32,
        )
        grad_value = jnp.dot(
            probs_ref[start : start + TILE, start:stop],
            value_grad_ref[start:stop, :],
            preferred_element_type=jnp.float32,
        )
        both_ref[:, start : start + TILE] = jnp.where(lanes < HEAD_DIM, grad_key, grad_value).T

    def turned_back(columns):
        former = columns[:HALF]
        latter = columns[HALF:]
        return jnp.concatenate(
            [former * cosine + latter * sine_part, latter * cosine - former * sine_part], axis=0
        )

    both = both_ref[...]
    grads = jnp.concatenate(
        [
            turned_back(grad_query_ref[...] * HEAD_DIM ** (-0.5)),
            turned_back(both[:HEAD_DIM]),
            both[HEAD_DIM:],
        ],
        axis=0,
    ).astype(jnp.bfloat16)
    sums = ndot(grads, onehot_ref[...]).astype(jnp.bfloat16)
    for matrix in range(3):
        rows = slice(matrix * HEAD_DIM, (matrix + 1) * HEAD_DIM)
        place = pl.ds(
            pl.multiple_of(matrix * GROUP_COLS + head * HEAD_DIM, HEAD_DIM), HEAD_DIM
        )
        for core in range(2):
            lane = core * half_vocab
            sums_ref[core, place, :] = sums[rows, lane : lane + half_vocab]
        for target in range(GROUPS):
            start = target * 2 * block
            even = grads[rows, start : start + block]
            odd = grads[rows, start + block : start + 2 * block]
            rows_ref[target, place, :] = jnp.where(meta_ref[GROUP_HEADS] == 0, even, odd)


def out_kernel(meta_ref, attended_ref, cotangent_ref, sums_ref, keep_ref, give_ref):
    total = jnp.dot(attended_ref[...], cotangent_ref[...], preferred_element_type=jnp.float32)
    rows = total.shape[0] // 2
    base = sums_ref.shape[1]
    lanes = keep_ref.shape[1]
    first = meta_ref[GROUP_HEADS + 2] == 0
    keep_ref[:base, :] = jnp.where(first, sums_ref[0], sums_ref[1])
    give_ref[:base, :] = jnp.where(first, sums_ref[1], sums_ref[0])
    for chunk in range(total.shape[1] // lanes):
        part = total[:, chunk * lanes : (chunk + 1) * lanes]
        place = slice(base + chunk * rows, base + (chunk + 1) * rows)
        keep_ref[place, :] = jnp.where(first, part[:rows], part[rows:]).astype(jnp.bfloat16)
        give_ref[place, :] = jnp.where(first, part[rows:], part[:rows]).astype(jnp.bfloat16)


def combine_kernel(meta_ref, here_ref, there_ref, after_ref, *piece_refs):
    del after_ref
    rows = GROUP_COLS
    for turn, piece_ref in enumerate(piece_refs):
        target = meta_ref[GROUP_HEADS + 1] ^ turn

        @pl.when(target < 3)
        def _(piece_ref=piece_ref, target=target):
            place = pl.ds(pl.multiple_of(target * rows, rows), rows)
            piece_ref[:rows, :] = here_ref[place, :] + there_ref[place, :]
            tail = piece_ref.shape[0] - rows
            piece_ref[rows:, :] = jnp.zeros((tail, piece_ref.shape[1]), jnp.bfloat16)

        @pl.when(target == 3)
        def _(piece_ref=piece_ref):
            piece_ref[...] = here_ref[3 * rows :, :] + there_ref[3 * rows :, :]


def gather_kernel(meta_ref, g0, g1, g2, g3, mine_ref, other_ref):
    rows = GROUP_COLS
    size = g0.shape[0]
    group = meta_ref[GROUP_HEADS + 1]

    @pl.when(group < 3)
    def _():
        for turn, got in enumerate((g0, g1, g2, g3)):
            place = pl.ds(pl.multiple_of((group ^ turn) * rows, rows), rows)
            mine_ref[place, :] = got[:rows, :]
        other_ref[...] = jnp.zeros_like(other_ref)

    @pl.when(group == 3)
    def _():
        first = meta_ref[GROUP_HEADS] == 0
        for part, (low, high) in enumerate(((g3, g1), (g2, g0))):
            place = slice(part * size, (part + 1) * size)
            mine_ref[place, :] = jnp.where(first, low[...], high[...])
            other_ref[place, :] = jnp.where(first, high[...], low[...])
        tail = mine_ref.shape[0] - 2 * size
        mine_ref[2 * size :, :] = jnp.zeros((tail, mine_ref.shape[1]), jnp.bfloat16)


def input_kernel(tokens_ref, table_ref, query_ref, key_ref, value_ref, rows_ref, out_ref):
    vocab = table_ref.shape[0]
    onehot = onehot_columns(tokens_ref[...], vocab)
    embedded = tdot(onehot, table_ref[...])
    inv_rms = lax.rsqrt(jnp.mean(embedded * embedded, axis=1, keepdims=True) + EPSILON)
    grad_normed = None
    for matrix, weights in enumerate((query_ref, key_ref, value_ref)):
        columns = jnp.concatenate(
            [
                rows_ref[group, matrix * GROUP_COLS : (matrix + 1) * GROUP_COLS, :]
                for group in range(GROUPS)
            ],
            axis=0,
        )
        part = ndot(columns.astype(jnp.float32).T.astype(jnp.bfloat16), weights[...])
        grad_normed = part if grad_normed is None else grad_normed + part
    scaled = embedded * inv_rms
    out_ref[...] = (
        inv_rms * (grad_normed - scaled * jnp.mean(grad_normed * scaled, axis=1, keepdims=True))
    ).astype(jnp.bfloat16)


def weight_kernel(meta_ref, normed_ref, mine_ref, other_ref, near_ref, far_ref, out_ref):
    half_vocab = mine_ref.shape[1]
    first_core = meta_ref[GROUP_HEADS + 2] == 0

    @pl.when(meta_ref[GROUP_HEADS + 1] < 3)
    def _():
        first = normed_ref[:half_vocab, :]
        second = normed_ref[half_vocab:, :]
        upper = jnp.where(first_core, first, second)
        lower = jnp.where(first_core, second, first)
        total = None
        for part, sums_ref in ((upper, mine_ref), (lower, other_ref)):
            term = lax.dot_general(
                part,
                sums_ref[...],
                (((0,), (1,)), ((), ())),
                preferred_element_type=jnp.float32,
            )
            total = term if total is None else total + term
        out_ref[...] = total

    @pl.when(meta_ref[GROUP_HEADS + 1] == 3)
    def _():
        rows = GROUP_COLS // 2
        first_side = meta_ref[GROUP_HEADS] == 0
        for half in range(2):
            for chunk in range(3):
                place = slice((half * 3 + chunk) * rows, (half * 3 + chunk + 1) * rows)
                for core in range(2):
                    same = first_core == (core == 0)
                    own = jnp.where(same, mine_ref[place, :], other_ref[place, :])
                    crossed = jnp.where(same, near_ref[place, :], far_ref[place, :])
                    row = half * GROUP_COLS + core * rows
                    for side in range(2):
                        value = jnp.where(first_side == (side == 0), own, crossed)
                        start = (side * 3 + chunk) * half_vocab
                        out_ref[row : row + rows, start : start + half_vocab] = value.astype(
                            jnp.float32
                        )


def whole(shape):
    return pl.BlockSpec(shape, lambda *_: (0,) * len(shape))


def swapped(block, axis, bit):
    route = [(i, i ^ bit) for i in range(lax.axis_size(axis))]
    return lax.ppermute(block, axis, route)


def rope_table(length):
    frequency = (10000.0 ** (-2.0 * np.arange(HALF, dtype=np.float32) / HEAD_DIM)).astype(np.float32)
    angles = frequency[:, None] * np.arange(length, dtype=np.float32)[None, :]
    angles = angles.astype(np.float64)
    return (
        jnp.asarray(np.cos(angles).astype(np.float32)),
        jnp.asarray(np.sin(angles).astype(np.float32)),
    )


def grouped_device(token_ids, cotangent, table, w_query, w_key, w_value, w_out, window):
    place = lax.axis_index("seq")
    core = lax.axis_index("dp") % 2
    group = place // 2
    side = place % 2
    block = token_ids.shape[1]
    features = table.shape[1]
    vocab = table.shape[0]
    blocks = lax.axis_size("seq")
    length = block * blocks
    grad_out = cotangent[0]
    meta = jnp.concatenate(
        [
            lax.dynamic_slice_in_dim(window, group * GROUP_HEADS, GROUP_HEADS, 0),
            jnp.stack([side, group, core]).astype(jnp.int32),
        ]
    )
    cosine, sine_part = rope_table(length)

    def call(
        body, operands, outs, scratch=(), steps=1, flops=10**8, moved=10**6, loose=0, grant=VMEM_BYTES
    ):
        spaces = [whole(operand.shape) for operand in operands]
        for index in range(loose):
            spaces[-1 - index] = pl.BlockSpec(memory_space=pl.ANY)
        if operands[0].ndim == 1:
            spaces[0] = pl.BlockSpec(memory_space=pltpu.SMEM)
        return pl.pallas_call(
            body,
            grid=(steps,),
            in_specs=spaces,
            out_specs=[whole(shape) for shape, _ in outs],
            out_shape=[jax.ShapeDtypeStruct(shape, dtype) for shape, dtype in outs],
            scratch_shapes=list(scratch),
            compiler_params=pltpu.CompilerParams(
                dimension_semantics=("arbitrary",), vmem_limit_bytes=grant
            ),
            cost_estimate=pl.CostEstimate(flops=flops, bytes_accessed=moved, transcendentals=0),
        )(*operands)

    half = jnp.bfloat16
    sent = call(
        send_kernel,
        (meta, token_ids, grad_out, w_out),
        [((GROUP_COLS + TOKEN_ROWS, block), half)] * GROUPS,
        [pltpu.VMEM((features, block), half)],
        grant=60 * 1024 * 1024,
    )
    early = [sent[0]] + [None] * (blocks - 1)
    for turn in (4, 6, 5, 7, 2, 3, 1):
        early[turn] = swapped(sent[turn // 2], "seq", turn)
    late, lookup, normed = call(
        prepare_kernel,
        (meta, grad_out, table, w_query, w_key, w_value),
        [
            ((blocks, block, features // 2), half),
            ((2, 3 * GROUP_COLS, vocab), half),
            ((vocab, features // 2), half),
        ],
        [pltpu.VMEM((features, vocab), jnp.float32)],
        flops=10**9,
        moved=5 * 10**6,
        grant=60 * 1024 * 1024,
    )
    late = lax.all_to_all(late, "seq", split_axis=0, concat_axis=0, tiled=True)
    heads_shape = (GROUP_HEADS, HEAD_DIM, length)
    rows_shape = (GROUP_HEADS, length, 2 * HEAD_DIM)
    rows, sums, attended = call(
        attention_kernel,
        (meta, lookup, cosine, sine_part, *early),
        [
            ((GROUPS, 3 * GROUP_COLS, block), half),
            ((2, 3 * GROUP_COLS, vocab // 2), half),
            ((GROUP_COLS, length), half),
        ],
        [
            pltpu.VMEM(rows_shape, half),
            pltpu.VMEM((GROUP_HEADS, 2 * HEAD_DIM, length), half),
            pltpu.VMEM(heads_shape, half),
            pltpu.VMEM(heads_shape, half),
            pltpu.VMEM(heads_shape, half),
            pltpu.VMEM((vocab, length), half),
            pltpu.VMEM((HEAD_DIM, length), jnp.float32),
            pltpu.VMEM((2 * HEAD_DIM, length), jnp.float32),
            pltpu.VMEM((length, 2 * HEAD_DIM), half),
            pltpu.VMEM((length, length), half),
            pltpu.VMEM((length, length), half),
        ],
        steps=GROUP_HEADS,
        flops=8 * 10**9,
        moved=8 * 10**6,
    )
    planes = [[2 * z + x for z in range(GROUPS)] for x in range(2)]

    def over_plane(chunks):
        return lax.all_to_all(
            chunks, "seq", split_axis=0, concat_axis=0, axis_index_groups=planes, tiled=True
        )

    got_rows = over_plane(rows)
    lanes = vocab // 2
    out_rows = 3 * GROUP_COLS // 2
    packed = 3 * GROUP_COLS + out_rows
    keep, give = call(
        out_kernel,
        (meta, attended, late.reshape(length, features // 2), sums),
        [((packed, lanes), half)] * 2,
    )
    here = keep + swapped(give, "dp", 1)
    there = swapped(here, "dp", 2)
    pieces = call(
        combine_kernel,
        (meta, here, there, got_rows),
        [((out_rows, lanes), half)] * GROUPS,
        loose=1,
    )
    got = [pieces[0]] + [None] * (GROUPS - 1)
    for turn in (2, 3, 1):
        got[turn] = swapped(pieces[turn], "seq", 2 * turn)
    mine, other = call(
        gather_kernel,
        (meta, *got),
        [((GROUPS * GROUP_COLS, lanes), half), ((2 * out_rows, lanes), half)],
    )
    (grad_input,) = call(
        input_kernel,
        (token_ids, table, w_query, w_key, w_value, got_rows),
        [((block, features), half)],
        flops=10**9,
        moved=5 * 10**6,
    )
    last = blocks - 2
    near = lax.ppermute(other, "seq", [(last, last + 1), (last + 1, last)])
    paired = swapped(mine, "dp", 1)
    far = lax.ppermute(
        near,
        ("dp", "seq"),
        [
            (blocks * d + last + x, blocks * (d ^ 1) + last + x)
            for d in range(lax.axis_size("dp"))
            for x in range(2)
        ],
    )
    (weight_grads,) = call(
        weight_kernel,
        (meta, normed, mine, paired, near, far),
        [((features // 2, features), jnp.float32)],
        flops=10**9,
        moved=5 * 10**6,
    )
    return (grad_input[None], weight_grads)


def on_device(token_ids, cotangent, table, w_query, w_key, w_value, w_out, window):
    fits = (
        lax.axis_size("seq") == 2 * GROUPS
        and lax.axis_size("dp") == 4
        and token_ids.shape == (1, 128)
        and table.shape == (256, HEADS * HEAD_DIM)
    )
    plan = grouped_device if fits else general_device
    return plan(token_ids, cotangent, table, w_query, w_key, w_value, w_out, window)


def solution(mesh):
    return jax.shard_map(
        on_device,
        mesh=mesh,
        in_specs=(P("dp", "seq"), P("dp", "seq", None), P(), P(), P(), P(), P(), P()),
        out_specs=(P("dp", "seq", None), P("seq", None)),
        check_vma=False,
    )
```

```python
import jax
import jax.numpy as jnp
import numpy as np
from jax import lax
from jax.experimental import pallas as pl
from jax.experimental.pallas import tpu as pltpu
from jax.sharding import PartitionSpec as P

HEADS = 12
HEAD_DIM = 64
WINDOW = 512


EPSILON = 1e-05


def shifted(block, axis, distance):
    devices = range(lax.axis_size(axis))
    route = [(i - distance, i) for i in devices if i - distance in devices]
    return lax.ppermute(block, axis, route)


def rotate(values, positions):
    row_count = values.shape[0]
    shaped = values.reshape(row_count, -1, HEAD_DIM)
    middle = HEAD_DIM // 2
    frequency = 10000.0 ** (-2.0 * jnp.arange(middle, dtype=jnp.float32) / HEAD_DIM)
    angles = positions.astype(jnp.float32)[:, None] * frequency[None, :]
    cosine = jnp.cos(angles)[:, None, :]
    sine_part = jnp.sin(angles)[:, None, :]
    former = shaped[..., :middle]
    latter = shaped[..., middle:]
    turned = jnp.concatenate(
        [former * cosine - latter * sine_part, latter * cosine + former * sine_part], axis=-1
    )
    return turned.reshape(row_count, -1)


def unrotate(values, positions):
    row_count = values.shape[0]
    shaped = values.reshape(row_count, -1, HEAD_DIM)
    middle = HEAD_DIM // 2
    frequency = 10000.0 ** (-2.0 * jnp.arange(middle, dtype=jnp.float32) / HEAD_DIM)
    angles = positions.astype(jnp.float32)[:, None] * frequency[None, :]
    cosine = jnp.cos(angles)[:, None, :]
    sine_part = jnp.sin(angles)[:, None, :]
    former = shaped[..., :middle]
    latter = shaped[..., middle:]
    turned = jnp.concatenate(
        [former * cosine + latter * sine_part, latter * cosine - former * sine_part], axis=-1
    )
    return turned.reshape(row_count, -1)


def tdot(left, right):
    return lax.dot_general(
        left, right, (((0,), (0,)), ((), ())), preferred_element_type=jnp.float32
    )


def ndot(left, right):
    return lax.dot_general(
        left, right, (((1,), (1,)), ((), ())), preferred_element_type=jnp.float32
    )


def embed_rows(byte_ids, table):
    onehot = (byte_ids[:, None] == jnp.arange(table.shape[0], dtype=jnp.int32)[None, :]).astype(
        jnp.bfloat16
    )
    return jnp.dot(onehot, table, preferred_element_type=jnp.float32).astype(jnp.bfloat16)


def normalize(embedded):
    widened = embedded.astype(jnp.float32)
    inv_rms = lax.rsqrt(jnp.mean(widened * widened, axis=1, keepdims=True) + EPSILON)
    return (widened, inv_rms, (widened * inv_rms).astype(jnp.bfloat16))


def keys_values(normed, positions, w_key, w_value):
    key_rows = rotate(jnp.dot(normed, w_key, preferred_element_type=jnp.float32), positions).astype(
        jnp.bfloat16
    )
    value_rows = jnp.dot(normed, w_value, preferred_element_type=jnp.float32).astype(jnp.bfloat16)
    return (key_rows, value_rows)


def head_group(
    query_heads, key_heads, value_heads, grad_heads, group_window, own_pos, key_pos, score_scale
):
    distance = own_pos[:, None] - key_pos[None, :]
    allowed = (
        (distance[None] >= 0)
        & (distance[None] < group_window[:, None, None])
        & (key_pos[None, None, :] >= 0)
    )
    scores = (
        jnp.einsum("qhd,khd->hqk", query_heads, key_heads, preferred_element_type=jnp.float32)
        * score_scale
    )
    masked = jnp.where(allowed, scores, -1e30)
    row_max = jnp.max(masked, axis=-1, keepdims=True)
    weights = jnp.where(allowed, jnp.exp(masked - row_max), 0.0)
    probs = weights / jnp.sum(weights, axis=-1, keepdims=True)
    probs_b = probs.astype(jnp.bfloat16)
    attended = jnp.einsum(
        "hqk,khd->qhd", probs_b, value_heads, preferred_element_type=jnp.float32
    ).astype(jnp.bfloat16)
    grad_probs = jnp.einsum(
        "qhd,khd->hqk", grad_heads, value_heads, preferred_element_type=jnp.float32
    )
    row_term = jnp.sum(probs * grad_probs, axis=-1, keepdims=True)
    grad_scores = (probs * (grad_probs - row_term) * score_scale).astype(jnp.bfloat16)
    grad_query = jnp.einsum(
        "hqk,khd->qhd", grad_scores, key_heads, preferred_element_type=jnp.float32
    )
    grad_key = jnp.einsum(
        "hqk,qhd->khd", grad_scores, query_heads, preferred_element_type=jnp.float32
    )
    grad_value = jnp.einsum("hqk,qhd->khd", probs_b, grad_heads, preferred_element_type=jnp.float32)
    return (attended, grad_query, grad_key, grad_value)


def general_device(token_ids, cotangent, table, w_query, w_key, w_value, w_out, window):
    local_ids = token_ids[0]
    grad_out = cotangent[0]
    length = local_ids.shape[0]
    features = table.shape[1]
    tail_rows = min(length, WINDOW)
    reach_devs = -(-WINDOW // length)
    halo_rows = reach_devs * tail_rows
    offset = lax.axis_index("seq") * length
    own_pos = offset + jnp.arange(length, dtype=jnp.int32)
    halo_pos = offset - halo_rows + jnp.arange(halo_rows, dtype=jnp.int32)
    score_scale = HEAD_DIM ** (-0.5)
    embedded = embed_rows(local_ids, table)
    widened, inv_rms, normed = normalize(embedded)
    query = rotate(jnp.dot(normed, w_query, preferred_element_type=jnp.float32), own_pos).astype(
        jnp.bfloat16
    )
    key_own, value_own = keys_values(normed, own_pos, w_key, w_value)
    key_pieces = []
    value_pieces = []
    for hop_index in range(reach_devs):
        far_keys, far_values = shifted((key_own, value_own), "seq", hop_index + 1)
        key_pieces.insert(0, far_keys)
        value_pieces.insert(0, far_values)
    key_halo = jnp.concatenate(key_pieces, axis=0)
    value_halo = jnp.concatenate(value_pieces, axis=0)
    span_rows = halo_rows + length
    key_all = jnp.concatenate([key_halo, key_own], axis=0)
    value_all = jnp.concatenate([value_halo, value_own], axis=0)
    key_pos = jnp.concatenate([halo_pos, own_pos], axis=0)
    query_heads = query.reshape(length, HEADS, HEAD_DIM)
    key_heads = key_all.reshape(span_rows, HEADS, HEAD_DIM)
    value_heads = value_all.reshape(span_rows, HEADS, HEAD_DIM)
    grad_att = ndot(grad_out, w_out).astype(jnp.bfloat16)
    grad_heads = grad_att.reshape(length, HEADS, HEAD_DIM)
    group_size = 4
    attended_parts = []
    query_parts = []
    key_parts = []
    value_parts = []
    for group_index in range(HEADS // group_size):
        lower = group_index * group_size
        upper = lower + group_size
        outputs = head_group(
            query_heads[:, lower:upper],
            key_heads[:, lower:upper],
            value_heads[:, lower:upper],
            grad_heads[:, lower:upper],
            window[lower:upper],
            own_pos,
            key_pos,
            score_scale,
        )
        attended_parts.append(outputs[0])
        query_parts.append(outputs[1])
        key_parts.append(outputs[2])
        value_parts.append(outputs[3])
    attended = jnp.concatenate(attended_parts, axis=1).reshape(length, features)
    grad_query = jnp.concatenate(query_parts, axis=1).reshape(length, features)
    grad_key = jnp.concatenate(key_parts, axis=1).reshape(span_rows, features)
    grad_value = jnp.concatenate(value_parts, axis=1).reshape(span_rows, features)
    tail_keys = grad_key[:halo_rows].reshape(reach_devs, tail_rows, features)
    tail_values = grad_value[:halo_rows].reshape(reach_devs, tail_rows, features)
    back_keys = jnp.zeros((tail_rows, features), jnp.float32)
    back_values = jnp.zeros((tail_rows, features), jnp.float32)
    for hop_index in range(reach_devs):
        got_keys, got_values = shifted(
            (tail_keys[reach_devs - 1 - hop_index], tail_values[reach_devs - 1 - hop_index]),
            "seq",
            -(hop_index + 1),
        )
        back_keys = back_keys + got_keys
        back_values = back_values + got_values
    own_keys = grad_key[halo_rows:]
    own_values = grad_value[halo_rows:]
    own_keys = jnp.concatenate([own_keys[: length - tail_rows], own_keys + back_keys], axis=0)
    own_values = jnp.concatenate(
        [own_values[: length - tail_rows], own_values + back_values], axis=0
    )
    grad_q_lin = unrotate(grad_query, own_pos).astype(jnp.bfloat16)
    grad_k_lin = unrotate(own_keys, own_pos).astype(jnp.bfloat16)
    grad_v_lin = own_values.astype(jnp.bfloat16)
    grad_normed = ndot(grad_q_lin, w_query) + ndot(grad_k_lin, w_key) + ndot(grad_v_lin, w_value)
    scaled = widened * inv_rms
    grad_input = (
        inv_rms * (grad_normed - scaled * jnp.mean(grad_normed * scaled, axis=1, keepdims=True))
    ).astype(jnp.bfloat16)
    term = jnp.concatenate(
        [
            tdot(normed, grad_q_lin),
            tdot(normed, grad_k_lin),
            tdot(normed, grad_v_lin),
            tdot(attended, grad_out),
        ],
        axis=0,
    )
    shares = lax.psum_scatter(term.astype(jnp.bfloat16), "seq", scatter_dimension=0, tiled=True)
    weight_grads = lax.psum(shares, "dp").astype(jnp.float32)
    return (grad_input[None], weight_grads)


GROUPS = 4
GROUP_HEADS = HEADS // GROUPS
GROUP_COLS = GROUP_HEADS * HEAD_DIM
TILE = 256
TOKEN_ROWS = 16
STRIP = 8
HALF = HEAD_DIM // 2
VMEM_BYTES = 48 * 1024 * 1024


def key_span(query_tile):
    first = max(0, query_tile - WINDOW // TILE)
    return (first * TILE, (query_tile - first + 1) * TILE)


def normed_table(table_ref):
    widened = table_ref[...].astype(jnp.float32)
    inv_rms = lax.rsqrt(jnp.mean(widened * widened, axis=1, keepdims=True) + EPSILON)
    return (widened * inv_rms).astype(jnp.bfloat16)


def onehot_columns(tokens, vocab):
    rows = lax.broadcasted_iota(jnp.int32, (vocab, tokens.shape[1]), 0)
    return (rows == tokens).astype(jnp.float32).astype(jnp.bfloat16)


def send_kernel(spot_ref, tokens_ref, cotangent_ref, out_weights_ref, *out_refs):
    early_refs, grads_ref = out_refs[:-1], out_refs[-1]
    grad_att = ndot(out_weights_ref[...], cotangent_ref[...]).astype(jnp.bfloat16)
    grads_ref[...] = grad_att
    block = tokens_ref.shape[1]
    tokens = jnp.broadcast_to(tokens_ref[...].astype(jnp.float32), (TOKEN_ROWS, block)).astype(
        jnp.bfloat16
    )
    for turn, early_ref in enumerate(early_refs):
        group = spot_ref[1] ^ turn
        place = pl.ds(pl.multiple_of(group * GROUP_COLS, GROUP_COLS), GROUP_COLS)
        early_ref[:GROUP_COLS, :] = grads_ref[place, :]
        early_ref[GROUP_COLS:, :] = tokens


def gate_kernel(*refs):
    del refs


def prepare_kernel(
    meta_ref,
    cotangent_ref,
    table_ref,
    query_ref,
    key_ref,
    value_ref,
    late_ref,
    lookup_ref,
    normed_ref,
    columns_ref,
):
    columns = late_ref.shape[2]
    for target in range(2 * GROUPS):
        side = target % 2
        late_ref[target] = cotangent_ref[:, side * columns : (side + 1) * columns]
    normed = normed_table(table_ref)
    half = normed.shape[1] // 2
    normed_ref[...] = jnp.where(meta_ref[GROUP_HEADS] == 0, normed[:, :half], normed[:, half:])
    place = pl.ds(pl.multiple_of(meta_ref[GROUP_HEADS + 1] * GROUP_COLS, GROUP_COLS), GROUP_COLS)
    for matrix, weights_ref in enumerate((query_ref, key_ref, value_ref)):
        columns_ref[...] = jnp.dot(
            normed, weights_ref[...], preferred_element_type=jnp.float32
        ).T
        mine = columns_ref[place, :]
        upper = mine.astype(jnp.bfloat16)
        rows = slice(matrix * GROUP_COLS, (matrix + 1) * GROUP_COLS)
        lookup_ref[0, rows, :] = upper
        lookup_ref[1, rows, :] = (mine - upper.astype(jnp.float32)).astype(jnp.bfloat16)


def attention_kernel(
    meta_ref,
    lookup_ref,
    cosine_ref,
    sine_ref,
    *rest,
):
    early_refs = rest[: 2 * GROUPS]
    attention_body(meta_ref, lookup_ref, cosine_ref, sine_ref, early_refs, *rest[2 * GROUPS :])


def attention_body(
    meta_ref,
    lookup_ref,
    cosine_ref,
    sine_ref,
    early_refs,
    rows_ref,
    sums_ref,
    attended_ref,
    value_key_ref,
    query_t_ref,
    key_t_ref,
    value_t_ref,
    grad_att_ref,
    onehot_ref,
    onehot_rows_ref,
    grad_query_ref,
    both_ref,
    scaled_ref,
    probs_ref,
    scores_ref,
    right_ref,
    products_ref,
    inverse_ref,
    term_ref,
):
    head = pl.program_id(0)
    block = early_refs[0].shape[1]
    length = len(early_refs) * block
    tiles = length // TILE
    vocab = lookup_ref.shape[2]
    half_vocab = vocab // 2
    half = jnp.bfloat16
    cosine = cosine_ref[...]
    sine_part = sine_ref[...]

    @pl.when(head == 0)
    def _():
        own = 2 * meta_ref[GROUP_HEADS + 1] + meta_ref[GROUP_HEADS]
        for turn, early_ref in enumerate(early_refs):
            lanes = pl.ds(pl.multiple_of((own ^ turn) * block, block), block)
            tokens = early_ref[GROUP_COLS : GROUP_COLS + TOKEN_ROWS, :]
            tokens = tokens.astype(jnp.float32)[:1].astype(jnp.int32)
            onehot_ref[:, lanes] = onehot_columns(tokens, vocab)
            grad_att_ref[:, :, lanes] = early_ref[:GROUP_COLS, :].reshape(
                GROUP_HEADS, HEAD_DIM, block
            )
        onehot = onehot_ref[...]
        onehot_rows_ref[...] = onehot.T
        size = 3 * GROUP_COLS
        chosen = jnp.dot(
            lookup_ref[...].reshape(2 * size, vocab), onehot, preferred_element_type=jnp.float32
        )

        def picked(start):
            lower = start + size
            return chosen[start : start + HEAD_DIM] + chosen[lower : lower + HEAD_DIM]

        def turned(columns):
            former = columns[:HALF]
            latter = columns[HALF:]
            return jnp.concatenate(
                [former * cosine - latter * sine_part, latter * cosine + former * sine_part], axis=0
            )

        for index in range(GROUP_HEADS):
            query = turned(picked(index * HEAD_DIM)) * HEAD_DIM ** (-0.5)
            keys = turned(picked(GROUP_COLS + index * HEAD_DIM)).astype(half)
            values = picked(2 * GROUP_COLS + index * HEAD_DIM).astype(half)
            value_key_ref[index] = jnp.concatenate([values, keys], axis=0).T
            query_t_ref[index] = query.astype(half)
            key_t_ref[index] = keys
            value_t_ref[index] = values

    width = meta_ref[head]
    grad_att = grad_att_ref[head]
    query_t = query_t_ref[head]
    blank = jnp.zeros((HEAD_DIM, TILE), half)
    base = lax.broadcasted_iota(jnp.int32, (STRIP, TILE), 1) - lax.broadcasted_iota(
        jnp.int32, (STRIP, TILE), 0
    )
    for tile in range(tiles):
        columns = slice(tile * TILE, (tile + 1) * TILE)
        right_ref[tile, :HEAD_DIM, :TILE] = grad_att[:, columns]
        right_ref[tile, HEAD_DIM:, :TILE] = blank
        right_ref[tile, :HEAD_DIM, TILE:] = blank
        right_ref[tile, HEAD_DIM:, TILE:] = query_t[:, columns]

    def multiply(tile):
        first, count = key_span(tile)
        products_ref[tile, :count, :] = jnp.dot(
            value_key_ref[head, first : first + count, :],
            right_ref[tile],
            preferred_element_type=jnp.float32,
        )

    def forward(tile):
        first, count = key_span(tile)
        columns = slice(tile * TILE, (tile + 1) * TILE)
        row_max = None
        for row in range(0, count, STRIP):
            offset = tile * TILE - first - row
            allowed = base < width - offset
            if offset - STRIP < 0:
                allowed = allowed & (base >= -offset)
            masked = jnp.where(allowed, products_ref[tile, row : row + STRIP, TILE:], -1e30)
            products_ref[tile, row : row + STRIP, TILE:] = masked
            row_max = masked if row_max is None else jnp.maximum(row_max, masked)
        row_max = jnp.max(row_max, axis=0, keepdims=True)
        total = None
        for row in range(0, count, 2 * STRIP):
            weights = jnp.exp(products_ref[tile, row : row + 2 * STRIP, TILE:] - row_max)
            total = weights if total is None else total + weights
            probs_ref[first + row : first + row + 2 * STRIP, columns] = weights.astype(half)
        inverse = 1.0 / jnp.sum(total, axis=0, keepdims=True)
        attended = inverse * jnp.dot(
            value_t_ref[head, :, first : first + count],
            probs_ref[first : first + count, columns],
            preferred_element_type=jnp.float32,
        )
        attended_ref[pl.ds(pl.multiple_of(head * HEAD_DIM, HEAD_DIM), HEAD_DIM), columns] = (
            attended.astype(half)
        )
        wide_grad = grad_att[:, columns].astype(jnp.float32)
        inverse_ref[:, columns] = inverse
        term_ref[:, columns] = jnp.sum(attended * wide_grad, axis=0, keepdims=True)
        scaled_ref[columns, :] = jnp.concatenate(
            [
                (inverse * query_t[:, columns].astype(jnp.float32)).astype(half),
                (inverse * wide_grad).astype(half),
            ],
            axis=0,
        ).T

    def backward(tile):
        first, count = key_span(tile)
        columns = slice(tile * TILE, (tile + 1) * TILE)
        row_term = term_ref[:, columns]
        for row in range(0, count, 2 * STRIP):
            strip = slice(first + row, first + row + 2 * STRIP)
            scores_ref[strip, columns] = (
                probs_ref[strip, columns].astype(jnp.float32)
                * (products_ref[tile, row : row + 2 * STRIP, :TILE] - row_term)
            ).astype(half)
        grad_query_ref[:, columns] = inverse_ref[:, columns] * jnp.dot(
            key_t_ref[head, :, first : first + count],
            scores_ref[first : first + count, columns],
            preferred_element_type=jnp.float32,
        )

    lanes = lax.broadcasted_iota(jnp.int32, (TILE, 2 * HEAD_DIM), 1)

    def collect(tile):
        start = tile * TILE
        stop = min(length, start + TILE + WINDOW)
        grad_key = jnp.dot(
            scores_ref[start : start + TILE, start:stop],
            scaled_ref[start:stop, :],
            preferred_element_type=jnp.float32,
        )
        grad_value = jnp.dot(
            probs_ref[start : start + TILE, start:stop],
            scaled_ref[start:stop, :],
            preferred_element_type=jnp.float32,
        )
        both_ref[:, start : start + TILE] = jnp.where(lanes < HEAD_DIM, grad_key, grad_value).T

    reach = WINDOW // TILE
    for step in range(tiles + 3 + reach):
        if step < tiles:
            multiply(step)
        if 0 <= step - 1 < tiles:
            forward(step - 1)
        if 0 <= step - 2 < tiles:
            backward(step - 2)
        ready = step - 3 - reach
        if 0 <= ready < tiles:
            collect(ready)
    def turned_back(columns):
        former = columns[:HALF]
        latter = columns[HALF:]
        return jnp.concatenate(
            [former * cosine + latter * sine_part, latter * cosine - former * sine_part], axis=0
        )

    both = both_ref[...]
    grads = jnp.concatenate(
        [
            turned_back(grad_query_ref[...] * HEAD_DIM ** (-0.5)),
            turned_back(both[:HEAD_DIM]),
            both[HEAD_DIM:],
        ],
        axis=0,
    ).astype(half)
    sums = jnp.dot(grads, onehot_rows_ref[...], preferred_element_type=jnp.float32).astype(half)
    for matrix in range(3):
        rows = slice(matrix * HEAD_DIM, (matrix + 1) * HEAD_DIM)
        place = pl.ds(
            pl.multiple_of(matrix * GROUP_COLS + head * HEAD_DIM, HEAD_DIM), HEAD_DIM
        )
        for core in range(2):
            lane = core * half_vocab
            sums_ref[core, place, :] = sums[rows, lane : lane + half_vocab]
        for target in range(GROUPS):
            start = target * 2 * block
            even = grads[rows, start : start + block]
            odd = grads[rows, start + block : start + 2 * block]
            rows_ref[target, place, :] = jnp.where(meta_ref[GROUP_HEADS] == 0, even, odd)


def out_kernel(meta_ref, attended_ref, cotangent_ref, sums_ref, keep_ref, give_ref):
    total = jnp.dot(attended_ref[...], cotangent_ref[...], preferred_element_type=jnp.float32)
    rows = total.shape[0] // 2
    base = sums_ref.shape[1]
    lanes = keep_ref.shape[1]
    first = meta_ref[GROUP_HEADS + 2] == 0
    keep_ref[:base, :] = jnp.where(first, sums_ref[0], sums_ref[1])
    give_ref[:base, :] = jnp.where(first, sums_ref[1], sums_ref[0])
    for chunk in range(total.shape[1] // lanes):
        part = total[:, chunk * lanes : (chunk + 1) * lanes]
        place = slice(base + chunk * rows, base + (chunk + 1) * rows)
        keep_ref[place, :] = jnp.where(first, part[:rows], part[rows:]).astype(jnp.bfloat16)
        give_ref[place, :] = jnp.where(first, part[rows:], part[:rows]).astype(jnp.bfloat16)


def core_kernel(keep_ref, got_ref, here_ref, out_ref):
    here_ref[...] = keep_ref[...] + got_ref[...]
    base = here_ref.shape[0] - out_ref.shape[0]
    out_ref[...] = here_ref[base:, :]


def combine_kernel(meta_ref, here_ref, there_ref, near_ref, far_ref, out_ref, *piece_refs):
    rows = GROUP_COLS
    for turn, piece_ref in enumerate(piece_refs):
        target = jnp.minimum(meta_ref[GROUP_HEADS + 1] ^ turn, 2)
        place = pl.ds(pl.multiple_of(target * rows, rows), rows)
        piece_ref[...] = here_ref[place, :] + there_ref[place, :]
    own = here_ref[3 * rows :, :] + there_ref[3 * rows :, :]
    other = near_ref[...] + far_ref[...]
    first = meta_ref[GROUP_HEADS] == 0
    size = own.shape[0]
    out_ref[:size, :] = jnp.where(first, own, other)
    out_ref[size:, :] = jnp.where(first, other, own)


def gather_kernel(meta_ref, s0, s1, s2, s3, own_ref, o0, o1, after_ref, mine_ref):
    del after_ref
    rows = GROUP_COLS
    size = own_ref.shape[0]
    group = meta_ref[GROUP_HEADS + 1]

    @pl.when(group < 3)
    def _():
        for turn, got in enumerate((s0, s1, s2, s3)):
            place = pl.ds(pl.multiple_of((group ^ turn) * rows, rows), rows)
            mine_ref[place, :] = got[...]
        tail = mine_ref.shape[0] - GROUPS * rows
        mine_ref[GROUPS * rows :, :] = jnp.zeros((tail, mine_ref.shape[1]), jnp.bfloat16)

    @pl.when(group == 3)
    def _():
        mine_ref[:size, :] = o0[...]
        mine_ref[size:, :] = jnp.where(meta_ref[GROUP_HEADS] == 0, o1[...], own_ref[...])


def input_kernel(tokens_ref, table_ref, query_ref, key_ref, value_ref, rows_ref, out_ref):
    vocab = table_ref.shape[0]
    onehot = onehot_columns(tokens_ref[...], vocab)
    embedded = tdot(onehot, table_ref[...])
    inv_rms = lax.rsqrt(jnp.mean(embedded * embedded, axis=1, keepdims=True) + EPSILON)
    grad_normed = None
    for matrix, weights in enumerate((query_ref, key_ref, value_ref)):
        columns = jnp.concatenate(
            [
                rows_ref[group, matrix * GROUP_COLS : (matrix + 1) * GROUP_COLS, :]
                for group in range(GROUPS)
            ],
            axis=0,
        )
        part = ndot(columns.astype(jnp.float32).T.astype(jnp.bfloat16), weights[...])
        grad_normed = part if grad_normed is None else grad_normed + part
    scaled = embedded * inv_rms
    out_ref[...] = (
        inv_rms * (grad_normed - scaled * jnp.mean(grad_normed * scaled, axis=1, keepdims=True))
    ).astype(jnp.bfloat16)


def weight_kernel(meta_ref, normed_ref, mine_ref, other_ref, out_ref):
    half_vocab = mine_ref.shape[1]
    first_core = meta_ref[GROUP_HEADS + 2] == 0

    @pl.when(meta_ref[GROUP_HEADS + 1] < 3)
    def _():
        first = normed_ref[:half_vocab, :]
        second = normed_ref[half_vocab:, :]
        upper = jnp.where(first_core, first, second)
        lower = jnp.where(first_core, second, first)
        total = None
        for part, sums_ref in ((upper, mine_ref), (lower, other_ref)):
            term = lax.dot_general(
                part,
                sums_ref[: GROUPS * GROUP_COLS, :],
                (((0,), (1,)), ((), ())),
                preferred_element_type=jnp.float32,
            )
            total = term if total is None else total + term
        out_ref[...] = total

    @pl.when(meta_ref[GROUP_HEADS + 1] == 3)
    def _():
        rows = GROUP_COLS // 2
        for half in range(2):
            for column in range(6):
                start = (half * 6 + column) * rows
                for core in range(2):
                    same = first_core == (core == 0)
                    value = jnp.where(
                        same, mine_ref[start : start + rows, :], other_ref[start : start + rows, :]
                    )
                    row = half * GROUP_COLS + core * rows
                    out_ref[
                        row : row + rows, column * half_vocab : (column + 1) * half_vocab
                    ] = value.astype(jnp.float32)


def whole(shape):
    return pl.BlockSpec(shape, lambda *_: (0,) * len(shape))


def swapped(block, axis, bit):
    route = [(i, i ^ bit) for i in range(lax.axis_size(axis))]
    return lax.ppermute(block, axis, route)


def rope_table(length):
    frequency = (10000.0 ** (-2.0 * np.arange(HALF, dtype=np.float32) / HEAD_DIM)).astype(np.float32)
    angles = frequency[:, None] * np.arange(length, dtype=np.float32)[None, :]
    angles = angles.astype(np.float64)
    return (
        jnp.asarray(np.cos(angles).astype(np.float32)),
        jnp.asarray(np.sin(angles).astype(np.float32)),
    )


def grouped_device(token_ids, cotangent, table, w_query, w_key, w_value, w_out, window):
    place = lax.axis_index("seq")
    core = lax.axis_index("dp") % 2
    group = place // 2
    side = place % 2
    block = token_ids.shape[1]
    features = table.shape[1]
    vocab = table.shape[0]
    blocks = lax.axis_size("seq")
    length = block * blocks
    grad_out = cotangent[0]
    meta = jnp.concatenate(
        [
            lax.dynamic_slice_in_dim(window, group * GROUP_HEADS, GROUP_HEADS, 0),
            jnp.stack([side, group, core]).astype(jnp.int32),
        ]
    )
    spot = jnp.stack([side, group, core]).astype(jnp.int32)
    cosine, sine_part = rope_table(length)

    def call(
        body, operands, outs, scratch=(), steps=1, flops=10**8, moved=10**6, loose=0, grant=VMEM_BYTES
    ):
        spaces = [whole(operand.shape) for operand in operands]
        for index in range(loose):
            spaces[-1 - index] = pl.BlockSpec(memory_space=pl.ANY)
        if operands[0].ndim == 1:
            spaces[0] = pl.BlockSpec(memory_space=pltpu.SMEM)
        return pl.pallas_call(
            body,
            grid=(steps,),
            in_specs=spaces,
            out_specs=[whole(shape) for shape, _ in outs],
            out_shape=[jax.ShapeDtypeStruct(shape, dtype) for shape, dtype in outs],
            scratch_shapes=list(scratch),
            compiler_params=pltpu.CompilerParams(
                dimension_semantics=("arbitrary",), vmem_limit_bytes=grant
            ),
            cost_estimate=pl.CostEstimate(flops=flops, bytes_accessed=moved, transcendentals=0),
        )(*operands)

    half = jnp.bfloat16
    sent = call(
        send_kernel,
        (spot, token_ids, grad_out, w_out),
        [((GROUP_COLS + TOKEN_ROWS, block), half)] * GROUPS,
        [pltpu.VMEM((features, block), half)],
        grant=60 * 1024 * 1024,
    )
    early = [sent[0]] + [None] * (blocks - 1)
    for turn in (4, 6, 5, 7, 2, 3, 1):
        early[turn] = swapped(sent[turn // 2], "seq", turn)
    late, lookup, normed = call(
        prepare_kernel,
        (meta, grad_out, table, w_query, w_key, w_value),
        [
            ((blocks, block, features // 2), half),
            ((2, 3 * GROUP_COLS, vocab), half),
            ((vocab, features // 2), half),
        ],
        [pltpu.VMEM((features, vocab), jnp.float32)],
        flops=10**9,
        moved=5 * 10**6,
        grant=60 * 1024 * 1024,
    )
    late = pl.pallas_call(
        gate_kernel,
        in_specs=[pl.BlockSpec(memory_space=pl.ANY)] * blocks,
        out_specs=pl.BlockSpec(memory_space=pl.ANY),
        out_shape=jax.ShapeDtypeStruct(late.shape, half),
        input_output_aliases={0: 0},
    )(late, *early[1:])
    late = lax.all_to_all(late, "seq", split_axis=0, concat_axis=0, tiled=True)
    heads_shape = (GROUP_HEADS, HEAD_DIM, length)
    rows_shape = (GROUP_HEADS, length, 2 * HEAD_DIM)
    rows, sums, attended = call(
        attention_kernel,
        (meta, lookup, cosine, sine_part, *early),
        [
            ((GROUPS, 3 * GROUP_COLS, block), half),
            ((2, 3 * GROUP_COLS, vocab // 2), half),
            ((GROUP_COLS, length), half),
        ],
        [
            pltpu.VMEM(rows_shape, half),
            pltpu.VMEM(heads_shape, half),
            pltpu.VMEM(heads_shape, half),
            pltpu.VMEM(heads_shape, half),
            pltpu.VMEM(heads_shape, half),
            pltpu.VMEM((vocab, length), half),
            pltpu.VMEM((length, vocab), half),
            pltpu.VMEM((HEAD_DIM, length), jnp.float32),
            pltpu.VMEM((2 * HEAD_DIM, length), jnp.float32),
            pltpu.VMEM((length, 2 * HEAD_DIM), half),
            pltpu.VMEM((length, length), half),
            pltpu.VMEM((length, length), half),
            pltpu.VMEM((length // TILE, 2 * HEAD_DIM, 2 * TILE), half),
            pltpu.VMEM((length // TILE, WINDOW + TILE, 2 * TILE), jnp.float32),
            pltpu.VMEM((1, length), jnp.float32),
            pltpu.VMEM((1, length), jnp.float32),
        ],
        steps=GROUP_HEADS,
        flops=8 * 10**9,
        moved=8 * 10**6,
    )
    planes = [[2 * z + x for z in range(GROUPS)] for x in range(2)]

    def over_plane(chunks):
        return lax.all_to_all(
            chunks, "seq", split_axis=0, concat_axis=0, axis_index_groups=planes, tiled=True
        )

    got_rows = over_plane(rows)
    lanes = vocab // 2
    out_rows = 3 * GROUP_COLS // 2
    packed = 3 * GROUP_COLS + out_rows
    keep, give = call(
        out_kernel,
        (meta, attended, late.reshape(length, features // 2), sums),
        [((packed, lanes), half)] * 2,
    )
    here, here_out = call(
        core_kernel,
        (keep, swapped(give, "dp", 1)),
        [((packed, lanes), half), ((out_rows, lanes), half)],
    )
    there = swapped(here, "dp", 2)
    inward = [(2 * z + 1 - z // 2, 2 * z + z // 2) for z in range(GROUPS)]
    near = lax.ppermute(here_out, "seq", inward)
    far = lax.ppermute(
        here_out,
        ("dp", "seq"),
        [
            (blocks * d + source, blocks * (d ^ 2) + target)
            for d in range(lax.axis_size("dp"))
            for source, target in inward
        ],
    )
    full_out, *pieces = call(
        combine_kernel,
        (meta, here, there, near, far),
        [((2 * out_rows, lanes), half)] + [((GROUP_COLS, lanes), half)] * GROUPS,
    )
    last = blocks - 2
    got_out = [
        lax.ppermute(full_out, "seq", [(0, last), (last - 1, last + 1)]),
        lax.ppermute(full_out, "seq", [(2, last)]),
    ]
    got = [pieces[0]] + [None] * (GROUPS - 1)
    for turn in (2, 3, 1):
        route = [(i, i ^ (2 * turn)) for i in range(blocks) if (i ^ (2 * turn)) < last]
        got[turn] = lax.ppermute(pieces[turn], "seq", route)
    (grad_input,) = call(
        input_kernel,
        (token_ids, table, w_query, w_key, w_value, got_rows),
        [((block, features), half)],
        flops=10**9,
        moved=5 * 10**6,
    )
    (mine,) = call(
        gather_kernel,
        (meta, *got, full_out, *got_out, grad_input),
        [((4 * out_rows, lanes), half)],
        loose=1,
    )
    (weight_grads,) = call(
        weight_kernel,
        (meta, normed, mine, swapped(mine, "dp", 1)),
        [((features // 2, features), jnp.float32)],
        flops=10**9,
        moved=5 * 10**6,
    )
    return (grad_input[None], weight_grads)


def on_device(token_ids, cotangent, table, w_query, w_key, w_value, w_out, window):
    fits = (
        lax.axis_size("seq") == 2 * GROUPS
        and lax.axis_size("dp") == 4
        and token_ids.shape == (1, 128)
        and table.shape == (256, HEADS * HEAD_DIM)
    )
    plan = grouped_device if fits else general_device
    return plan(token_ids, cotangent, table, w_query, w_key, w_value, w_out, window)


def solution(mesh):
    return jax.shard_map(
        on_device,
        mesh=mesh,
        in_specs=(P("dp", "seq"), P("dp", "seq", None), P(), P(), P(), P(), P(), P()),
        out_specs=(P("dp", "seq", None), P("seq", None)),
        check_vma=False,
    )
```

```python
import jax
import jax.numpy as jnp
import numpy as np
from jax import lax
from jax.experimental import pallas as pl
from jax.experimental.pallas import tpu as pltpu
from jax.sharding import PartitionSpec as P

HEADS = 12
HEAD_DIM = 64
WINDOW = 512


EPSILON = 1e-05


def shifted(block, axis, distance):
    devices = range(lax.axis_size(axis))
    route = [(i - distance, i) for i in devices if i - distance in devices]
    return lax.ppermute(block, axis, route)


def rotate(values, positions):
    row_count = values.shape[0]
    shaped = values.reshape(row_count, -1, HEAD_DIM)
    middle = HEAD_DIM // 2
    frequency = 10000.0 ** (-2.0 * jnp.arange(middle, dtype=jnp.float32) / HEAD_DIM)
    angles = positions.astype(jnp.float32)[:, None] * frequency[None, :]
    cosine = jnp.cos(angles)[:, None, :]
    sine_part = jnp.sin(angles)[:, None, :]
    former = shaped[..., :middle]
    latter = shaped[..., middle:]
    turned = jnp.concatenate(
        [former * cosine - latter * sine_part, latter * cosine + former * sine_part], axis=-1
    )
    return turned.reshape(row_count, -1)


def unrotate(values, positions):
    row_count = values.shape[0]
    shaped = values.reshape(row_count, -1, HEAD_DIM)
    middle = HEAD_DIM // 2
    frequency = 10000.0 ** (-2.0 * jnp.arange(middle, dtype=jnp.float32) / HEAD_DIM)
    angles = positions.astype(jnp.float32)[:, None] * frequency[None, :]
    cosine = jnp.cos(angles)[:, None, :]
    sine_part = jnp.sin(angles)[:, None, :]
    former = shaped[..., :middle]
    latter = shaped[..., middle:]
    turned = jnp.concatenate(
        [former * cosine + latter * sine_part, latter * cosine - former * sine_part], axis=-1
    )
    return turned.reshape(row_count, -1)


def tdot(left, right):
    return lax.dot_general(
        left, right, (((0,), (0,)), ((), ())), preferred_element_type=jnp.float32
    )


def ndot(left, right):
    return lax.dot_general(
        left, right, (((1,), (1,)), ((), ())), preferred_element_type=jnp.float32
    )


def embed_rows(byte_ids, table):
    onehot = (byte_ids[:, None] == jnp.arange(table.shape[0], dtype=jnp.int32)[None, :]).astype(
        jnp.bfloat16
    )
    return jnp.dot(onehot, table, preferred_element_type=jnp.float32).astype(jnp.bfloat16)


def normalize(embedded):
    widened = embedded.astype(jnp.float32)
    inv_rms = lax.rsqrt(jnp.mean(widened * widened, axis=1, keepdims=True) + EPSILON)
    return (widened, inv_rms, (widened * inv_rms).astype(jnp.bfloat16))


def keys_values(normed, positions, w_key, w_value):
    key_rows = rotate(jnp.dot(normed, w_key, preferred_element_type=jnp.float32), positions).astype(
        jnp.bfloat16
    )
    value_rows = jnp.dot(normed, w_value, preferred_element_type=jnp.float32).astype(jnp.bfloat16)
    return (key_rows, value_rows)


def head_group(
    query_heads, key_heads, value_heads, grad_heads, group_window, own_pos, key_pos, score_scale
):
    distance = own_pos[:, None] - key_pos[None, :]
    allowed = (
        (distance[None] >= 0)
        & (distance[None] < group_window[:, None, None])
        & (key_pos[None, None, :] >= 0)
    )
    scores = (
        jnp.einsum("qhd,khd->hqk", query_heads, key_heads, preferred_element_type=jnp.float32)
        * score_scale
    )
    masked = jnp.where(allowed, scores, -1e30)
    row_max = jnp.max(masked, axis=-1, keepdims=True)
    weights = jnp.where(allowed, jnp.exp(masked - row_max), 0.0)
    probs = weights / jnp.sum(weights, axis=-1, keepdims=True)
    probs_b = probs.astype(jnp.bfloat16)
    attended = jnp.einsum(
        "hqk,khd->qhd", probs_b, value_heads, preferred_element_type=jnp.float32
    ).astype(jnp.bfloat16)
    grad_probs = jnp.einsum(
        "qhd,khd->hqk", grad_heads, value_heads, preferred_element_type=jnp.float32
    )
    row_term = jnp.sum(probs * grad_probs, axis=-1, keepdims=True)
    grad_scores = (probs * (grad_probs - row_term) * score_scale).astype(jnp.bfloat16)
    grad_query = jnp.einsum(
        "hqk,khd->qhd", grad_scores, key_heads, preferred_element_type=jnp.float32
    )
    grad_key = jnp.einsum(
        "hqk,qhd->khd", grad_scores, query_heads, preferred_element_type=jnp.float32
    )
    grad_value = jnp.einsum("hqk,qhd->khd", probs_b, grad_heads, preferred_element_type=jnp.float32)
    return (attended, grad_query, grad_key, grad_value)


def general_device(token_ids, cotangent, table, w_query, w_key, w_value, w_out, window):
    local_ids = token_ids[0]
    grad_out = cotangent[0]
    length = local_ids.shape[0]
    features = table.shape[1]
    tail_rows = min(length, WINDOW)
    reach_devs = -(-WINDOW // length)
    halo_rows = reach_devs * tail_rows
    offset = lax.axis_index("seq") * length
    own_pos = offset + jnp.arange(length, dtype=jnp.int32)
    halo_pos = offset - halo_rows + jnp.arange(halo_rows, dtype=jnp.int32)
    score_scale = HEAD_DIM ** (-0.5)
    embedded = embed_rows(local_ids, table)
    widened, inv_rms, normed = normalize(embedded)
    query = rotate(jnp.dot(normed, w_query, preferred_element_type=jnp.float32), own_pos).astype(
        jnp.bfloat16
    )
    key_own, value_own = keys_values(normed, own_pos, w_key, w_value)
    key_pieces = []
    value_pieces = []
    for hop_index in range(reach_devs):
        far_keys, far_values = shifted((key_own, value_own), "seq", hop_index + 1)
        key_pieces.insert(0, far_keys)
        value_pieces.insert(0, far_values)
    key_halo = jnp.concatenate(key_pieces, axis=0)
    value_halo = jnp.concatenate(value_pieces, axis=0)
    span_rows = halo_rows + length
    key_all = jnp.concatenate([key_halo, key_own], axis=0)
    value_all = jnp.concatenate([value_halo, value_own], axis=0)
    key_pos = jnp.concatenate([halo_pos, own_pos], axis=0)
    query_heads = query.reshape(length, HEADS, HEAD_DIM)
    key_heads = key_all.reshape(span_rows, HEADS, HEAD_DIM)
    value_heads = value_all.reshape(span_rows, HEADS, HEAD_DIM)
    grad_att = ndot(grad_out, w_out).astype(jnp.bfloat16)
    grad_heads = grad_att.reshape(length, HEADS, HEAD_DIM)
    group_size = 4
    attended_parts = []
    query_parts = []
    key_parts = []
    value_parts = []
    for group_index in range(HEADS // group_size):
        lower = group_index * group_size
        upper = lower + group_size
        outputs = head_group(
            query_heads[:, lower:upper],
            key_heads[:, lower:upper],
            value_heads[:, lower:upper],
            grad_heads[:, lower:upper],
            window[lower:upper],
            own_pos,
            key_pos,
            score_scale,
        )
        attended_parts.append(outputs[0])
        query_parts.append(outputs[1])
        key_parts.append(outputs[2])
        value_parts.append(outputs[3])
    attended = jnp.concatenate(attended_parts, axis=1).reshape(length, features)
    grad_query = jnp.concatenate(query_parts, axis=1).reshape(length, features)
    grad_key = jnp.concatenate(key_parts, axis=1).reshape(span_rows, features)
    grad_value = jnp.concatenate(value_parts, axis=1).reshape(span_rows, features)
    tail_keys = grad_key[:halo_rows].reshape(reach_devs, tail_rows, features)
    tail_values = grad_value[:halo_rows].reshape(reach_devs, tail_rows, features)
    back_keys = jnp.zeros((tail_rows, features), jnp.float32)
    back_values = jnp.zeros((tail_rows, features), jnp.float32)
    for hop_index in range(reach_devs):
        got_keys, got_values = shifted(
            (tail_keys[reach_devs - 1 - hop_index], tail_values[reach_devs - 1 - hop_index]),
            "seq",
            -(hop_index + 1),
        )
        back_keys = back_keys + got_keys
        back_values = back_values + got_values
    own_keys = grad_key[halo_rows:]
    own_values = grad_value[halo_rows:]
    own_keys = jnp.concatenate([own_keys[: length - tail_rows], own_keys + back_keys], axis=0)
    own_values = jnp.concatenate(
        [own_values[: length - tail_rows], own_values + back_values], axis=0
    )
    grad_q_lin = unrotate(grad_query, own_pos).astype(jnp.bfloat16)
    grad_k_lin = unrotate(own_keys, own_pos).astype(jnp.bfloat16)
    grad_v_lin = own_values.astype(jnp.bfloat16)
    grad_normed = ndot(grad_q_lin, w_query) + ndot(grad_k_lin, w_key) + ndot(grad_v_lin, w_value)
    scaled = widened * inv_rms
    grad_input = (
        inv_rms * (grad_normed - scaled * jnp.mean(grad_normed * scaled, axis=1, keepdims=True))
    ).astype(jnp.bfloat16)
    term = jnp.concatenate(
        [
            tdot(normed, grad_q_lin),
            tdot(normed, grad_k_lin),
            tdot(normed, grad_v_lin),
            tdot(attended, grad_out),
        ],
        axis=0,
    )
    shares = lax.psum_scatter(term.astype(jnp.bfloat16), "seq", scatter_dimension=0, tiled=True)
    weight_grads = lax.psum(shares, "dp").astype(jnp.float32)
    return (grad_input[None], weight_grads)


GROUPS = 4
GROUP_HEADS = HEADS // GROUPS
GROUP_COLS = GROUP_HEADS * HEAD_DIM
TILE = 256
TOKEN_ROWS = 16
STRIP = 8
HALF = HEAD_DIM // 2
VMEM_BYTES = 48 * 1024 * 1024


def key_span(query_tile):
    first = max(0, query_tile - WINDOW // TILE)
    return (first * TILE, (query_tile - first + 1) * TILE)


def normed_table(table_ref):
    widened = table_ref[...].astype(jnp.float32)
    inv_rms = lax.rsqrt(jnp.mean(widened * widened, axis=1, keepdims=True) + EPSILON)
    return (widened * inv_rms).astype(jnp.bfloat16)


def onehot_columns(tokens, vocab):
    rows = lax.broadcasted_iota(jnp.int32, (vocab, tokens.shape[1]), 0)
    return (rows == tokens).astype(jnp.float32).astype(jnp.bfloat16)


def send_kernel(spot_ref, tokens_ref, cotangent_ref, out_weights_ref, *out_refs):
    early_refs, grads_ref = out_refs[:-1], out_refs[-1]
    grad_att = ndot(out_weights_ref[...], cotangent_ref[...]).astype(jnp.bfloat16)
    grads_ref[...] = grad_att
    block = tokens_ref.shape[1]
    tokens = jnp.broadcast_to(tokens_ref[...].astype(jnp.float32), (TOKEN_ROWS, block)).astype(
        jnp.bfloat16
    )
    for turn, early_ref in enumerate(early_refs):
        group = spot_ref[1] ^ turn
        place = pl.ds(pl.multiple_of(group * GROUP_COLS, GROUP_COLS), GROUP_COLS)
        early_ref[:GROUP_COLS, :] = grads_ref[place, :]
        early_ref[GROUP_COLS:, :] = tokens


def prepare_kernel(
    meta_ref,
    cotangent_ref,
    table_ref,
    query_ref,
    key_ref,
    value_ref,
    first_ref,
    second_ref,
    late_ref,
    lookup_ref,
    normed_ref,
    columns_ref,
):
    del first_ref, second_ref
    columns = late_ref.shape[2]
    for target in range(2 * GROUPS):
        side = target % 2
        late_ref[target] = cotangent_ref[:, side * columns : (side + 1) * columns]
    normed = normed_table(table_ref)
    half = normed.shape[1] // 2
    normed_ref[...] = jnp.where(meta_ref[GROUP_HEADS] == 0, normed[:, :half], normed[:, half:])
    place = pl.ds(pl.multiple_of(meta_ref[GROUP_HEADS + 1] * GROUP_COLS, GROUP_COLS), GROUP_COLS)
    for matrix, weights_ref in enumerate((query_ref, key_ref, value_ref)):
        columns_ref[...] = jnp.dot(
            normed, weights_ref[...], preferred_element_type=jnp.float32
        ).T
        mine = columns_ref[place, :]
        upper = mine.astype(jnp.bfloat16)
        rows = slice(matrix * GROUP_COLS, (matrix + 1) * GROUP_COLS)
        lookup_ref[0, rows, :] = upper
        lookup_ref[1, rows, :] = (mine - upper.astype(jnp.float32)).astype(jnp.bfloat16)


def attention_kernel(
    meta_ref,
    lookup_ref,
    cosine_ref,
    sine_ref,
    *rest,
):
    early_refs = rest[: 2 * GROUPS]
    attention_body(meta_ref, lookup_ref, cosine_ref, sine_ref, early_refs, *rest[2 * GROUPS :])


def attention_body(
    meta_ref,
    lookup_ref,
    cosine_ref,
    sine_ref,
    early_refs,
    rows_ref,
    sums_ref,
    attended_ref,
    value_key_ref,
    query_t_ref,
    key_t_ref,
    value_t_ref,
    grad_att_ref,
    onehot_ref,
    onehot_rows_ref,
    grad_query_ref,
    both_ref,
    scaled_ref,
    probs_ref,
    scores_ref,
    right_ref,
    products_ref,
    inverse_ref,
    term_ref,
):
    head = pl.program_id(0)
    block = early_refs[0].shape[1]
    length = len(early_refs) * block
    tiles = length // TILE
    vocab = lookup_ref.shape[2]
    half_vocab = vocab // 2
    half = jnp.bfloat16
    cosine = cosine_ref[...]
    sine_part = sine_ref[...]

    @pl.when(head == 0)
    def _():
        own = 2 * meta_ref[GROUP_HEADS + 1] + meta_ref[GROUP_HEADS]
        for turn, early_ref in enumerate(early_refs):
            lanes = pl.ds(pl.multiple_of((own ^ turn) * block, block), block)
            tokens = early_ref[GROUP_COLS : GROUP_COLS + TOKEN_ROWS, :]
            tokens = tokens.astype(jnp.float32)[:1].astype(jnp.int32)
            onehot_ref[:, lanes] = onehot_columns(tokens, vocab)
            grad_att_ref[:, :, lanes] = early_ref[:GROUP_COLS, :].reshape(
                GROUP_HEADS, HEAD_DIM, block
            )
        onehot = onehot_ref[...]
        onehot_rows_ref[...] = onehot.T
        size = 3 * GROUP_COLS
        chosen = jnp.dot(
            lookup_ref[...].reshape(2 * size, vocab), onehot, preferred_element_type=jnp.float32
        )

        def picked(start):
            lower = start + size
            return chosen[start : start + HEAD_DIM] + chosen[lower : lower + HEAD_DIM]

        def turned(columns):
            former = columns[:HALF]
            latter = columns[HALF:]
            return jnp.concatenate(
                [former * cosine - latter * sine_part, latter * cosine + former * sine_part], axis=0
            )

        for index in range(GROUP_HEADS):
            query = turned(picked(index * HEAD_DIM)) * HEAD_DIM ** (-0.5)
            keys = turned(picked(GROUP_COLS + index * HEAD_DIM)).astype(half)
            values = picked(2 * GROUP_COLS + index * HEAD_DIM).astype(half)
            value_key_ref[index] = jnp.concatenate([values, keys], axis=0).T
            query_t_ref[index] = query.astype(half)
            key_t_ref[index] = keys
            value_t_ref[index] = values

    width = meta_ref[head]
    grad_att = grad_att_ref[head]
    query_t = query_t_ref[head]
    blank = jnp.zeros((HEAD_DIM, TILE), half)
    base = lax.broadcasted_iota(jnp.int32, (STRIP, TILE), 1) - lax.broadcasted_iota(
        jnp.int32, (STRIP, TILE), 0
    )
    for tile in range(tiles):
        columns = slice(tile * TILE, (tile + 1) * TILE)
        right_ref[tile, :HEAD_DIM, :TILE] = grad_att[:, columns]
        right_ref[tile, HEAD_DIM:, :TILE] = blank
        right_ref[tile, :HEAD_DIM, TILE:] = blank
        right_ref[tile, HEAD_DIM:, TILE:] = query_t[:, columns]

    def multiply(tile):
        first, count = key_span(tile)
        products_ref[tile, :count, :] = jnp.dot(
            value_key_ref[head, first : first + count, :],
            right_ref[tile],
            preferred_element_type=jnp.float32,
        )

    def forward(tile):
        first, count = key_span(tile)
        columns = slice(tile * TILE, (tile + 1) * TILE)
        row_max = None
        for row in range(0, count, STRIP):
            offset = tile * TILE - first - row
            allowed = base < width - offset
            if offset - STRIP < 0:
                allowed = allowed & (base >= -offset)
            masked = jnp.where(allowed, products_ref[tile, row : row + STRIP, TILE:], -1e30)
            products_ref[tile, row : row + STRIP, TILE:] = masked
            row_max = masked if row_max is None else jnp.maximum(row_max, masked)
        row_max = jnp.max(row_max, axis=0, keepdims=True)
        total = None
        for row in range(0, count, 2 * STRIP):
            weights = jnp.exp(products_ref[tile, row : row + 2 * STRIP, TILE:] - row_max)
            total = weights if total is None else total + weights
            probs_ref[first + row : first + row + 2 * STRIP, columns] = weights.astype(half)
        inverse = 1.0 / jnp.sum(total, axis=0, keepdims=True)
        attended = inverse * jnp.dot(
            value_t_ref[head, :, first : first + count],
            probs_ref[first : first + count, columns],
            preferred_element_type=jnp.float32,
        )
        attended_ref[pl.ds(pl.multiple_of(head * HEAD_DIM, HEAD_DIM), HEAD_DIM), columns] = (
            attended.astype(half)
        )
        wide_grad = grad_att[:, columns].astype(jnp.float32)
        inverse_ref[:, columns] = inverse
        term_ref[:, columns] = jnp.sum(attended * wide_grad, axis=0, keepdims=True)
        scaled_ref[columns, :] = jnp.concatenate(
            [
                (inverse * query_t[:, columns].astype(jnp.float32)).astype(half),
                (inverse * wide_grad).astype(half),
            ],
            axis=0,
        ).T

    def backward(tile):
        first, count = key_span(tile)
        columns = slice(tile * TILE, (tile + 1) * TILE)
        row_term = term_ref[:, columns]
        for row in range(0, count, 2 * STRIP):
            strip = slice(first + row, first + row + 2 * STRIP)
            scores_ref[strip, columns] = (
                probs_ref[strip, columns].astype(jnp.float32)
                * (products_ref[tile, row : row + 2 * STRIP, :TILE] - row_term)
            ).astype(half)
        grad_query_ref[:, columns] = inverse_ref[:, columns] * jnp.dot(
            key_t_ref[head, :, first : first + count],
            scores_ref[first : first + count, columns],
            preferred_element_type=jnp.float32,
        )

    lanes = lax.broadcasted_iota(jnp.int32, (TILE, 2 * HEAD_DIM), 1)

    def collect(tile):
        start = tile * TILE
        stop = min(length, start + TILE + WINDOW)
        grad_key = jnp.dot(
            scores_ref[start : start + TILE, start:stop],
            scaled_ref[start:stop, :],
            preferred_element_type=jnp.float32,
        )
        grad_value = jnp.dot(
            probs_ref[start : start + TILE, start:stop],
            scaled_ref[start:stop, :],
            preferred_element_type=jnp.float32,
        )
        both_ref[:, start : start + TILE] = jnp.where(lanes < HEAD_DIM, grad_key, grad_value).T

    reach = WINDOW // TILE
    for step in range(tiles + 3 + reach):
        if step < tiles:
            multiply(step)
        if 0 <= step - 1 < tiles:
            forward(step - 1)
        if 0 <= step - 2 < tiles:
            backward(step - 2)
        ready = step - 3 - reach
        if 0 <= ready < tiles:
            collect(ready)
    def turned_back(columns):
        former = columns[:HALF]
        latter = columns[HALF:]
        return jnp.concatenate(
            [former * cosine + latter * sine_part, latter * cosine - former * sine_part], axis=0
        )

    both = both_ref[...]
    grads = jnp.concatenate(
        [
            turned_back(grad_query_ref[...] * HEAD_DIM ** (-0.5)),
            turned_back(both[:HEAD_DIM]),
            both[HEAD_DIM:],
        ],
        axis=0,
    ).astype(half)
    sums = jnp.dot(grads, onehot_rows_ref[...], preferred_element_type=jnp.float32).astype(half)
    for matrix in range(3):
        rows = slice(matrix * HEAD_DIM, (matrix + 1) * HEAD_DIM)
        place = pl.ds(
            pl.multiple_of(matrix * GROUP_COLS + head * HEAD_DIM, HEAD_DIM), HEAD_DIM
        )
        for core in range(2):
            lane = core * half_vocab
            sums_ref[core, place, :] = sums[rows, lane : lane + half_vocab]
        for target in range(GROUPS):
            start = target * 2 * block
            even = grads[rows, start : start + block]
            odd = grads[rows, start + block : start + 2 * block]
            rows_ref[target, place, :] = jnp.where(meta_ref[GROUP_HEADS] == 0, even, odd)


def out_kernel(meta_ref, attended_ref, cotangent_ref, sums_ref, keep_ref, give_ref):
    total = jnp.dot(attended_ref[...], cotangent_ref[...], preferred_element_type=jnp.float32)
    rows = total.shape[0] // 2
    base = sums_ref.shape[1]
    lanes = keep_ref.shape[1]
    first = meta_ref[GROUP_HEADS + 2] == 0
    keep_ref[:base, :] = jnp.where(first, sums_ref[0], sums_ref[1])
    give_ref[:base, :] = jnp.where(first, sums_ref[1], sums_ref[0])
    for chunk in range(total.shape[1] // lanes):
        part = total[:, chunk * lanes : (chunk + 1) * lanes]
        place = slice(base + chunk * rows, base + (chunk + 1) * rows)
        keep_ref[place, :] = jnp.where(first, part[:rows], part[rows:]).astype(jnp.bfloat16)
        give_ref[place, :] = jnp.where(first, part[rows:], part[:rows]).astype(jnp.bfloat16)


def combine_kernel(meta_ref, here_ref, there_ref, after_ref, *piece_refs):
    del after_ref
    rows = GROUP_COLS
    for turn, piece_ref in enumerate(piece_refs):
        target = meta_ref[GROUP_HEADS + 1] ^ turn

        @pl.when(target < 3)
        def _(piece_ref=piece_ref, target=target):
            place = pl.ds(pl.multiple_of(target * rows, rows), rows)
            piece_ref[:rows, :] = here_ref[place, :] + there_ref[place, :]
            tail = piece_ref.shape[0] - rows
            piece_ref[rows:, :] = jnp.zeros((tail, piece_ref.shape[1]), jnp.bfloat16)

        @pl.when(target == 3)
        def _(piece_ref=piece_ref):
            piece_ref[...] = here_ref[3 * rows :, :] + there_ref[3 * rows :, :]


def cross_kernel(meta_ref, low_ref, high_ref, out_ref):
    out_ref[...] = jnp.where(meta_ref[GROUP_HEADS] == 0, low_ref[...], high_ref[...])


def gather_kernel(meta_ref, g0, g1, g2, g3, early_ref, late_ref, after_ref, mine_ref):
    del after_ref
    rows = GROUP_COLS
    size = g0.shape[0]
    group = meta_ref[GROUP_HEADS + 1]
    first = meta_ref[GROUP_HEADS] == 0

    @pl.when(group < 3)
    def _():
        for turn, got in enumerate((g0, g1, g2, g3)):
            place = pl.ds(pl.multiple_of((group ^ turn) * rows, rows), rows)
            mine_ref[place, :] = got[:rows, :]
        tail = mine_ref.shape[0] - GROUPS * rows
        mine_ref[GROUPS * rows :, :] = jnp.zeros((tail, mine_ref.shape[1]), jnp.bfloat16)

    @pl.when((group == 3) & first)
    def _():
        for place, piece in enumerate((g3, late_ref, g2, early_ref)):
            mine_ref[place * size : (place + 1) * size, :] = piece[...]

    @pl.when((group == 3) & jnp.logical_not(first))
    def _():
        for place, piece in enumerate((late_ref, g1, early_ref, g0)):
            mine_ref[place * size : (place + 1) * size, :] = piece[...]


def input_kernel(tokens_ref, table_ref, query_ref, key_ref, value_ref, rows_ref, out_ref):
    vocab = table_ref.shape[0]
    onehot = onehot_columns(tokens_ref[...], vocab)
    embedded = tdot(onehot, table_ref[...])
    inv_rms = lax.rsqrt(jnp.mean(embedded * embedded, axis=1, keepdims=True) + EPSILON)
    grad_normed = None
    for matrix, weights in enumerate((query_ref, key_ref, value_ref)):
        columns = jnp.concatenate(
            [
                rows_ref[group, matrix * GROUP_COLS : (matrix + 1) * GROUP_COLS, :]
                for group in range(GROUPS)
            ],
            axis=0,
        )
        part = ndot(columns.astype(jnp.float32).T.astype(jnp.bfloat16), weights[...])
        grad_normed = part if grad_normed is None else grad_normed + part
    scaled = embedded * inv_rms
    out_ref[...] = (
        inv_rms * (grad_normed - scaled * jnp.mean(grad_normed * scaled, axis=1, keepdims=True))
    ).astype(jnp.bfloat16)


def weight_kernel(meta_ref, normed_ref, mine_ref, other_ref, out_ref):
    half_vocab = mine_ref.shape[1]
    first_core = meta_ref[GROUP_HEADS + 2] == 0

    @pl.when(meta_ref[GROUP_HEADS + 1] < 3)
    def _():
        first = normed_ref[:half_vocab, :]
        second = normed_ref[half_vocab:, :]
        upper = jnp.where(first_core, first, second)
        lower = jnp.where(first_core, second, first)
        total = None
        for part, sums_ref in ((upper, mine_ref), (lower, other_ref)):
            term = lax.dot_general(
                part,
                sums_ref[: GROUPS * GROUP_COLS, :],
                (((0,), (1,)), ((), ())),
                preferred_element_type=jnp.float32,
            )
            total = term if total is None else total + term
        out_ref[...] = total

    @pl.when(meta_ref[GROUP_HEADS + 1] == 3)
    def _():
        rows = GROUP_COLS // 2
        for half in range(2):
            for column in range(6):
                start = (half * 6 + column) * rows
                for core in range(2):
                    same = first_core == (core == 0)
                    value = jnp.where(
                        same, mine_ref[start : start + rows, :], other_ref[start : start + rows, :]
                    )
                    row = half * GROUP_COLS + core * rows
                    out_ref[
                        row : row + rows, column * half_vocab : (column + 1) * half_vocab
                    ] = value.astype(jnp.float32)


def whole(shape):
    return pl.BlockSpec(shape, lambda *_: (0,) * len(shape))


def swapped(block, axis, bit):
    route = [(i, i ^ bit) for i in range(lax.axis_size(axis))]
    return lax.ppermute(block, axis, route)


def rope_table(length):
    frequency = (10000.0 ** (-2.0 * np.arange(HALF, dtype=np.float32) / HEAD_DIM)).astype(np.float32)
    angles = frequency[:, None] * np.arange(length, dtype=np.float32)[None, :]
    angles = angles.astype(np.float64)
    return (
        jnp.asarray(np.cos(angles).astype(np.float32)),
        jnp.asarray(np.sin(angles).astype(np.float32)),
    )


def grouped_device(token_ids, cotangent, table, w_query, w_key, w_value, w_out, window):
    place = lax.axis_index("seq")
    core = lax.axis_index("dp") % 2
    group = place // 2
    side = place % 2
    block = token_ids.shape[1]
    features = table.shape[1]
    vocab = table.shape[0]
    blocks = lax.axis_size("seq")
    length = block * blocks
    grad_out = cotangent[0]
    meta = jnp.concatenate(
        [
            lax.dynamic_slice_in_dim(window, group * GROUP_HEADS, GROUP_HEADS, 0),
            jnp.stack([side, group, core]).astype(jnp.int32),
        ]
    )
    spot = jnp.stack([side, group, core]).astype(jnp.int32)
    cosine, sine_part = rope_table(length)

    def call(
        body, operands, outs, scratch=(), steps=1, flops=10**8, moved=10**6, loose=0, peeked=0, grant=VMEM_BYTES
    ):
        spaces = [whole(operand.shape) for operand in operands]
        for index in range(loose):
            spaces[-1 - index] = pl.BlockSpec(memory_space=pl.ANY)
        for index in range(peeked):
            spaces[-1 - index] = whole((16, 128))
        if operands[0].ndim == 1:
            spaces[0] = pl.BlockSpec(memory_space=pltpu.SMEM)
        return pl.pallas_call(
            body,
            grid=(steps,),
            in_specs=spaces,
            out_specs=[whole(shape) for shape, _ in outs],
            out_shape=[jax.ShapeDtypeStruct(shape, dtype) for shape, dtype in outs],
            scratch_shapes=list(scratch),
            compiler_params=pltpu.CompilerParams(
                dimension_semantics=("arbitrary",), vmem_limit_bytes=grant
            ),
            cost_estimate=pl.CostEstimate(flops=flops, bytes_accessed=moved, transcendentals=0),
        )(*operands)

    half = jnp.bfloat16
    sent = call(
        send_kernel,
        (spot, token_ids, grad_out, w_out),
        [((GROUP_COLS + TOKEN_ROWS, block), half)] * GROUPS,
        [pltpu.VMEM((features, block), half)],
        grant=60 * 1024 * 1024,
    )
    early = [sent[0]] + [None] * (blocks - 1)
    for turn in (4, 6, 5, 7, 2, 3, 1):
        early[turn] = swapped(sent[turn // 2], "seq", turn)
    late, lookup, normed = call(
        prepare_kernel,
        (meta, grad_out, table, w_query, w_key, w_value, early[1], early[2]),
        [
            ((blocks, block, features // 2), half),
            ((2, 3 * GROUP_COLS, vocab), half),
            ((vocab, features // 2), half),
        ],
        [pltpu.VMEM((features, vocab), jnp.float32)],
        flops=10**9,
        moved=5 * 10**6,
        peeked=2,
        grant=60 * 1024 * 1024,
    )
    late = lax.all_to_all(late, "seq", split_axis=0, concat_axis=0, tiled=True)
    heads_shape = (GROUP_HEADS, HEAD_DIM, length)
    rows_shape = (GROUP_HEADS, length, 2 * HEAD_DIM)
    rows, sums, attended = call(
        attention_kernel,
        (meta, lookup, cosine, sine_part, *early),
        [
            ((GROUPS, 3 * GROUP_COLS, block), half),
            ((2, 3 * GROUP_COLS, vocab // 2), half),
            ((GROUP_COLS, length), half),
        ],
        [
            pltpu.VMEM(rows_shape, half),
            pltpu.VMEM(heads_shape, half),
            pltpu.VMEM(heads_shape, half),
            pltpu.VMEM(heads_shape, half),
            pltpu.VMEM(heads_shape, half),
            pltpu.VMEM((vocab, length), half),
            pltpu.VMEM((length, vocab), half),
            pltpu.VMEM((HEAD_DIM, length), jnp.float32),
            pltpu.VMEM((2 * HEAD_DIM, length), jnp.float32),
            pltpu.VMEM((length, 2 * HEAD_DIM), half),
            pltpu.VMEM((length, length), half),
            pltpu.VMEM((length, length), half),
            pltpu.VMEM((length // TILE, 2 * HEAD_DIM, 2 * TILE), half),
            pltpu.VMEM((length // TILE, WINDOW + TILE, 2 * TILE), jnp.float32),
            pltpu.VMEM((1, length), jnp.float32),
            pltpu.VMEM((1, length), jnp.float32),
        ],
        steps=GROUP_HEADS,
        flops=8 * 10**9,
        moved=8 * 10**6,
    )
    planes = [[2 * z + x for z in range(GROUPS)] for x in range(2)]

    def over_plane(chunks):
        return lax.all_to_all(
            chunks, "seq", split_axis=0, concat_axis=0, axis_index_groups=planes, tiled=True
        )

    got_rows = over_plane(rows)
    lanes = vocab // 2
    out_rows = 3 * GROUP_COLS // 2
    packed = 3 * GROUP_COLS + out_rows
    keep, give = call(
        out_kernel,
        (meta, attended, late.reshape(length, features // 2), sums),
        [((packed, lanes), half)] * 2,
    )
    here = keep + swapped(give, "dp", 1)
    there = swapped(here, "dp", 2)
    pieces = call(
        combine_kernel,
        (meta, here, there, got_rows),
        [((out_rows, lanes), half)] * GROUPS,
        loose=1,
    )
    got = [pieces[0]] + [None] * (GROUPS - 1)
    for turn in (2, 3, 1):
        got[turn] = swapped(pieces[turn], "seq", 2 * turn)
    (grad_input,) = call(
        input_kernel,
        (token_ids, table, w_query, w_key, w_value, got_rows),
        [((block, features), half)],
        flops=10**9,
        moved=5 * 10**6,
    )
    last = blocks - 2
    between = [(last, last + 1), (last + 1, last)]
    crossed = []
    for low, high in ((got[0], got[2]), (got[1], got[3])):
        (piece,) = call(cross_kernel, (meta, low, high), [(low.shape, half)])
        crossed.append(lax.ppermute(piece, "seq", between))
    (mine,) = call(
        gather_kernel,
        (meta, *got, *crossed, grad_input),
        [((4 * out_rows, lanes), half)],
        loose=1,
    )
    (weight_grads,) = call(
        weight_kernel,
        (meta, normed, mine, swapped(mine, "dp", 1)),
        [((features // 2, features), jnp.float32)],
        flops=10**9,
        moved=5 * 10**6,
    )
    return (grad_input[None], weight_grads)


def on_device(token_ids, cotangent, table, w_query, w_key, w_value, w_out, window):
    fits = (
        lax.axis_size("seq") == 2 * GROUPS
        and lax.axis_size("dp") == 4
        and token_ids.shape == (1, 128)
        and table.shape == (256, HEADS * HEAD_DIM)
    )
    plan = grouped_device if fits else general_device
    return plan(token_ids, cotangent, table, w_query, w_key, w_value, w_out, window)


def solution(mesh):
    return jax.shard_map(
        on_device,
        mesh=mesh,
        in_specs=(P("dp", "seq"), P("dp", "seq", None), P(), P(), P(), P(), P(), P()),
        out_specs=(P("dp", "seq", None), P("seq", None)),
        check_vma=False,
    )
```

```python
import jax
import jax.numpy as jnp
import numpy as np
from jax import lax
from jax.experimental import pallas as pl
from jax.experimental.pallas import tpu as pltpu
from jax.sharding import PartitionSpec as P

HEADS = 12
HEAD_DIM = 64
WINDOW = 512


EPSILON = 1e-05


def shifted(block, axis, distance):
    devices = range(lax.axis_size(axis))
    route = [(i - distance, i) for i in devices if i - distance in devices]
    return lax.ppermute(block, axis, route)


def rotate(values, positions):
    row_count = values.shape[0]
    shaped = values.reshape(row_count, -1, HEAD_DIM)
    middle = HEAD_DIM // 2
    frequency = 10000.0 ** (-2.0 * jnp.arange(middle, dtype=jnp.float32) / HEAD_DIM)
    angles = positions.astype(jnp.float32)[:, None] * frequency[None, :]
    cosine = jnp.cos(angles)[:, None, :]
    sine_part = jnp.sin(angles)[:, None, :]
    former = shaped[..., :middle]
    latter = shaped[..., middle:]
    turned = jnp.concatenate(
        [former * cosine - latter * sine_part, latter * cosine + former * sine_part], axis=-1
    )
    return turned.reshape(row_count, -1)


def unrotate(values, positions):
    row_count = values.shape[0]
    shaped = values.reshape(row_count, -1, HEAD_DIM)
    middle = HEAD_DIM // 2
    frequency = 10000.0 ** (-2.0 * jnp.arange(middle, dtype=jnp.float32) / HEAD_DIM)
    angles = positions.astype(jnp.float32)[:, None] * frequency[None, :]
    cosine = jnp.cos(angles)[:, None, :]
    sine_part = jnp.sin(angles)[:, None, :]
    former = shaped[..., :middle]
    latter = shaped[..., middle:]
    turned = jnp.concatenate(
        [former * cosine + latter * sine_part, latter * cosine - former * sine_part], axis=-1
    )
    return turned.reshape(row_count, -1)


def tdot(left, right):
    return lax.dot_general(
        left, right, (((0,), (0,)), ((), ())), preferred_element_type=jnp.float32
    )


def ndot(left, right):
    return lax.dot_general(
        left, right, (((1,), (1,)), ((), ())), preferred_element_type=jnp.float32
    )


def embed_rows(byte_ids, table):
    onehot = (byte_ids[:, None] == jnp.arange(table.shape[0], dtype=jnp.int32)[None, :]).astype(
        jnp.bfloat16
    )
    return jnp.dot(onehot, table, preferred_element_type=jnp.float32).astype(jnp.bfloat16)


def normalize(embedded):
    widened = embedded.astype(jnp.float32)
    inv_rms = lax.rsqrt(jnp.mean(widened * widened, axis=1, keepdims=True) + EPSILON)
    return (widened, inv_rms, (widened * inv_rms).astype(jnp.bfloat16))


def keys_values(normed, positions, w_key, w_value):
    key_rows = rotate(jnp.dot(normed, w_key, preferred_element_type=jnp.float32), positions).astype(
        jnp.bfloat16
    )
    value_rows = jnp.dot(normed, w_value, preferred_element_type=jnp.float32).astype(jnp.bfloat16)
    return (key_rows, value_rows)


def head_group(
    query_heads, key_heads, value_heads, grad_heads, group_window, own_pos, key_pos, score_scale
):
    distance = own_pos[:, None] - key_pos[None, :]
    allowed = (
        (distance[None] >= 0)
        & (distance[None] < group_window[:, None, None])
        & (key_pos[None, None, :] >= 0)
    )
    scores = (
        jnp.einsum("qhd,khd->hqk", query_heads, key_heads, preferred_element_type=jnp.float32)
        * score_scale
    )
    masked = jnp.where(allowed, scores, -1e30)
    row_max = jnp.max(masked, axis=-1, keepdims=True)
    weights = jnp.where(allowed, jnp.exp(masked - row_max), 0.0)
    probs = weights / jnp.sum(weights, axis=-1, keepdims=True)
    probs_b = probs.astype(jnp.bfloat16)
    attended = jnp.einsum(
        "hqk,khd->qhd", probs_b, value_heads, preferred_element_type=jnp.float32
    ).astype(jnp.bfloat16)
    grad_probs = jnp.einsum(
        "qhd,khd->hqk", grad_heads, value_heads, preferred_element_type=jnp.float32
    )
    row_term = jnp.sum(probs * grad_probs, axis=-1, keepdims=True)
    grad_scores = (probs * (grad_probs - row_term) * score_scale).astype(jnp.bfloat16)
    grad_query = jnp.einsum(
        "hqk,khd->qhd", grad_scores, key_heads, preferred_element_type=jnp.float32
    )
    grad_key = jnp.einsum(
        "hqk,qhd->khd", grad_scores, query_heads, preferred_element_type=jnp.float32
    )
    grad_value = jnp.einsum("hqk,qhd->khd", probs_b, grad_heads, preferred_element_type=jnp.float32)
    return (attended, grad_query, grad_key, grad_value)


def general_device(token_ids, cotangent, table, w_query, w_key, w_value, w_out, window):
    local_ids = token_ids[0]
    grad_out = cotangent[0]
    length = local_ids.shape[0]
    features = table.shape[1]
    tail_rows = min(length, WINDOW)
    reach_devs = -(-WINDOW // length)
    halo_rows = reach_devs * tail_rows
    offset = lax.axis_index("seq") * length
    own_pos = offset + jnp.arange(length, dtype=jnp.int32)
    halo_pos = offset - halo_rows + jnp.arange(halo_rows, dtype=jnp.int32)
    score_scale = HEAD_DIM ** (-0.5)
    embedded = embed_rows(local_ids, table)
    widened, inv_rms, normed = normalize(embedded)
    query = rotate(jnp.dot(normed, w_query, preferred_element_type=jnp.float32), own_pos).astype(
        jnp.bfloat16
    )
    key_own, value_own = keys_values(normed, own_pos, w_key, w_value)
    key_pieces = []
    value_pieces = []
    for hop_index in range(reach_devs):
        far_keys, far_values = shifted((key_own, value_own), "seq", hop_index + 1)
        key_pieces.insert(0, far_keys)
        value_pieces.insert(0, far_values)
    key_halo = jnp.concatenate(key_pieces, axis=0)
    value_halo = jnp.concatenate(value_pieces, axis=0)
    span_rows = halo_rows + length
    key_all = jnp.concatenate([key_halo, key_own], axis=0)
    value_all = jnp.concatenate([value_halo, value_own], axis=0)
    key_pos = jnp.concatenate([halo_pos, own_pos], axis=0)
    query_heads = query.reshape(length, HEADS, HEAD_DIM)
    key_heads = key_all.reshape(span_rows, HEADS, HEAD_DIM)
    value_heads = value_all.reshape(span_rows, HEADS, HEAD_DIM)
    grad_att = ndot(grad_out, w_out).astype(jnp.bfloat16)
    grad_heads = grad_att.reshape(length, HEADS, HEAD_DIM)
    group_size = 4
    attended_parts = []
    query_parts = []
    key_parts = []
    value_parts = []
    for group_index in range(HEADS // group_size):
        lower = group_index * group_size
        upper = lower + group_size
        outputs = head_group(
            query_heads[:, lower:upper],
            key_heads[:, lower:upper],
            value_heads[:, lower:upper],
            grad_heads[:, lower:upper],
            window[lower:upper],
            own_pos,
            key_pos,
            score_scale,
        )
        attended_parts.append(outputs[0])
        query_parts.append(outputs[1])
        key_parts.append(outputs[2])
        value_parts.append(outputs[3])
    attended = jnp.concatenate(attended_parts, axis=1).reshape(length, features)
    grad_query = jnp.concatenate(query_parts, axis=1).reshape(length, features)
    grad_key = jnp.concatenate(key_parts, axis=1).reshape(span_rows, features)
    grad_value = jnp.concatenate(value_parts, axis=1).reshape(span_rows, features)
    tail_keys = grad_key[:halo_rows].reshape(reach_devs, tail_rows, features)
    tail_values = grad_value[:halo_rows].reshape(reach_devs, tail_rows, features)
    back_keys = jnp.zeros((tail_rows, features), jnp.float32)
    back_values = jnp.zeros((tail_rows, features), jnp.float32)
    for hop_index in range(reach_devs):
        got_keys, got_values = shifted(
            (tail_keys[reach_devs - 1 - hop_index], tail_values[reach_devs - 1 - hop_index]),
            "seq",
            -(hop_index + 1),
        )
        back_keys = back_keys + got_keys
        back_values = back_values + got_values
    own_keys = grad_key[halo_rows:]
    own_values = grad_value[halo_rows:]
    own_keys = jnp.concatenate([own_keys[: length - tail_rows], own_keys + back_keys], axis=0)
    own_values = jnp.concatenate(
        [own_values[: length - tail_rows], own_values + back_values], axis=0
    )
    grad_q_lin = unrotate(grad_query, own_pos).astype(jnp.bfloat16)
    grad_k_lin = unrotate(own_keys, own_pos).astype(jnp.bfloat16)
    grad_v_lin = own_values.astype(jnp.bfloat16)
    grad_normed = ndot(grad_q_lin, w_query) + ndot(grad_k_lin, w_key) + ndot(grad_v_lin, w_value)
    scaled = widened * inv_rms
    grad_input = (
        inv_rms * (grad_normed - scaled * jnp.mean(grad_normed * scaled, axis=1, keepdims=True))
    ).astype(jnp.bfloat16)
    term = jnp.concatenate(
        [
            tdot(normed, grad_q_lin),
            tdot(normed, grad_k_lin),
            tdot(normed, grad_v_lin),
            tdot(attended, grad_out),
        ],
        axis=0,
    )
    shares = lax.psum_scatter(term.astype(jnp.bfloat16), "seq", scatter_dimension=0, tiled=True)
    weight_grads = lax.psum(shares, "dp").astype(jnp.float32)
    return (grad_input[None], weight_grads)


GROUPS = 4
GROUP_HEADS = HEADS // GROUPS
GROUP_COLS = GROUP_HEADS * HEAD_DIM
TILE = 256
TOKEN_ROWS = 16
STRIP = 8
HALF = HEAD_DIM // 2
VMEM_BYTES = 48 * 1024 * 1024
LARGE_BYTES = 60 * 1024 * 1024


def key_span(query_tile):
    first = max(0, query_tile - WINDOW // TILE)
    return (first * TILE, (query_tile - first + 1) * TILE)


def normed_table(table_ref):
    widened = table_ref[...].astype(jnp.float32)
    inv_rms = lax.rsqrt(jnp.mean(widened * widened, axis=1, keepdims=True) + EPSILON)
    return (widened * inv_rms).astype(jnp.bfloat16)


def onehot_columns(tokens, vocab):
    rows = lax.broadcasted_iota(jnp.int32, (vocab, tokens.shape[1]), 0)
    return (rows == tokens).astype(jnp.float32).astype(jnp.bfloat16)


def send_kernel(spot_ref, tokens_ref, cotangent_ref, out_weights_ref, *out_refs):
    early_refs, grads_ref = out_refs[:-1], out_refs[-1]
    grad_att = ndot(out_weights_ref[...], cotangent_ref[...]).astype(jnp.bfloat16)
    grads_ref[...] = grad_att
    block = tokens_ref.shape[1]
    tokens = jnp.broadcast_to(tokens_ref[...].astype(jnp.float32), (TOKEN_ROWS, block)).astype(
        jnp.bfloat16
    )
    for turn, early_ref in enumerate(early_refs):
        group = spot_ref[1] ^ turn
        place = pl.ds(pl.multiple_of(group * GROUP_COLS, GROUP_COLS), GROUP_COLS)
        early_ref[:GROUP_COLS, :] = grads_ref[place, :]
        early_ref[GROUP_COLS:, :] = tokens


def gate_kernel(*refs):
    del refs


def gated(block, *others):
    return pl.pallas_call(
        gate_kernel,
        grid=(1,),
        in_specs=[pl.BlockSpec(memory_space=pl.ANY)] + [whole((16, 128))] * len(others),
        out_specs=pl.BlockSpec(memory_space=pl.ANY),
        out_shape=jax.ShapeDtypeStruct(block.shape, block.dtype),
        input_output_aliases={0: 0},
        compiler_params=pltpu.CompilerParams(vmem_limit_bytes=LARGE_BYTES),
    )(block, *others)


def prepare_kernel(
    meta_ref,
    cotangent_ref,
    table_ref,
    query_ref,
    key_ref,
    value_ref,
    late_ref,
    lookup_ref,
    normed_ref,
    columns_ref,
):
    columns = late_ref.shape[2]
    for target in range(2 * GROUPS):
        side = target % 2
        late_ref[target] = cotangent_ref[:, side * columns : (side + 1) * columns]
    normed = normed_table(table_ref)
    half = normed.shape[1] // 2
    normed_ref[...] = jnp.where(meta_ref[GROUP_HEADS] == 0, normed[:, :half], normed[:, half:])
    place = pl.ds(pl.multiple_of(meta_ref[GROUP_HEADS + 1] * GROUP_COLS, GROUP_COLS), GROUP_COLS)
    for matrix, weights_ref in enumerate((query_ref, key_ref, value_ref)):
        columns_ref[...] = jnp.dot(
            normed, weights_ref[...], preferred_element_type=jnp.float32
        ).T
        mine = columns_ref[place, :]
        upper = mine.astype(jnp.bfloat16)
        rows = slice(matrix * GROUP_COLS, (matrix + 1) * GROUP_COLS)
        lookup_ref[0, rows, :] = upper
        lookup_ref[1, rows, :] = (mine - upper.astype(jnp.float32)).astype(jnp.bfloat16)


def attention_kernel(
    meta_ref,
    lookup_ref,
    cosine_ref,
    sine_ref,
    *rest,
):
    early_refs = rest[: 2 * GROUPS]
    attention_body(meta_ref, lookup_ref, cosine_ref, sine_ref, early_refs, *rest[2 * GROUPS :])


def attention_body(
    meta_ref,
    lookup_ref,
    cosine_ref,
    sine_ref,
    early_refs,
    rows_ref,
    tail_ref,
    sums_ref,
    attended_ref,
    value_key_ref,
    query_t_ref,
    key_t_ref,
    value_t_ref,
    grad_att_ref,
    onehot_ref,
    onehot_rows_ref,
    grad_query_ref,
    both_ref,
    scaled_ref,
    probs_ref,
    scores_ref,
    right_ref,
    products_ref,
    inverse_ref,
    term_ref,
):
    head = pl.program_id(0)
    block = early_refs[0].shape[1]
    length = len(early_refs) * block
    tiles = length // TILE
    vocab = lookup_ref.shape[2]
    half_vocab = vocab // 2
    half = jnp.bfloat16
    cosine = cosine_ref[...]
    sine_part = sine_ref[...]

    @pl.when(head == 0)
    def _():
        own = 2 * meta_ref[GROUP_HEADS + 1] + meta_ref[GROUP_HEADS]
        for turn, early_ref in enumerate(early_refs):
            lanes = pl.ds(pl.multiple_of((own ^ turn) * block, block), block)
            tokens = early_ref[GROUP_COLS : GROUP_COLS + TOKEN_ROWS, :]
            tokens = tokens.astype(jnp.float32)[:1].astype(jnp.int32)
            onehot_ref[:, lanes] = onehot_columns(tokens, vocab)
            grad_att_ref[:, :, lanes] = early_ref[:GROUP_COLS, :].reshape(
                GROUP_HEADS, HEAD_DIM, block
            )
        onehot = onehot_ref[...]
        onehot_rows_ref[...] = onehot.T
        size = 3 * GROUP_COLS
        chosen = jnp.dot(
            lookup_ref[...].reshape(2 * size, vocab), onehot, preferred_element_type=jnp.float32
        )

        def picked(start):
            lower = start + size
            return chosen[start : start + HEAD_DIM] + chosen[lower : lower + HEAD_DIM]

        def turned(columns):
            former = columns[:HALF]
            latter = columns[HALF:]
            return jnp.concatenate(
                [former * cosine - latter * sine_part, latter * cosine + former * sine_part], axis=0
            )

        for index in range(GROUP_HEADS):
            query = turned(picked(index * HEAD_DIM)) * HEAD_DIM ** (-0.5)
            keys = turned(picked(GROUP_COLS + index * HEAD_DIM)).astype(half)
            values = picked(2 * GROUP_COLS + index * HEAD_DIM).astype(half)
            value_key_ref[index] = jnp.concatenate([values, keys], axis=0).T
            query_t_ref[index] = query.astype(half)
            key_t_ref[index] = keys
            value_t_ref[index] = values

    width = meta_ref[head]
    grad_att = grad_att_ref[head]
    query_t = query_t_ref[head]
    blank = jnp.zeros((HEAD_DIM, TILE), half)
    base = lax.broadcasted_iota(jnp.int32, (STRIP, TILE), 1) - lax.broadcasted_iota(
        jnp.int32, (STRIP, TILE), 0
    )
    for tile in range(tiles):
        columns = slice(tile * TILE, (tile + 1) * TILE)
        right_ref[tile, :HEAD_DIM, :TILE] = grad_att[:, columns]
        right_ref[tile, HEAD_DIM:, :TILE] = blank
        right_ref[tile, :HEAD_DIM, TILE:] = blank
        right_ref[tile, HEAD_DIM:, TILE:] = query_t[:, columns]

    def multiply(tile):
        first, count = key_span(tile)
        products_ref[tile, :count, :] = jnp.dot(
            value_key_ref[head, first : first + count, :],
            right_ref[tile],
            preferred_element_type=jnp.float32,
        )

    def forward(tile):
        first, count = key_span(tile)
        columns = slice(tile * TILE, (tile + 1) * TILE)
        row_max = None
        for row in range(0, count, STRIP):
            offset = tile * TILE - first - row
            allowed = base < width - offset
            if offset - STRIP < 0:
                allowed = allowed & (base >= -offset)
            masked = jnp.where(allowed, products_ref[tile, row : row + STRIP, TILE:], -1e30)
            products_ref[tile, row : row + STRIP, TILE:] = masked
            row_max = masked if row_max is None else jnp.maximum(row_max, masked)
        row_max = jnp.max(row_max, axis=0, keepdims=True)
        total = None
        for row in range(0, count, 2 * STRIP):
            weights = jnp.exp(products_ref[tile, row : row + 2 * STRIP, TILE:] - row_max)
            total = weights if total is None else total + weights
            probs_ref[first + row : first + row + 2 * STRIP, columns] = weights.astype(half)
        inverse = 1.0 / jnp.sum(total, axis=0, keepdims=True)
        attended = inverse * jnp.dot(
            value_t_ref[head, :, first : first + count],
            probs_ref[first : first + count, columns],
            preferred_element_type=jnp.float32,
        )
        attended_ref[pl.ds(pl.multiple_of(head * HEAD_DIM, HEAD_DIM), HEAD_DIM), columns] = (
            attended.astype(half)
        )
        wide_grad = grad_att[:, columns].astype(jnp.float32)
        inverse_ref[:, columns] = inverse
        term_ref[:, columns] = jnp.sum(attended * wide_grad, axis=0, keepdims=True)
        scaled_ref[columns, :] = jnp.concatenate(
            [
                (inverse * query_t[:, columns].astype(jnp.float32)).astype(half),
                (inverse * wide_grad).astype(half),
            ],
            axis=0,
        ).T

    def backward(tile):
        first, count = key_span(tile)
        columns = slice(tile * TILE, (tile + 1) * TILE)
        row_term = term_ref[:, columns]
        for row in range(0, count, 2 * STRIP):
            strip = slice(first + row, first + row + 2 * STRIP)
            scores_ref[strip, columns] = (
                probs_ref[strip, columns].astype(jnp.float32)
                * (products_ref[tile, row : row + 2 * STRIP, :TILE] - row_term)
            ).astype(half)
        grad_query_ref[:, columns] = inverse_ref[:, columns] * jnp.dot(
            key_t_ref[head, :, first : first + count],
            scores_ref[first : first + count, columns],
            preferred_element_type=jnp.float32,
        )

    lanes = lax.broadcasted_iota(jnp.int32, (TILE, 2 * HEAD_DIM), 1)

    def collect(tile):
        start = tile * TILE
        stop = min(length, start + TILE + WINDOW)
        grad_key = jnp.dot(
            scores_ref[start : start + TILE, start:stop],
            scaled_ref[start:stop, :],
            preferred_element_type=jnp.float32,
        )
        grad_value = jnp.dot(
            probs_ref[start : start + TILE, start:stop],
            scaled_ref[start:stop, :],
            preferred_element_type=jnp.float32,
        )
        both_ref[:, start : start + TILE] = jnp.where(lanes < HEAD_DIM, grad_key, grad_value).T

    reach = WINDOW // TILE
    for step in range(tiles + 3 + reach):
        if step < tiles:
            multiply(step)
        if 0 <= step - 1 < tiles:
            forward(step - 1)
        if 0 <= step - 2 < tiles:
            backward(step - 2)
        ready = step - 3 - reach
        if 0 <= ready < tiles:
            collect(ready)
    def turned_back(columns):
        former = columns[:HALF]
        latter = columns[HALF:]
        return jnp.concatenate(
            [former * cosine + latter * sine_part, latter * cosine - former * sine_part], axis=0
        )

    both = both_ref[...]
    grads = jnp.concatenate(
        [
            turned_back(grad_query_ref[...] * HEAD_DIM ** (-0.5)),
            turned_back(both[:HEAD_DIM]),
            both[HEAD_DIM:],
        ],
        axis=0,
    ).astype(half)
    sums = jnp.dot(grads, onehot_rows_ref[...], preferred_element_type=jnp.float32).astype(half)
    tail = pl.multiple_of(head * HEAD_DIM, HEAD_DIM)
    for matrix in range(3):
        rows = slice(matrix * HEAD_DIM, (matrix + 1) * HEAD_DIM)
        place = pl.ds(
            pl.multiple_of(matrix * GROUP_COLS + head * HEAD_DIM, HEAD_DIM), HEAD_DIM
        )
        for core in range(2):
            lane = core * half_vocab
            sums_ref[core, place, :] = sums[rows, lane : lane + half_vocab]
        for target in range(GROUPS):
            start = target * 2 * block
            even = grads[rows, start : start + block]
            odd = grads[rows, start + block : start + 2 * block]
            mine = jnp.where(meta_ref[GROUP_HEADS] == 0, even, odd)
            if matrix < 2:
                rows_ref[target, place, :] = mine
            else:
                tail_ref[target, pl.ds(tail, HEAD_DIM), :] = mine


def out_kernel(meta_ref, attended_ref, cotangent_ref, sums_ref, keep_ref, give_ref):
    total = jnp.dot(attended_ref[...], cotangent_ref[...], preferred_element_type=jnp.float32)
    rows = total.shape[0] // 2
    base = sums_ref.shape[1]
    lanes = keep_ref.shape[1]
    first = meta_ref[GROUP_HEADS + 2] == 0
    keep_ref[:base, :] = jnp.where(first, sums_ref[0], sums_ref[1])
    give_ref[:base, :] = jnp.where(first, sums_ref[1], sums_ref[0])
    for chunk in range(total.shape[1] // lanes):
        part = total[:, chunk * lanes : (chunk + 1) * lanes]
        place = slice(base + chunk * rows, base + (chunk + 1) * rows)
        keep_ref[place, :] = jnp.where(first, part[:rows], part[rows:]).astype(jnp.bfloat16)
        give_ref[place, :] = jnp.where(first, part[rows:], part[:rows]).astype(jnp.bfloat16)


def combine_kernel(meta_ref, here_ref, there_ref, after_ref, *piece_refs):
    del after_ref
    rows = GROUP_COLS
    for turn, piece_ref in enumerate(piece_refs):
        target = meta_ref[GROUP_HEADS + 1] ^ turn

        @pl.when(target < 3)
        def _(piece_ref=piece_ref, target=target):
            place = pl.ds(pl.multiple_of(target * rows, rows), rows)
            piece_ref[:rows, :] = here_ref[place, :] + there_ref[place, :]
            tail = piece_ref.shape[0] - rows
            piece_ref[rows:, :] = jnp.zeros((tail, piece_ref.shape[1]), jnp.bfloat16)

        @pl.when(target == 3)
        def _(piece_ref=piece_ref):
            piece_ref[...] = here_ref[3 * rows :, :] + there_ref[3 * rows :, :]


def cross_kernel(meta_ref, low_ref, high_ref, out_ref):
    out_ref[...] = jnp.where(meta_ref[GROUP_HEADS] == 0, low_ref[...], high_ref[...])


def gather_kernel(meta_ref, g0, g1, g2, g3, early_ref, late_ref, mine_ref):
    rows = GROUP_COLS
    size = g0.shape[0]
    group = meta_ref[GROUP_HEADS + 1]
    first = meta_ref[GROUP_HEADS] == 0

    @pl.when(group < 3)
    def _():
        for turn, got in enumerate((g0, g1, g2, g3)):
            place = pl.ds(pl.multiple_of((group ^ turn) * rows, rows), rows)
            mine_ref[place, :] = got[:rows, :]
        tail = mine_ref.shape[0] - GROUPS * rows
        mine_ref[GROUPS * rows :, :] = jnp.zeros((tail, mine_ref.shape[1]), jnp.bfloat16)

    @pl.when((group == 3) & first)
    def _():
        for place, piece in enumerate((g3, late_ref, g2, early_ref)):
            mine_ref[place * size : (place + 1) * size, :] = piece[...]

    @pl.when((group == 3) & jnp.logical_not(first))
    def _():
        for place, piece in enumerate((late_ref, g1, early_ref, g0)):
            mine_ref[place * size : (place + 1) * size, :] = piece[...]


def input_kernel(
    tokens_ref, table_ref, query_ref, key_ref, value_ref, rows_ref, tail_ref, out_ref
):
    vocab = table_ref.shape[0]
    onehot = onehot_columns(tokens_ref[...], vocab)
    embedded = tdot(onehot, table_ref[...])
    inv_rms = lax.rsqrt(jnp.mean(embedded * embedded, axis=1, keepdims=True) + EPSILON)
    grad_normed = None
    for matrix, weights in enumerate((query_ref, key_ref, value_ref)):
        place = slice(matrix * GROUP_COLS, (matrix + 1) * GROUP_COLS)
        columns = jnp.concatenate(
            [
                rows_ref[group, place, :] if matrix < 2 else tail_ref[group]
                for group in range(GROUPS)
            ],
            axis=0,
        )
        part = ndot(columns.astype(jnp.float32).T.astype(jnp.bfloat16), weights[...])
        grad_normed = part if grad_normed is None else grad_normed + part
    scaled = embedded * inv_rms
    out_ref[...] = (
        inv_rms * (grad_normed - scaled * jnp.mean(grad_normed * scaled, axis=1, keepdims=True))
    ).astype(jnp.bfloat16)


def weight_kernel(meta_ref, normed_ref, mine_ref, other_ref, out_ref):
    half_vocab = mine_ref.shape[1]
    first_core = meta_ref[GROUP_HEADS + 2] == 0

    @pl.when(meta_ref[GROUP_HEADS + 1] < 3)
    def _():
        first = normed_ref[:half_vocab, :]
        second = normed_ref[half_vocab:, :]
        upper = jnp.where(first_core, first, second)
        lower = jnp.where(first_core, second, first)
        total = None
        for part, sums_ref in ((upper, mine_ref), (lower, other_ref)):
            term = lax.dot_general(
                part,
                sums_ref[: GROUPS * GROUP_COLS, :],
                (((0,), (1,)), ((), ())),
                preferred_element_type=jnp.float32,
            )
            total = term if total is None else total + term
        out_ref[...] = total

    @pl.when(meta_ref[GROUP_HEADS + 1] == 3)
    def _():
        rows = GROUP_COLS // 2
        for half in range(2):
            for column in range(6):
                start = (half * 6 + column) * rows
                for core in range(2):
                    same = first_core == (core == 0)
                    value = jnp.where(
                        same, mine_ref[start : start + rows, :], other_ref[start : start + rows, :]
                    )
                    row = half * GROUP_COLS + core * rows
                    out_ref[
                        row : row + rows, column * half_vocab : (column + 1) * half_vocab
                    ] = value.astype(jnp.float32)


def whole(shape):
    return pl.BlockSpec(shape, lambda *_: (0,) * len(shape))


def swapped(block, axis, bit):
    route = [(i, i ^ bit) for i in range(lax.axis_size(axis))]
    return lax.ppermute(block, axis, route)


def rope_table(length):
    frequency = (10000.0 ** (-2.0 * np.arange(HALF, dtype=np.float32) / HEAD_DIM)).astype(np.float32)
    angles = frequency[:, None] * np.arange(length, dtype=np.float32)[None, :]
    angles = angles.astype(np.float64)
    return (
        jnp.asarray(np.cos(angles).astype(np.float32)),
        jnp.asarray(np.sin(angles).astype(np.float32)),
    )


def grouped_device(token_ids, cotangent, table, w_query, w_key, w_value, w_out, window):
    place = lax.axis_index("seq")
    core = lax.axis_index("dp") % 2
    group = place // 2
    side = place % 2
    block = token_ids.shape[1]
    features = table.shape[1]
    vocab = table.shape[0]
    blocks = lax.axis_size("seq")
    length = block * blocks
    grad_out = cotangent[0]
    meta = jnp.concatenate(
        [
            lax.dynamic_slice_in_dim(window, group * GROUP_HEADS, GROUP_HEADS, 0),
            jnp.stack([side, group, core]).astype(jnp.int32),
        ]
    )
    spot = jnp.stack([side, group, core]).astype(jnp.int32)
    cosine, sine_part = rope_table(length)

    def call(
        body, operands, outs, scratch=(), steps=1, flops=10**8, moved=10**6, loose=0, grant=VMEM_BYTES
    ):
        spaces = [whole(operand.shape) for operand in operands]
        for index in range(loose):
            spaces[-1 - index] = pl.BlockSpec(memory_space=pl.ANY)
        if operands[0].ndim == 1:
            spaces[0] = pl.BlockSpec(memory_space=pltpu.SMEM)
        return pl.pallas_call(
            body,
            grid=(steps,),
            in_specs=spaces,
            out_specs=[whole(shape) for shape, _ in outs],
            out_shape=[jax.ShapeDtypeStruct(shape, dtype) for shape, dtype in outs],
            scratch_shapes=list(scratch),
            compiler_params=pltpu.CompilerParams(
                dimension_semantics=("arbitrary",), vmem_limit_bytes=grant
            ),
            cost_estimate=pl.CostEstimate(flops=flops, bytes_accessed=moved, transcendentals=0),
        )(*operands)

    half = jnp.bfloat16
    sent = call(
        send_kernel,
        (spot, token_ids, grad_out, w_out),
        [((GROUP_COLS + TOKEN_ROWS, block), half)] * GROUPS,
        [pltpu.VMEM((features, block), half)],
        grant=LARGE_BYTES,
    )
    early = [sent[0]] + [None] * (blocks - 1)
    for turn in (4, 6, 5, 7, 2, 3, 1):
        early[turn] = swapped(sent[turn // 2], "seq", turn)
    late, lookup, normed = call(
        prepare_kernel,
        (meta, grad_out, table, w_query, w_key, w_value),
        [
            ((blocks, block, features // 2), half),
            ((2, 3 * GROUP_COLS, vocab), half),
            ((vocab, features // 2), half),
        ],
        [pltpu.VMEM((features, vocab), jnp.float32)],
        flops=10**9,
        moved=5 * 10**6,
        grant=LARGE_BYTES,
    )
    late = gated(late, *early[1:])
    late = lax.all_to_all(late, "seq", split_axis=0, concat_axis=0, tiled=True)
    heads_shape = (GROUP_HEADS, HEAD_DIM, length)
    rows_shape = (GROUP_HEADS, length, 2 * HEAD_DIM)
    rows, tail, sums, attended = call(
        attention_kernel,
        (meta, lookup, cosine, sine_part, *early),
        [
            ((GROUPS, 2 * GROUP_COLS, block), half),
            ((GROUPS, GROUP_COLS, block), half),
            ((2, 3 * GROUP_COLS, vocab // 2), half),
            ((GROUP_COLS, length), half),
        ],
        [
            pltpu.VMEM(rows_shape, half),
            pltpu.VMEM(heads_shape, half),
            pltpu.VMEM(heads_shape, half),
            pltpu.VMEM(heads_shape, half),
            pltpu.VMEM(heads_shape, half),
            pltpu.VMEM((vocab, length), half),
            pltpu.VMEM((length, vocab), half),
            pltpu.VMEM((HEAD_DIM, length), jnp.float32),
            pltpu.VMEM((2 * HEAD_DIM, length), jnp.float32),
            pltpu.VMEM((length, 2 * HEAD_DIM), half),
            pltpu.VMEM((length, length), half),
            pltpu.VMEM((length, length), half),
            pltpu.VMEM((length // TILE, 2 * HEAD_DIM, 2 * TILE), half),
            pltpu.VMEM((length // TILE, WINDOW + TILE, 2 * TILE), jnp.float32),
            pltpu.VMEM((1, length), jnp.float32),
            pltpu.VMEM((1, length), jnp.float32),
        ],
        steps=GROUP_HEADS,
        flops=8 * 10**9,
        moved=8 * 10**6,
    )
    planes = [[2 * z + x for z in range(GROUPS)] for x in range(2)]

    def over_plane(chunks):
        return lax.all_to_all(
            chunks, "seq", split_axis=0, concat_axis=0, axis_index_groups=planes, tiled=True
        )

    got_rows = over_plane(rows)
    lanes = vocab // 2
    out_rows = 3 * GROUP_COLS // 2
    packed = 3 * GROUP_COLS + out_rows
    keep, give = call(
        out_kernel,
        (meta, attended, late.reshape(length, features // 2), sums),
        [((packed, lanes), half)] * 2,
    )
    here = keep + swapped(give, "dp", 1)
    there = swapped(here, "dp", 2)
    pieces = call(
        combine_kernel,
        (meta, here, there, got_rows),
        [((out_rows, lanes), half)] * GROUPS,
        loose=1,
    )
    got = [pieces[0]] + [None] * (GROUPS - 1)
    for turn in (2, 3, 1):
        got[turn] = swapped(pieces[turn], "seq", 2 * turn)
    got_tail = over_plane(gated(tail, got[2]))
    (grad_input,) = call(
        input_kernel,
        (token_ids, table, w_query, w_key, w_value, got_rows, got_tail),
        [((block, features), half)],
        flops=10**9,
        moved=5 * 10**6,
    )
    last = blocks - 2
    between = [(last, last + 1), (last + 1, last)]
    crossed = []
    for low, high in ((got[0], got[2]), (got[1], got[3])):
        (piece,) = call(cross_kernel, (meta, low, high), [(low.shape, half)])
        crossed.append(lax.ppermute(piece, "seq", between))
    (mine,) = call(
        gather_kernel,
        (meta, *got, *crossed),
        [((4 * out_rows, lanes), half)],
    )
    (weight_grads,) = call(
        weight_kernel,
        (meta, normed, mine, swapped(mine, "dp", 1)),
        [((features // 2, features), jnp.float32)],
        flops=10**9,
        moved=5 * 10**6,
    )
    return (grad_input[None], weight_grads)


def on_device(token_ids, cotangent, table, w_query, w_key, w_value, w_out, window):
    fits = (
        lax.axis_size("seq") == 2 * GROUPS
        and lax.axis_size("dp") == 4
        and token_ids.shape == (1, 128)
        and table.shape == (256, HEADS * HEAD_DIM)
    )
    plan = grouped_device if fits else general_device
    return plan(token_ids, cotangent, table, w_query, w_key, w_value, w_out, window)


def solution(mesh):
    return jax.shard_map(
        on_device,
        mesh=mesh,
        in_specs=(P("dp", "seq"), P("dp", "seq", None), P(), P(), P(), P(), P(), P()),
        out_specs=(P("dp", "seq", None), P("seq", None)),
        check_vma=False,
    )
```

```python
import jax
import jax.numpy as jnp
import numpy as np
from jax import lax
from jax.experimental import pallas as pl
from jax.experimental.pallas import tpu as pltpu
from jax.sharding import PartitionSpec as P

HEADS = 12
HEAD_DIM = 64
WINDOW = 512


EPSILON = 1e-05


def shifted(block, axis, distance):
    devices = range(lax.axis_size(axis))
    route = [(i - distance, i) for i in devices if i - distance in devices]
    return lax.ppermute(block, axis, route)


def rotate(values, positions):
    row_count = values.shape[0]
    shaped = values.reshape(row_count, -1, HEAD_DIM)
    middle = HEAD_DIM // 2
    frequency = 10000.0 ** (-2.0 * jnp.arange(middle, dtype=jnp.float32) / HEAD_DIM)
    angles = positions.astype(jnp.float32)[:, None] * frequency[None, :]
    cosine = jnp.cos(angles)[:, None, :]
    sine_part = jnp.sin(angles)[:, None, :]
    former = shaped[..., :middle]
    latter = shaped[..., middle:]
    turned = jnp.concatenate(
        [former * cosine - latter * sine_part, latter * cosine + former * sine_part], axis=-1
    )
    return turned.reshape(row_count, -1)


def unrotate(values, positions):
    row_count = values.shape[0]
    shaped = values.reshape(row_count, -1, HEAD_DIM)
    middle = HEAD_DIM // 2
    frequency = 10000.0 ** (-2.0 * jnp.arange(middle, dtype=jnp.float32) / HEAD_DIM)
    angles = positions.astype(jnp.float32)[:, None] * frequency[None, :]
    cosine = jnp.cos(angles)[:, None, :]
    sine_part = jnp.sin(angles)[:, None, :]
    former = shaped[..., :middle]
    latter = shaped[..., middle:]
    turned = jnp.concatenate(
        [former * cosine + latter * sine_part, latter * cosine - former * sine_part], axis=-1
    )
    return turned.reshape(row_count, -1)


def tdot(left, right):
    return lax.dot_general(
        left, right, (((0,), (0,)), ((), ())), preferred_element_type=jnp.float32
    )


def ndot(left, right):
    return lax.dot_general(
        left, right, (((1,), (1,)), ((), ())), preferred_element_type=jnp.float32
    )


def embed_rows(byte_ids, table):
    onehot = (byte_ids[:, None] == jnp.arange(table.shape[0], dtype=jnp.int32)[None, :]).astype(
        jnp.bfloat16
    )
    return jnp.dot(onehot, table, preferred_element_type=jnp.float32).astype(jnp.bfloat16)


def normalize(embedded):
    widened = embedded.astype(jnp.float32)
    inv_rms = lax.rsqrt(jnp.mean(widened * widened, axis=1, keepdims=True) + EPSILON)
    return (widened, inv_rms, (widened * inv_rms).astype(jnp.bfloat16))


def keys_values(normed, positions, w_key, w_value):
    key_rows = rotate(jnp.dot(normed, w_key, preferred_element_type=jnp.float32), positions).astype(
        jnp.bfloat16
    )
    value_rows = jnp.dot(normed, w_value, preferred_element_type=jnp.float32).astype(jnp.bfloat16)
    return (key_rows, value_rows)


def head_group(
    query_heads, key_heads, value_heads, grad_heads, group_window, own_pos, key_pos, score_scale
):
    distance = own_pos[:, None] - key_pos[None, :]
    allowed = (
        (distance[None] >= 0)
        & (distance[None] < group_window[:, None, None])
        & (key_pos[None, None, :] >= 0)
    )
    scores = (
        jnp.einsum("qhd,khd->hqk", query_heads, key_heads, preferred_element_type=jnp.float32)
        * score_scale
    )
    masked = jnp.where(allowed, scores, -1e30)
    row_max = jnp.max(masked, axis=-1, keepdims=True)
    weights = jnp.where(allowed, jnp.exp(masked - row_max), 0.0)
    probs = weights / jnp.sum(weights, axis=-1, keepdims=True)
    probs_b = probs.astype(jnp.bfloat16)
    attended = jnp.einsum(
        "hqk,khd->qhd", probs_b, value_heads, preferred_element_type=jnp.float32
    ).astype(jnp.bfloat16)
    grad_probs = jnp.einsum(
        "qhd,khd->hqk", grad_heads, value_heads, preferred_element_type=jnp.float32
    )
    row_term = jnp.sum(probs * grad_probs, axis=-1, keepdims=True)
    grad_scores = (probs * (grad_probs - row_term) * score_scale).astype(jnp.bfloat16)
    grad_query = jnp.einsum(
        "hqk,khd->qhd", grad_scores, key_heads, preferred_element_type=jnp.float32
    )
    grad_key = jnp.einsum(
        "hqk,qhd->khd", grad_scores, query_heads, preferred_element_type=jnp.float32
    )
    grad_value = jnp.einsum("hqk,qhd->khd", probs_b, grad_heads, preferred_element_type=jnp.float32)
    return (attended, grad_query, grad_key, grad_value)


def general_device(token_ids, cotangent, table, w_query, w_key, w_value, w_out, window):
    local_ids = token_ids[0]
    grad_out = cotangent[0]
    length = local_ids.shape[0]
    features = table.shape[1]
    tail_rows = min(length, WINDOW)
    reach_devs = -(-WINDOW // length)
    halo_rows = reach_devs * tail_rows
    offset = lax.axis_index("seq") * length
    own_pos = offset + jnp.arange(length, dtype=jnp.int32)
    halo_pos = offset - halo_rows + jnp.arange(halo_rows, dtype=jnp.int32)
    score_scale = HEAD_DIM ** (-0.5)
    embedded = embed_rows(local_ids, table)
    widened, inv_rms, normed = normalize(embedded)
    query = rotate(jnp.dot(normed, w_query, preferred_element_type=jnp.float32), own_pos).astype(
        jnp.bfloat16
    )
    key_own, value_own = keys_values(normed, own_pos, w_key, w_value)
    key_pieces = []
    value_pieces = []
    for hop_index in range(reach_devs):
        far_keys, far_values = shifted((key_own, value_own), "seq", hop_index + 1)
        key_pieces.insert(0, far_keys)
        value_pieces.insert(0, far_values)
    key_halo = jnp.concatenate(key_pieces, axis=0)
    value_halo = jnp.concatenate(value_pieces, axis=0)
    span_rows = halo_rows + length
    key_all = jnp.concatenate([key_halo, key_own], axis=0)
    value_all = jnp.concatenate([value_halo, value_own], axis=0)
    key_pos = jnp.concatenate([halo_pos, own_pos], axis=0)
    query_heads = query.reshape(length, HEADS, HEAD_DIM)
    key_heads = key_all.reshape(span_rows, HEADS, HEAD_DIM)
    value_heads = value_all.reshape(span_rows, HEADS, HEAD_DIM)
    grad_att = ndot(grad_out, w_out).astype(jnp.bfloat16)
    grad_heads = grad_att.reshape(length, HEADS, HEAD_DIM)
    group_size = 4
    attended_parts = []
    query_parts = []
    key_parts = []
    value_parts = []
    for group_index in range(HEADS // group_size):
        lower = group_index * group_size
        upper = lower + group_size
        outputs = head_group(
            query_heads[:, lower:upper],
            key_heads[:, lower:upper],
            value_heads[:, lower:upper],
            grad_heads[:, lower:upper],
            window[lower:upper],
            own_pos,
            key_pos,
            score_scale,
        )
        attended_parts.append(outputs[0])
        query_parts.append(outputs[1])
        key_parts.append(outputs[2])
        value_parts.append(outputs[3])
    attended = jnp.concatenate(attended_parts, axis=1).reshape(length, features)
    grad_query = jnp.concatenate(query_parts, axis=1).reshape(length, features)
    grad_key = jnp.concatenate(key_parts, axis=1).reshape(span_rows, features)
    grad_value = jnp.concatenate(value_parts, axis=1).reshape(span_rows, features)
    tail_keys = grad_key[:halo_rows].reshape(reach_devs, tail_rows, features)
    tail_values = grad_value[:halo_rows].reshape(reach_devs, tail_rows, features)
    back_keys = jnp.zeros((tail_rows, features), jnp.float32)
    back_values = jnp.zeros((tail_rows, features), jnp.float32)
    for hop_index in range(reach_devs):
        got_keys, got_values = shifted(
            (tail_keys[reach_devs - 1 - hop_index], tail_values[reach_devs - 1 - hop_index]),
            "seq",
            -(hop_index + 1),
        )
        back_keys = back_keys + got_keys
        back_values = back_values + got_values
    own_keys = grad_key[halo_rows:]
    own_values = grad_value[halo_rows:]
    own_keys = jnp.concatenate([own_keys[: length - tail_rows], own_keys + back_keys], axis=0)
    own_values = jnp.concatenate(
        [own_values[: length - tail_rows], own_values + back_values], axis=0
    )
    grad_q_lin = unrotate(grad_query, own_pos).astype(jnp.bfloat16)
    grad_k_lin = unrotate(own_keys, own_pos).astype(jnp.bfloat16)
    grad_v_lin = own_values.astype(jnp.bfloat16)
    grad_normed = ndot(grad_q_lin, w_query) + ndot(grad_k_lin, w_key) + ndot(grad_v_lin, w_value)
    scaled = widened * inv_rms
    grad_input = (
        inv_rms * (grad_normed - scaled * jnp.mean(grad_normed * scaled, axis=1, keepdims=True))
    ).astype(jnp.bfloat16)
    term = jnp.concatenate(
        [
            tdot(normed, grad_q_lin),
            tdot(normed, grad_k_lin),
            tdot(normed, grad_v_lin),
            tdot(attended, grad_out),
        ],
        axis=0,
    )
    shares = lax.psum_scatter(term.astype(jnp.bfloat16), "seq", scatter_dimension=0, tiled=True)
    weight_grads = lax.psum(shares, "dp").astype(jnp.float32)
    return (grad_input[None], weight_grads)


GROUPS = 4
GROUP_HEADS = HEADS // GROUPS
GROUP_COLS = GROUP_HEADS * HEAD_DIM
TILE = 256
TOKEN_ROWS = 16
STRIP = 8
HALF = HEAD_DIM // 2
VMEM_BYTES = 40 * 1024 * 1024
MIDDLE_BYTES = 24 * 1024 * 1024
SMALL_BYTES = 12 * 1024 * 1024


def key_span(query_tile):
    first = max(0, query_tile - WINDOW // TILE)
    return (first * TILE, (query_tile - first + 1) * TILE)


def normed_table(table_ref):
    widened = table_ref[...].astype(jnp.float32)
    inv_rms = lax.rsqrt(jnp.mean(widened * widened, axis=1, keepdims=True) + EPSILON)
    return (widened * inv_rms).astype(jnp.bfloat16)


def onehot_columns(tokens, vocab):
    rows = lax.broadcasted_iota(jnp.int32, (vocab, tokens.shape[1]), 0)
    return (rows == tokens).astype(jnp.float32).astype(jnp.bfloat16)


def send_kernel(spot_ref, tokens_ref, cotangent_ref, out_weights_ref, *out_refs):
    early_refs, grads_ref = out_refs[:-1], out_refs[-1]
    grad_att = ndot(out_weights_ref[...], cotangent_ref[...]).astype(jnp.bfloat16)
    grads_ref[...] = grad_att
    block = tokens_ref.shape[1]
    tokens = jnp.broadcast_to(tokens_ref[...].astype(jnp.float32), (TOKEN_ROWS, block)).astype(
        jnp.bfloat16
    )
    for turn, early_ref in enumerate(early_refs):
        group = spot_ref[1] ^ turn
        place = pl.ds(pl.multiple_of(group * GROUP_COLS, GROUP_COLS), GROUP_COLS)
        early_ref[:GROUP_COLS, :] = grads_ref[place, :]
        early_ref[GROUP_COLS:, :] = tokens


def late_kernel(cotangent_ref, *rest):
    late_ref = rest[-1]
    columns = late_ref.shape[2]
    for target in range(2 * GROUPS):
        side = target % 2
        late_ref[target] = cotangent_ref[:, side * columns : (side + 1) * columns]


def prepare_kernel(
    meta_ref,
    table_ref,
    query_ref,
    key_ref,
    value_ref,
    lookup_ref,
    normed_ref,
    columns_ref,
):
    normed = normed_table(table_ref)
    half = normed.shape[1] // 2
    normed_ref[...] = jnp.where(meta_ref[GROUP_HEADS] == 0, normed[:, :half], normed[:, half:])
    place = pl.ds(pl.multiple_of(meta_ref[GROUP_HEADS + 1] * GROUP_COLS, GROUP_COLS), GROUP_COLS)
    for matrix, weights_ref in enumerate((query_ref, key_ref, value_ref)):
        columns_ref[...] = jnp.dot(
            normed, weights_ref[...], preferred_element_type=jnp.float32
        ).T
        mine = columns_ref[place, :]
        upper = mine.astype(jnp.bfloat16)
        rows = slice(matrix * GROUP_COLS, (matrix + 1) * GROUP_COLS)
        lookup_ref[0, rows, :] = upper
        lookup_ref[1, rows, :] = (mine - upper.astype(jnp.float32)).astype(jnp.bfloat16)


def attention_kernel(
    meta_ref,
    lookup_ref,
    cosine_ref,
    sine_ref,
    *rest,
):
    early_refs = rest[: 2 * GROUPS]
    rest = rest[2 * GROUPS + 1 :]
    attention_body(meta_ref, lookup_ref, cosine_ref, sine_ref, early_refs, *rest)


def attention_body(
    meta_ref,
    lookup_ref,
    cosine_ref,
    sine_ref,
    early_refs,
    own_rows_ref,
    rows1_ref,
    rows2_ref,
    rows3_ref,
    sums_ref,
    attended_ref,
    value_key_ref,
    query_t_ref,
    key_t_ref,
    value_t_ref,
    grad_att_ref,
    onehot_ref,
    onehot_rows_ref,
    grad_query_ref,
    both_ref,
    scaled_ref,
    probs_ref,
    scores_ref,
    right_ref,
    products_ref,
    inverse_ref,
    term_ref,
    grads_ref,
):
    head = pl.program_id(0)
    block = early_refs[0].shape[1]
    length = len(early_refs) * block
    tiles = length // TILE
    vocab = lookup_ref.shape[2]
    half_vocab = vocab // 2
    half = jnp.bfloat16
    cosine = cosine_ref[...]
    sine_part = sine_ref[...]

    @pl.when(head == 0)
    def _():
        own = 2 * meta_ref[GROUP_HEADS + 1] + meta_ref[GROUP_HEADS]
        for turn, early_ref in enumerate(early_refs):
            lanes = pl.ds(pl.multiple_of((own ^ turn) * block, block), block)
            tokens = early_ref[GROUP_COLS : GROUP_COLS + TOKEN_ROWS, :]
            tokens = tokens.astype(jnp.float32)[:1].astype(jnp.int32)
            onehot_ref[:, lanes] = onehot_columns(tokens, vocab)
            grad_att_ref[:, :, lanes] = early_ref[:GROUP_COLS, :].reshape(
                GROUP_HEADS, HEAD_DIM, block
            )
        onehot = onehot_ref[...]
        onehot_rows_ref[...] = onehot.T
        size = 3 * GROUP_COLS
        chosen = jnp.dot(
            lookup_ref[...].reshape(2 * size, vocab), onehot, preferred_element_type=jnp.float32
        )

        def picked(start):
            lower = start + size
            return chosen[start : start + HEAD_DIM] + chosen[lower : lower + HEAD_DIM]

        def turned(columns):
            former = columns[:HALF]
            latter = columns[HALF:]
            return jnp.concatenate(
                [former * cosine - latter * sine_part, latter * cosine + former * sine_part], axis=0
            )

        for index in range(GROUP_HEADS):
            query = turned(picked(index * HEAD_DIM)) * HEAD_DIM ** (-0.5)
            keys = turned(picked(GROUP_COLS + index * HEAD_DIM)).astype(half)
            values = picked(2 * GROUP_COLS + index * HEAD_DIM).astype(half)
            value_key_ref[index] = jnp.concatenate([values, keys], axis=0).T
            query_t_ref[index] = query.astype(half)
            key_t_ref[index] = keys
            value_t_ref[index] = values

    width = meta_ref[head]
    grad_att = grad_att_ref[head]
    query_t = query_t_ref[head]
    blank = jnp.zeros((HEAD_DIM, TILE), half)
    base = lax.broadcasted_iota(jnp.int32, (STRIP, TILE), 1) - lax.broadcasted_iota(
        jnp.int32, (STRIP, TILE), 0
    )
    for tile in range(tiles):
        columns = slice(tile * TILE, (tile + 1) * TILE)
        right_ref[tile, :HEAD_DIM, :TILE] = grad_att[:, columns]
        right_ref[tile, HEAD_DIM:, :TILE] = blank
        right_ref[tile, :HEAD_DIM, TILE:] = blank
        right_ref[tile, HEAD_DIM:, TILE:] = query_t[:, columns]

    def multiply(tile):
        first, count = key_span(tile)
        products_ref[tile, :count, :] = jnp.dot(
            value_key_ref[head, first : first + count, :],
            right_ref[tile],
            preferred_element_type=jnp.float32,
        )

    def forward(tile):
        first, count = key_span(tile)
        columns = slice(tile * TILE, (tile + 1) * TILE)
        row_max = None
        for row in range(0, count, STRIP):
            offset = tile * TILE - first - row
            allowed = base < width - offset
            if offset - STRIP < 0:
                allowed = allowed & (base >= -offset)
            masked = jnp.where(allowed, products_ref[tile, row : row + STRIP, TILE:], -1e30)
            products_ref[tile, row : row + STRIP, TILE:] = masked
            row_max = masked if row_max is None else jnp.maximum(row_max, masked)
        row_max = jnp.max(row_max, axis=0, keepdims=True)
        total = None
        for row in range(0, count, 2 * STRIP):
            weights = jnp.exp(products_ref[tile, row : row + 2 * STRIP, TILE:] - row_max)
            total = weights if total is None else total + weights
            probs_ref[first + row : first + row + 2 * STRIP, columns] = weights.astype(half)
        inverse = 1.0 / jnp.sum(total, axis=0, keepdims=True)
        attended = inverse * jnp.dot(
            value_t_ref[head, :, first : first + count],
            probs_ref[first : first + count, columns],
            preferred_element_type=jnp.float32,
        )
        attended_ref[pl.ds(pl.multiple_of(head * HEAD_DIM, HEAD_DIM), HEAD_DIM), columns] = (
            attended.astype(half)
        )
        wide_grad = grad_att[:, columns].astype(jnp.float32)
        inverse_ref[:, columns] = inverse
        term_ref[:, columns] = jnp.sum(attended * wide_grad, axis=0, keepdims=True)
        scaled_ref[columns, :] = jnp.concatenate(
            [
                (inverse * query_t[:, columns].astype(jnp.float32)).astype(half),
                (inverse * wide_grad).astype(half),
            ],
            axis=0,
        ).T

    def backward(tile):
        first, count = key_span(tile)
        columns = slice(tile * TILE, (tile + 1) * TILE)
        row_term = term_ref[:, columns]
        for row in range(0, count, 2 * STRIP):
            strip = slice(first + row, first + row + 2 * STRIP)
            scores_ref[strip, columns] = (
                probs_ref[strip, columns].astype(jnp.float32)
                * (products_ref[tile, row : row + 2 * STRIP, :TILE] - row_term)
            ).astype(half)
        grad_query_ref[:, columns] = inverse_ref[:, columns] * jnp.dot(
            key_t_ref[head, :, first : first + count],
            scores_ref[first : first + count, columns],
            preferred_element_type=jnp.float32,
        )

    lanes = lax.broadcasted_iota(jnp.int32, (TILE, 2 * HEAD_DIM), 1)

    def collect(tile):
        start = tile * TILE
        stop = min(length, start + TILE + WINDOW)
        grad_key = jnp.dot(
            scores_ref[start : start + TILE, start:stop],
            scaled_ref[start:stop, :],
            preferred_element_type=jnp.float32,
        )
        grad_value = jnp.dot(
            probs_ref[start : start + TILE, start:stop],
            scaled_ref[start:stop, :],
            preferred_element_type=jnp.float32,
        )
        both_ref[:, start : start + TILE] = jnp.where(lanes < HEAD_DIM, grad_key, grad_value).T

    reach = WINDOW // TILE
    for step in range(tiles + 3 + reach):
        if step < tiles:
            multiply(step)
        if 0 <= step - 1 < tiles:
            forward(step - 1)
        if 0 <= step - 2 < tiles:
            backward(step - 2)
        ready = step - 3 - reach
        if 0 <= ready < tiles:
            collect(ready)
    def turned_back(columns):
        former = columns[:HALF]
        latter = columns[HALF:]
        return jnp.concatenate(
            [former * cosine + latter * sine_part, latter * cosine - former * sine_part], axis=0
        )

    both = both_ref[...]
    grads = jnp.concatenate(
        [
            turned_back(grad_query_ref[...] * HEAD_DIM ** (-0.5)),
            turned_back(both[:HEAD_DIM]),
            both[HEAD_DIM:],
        ],
        axis=0,
    ).astype(half)
    grads_ref[...] = grads
    sums = jnp.dot(grads, onehot_rows_ref[...], preferred_element_type=jnp.float32).astype(half)
    for matrix in range(3):
        rows = slice(matrix * HEAD_DIM, (matrix + 1) * HEAD_DIM)
        place = pl.ds(
            pl.multiple_of(matrix * GROUP_COLS + head * HEAD_DIM, HEAD_DIM), HEAD_DIM
        )
        for core in range(2):
            lane = core * half_vocab
            sums_ref[core, place, :] = sums[rows, lane : lane + half_vocab]
        for turn, rows_ref in enumerate((own_rows_ref, rows1_ref, rows2_ref, rows3_ref)):
            target = 2 * (meta_ref[GROUP_HEADS + 1] ^ turn) + meta_ref[GROUP_HEADS]
            rows_ref[place, :] = grads_ref[rows, pl.ds(pl.multiple_of(target * block, block), block)]


def out_kernel(meta_ref, attended_ref, cotangent_ref, sums_ref, after_ref, keep_ref, give_ref):
    del after_ref
    total = jnp.dot(attended_ref[...], cotangent_ref[...], preferred_element_type=jnp.float32)
    rows = total.shape[0] // 2
    base = sums_ref.shape[1]
    lanes = keep_ref.shape[1]
    first = meta_ref[GROUP_HEADS + 2] == 0
    keep_ref[:base, :] = jnp.where(first, sums_ref[0], sums_ref[1])
    give_ref[:base, :] = jnp.where(first, sums_ref[1], sums_ref[0])
    for chunk in range(total.shape[1] // lanes):
        part = total[:, chunk * lanes : (chunk + 1) * lanes]
        place = slice(base + chunk * rows, base + (chunk + 1) * rows)
        keep_ref[place, :] = jnp.where(first, part[:rows], part[rows:]).astype(jnp.bfloat16)
        give_ref[place, :] = jnp.where(first, part[rows:], part[:rows]).astype(jnp.bfloat16)


def combine_kernel(meta_ref, here_ref, there_ref, *rest):
    piece_refs = rest[-GROUPS:]
    rows = GROUP_COLS
    for turn, piece_ref in enumerate(piece_refs):
        target = meta_ref[GROUP_HEADS + 1] ^ turn

        @pl.when(target < 3)
        def _(piece_ref=piece_ref, target=target):
            place = pl.ds(pl.multiple_of(target * rows, rows), rows)
            piece_ref[:rows, :] = here_ref[place, :] + there_ref[place, :]
            tail = piece_ref.shape[0] - rows
            piece_ref[rows:, :] = jnp.zeros((tail, piece_ref.shape[1]), jnp.bfloat16)

        @pl.when(target == 3)
        def _(piece_ref=piece_ref):
            piece_ref[...] = here_ref[3 * rows :, :] + there_ref[3 * rows :, :]


def cross_kernel(meta_ref, low_ref, high_ref, after_ref, out_ref):
    del after_ref
    out_ref[...] = jnp.where(meta_ref[GROUP_HEADS] == 0, low_ref[...], high_ref[...])


def gather_kernel(meta_ref, g0, g1, g2, g3, early_ref, late_ref, mine_ref):
    rows = GROUP_COLS
    size = g0.shape[0]
    group = meta_ref[GROUP_HEADS + 1]
    first = meta_ref[GROUP_HEADS] == 0

    @pl.when(group < 3)
    def _():
        for turn, got in enumerate((g0, g1, g2, g3)):
            place = pl.ds(pl.multiple_of((group ^ turn) * rows, rows), rows)
            mine_ref[place, :] = got[:rows, :]
        tail = mine_ref.shape[0] - GROUPS * rows
        mine_ref[GROUPS * rows :, :] = jnp.zeros((tail, mine_ref.shape[1]), jnp.bfloat16)

    @pl.when((group == 3) & first)
    def _():
        for place, piece in enumerate((g3, late_ref, g2, early_ref)):
            mine_ref[place * size : (place + 1) * size, :] = piece[...]

    @pl.when((group == 3) & jnp.logical_not(first))
    def _():
        for place, piece in enumerate((late_ref, g1, early_ref, g0)):
            mine_ref[place * size : (place + 1) * size, :] = piece[...]


def input_kernel(
    meta_ref,
    tokens_ref,
    table_ref,
    query_ref,
    key_ref,
    value_ref,
    own_ref,
    first_ref,
    second_ref,
    third_ref,
    out_ref,
    columns_ref,
):
    group = meta_ref[GROUP_HEADS + 1]
    for turn, got in enumerate((own_ref, first_ref, second_ref, third_ref)):
        source = group ^ turn
        for matrix in range(3):
            columns_ref[
                matrix, pl.ds(pl.multiple_of(source * GROUP_COLS, GROUP_COLS), GROUP_COLS), :
            ] = got[matrix * GROUP_COLS : (matrix + 1) * GROUP_COLS, :]
    onehot = onehot_columns(tokens_ref[...], table_ref.shape[0])
    embedded = tdot(onehot, table_ref[...])
    inv_rms = lax.rsqrt(jnp.mean(embedded * embedded, axis=1, keepdims=True) + EPSILON)
    grad_normed = None
    for matrix, weights in enumerate((query_ref, key_ref, value_ref)):
        columns = columns_ref[matrix].astype(jnp.float32).T.astype(jnp.bfloat16)
        part = ndot(columns, weights[...])
        grad_normed = part if grad_normed is None else grad_normed + part
    scaled = embedded * inv_rms
    out_ref[...] = (
        inv_rms * (grad_normed - scaled * jnp.mean(grad_normed * scaled, axis=1, keepdims=True))
    ).astype(jnp.bfloat16)


def weight_kernel(meta_ref, normed_ref, mine_ref, other_ref, out_ref):
    half_vocab = mine_ref.shape[1]
    first_core = meta_ref[GROUP_HEADS + 2] == 0

    @pl.when(meta_ref[GROUP_HEADS + 1] < 3)
    def _():
        first = normed_ref[:half_vocab, :]
        second = normed_ref[half_vocab:, :]
        upper = jnp.where(first_core, first, second)
        lower = jnp.where(first_core, second, first)
        total = None
        for part, sums_ref in ((upper, mine_ref), (lower, other_ref)):
            term = lax.dot_general(
                part,
                sums_ref[: GROUPS * GROUP_COLS, :],
                (((0,), (1,)), ((), ())),
                preferred_element_type=jnp.float32,
            )
            total = term if total is None else total + term
        out_ref[...] = total

    @pl.when(meta_ref[GROUP_HEADS + 1] == 3)
    def _():
        rows = GROUP_COLS // 2
        for half in range(2):
            for column in range(6):
                start = (half * 6 + column) * rows
                for core in range(2):
                    same = first_core == (core == 0)
                    value = jnp.where(
                        same, mine_ref[start : start + rows, :], other_ref[start : start + rows, :]
                    )
                    row = half * GROUP_COLS + core * rows
                    out_ref[
                        row : row + rows, column * half_vocab : (column + 1) * half_vocab
                    ] = value.astype(jnp.float32)


def whole(shape):
    return pl.BlockSpec(shape, lambda *_: (0,) * len(shape))


def swapped(block, axis, bit):
    route = [(i, i ^ bit) for i in range(lax.axis_size(axis))]
    return lax.ppermute(block, axis, route)


def rope_table(length):
    frequency = (10000.0 ** (-2.0 * np.arange(HALF, dtype=np.float32) / HEAD_DIM)).astype(np.float32)
    angles = frequency[:, None] * np.arange(length, dtype=np.float32)[None, :]
    angles = angles.astype(np.float64)
    return (
        jnp.asarray(np.cos(angles).astype(np.float32)),
        jnp.asarray(np.sin(angles).astype(np.float32)),
    )


def grouped_device(token_ids, cotangent, table, w_query, w_key, w_value, w_out, window):
    place = lax.axis_index("seq")
    core = lax.axis_index("dp") % 2
    group = place // 2
    side = place % 2
    block = token_ids.shape[1]
    features = table.shape[1]
    vocab = table.shape[0]
    blocks = lax.axis_size("seq")
    length = block * blocks
    grad_out = cotangent[0]
    meta = jnp.concatenate(
        [
            lax.dynamic_slice_in_dim(window, group * GROUP_HEADS, GROUP_HEADS, 0),
            jnp.stack([side, group, core]).astype(jnp.int32),
        ]
    )
    spot = jnp.stack([side, group, core]).astype(jnp.int32)
    cosine, sine_part = rope_table(length)

    def call(
        body, operands, outs, scratch=(), steps=1, flops=10**8, moved=10**6, loose=0, grant=VMEM_BYTES
    ):
        spaces = [whole(operand.shape) for operand in operands]
        for index in range(loose):
            spaces[-1 - index] = pl.BlockSpec(memory_space=pl.ANY)
        if operands[0].ndim == 1:
            spaces[0] = pl.BlockSpec(memory_space=pltpu.SMEM)
        return pl.pallas_call(
            body,
            grid=(steps,),
            in_specs=spaces,
            out_specs=[whole(shape) for shape, _ in outs],
            out_shape=[jax.ShapeDtypeStruct(shape, dtype) for shape, dtype in outs],
            scratch_shapes=list(scratch),
            compiler_params=pltpu.CompilerParams(
                dimension_semantics=("arbitrary",), vmem_limit_bytes=grant
            ),
            cost_estimate=pl.CostEstimate(flops=flops, bytes_accessed=moved, transcendentals=0),
        )(*operands)

    half = jnp.bfloat16
    sent = call(
        send_kernel,
        (spot, token_ids, grad_out, w_out),
        [((GROUP_COLS + TOKEN_ROWS, block), half)] * GROUPS,
        [pltpu.VMEM((features, block), half)],
        grant=60 * 1024 * 1024,
    )
    early = [sent[0]] + [None] * (blocks - 1)
    for turn in (4, 6, 5, 7, 2, 3, 1):
        early[turn] = swapped(sent[turn // 2], "seq", turn)
    lookup, normed = call(
        prepare_kernel,
        (meta, table, w_query, w_key, w_value),
        [((2, 3 * GROUP_COLS, vocab), half), ((vocab, features // 2), half)],
        [pltpu.VMEM((features, vocab), jnp.float32)],
        flops=10**9,
        moved=5 * 10**6,
        grant=60 * 1024 * 1024,
    )
    (late,) = call(
        late_kernel,
        (grad_out, lookup, *early[1:]),
        [((blocks, block, features // 2), half)],
        loose=blocks,
        grant=SMALL_BYTES,
    )
    chunks = late
    late = lax.all_to_all(late, "seq", split_axis=0, concat_axis=0, tiled=True)
    heads_shape = (GROUP_HEADS, HEAD_DIM, length)
    rows_shape = (GROUP_HEADS, length, 2 * HEAD_DIM)
    *rows, sums, attended = call(
        attention_kernel,
        (meta, lookup, cosine, sine_part, *early, chunks),
        [
            *[((3 * GROUP_COLS, block), half)] * GROUPS,
            ((2, 3 * GROUP_COLS, vocab // 2), half),
            ((GROUP_COLS, length), half),
        ],
        [
            pltpu.VMEM(rows_shape, half),
            pltpu.VMEM(heads_shape, half),
            pltpu.VMEM(heads_shape, half),
            pltpu.VMEM(heads_shape, half),
            pltpu.VMEM(heads_shape, half),
            pltpu.VMEM((vocab, length), half),
            pltpu.VMEM((length, vocab), half),
            pltpu.VMEM((HEAD_DIM, length), jnp.float32),
            pltpu.VMEM((2 * HEAD_DIM, length), jnp.float32),
            pltpu.VMEM((length, 2 * HEAD_DIM), half),
            pltpu.VMEM((length, length), half),
            pltpu.VMEM((length, length), half),
            pltpu.VMEM((length // TILE, 2 * HEAD_DIM, 2 * TILE), half),
            pltpu.VMEM((length // TILE, WINDOW + TILE, 2 * TILE), jnp.float32),
            pltpu.VMEM((1, length), jnp.float32),
            pltpu.VMEM((1, length), jnp.float32),
            pltpu.VMEM((3 * HEAD_DIM, length), half),
        ],
        loose=1,
        steps=GROUP_HEADS,
        flops=8 * 10**9,
        moved=8 * 10**6,
    )
    got_rows = [rows[0]] + [swapped(rows[turn], "seq", 2 * turn) for turn in (1, 2, 3)]
    lanes = vocab // 2
    out_rows = 3 * GROUP_COLS // 2
    packed = 3 * GROUP_COLS + out_rows
    keep, give = call(
        out_kernel,
        (meta, attended, late.reshape(length, features // 2), sums, got_rows[1]),
        [((packed, lanes), half)] * 2,
        loose=1,
        grant=SMALL_BYTES,
    )
    here = keep + swapped(give, "dp", 1)
    there = swapped(here, "dp", 2)
    pieces = call(
        combine_kernel,
        (meta, here, there, *got_rows[1:]),
        [((out_rows, lanes), half)] * GROUPS,
        loose=GROUPS - 1,
        grant=SMALL_BYTES,
    )
    got = [pieces[0]] + [None] * (GROUPS - 1)
    for turn in (2, 3, 1):
        got[turn] = swapped(pieces[turn], "seq", 2 * turn)
    (grad_input,) = call(
        input_kernel,
        (meta, token_ids, table, w_query, w_key, w_value, *got_rows),
        [((block, features), half)],
        [pltpu.VMEM((3, features, block), half)],
        flops=10**9,
        moved=5 * 10**6,
        grant=MIDDLE_BYTES,
    )
    last = blocks - 2
    between = [(last, last + 1), (last + 1, last)]
    crossed = []
    for low, high in ((got[0], got[2]), (got[1], got[3])):
        (piece,) = call(
            cross_kernel,
            (meta, low, high, grad_input),
            [(low.shape, half)],
            loose=1,
            grant=SMALL_BYTES,
        )
        crossed.append(lax.ppermute(piece, "seq", between))
    (mine,) = call(
        gather_kernel,
        (meta, *got, *crossed),
        [((4 * out_rows, lanes), half)],
        grant=SMALL_BYTES,
    )
    (weight_grads,) = call(
        weight_kernel,
        (meta, normed, mine, swapped(mine, "dp", 1)),
        [((features // 2, features), jnp.float32)],
        grant=SMALL_BYTES,
        flops=10**9,
        moved=5 * 10**6,
    )
    return (grad_input[None], weight_grads)


def on_device(token_ids, cotangent, table, w_query, w_key, w_value, w_out, window):
    fits = (
        lax.axis_size("seq") == 2 * GROUPS
        and lax.axis_size("dp") == 4
        and token_ids.shape == (1, 128)
        and table.shape == (256, HEADS * HEAD_DIM)
    )
    plan = grouped_device if fits else general_device
    return plan(token_ids, cotangent, table, w_query, w_key, w_value, w_out, window)


def solution(mesh):
    return jax.shard_map(
        on_device,
        mesh=mesh,
        in_specs=(P("dp", "seq"), P("dp", "seq", None), P(), P(), P(), P(), P(), P()),
        out_specs=(P("dp", "seq", None), P("seq", None)),
        check_vma=False,
    )
```

```python
import jax
import jax.numpy as jnp
import numpy as np
from jax import lax
from jax.experimental import pallas as pl
from jax.experimental.pallas import tpu as pltpu
from jax.sharding import PartitionSpec as P

HEADS = 12
HEAD_DIM = 64
WINDOW = 512


EPSILON = 1e-05


def shifted(block, axis, distance):
    devices = range(lax.axis_size(axis))
    route = [(i - distance, i) for i in devices if i - distance in devices]
    return lax.ppermute(block, axis, route)


def rotate(values, positions):
    row_count = values.shape[0]
    shaped = values.reshape(row_count, -1, HEAD_DIM)
    middle = HEAD_DIM // 2
    frequency = 10000.0 ** (-2.0 * jnp.arange(middle, dtype=jnp.float32) / HEAD_DIM)
    angles = positions.astype(jnp.float32)[:, None] * frequency[None, :]
    cosine = jnp.cos(angles)[:, None, :]
    sine_part = jnp.sin(angles)[:, None, :]
    former = shaped[..., :middle]
    latter = shaped[..., middle:]
    turned = jnp.concatenate(
        [former * cosine - latter * sine_part, latter * cosine + former * sine_part], axis=-1
    )
    return turned.reshape(row_count, -1)


def unrotate(values, positions):
    row_count = values.shape[0]
    shaped = values.reshape(row_count, -1, HEAD_DIM)
    middle = HEAD_DIM // 2
    frequency = 10000.0 ** (-2.0 * jnp.arange(middle, dtype=jnp.float32) / HEAD_DIM)
    angles = positions.astype(jnp.float32)[:, None] * frequency[None, :]
    cosine = jnp.cos(angles)[:, None, :]
    sine_part = jnp.sin(angles)[:, None, :]
    former = shaped[..., :middle]
    latter = shaped[..., middle:]
    turned = jnp.concatenate(
        [former * cosine + latter * sine_part, latter * cosine - former * sine_part], axis=-1
    )
    return turned.reshape(row_count, -1)


def tdot(left, right):
    return lax.dot_general(
        left, right, (((0,), (0,)), ((), ())), preferred_element_type=jnp.float32
    )


def ndot(left, right):
    return lax.dot_general(
        left, right, (((1,), (1,)), ((), ())), preferred_element_type=jnp.float32
    )


def embed_rows(byte_ids, table):
    onehot = (byte_ids[:, None] == jnp.arange(table.shape[0], dtype=jnp.int32)[None, :]).astype(
        jnp.bfloat16
    )
    return jnp.dot(onehot, table, preferred_element_type=jnp.float32).astype(jnp.bfloat16)


def normalize(embedded):
    widened = embedded.astype(jnp.float32)
    inv_rms = lax.rsqrt(jnp.mean(widened * widened, axis=1, keepdims=True) + EPSILON)
    return (widened, inv_rms, (widened * inv_rms).astype(jnp.bfloat16))


def keys_values(normed, positions, w_key, w_value):
    key_rows = rotate(jnp.dot(normed, w_key, preferred_element_type=jnp.float32), positions).astype(
        jnp.bfloat16
    )
    value_rows = jnp.dot(normed, w_value, preferred_element_type=jnp.float32).astype(jnp.bfloat16)
    return (key_rows, value_rows)


def head_group(
    query_heads, key_heads, value_heads, grad_heads, group_window, own_pos, key_pos, score_scale
):
    distance = own_pos[:, None] - key_pos[None, :]
    allowed = (
        (distance[None] >= 0)
        & (distance[None] < group_window[:, None, None])
        & (key_pos[None, None, :] >= 0)
    )
    scores = (
        jnp.einsum("qhd,khd->hqk", query_heads, key_heads, preferred_element_type=jnp.float32)
        * score_scale
    )
    masked = jnp.where(allowed, scores, -1e30)
    row_max = jnp.max(masked, axis=-1, keepdims=True)
    weights = jnp.where(allowed, jnp.exp(masked - row_max), 0.0)
    probs = weights / jnp.sum(weights, axis=-1, keepdims=True)
    probs_b = probs.astype(jnp.bfloat16)
    attended = jnp.einsum(
        "hqk,khd->qhd", probs_b, value_heads, preferred_element_type=jnp.float32
    ).astype(jnp.bfloat16)
    grad_probs = jnp.einsum(
        "qhd,khd->hqk", grad_heads, value_heads, preferred_element_type=jnp.float32
    )
    row_term = jnp.sum(probs * grad_probs, axis=-1, keepdims=True)
    grad_scores = (probs * (grad_probs - row_term) * score_scale).astype(jnp.bfloat16)
    grad_query = jnp.einsum(
        "hqk,khd->qhd", grad_scores, key_heads, preferred_element_type=jnp.float32
    )
    grad_key = jnp.einsum(
        "hqk,qhd->khd", grad_scores, query_heads, preferred_element_type=jnp.float32
    )
    grad_value = jnp.einsum("hqk,qhd->khd", probs_b, grad_heads, preferred_element_type=jnp.float32)
    return (attended, grad_query, grad_key, grad_value)


def general_device(token_ids, cotangent, table, w_query, w_key, w_value, w_out, window):
    local_ids = token_ids[0]
    grad_out = cotangent[0]
    length = local_ids.shape[0]
    features = table.shape[1]
    tail_rows = min(length, WINDOW)
    reach_devs = -(-WINDOW // length)
    halo_rows = reach_devs * tail_rows
    offset = lax.axis_index("seq") * length
    own_pos = offset + jnp.arange(length, dtype=jnp.int32)
    halo_pos = offset - halo_rows + jnp.arange(halo_rows, dtype=jnp.int32)
    score_scale = HEAD_DIM ** (-0.5)
    embedded = embed_rows(local_ids, table)
    widened, inv_rms, normed = normalize(embedded)
    query = rotate(jnp.dot(normed, w_query, preferred_element_type=jnp.float32), own_pos).astype(
        jnp.bfloat16
    )
    key_own, value_own = keys_values(normed, own_pos, w_key, w_value)
    key_pieces = []
    value_pieces = []
    for hop_index in range(reach_devs):
        far_keys, far_values = shifted((key_own, value_own), "seq", hop_index + 1)
        key_pieces.insert(0, far_keys)
        value_pieces.insert(0, far_values)
    key_halo = jnp.concatenate(key_pieces, axis=0)
    value_halo = jnp.concatenate(value_pieces, axis=0)
    span_rows = halo_rows + length
    key_all = jnp.concatenate([key_halo, key_own], axis=0)
    value_all = jnp.concatenate([value_halo, value_own], axis=0)
    key_pos = jnp.concatenate([halo_pos, own_pos], axis=0)
    query_heads = query.reshape(length, HEADS, HEAD_DIM)
    key_heads = key_all.reshape(span_rows, HEADS, HEAD_DIM)
    value_heads = value_all.reshape(span_rows, HEADS, HEAD_DIM)
    grad_att = ndot(grad_out, w_out).astype(jnp.bfloat16)
    grad_heads = grad_att.reshape(length, HEADS, HEAD_DIM)
    group_size = 4
    attended_parts = []
    query_parts = []
    key_parts = []
    value_parts = []
    for group_index in range(HEADS // group_size):
        lower = group_index * group_size
        upper = lower + group_size
        outputs = head_group(
            query_heads[:, lower:upper],
            key_heads[:, lower:upper],
            value_heads[:, lower:upper],
            grad_heads[:, lower:upper],
            window[lower:upper],
            own_pos,
            key_pos,
            score_scale,
        )
        attended_parts.append(outputs[0])
        query_parts.append(outputs[1])
        key_parts.append(outputs[2])
        value_parts.append(outputs[3])
    attended = jnp.concatenate(attended_parts, axis=1).reshape(length, features)
    grad_query = jnp.concatenate(query_parts, axis=1).reshape(length, features)
    grad_key = jnp.concatenate(key_parts, axis=1).reshape(span_rows, features)
    grad_value = jnp.concatenate(value_parts, axis=1).reshape(span_rows, features)
    tail_keys = grad_key[:halo_rows].reshape(reach_devs, tail_rows, features)
    tail_values = grad_value[:halo_rows].reshape(reach_devs, tail_rows, features)
    back_keys = jnp.zeros((tail_rows, features), jnp.float32)
    back_values = jnp.zeros((tail_rows, features), jnp.float32)
    for hop_index in range(reach_devs):
        got_keys, got_values = shifted(
            (tail_keys[reach_devs - 1 - hop_index], tail_values[reach_devs - 1 - hop_index]),
            "seq",
            -(hop_index + 1),
        )
        back_keys = back_keys + got_keys
        back_values = back_values + got_values
    own_keys = grad_key[halo_rows:]
    own_values = grad_value[halo_rows:]
    own_keys = jnp.concatenate([own_keys[: length - tail_rows], own_keys + back_keys], axis=0)
    own_values = jnp.concatenate(
        [own_values[: length - tail_rows], own_values + back_values], axis=0
    )
    grad_q_lin = unrotate(grad_query, own_pos).astype(jnp.bfloat16)
    grad_k_lin = unrotate(own_keys, own_pos).astype(jnp.bfloat16)
    grad_v_lin = own_values.astype(jnp.bfloat16)
    grad_normed = ndot(grad_q_lin, w_query) + ndot(grad_k_lin, w_key) + ndot(grad_v_lin, w_value)
    scaled = widened * inv_rms
    grad_input = (
        inv_rms * (grad_normed - scaled * jnp.mean(grad_normed * scaled, axis=1, keepdims=True))
    ).astype(jnp.bfloat16)
    term = jnp.concatenate(
        [
            tdot(normed, grad_q_lin),
            tdot(normed, grad_k_lin),
            tdot(normed, grad_v_lin),
            tdot(attended, grad_out),
        ],
        axis=0,
    )
    shares = lax.psum_scatter(term.astype(jnp.bfloat16), "seq", scatter_dimension=0, tiled=True)
    weight_grads = lax.psum(shares, "dp").astype(jnp.float32)
    return (grad_input[None], weight_grads)


GROUPS = 4
GROUP_HEADS = HEADS // GROUPS
GROUP_COLS = GROUP_HEADS * HEAD_DIM
TILE = 256
TOKEN_ROWS = 16
STRIP = 8
HALF = HEAD_DIM // 2
VMEM_BYTES = 48 * 1024 * 1024


def key_span(query_tile):
    first = max(0, query_tile - WINDOW // TILE)
    return (first * TILE, (query_tile - first + 1) * TILE)


def normed_table(table_ref):
    widened = table_ref[...].astype(jnp.float32)
    inv_rms = lax.rsqrt(jnp.mean(widened * widened, axis=1, keepdims=True) + EPSILON)
    return (widened * inv_rms).astype(jnp.bfloat16)


def onehot_columns(tokens, vocab):
    rows = lax.broadcasted_iota(jnp.int32, (vocab, tokens.shape[1]), 0)
    return (rows == tokens).astype(jnp.float32).astype(jnp.bfloat16)


def send_kernel(spot_ref, tokens_ref, cotangent_ref, out_weights_ref, *out_refs):
    early_refs, grads_ref = out_refs[:-1], out_refs[-1]
    grad_att = ndot(out_weights_ref[...], cotangent_ref[...]).astype(jnp.bfloat16)
    grads_ref[...] = grad_att
    block = tokens_ref.shape[1]
    tokens = jnp.broadcast_to(tokens_ref[...].astype(jnp.float32), (TOKEN_ROWS, block)).astype(
        jnp.bfloat16
    )
    for turn, early_ref in enumerate(early_refs):
        group = spot_ref[1] ^ turn
        place = pl.ds(pl.multiple_of(group * GROUP_COLS, GROUP_COLS), GROUP_COLS)
        early_ref[:GROUP_COLS, :] = grads_ref[place, :]
        early_ref[GROUP_COLS:, :] = tokens


def late_kernel(cotangent_ref, *rest):
    late_ref = rest[-1]
    columns = late_ref.shape[2]
    for target in range(2 * GROUPS):
        side = target % 2
        late_ref[target] = cotangent_ref[:, side * columns : (side + 1) * columns]


def prepare_kernel(
    meta_ref,
    table_ref,
    query_ref,
    key_ref,
    value_ref,
    lookup_ref,
    normed_ref,
    columns_ref,
):
    normed = normed_table(table_ref)
    half = normed.shape[1] // 2
    normed_ref[...] = jnp.where(meta_ref[GROUP_HEADS] == 0, normed[:, :half], normed[:, half:])
    place = pl.ds(pl.multiple_of(meta_ref[GROUP_HEADS + 1] * GROUP_COLS, GROUP_COLS), GROUP_COLS)
    for matrix, weights_ref in enumerate((query_ref, key_ref, value_ref)):
        columns_ref[...] = jnp.dot(
            normed, weights_ref[...], preferred_element_type=jnp.float32
        ).T
        mine = columns_ref[place, :]
        upper = mine.astype(jnp.bfloat16)
        rows = slice(matrix * GROUP_COLS, (matrix + 1) * GROUP_COLS)
        lookup_ref[0, rows, :] = upper
        lookup_ref[1, rows, :] = (mine - upper.astype(jnp.float32)).astype(jnp.bfloat16)


def attention_kernel(
    meta_ref,
    lookup_ref,
    cosine_ref,
    sine_ref,
    *rest,
):
    early_refs = rest[: 2 * GROUPS]
    attention_body(meta_ref, lookup_ref, cosine_ref, sine_ref, early_refs, *rest[2 * GROUPS :])


def attention_body(
    meta_ref,
    lookup_ref,
    cosine_ref,
    sine_ref,
    early_refs,
    rows_ref,
    sums_ref,
    attended_ref,
    value_key_ref,
    query_t_ref,
    key_t_ref,
    value_t_ref,
    grad_att_ref,
    onehot_ref,
    onehot_rows_ref,
    grad_query_ref,
    both_ref,
    scaled_ref,
    probs_ref,
    scores_ref,
    right_ref,
    products_ref,
    inverse_ref,
    term_ref,
):
    head = pl.program_id(0)
    block = early_refs[0].shape[1]
    length = len(early_refs) * block
    tiles = length // TILE
    vocab = lookup_ref.shape[2]
    half_vocab = vocab // 2
    half = jnp.bfloat16
    cosine = cosine_ref[...]
    sine_part = sine_ref[...]

    @pl.when(head == 0)
    def _():
        own = 2 * meta_ref[GROUP_HEADS + 1] + meta_ref[GROUP_HEADS]
        for turn, early_ref in enumerate(early_refs):
            lanes = pl.ds(pl.multiple_of((own ^ turn) * block, block), block)
            tokens = early_ref[GROUP_COLS : GROUP_COLS + TOKEN_ROWS, :]
            tokens = tokens.astype(jnp.float32)[:1].astype(jnp.int32)
            onehot_ref[:, lanes] = onehot_columns(tokens, vocab)
            grad_att_ref[:, :, lanes] = early_ref[:GROUP_COLS, :].reshape(
                GROUP_HEADS, HEAD_DIM, block
            )
        onehot = onehot_ref[...]
        onehot_rows_ref[...] = onehot.T
        size = 3 * GROUP_COLS
        chosen = jnp.dot(
            lookup_ref[...].reshape(2 * size, vocab), onehot, preferred_element_type=jnp.float32
        )

        def picked(start):
            lower = start + size
            return chosen[start : start + HEAD_DIM] + chosen[lower : lower + HEAD_DIM]

        def turned(columns):
            former = columns[:HALF]
            latter = columns[HALF:]
            return jnp.concatenate(
                [former * cosine - latter * sine_part, latter * cosine + former * sine_part], axis=0
            )

        for index in range(GROUP_HEADS):
            query = turned(picked(index * HEAD_DIM)) * HEAD_DIM ** (-0.5)
            keys = turned(picked(GROUP_COLS + index * HEAD_DIM)).astype(half)
            values = picked(2 * GROUP_COLS + index * HEAD_DIM).astype(half)
            value_key_ref[index] = jnp.concatenate([values, keys], axis=0).T
            query_t_ref[index] = query.astype(half)
            key_t_ref[index] = keys
            value_t_ref[index] = values

    width = meta_ref[head]
    grad_att = grad_att_ref[head]
    query_t = query_t_ref[head]
    blank = jnp.zeros((HEAD_DIM, TILE), half)
    base = lax.broadcasted_iota(jnp.int32, (STRIP, TILE), 1) - lax.broadcasted_iota(
        jnp.int32, (STRIP, TILE), 0
    )
    for tile in range(tiles):
        columns = slice(tile * TILE, (tile + 1) * TILE)
        right_ref[tile, :HEAD_DIM, :TILE] = grad_att[:, columns]
        right_ref[tile, HEAD_DIM:, :TILE] = blank
        right_ref[tile, :HEAD_DIM, TILE:] = blank
        right_ref[tile, HEAD_DIM:, TILE:] = query_t[:, columns]

    def multiply(tile):
        first, count = key_span(tile)
        products_ref[tile, :count, :] = jnp.dot(
            value_key_ref[head, first : first + count, :],
            right_ref[tile],
            preferred_element_type=jnp.float32,
        )

    def forward(tile):
        first, count = key_span(tile)
        columns = slice(tile * TILE, (tile + 1) * TILE)
        row_max = None
        for row in range(0, count, STRIP):
            offset = tile * TILE - first - row
            allowed = base < width - offset
            if offset - STRIP < 0:
                allowed = allowed & (base >= -offset)
            masked = jnp.where(allowed, products_ref[tile, row : row + STRIP, TILE:], -1e30)
            products_ref[tile, row : row + STRIP, TILE:] = masked
            row_max = masked if row_max is None else jnp.maximum(row_max, masked)
        row_max = jnp.max(row_max, axis=0, keepdims=True)
        total = None
        for row in range(0, count, 2 * STRIP):
            weights = jnp.exp(products_ref[tile, row : row + 2 * STRIP, TILE:] - row_max)
            total = weights if total is None else total + weights
            probs_ref[first + row : first + row + 2 * STRIP, columns] = weights.astype(half)
        inverse = 1.0 / jnp.sum(total, axis=0, keepdims=True)
        attended = inverse * jnp.dot(
            value_t_ref[head, :, first : first + count],
            probs_ref[first : first + count, columns],
            preferred_element_type=jnp.float32,
        )
        attended_ref[pl.ds(pl.multiple_of(head * HEAD_DIM, HEAD_DIM), HEAD_DIM), columns] = (
            attended.astype(half)
        )
        wide_grad = grad_att[:, columns].astype(jnp.float32)
        inverse_ref[:, columns] = inverse
        term_ref[:, columns] = jnp.sum(attended * wide_grad, axis=0, keepdims=True)
        scaled_ref[columns, :] = jnp.concatenate(
            [
                (inverse * query_t[:, columns].astype(jnp.float32)).astype(half),
                (inverse * wide_grad).astype(half),
            ],
            axis=0,
        ).T

    def backward(tile):
        first, count = key_span(tile)
        columns = slice(tile * TILE, (tile + 1) * TILE)
        row_term = term_ref[:, columns]
        for row in range(0, count, 2 * STRIP):
            strip = slice(first + row, first + row + 2 * STRIP)
            scores_ref[strip, columns] = (
                probs_ref[strip, columns].astype(jnp.float32)
                * (products_ref[tile, row : row + 2 * STRIP, :TILE] - row_term)
            ).astype(half)
        grad_query_ref[:, columns] = inverse_ref[:, columns] * jnp.dot(
            key_t_ref[head, :, first : first + count],
            scores_ref[first : first + count, columns],
            preferred_element_type=jnp.float32,
        )

    lanes = lax.broadcasted_iota(jnp.int32, (TILE, 2 * HEAD_DIM), 1)

    def collect(tile):
        start = tile * TILE
        stop = min(length, start + TILE + WINDOW)
        grad_key = jnp.dot(
            scores_ref[start : start + TILE, start:stop],
            scaled_ref[start:stop, :],
            preferred_element_type=jnp.float32,
        )
        grad_value = jnp.dot(
            probs_ref[start : start + TILE, start:stop],
            scaled_ref[start:stop, :],
            preferred_element_type=jnp.float32,
        )
        both_ref[:, start : start + TILE] = jnp.where(lanes < HEAD_DIM, grad_key, grad_value).T

    reach = WINDOW // TILE
    for step in range(tiles + 3 + reach):
        if step < tiles:
            multiply(step)
        if 0 <= step - 1 < tiles:
            forward(step - 1)
        if 0 <= step - 2 < tiles:
            backward(step - 2)
        ready = step - 3 - reach
        if 0 <= ready < tiles:
            collect(ready)
    def turned_back(columns):
        former = columns[:HALF]
        latter = columns[HALF:]
        return jnp.concatenate(
            [former * cosine + latter * sine_part, latter * cosine - former * sine_part], axis=0
        )

    both = both_ref[...]
    grads = jnp.concatenate(
        [
            turned_back(grad_query_ref[...] * HEAD_DIM ** (-0.5)),
            turned_back(both[:HEAD_DIM]),
            both[HEAD_DIM:],
        ],
        axis=0,
    ).astype(half)
    sums = jnp.dot(grads, onehot_rows_ref[...], preferred_element_type=jnp.float32).astype(half)
    for matrix in range(3):
        rows = slice(matrix * HEAD_DIM, (matrix + 1) * HEAD_DIM)
        place = pl.ds(
            pl.multiple_of(matrix * GROUP_COLS + head * HEAD_DIM, HEAD_DIM), HEAD_DIM
        )
        for core in range(2):
            lane = core * half_vocab
            sums_ref[core, place, :] = sums[rows, lane : lane + half_vocab]
        for target in range(GROUPS):
            start = target * 2 * block
            even = grads[rows, start : start + block]
            odd = grads[rows, start + block : start + 2 * block]
            rows_ref[target, place, :] = jnp.where(meta_ref[GROUP_HEADS] == 0, even, odd)


def out_kernel(meta_ref, attended_ref, cotangent_ref, sums_ref, keep_ref, give_ref):
    total = jnp.dot(attended_ref[...], cotangent_ref[...], preferred_element_type=jnp.float32)
    rows = total.shape[0] // 2
    base = sums_ref.shape[1]
    lanes = keep_ref.shape[1]
    first = meta_ref[GROUP_HEADS + 2] == 0
    keep_ref[:base, :] = jnp.where(first, sums_ref[0], sums_ref[1])
    give_ref[:base, :] = jnp.where(first, sums_ref[1], sums_ref[0])
    for chunk in range(total.shape[1] // lanes):
        part = total[:, chunk * lanes : (chunk + 1) * lanes]
        place = slice(base + chunk * rows, base + (chunk + 1) * rows)
        keep_ref[place, :] = jnp.where(first, part[:rows], part[rows:]).astype(jnp.bfloat16)
        give_ref[place, :] = jnp.where(first, part[rows:], part[:rows]).astype(jnp.bfloat16)


def core_kernel(keep_ref, got_ref, here_ref, out_ref):
    here_ref[...] = keep_ref[...] + got_ref[...]
    base = here_ref.shape[0] - out_ref.shape[0]
    out_ref[...] = here_ref[base:, :]


def combine_kernel(meta_ref, here_ref, there_ref, near_ref, far_ref, after_ref, *piece_refs):
    del after_ref
    rows = GROUP_COLS
    for turn, piece_ref in enumerate(piece_refs):
        target = meta_ref[GROUP_HEADS + 1] ^ turn

        @pl.when(target < 3)
        def _(piece_ref=piece_ref, target=target):
            place = pl.ds(pl.multiple_of(target * rows, rows), rows)
            piece_ref[:rows, :] = here_ref[place, :] + there_ref[place, :]
            tail = piece_ref.shape[0] - rows
            piece_ref[rows:, :] = jnp.zeros((tail, piece_ref.shape[1]), jnp.bfloat16)

        @pl.when(target == 3)
        def _(piece_ref=piece_ref):
            stays = meta_ref[GROUP_HEADS + 1] // 2 == meta_ref[GROUP_HEADS]
            own = here_ref[3 * rows :, :] + there_ref[3 * rows :, :]
            piece_ref[...] = jnp.where(stays, own, near_ref[...] + far_ref[...])


def gather_kernel(meta_ref, g0, g1, g2, g3, after_ref, mine_ref):
    del after_ref
    rows = GROUP_COLS
    size = g0.shape[0]
    group = meta_ref[GROUP_HEADS + 1]

    @pl.when(group < 3)
    def _():
        for turn, got in enumerate((g0, g1, g2, g3)):
            place = pl.ds(pl.multiple_of((group ^ turn) * rows, rows), rows)
            mine_ref[place, :] = got[:rows, :]
        tail = mine_ref.shape[0] - GROUPS * rows
        mine_ref[GROUPS * rows :, :] = jnp.zeros((tail, mine_ref.shape[1]), jnp.bfloat16)

    @pl.when(group == 3)
    def _():
        for place, piece in enumerate((g3, g1, g2, g0)):
            mine_ref[place * size : (place + 1) * size, :] = piece[...]


def input_kernel(tokens_ref, table_ref, query_ref, key_ref, value_ref, rows_ref, out_ref):
    vocab = table_ref.shape[0]
    onehot = onehot_columns(tokens_ref[...], vocab)
    embedded = tdot(onehot, table_ref[...])
    inv_rms = lax.rsqrt(jnp.mean(embedded * embedded, axis=1, keepdims=True) + EPSILON)
    grad_normed = None
    for matrix, weights in enumerate((query_ref, key_ref, value_ref)):
        columns = jnp.concatenate(
            [
                rows_ref[group, matrix * GROUP_COLS : (matrix + 1) * GROUP_COLS, :]
                for group in range(GROUPS)
            ],
            axis=0,
        )
        part = ndot(columns.astype(jnp.float32).T.astype(jnp.bfloat16), weights[...])
        grad_normed = part if grad_normed is None else grad_normed + part
    scaled = embedded * inv_rms
    out_ref[...] = (
        inv_rms * (grad_normed - scaled * jnp.mean(grad_normed * scaled, axis=1, keepdims=True))
    ).astype(jnp.bfloat16)


def weight_kernel(meta_ref, normed_ref, mine_ref, other_ref, out_ref):
    half_vocab = mine_ref.shape[1]
    first_core = meta_ref[GROUP_HEADS + 2] == 0

    @pl.when(meta_ref[GROUP_HEADS + 1] < 3)
    def _():
        first = normed_ref[:half_vocab, :]
        second = normed_ref[half_vocab:, :]
        upper = jnp.where(first_core, first, second)
        lower = jnp.where(first_core, second, first)
        total = None
        for part, sums_ref in ((upper, mine_ref), (lower, other_ref)):
            term = lax.dot_general(
                part,
                sums_ref[: GROUPS * GROUP_COLS, :],
                (((0,), (1,)), ((), ())),
                preferred_element_type=jnp.float32,
            )
            total = term if total is None else total + term
        out_ref[...] = total

    @pl.when(meta_ref[GROUP_HEADS + 1] == 3)
    def _():
        rows = GROUP_COLS // 2
        for half in range(2):
            for column in range(6):
                start = (half * 6 + column) * rows
                for core in range(2):
                    same = first_core == (core == 0)
                    value = jnp.where(
                        same, mine_ref[start : start + rows, :], other_ref[start : start + rows, :]
                    )
                    row = half * GROUP_COLS + core * rows
                    out_ref[
                        row : row + rows, column * half_vocab : (column + 1) * half_vocab
                    ] = value.astype(jnp.float32)


def whole(shape):
    return pl.BlockSpec(shape, lambda *_: (0,) * len(shape))


def swapped(block, axis, bit):
    route = [(i, i ^ bit) for i in range(lax.axis_size(axis))]
    return lax.ppermute(block, axis, route)


def rope_table(length):
    frequency = (10000.0 ** (-2.0 * np.arange(HALF, dtype=np.float32) / HEAD_DIM)).astype(np.float32)
    angles = frequency[:, None] * np.arange(length, dtype=np.float32)[None, :]
    angles = angles.astype(np.float64)
    return (
        jnp.asarray(np.cos(angles).astype(np.float32)),
        jnp.asarray(np.sin(angles).astype(np.float32)),
    )


def grouped_device(token_ids, cotangent, table, w_query, w_key, w_value, w_out, window):
    place = lax.axis_index("seq")
    core = lax.axis_index("dp") % 2
    group = place // 2
    side = place % 2
    block = token_ids.shape[1]
    features = table.shape[1]
    vocab = table.shape[0]
    blocks = lax.axis_size("seq")
    length = block * blocks
    grad_out = cotangent[0]
    meta = jnp.concatenate(
        [
            lax.dynamic_slice_in_dim(window, group * GROUP_HEADS, GROUP_HEADS, 0),
            jnp.stack([side, group, core]).astype(jnp.int32),
        ]
    )
    spot = jnp.stack([side, group, core]).astype(jnp.int32)
    cosine, sine_part = rope_table(length)

    def call(
        body, operands, outs, scratch=(), steps=1, flops=10**8, moved=10**6, loose=0, grant=VMEM_BYTES
    ):
        spaces = [whole(operand.shape) for operand in operands]
        for index in range(loose):
            spaces[-1 - index] = pl.BlockSpec(memory_space=pl.ANY)
        if operands[0].ndim == 1:
            spaces[0] = pl.BlockSpec(memory_space=pltpu.SMEM)
        return pl.pallas_call(
            body,
            grid=(steps,),
            in_specs=spaces,
            out_specs=[whole(shape) for shape, _ in outs],
            out_shape=[jax.ShapeDtypeStruct(shape, dtype) for shape, dtype in outs],
            scratch_shapes=list(scratch),
            compiler_params=pltpu.CompilerParams(
                dimension_semantics=("arbitrary",), vmem_limit_bytes=grant
            ),
            cost_estimate=pl.CostEstimate(flops=flops, bytes_accessed=moved, transcendentals=0),
        )(*operands)

    half = jnp.bfloat16
    sent = call(
        send_kernel,
        (spot, token_ids, grad_out, w_out),
        [((GROUP_COLS + TOKEN_ROWS, block), half)] * GROUPS,
        [pltpu.VMEM((features, block), half)],
        grant=60 * 1024 * 1024,
    )
    early = [sent[0]] + [None] * (blocks - 1)
    for turn in (4, 6, 5, 7, 2, 3, 1):
        early[turn] = swapped(sent[turn // 2], "seq", turn)
    lookup, normed = call(
        prepare_kernel,
        (meta, table, w_query, w_key, w_value),
        [((2, 3 * GROUP_COLS, vocab), half), ((vocab, features // 2), half)],
        [pltpu.VMEM((features, vocab), jnp.float32)],
        flops=10**9,
        moved=5 * 10**6,
        grant=60 * 1024 * 1024,
    )
    (late,) = call(
        late_kernel,
        (grad_out, lookup, *early[1:]),
        [((blocks, block, features // 2), half)],
        loose=blocks,
    )
    late = lax.all_to_all(late, "seq", split_axis=0, concat_axis=0, tiled=True)
    heads_shape = (GROUP_HEADS, HEAD_DIM, length)
    rows_shape = (GROUP_HEADS, length, 2 * HEAD_DIM)
    rows, sums, attended = call(
        attention_kernel,
        (meta, lookup, cosine, sine_part, *early),
        [
            ((GROUPS, 3 * GROUP_COLS, block), half),
            ((2, 3 * GROUP_COLS, vocab // 2), half),
            ((GROUP_COLS, length), half),
        ],
        [
            pltpu.VMEM(rows_shape, half),
            pltpu.VMEM(heads_shape, half),
            pltpu.VMEM(heads_shape, half),
            pltpu.VMEM(heads_shape, half),
            pltpu.VMEM(heads_shape, half),
            pltpu.VMEM((vocab, length), half),
            pltpu.VMEM((length, vocab), half),
            pltpu.VMEM((HEAD_DIM, length), jnp.float32),
            pltpu.VMEM((2 * HEAD_DIM, length), jnp.float32),
            pltpu.VMEM((length, 2 * HEAD_DIM), half),
            pltpu.VMEM((length, length), half),
            pltpu.VMEM((length, length), half),
            pltpu.VMEM((length // TILE, 2 * HEAD_DIM, 2 * TILE), half),
            pltpu.VMEM((length // TILE, WINDOW + TILE, 2 * TILE), jnp.float32),
            pltpu.VMEM((1, length), jnp.float32),
            pltpu.VMEM((1, length), jnp.float32),
        ],
        steps=GROUP_HEADS,
        flops=8 * 10**9,
        moved=8 * 10**6,
    )
    planes = [[2 * z + x for z in range(GROUPS)] for x in range(2)]

    def over_plane(chunks):
        return lax.all_to_all(
            chunks, "seq", split_axis=0, concat_axis=0, axis_index_groups=planes, tiled=True
        )

    got_rows = over_plane(rows)
    lanes = vocab // 2
    out_rows = 3 * GROUP_COLS // 2
    packed = 3 * GROUP_COLS + out_rows
    keep, give = call(
        out_kernel,
        (meta, attended, late.reshape(length, features // 2), sums),
        [((packed, lanes), half)] * 2,
    )
    here, here_out = call(
        core_kernel,
        (keep, swapped(give, "dp", 1)),
        [((packed, lanes), half), ((out_rows, lanes), half)],
    )
    there = swapped(here, "dp", 2)
    astray = [(i, i ^ 5) for i in range(blocks) if i // 4 != i % 2]
    near = lax.ppermute(here_out, "seq", astray)
    far = lax.ppermute(
        here_out,
        ("dp", "seq"),
        [
            (blocks * d + source, blocks * (d ^ 2) + target)
            for d in range(lax.axis_size("dp"))
            for source, target in astray
        ],
    )
    pieces = call(
        combine_kernel,
        (meta, here, there, near, far, got_rows),
        [((out_rows, lanes), half)] * GROUPS,
        loose=1,
    )
    got = [pieces[0]] + [None] * (GROUPS - 1)
    for turn in (2, 3, 1):
        got[turn] = swapped(pieces[turn], "seq", 2 * turn)
    (grad_input,) = call(
        input_kernel,
        (token_ids, table, w_query, w_key, w_value, got_rows),
        [((block, features), half)],
        flops=10**9,
        moved=5 * 10**6,
    )
    (mine,) = call(
        gather_kernel,
        (meta, *got, grad_input),
        [((4 * out_rows, lanes), half)],
        loose=1,
    )
    (weight_grads,) = call(
        weight_kernel,
        (meta, normed, mine, swapped(mine, "dp", 1)),
        [((features // 2, features), jnp.float32)],
        flops=10**9,
        moved=5 * 10**6,
    )
    return (grad_input[None], weight_grads)


def on_device(token_ids, cotangent, table, w_query, w_key, w_value, w_out, window):
    fits = (
        lax.axis_size("seq") == 2 * GROUPS
        and lax.axis_size("dp") == 4
        and token_ids.shape == (1, 128)
        and table.shape == (256, HEADS * HEAD_DIM)
    )
    plan = grouped_device if fits else general_device
    return plan(token_ids, cotangent, table, w_query, w_key, w_value, w_out, window)


def solution(mesh):
    return jax.shard_map(
        on_device,
        mesh=mesh,
        in_specs=(P("dp", "seq"), P("dp", "seq", None), P(), P(), P(), P(), P(), P()),
        out_specs=(P("dp", "seq", None), P("seq", None)),
        check_vma=False,
    )
```

```python
import jax
import jax.numpy as jnp
import numpy as np
from jax import lax
from jax.experimental import pallas as pl
from jax.experimental.pallas import tpu as pltpu
from jax.sharding import PartitionSpec as P

HEADS = 12
HEAD_DIM = 64
WINDOW = 512


EPSILON = 1e-05


def shifted(block, axis, distance):
    devices = range(lax.axis_size(axis))
    route = [(i - distance, i) for i in devices if i - distance in devices]
    return lax.ppermute(block, axis, route)


def rotate(values, positions):
    row_count = values.shape[0]
    shaped = values.reshape(row_count, -1, HEAD_DIM)
    middle = HEAD_DIM // 2
    frequency = 10000.0 ** (-2.0 * jnp.arange(middle, dtype=jnp.float32) / HEAD_DIM)
    angles = positions.astype(jnp.float32)[:, None] * frequency[None, :]
    cosine = jnp.cos(angles)[:, None, :]
    sine_part = jnp.sin(angles)[:, None, :]
    former = shaped[..., :middle]
    latter = shaped[..., middle:]
    turned = jnp.concatenate(
        [former * cosine - latter * sine_part, latter * cosine + former * sine_part], axis=-1
    )
    return turned.reshape(row_count, -1)


def unrotate(values, positions):
    row_count = values.shape[0]
    shaped = values.reshape(row_count, -1, HEAD_DIM)
    middle = HEAD_DIM // 2
    frequency = 10000.0 ** (-2.0 * jnp.arange(middle, dtype=jnp.float32) / HEAD_DIM)
    angles = positions.astype(jnp.float32)[:, None] * frequency[None, :]
    cosine = jnp.cos(angles)[:, None, :]
    sine_part = jnp.sin(angles)[:, None, :]
    former = shaped[..., :middle]
    latter = shaped[..., middle:]
    turned = jnp.concatenate(
        [former * cosine + latter * sine_part, latter * cosine - former * sine_part], axis=-1
    )
    return turned.reshape(row_count, -1)


def tdot(left, right):
    return lax.dot_general(
        left, right, (((0,), (0,)), ((), ())), preferred_element_type=jnp.float32
    )


def ndot(left, right):
    return lax.dot_general(
        left, right, (((1,), (1,)), ((), ())), preferred_element_type=jnp.float32
    )


def embed_rows(byte_ids, table):
    onehot = (byte_ids[:, None] == jnp.arange(table.shape[0], dtype=jnp.int32)[None, :]).astype(
        jnp.bfloat16
    )
    return jnp.dot(onehot, table, preferred_element_type=jnp.float32).astype(jnp.bfloat16)


def normalize(embedded):
    widened = embedded.astype(jnp.float32)
    inv_rms = lax.rsqrt(jnp.mean(widened * widened, axis=1, keepdims=True) + EPSILON)
    return (widened, inv_rms, (widened * inv_rms).astype(jnp.bfloat16))


def keys_values(normed, positions, w_key, w_value):
    key_rows = rotate(jnp.dot(normed, w_key, preferred_element_type=jnp.float32), positions).astype(
        jnp.bfloat16
    )
    value_rows = jnp.dot(normed, w_value, preferred_element_type=jnp.float32).astype(jnp.bfloat16)
    return (key_rows, value_rows)


def head_group(
    query_heads, key_heads, value_heads, grad_heads, group_window, own_pos, key_pos, score_scale
):
    distance = own_pos[:, None] - key_pos[None, :]
    allowed = (
        (distance[None] >= 0)
        & (distance[None] < group_window[:, None, None])
        & (key_pos[None, None, :] >= 0)
    )
    scores = (
        jnp.einsum("qhd,khd->hqk", query_heads, key_heads, preferred_element_type=jnp.float32)
        * score_scale
    )
    masked = jnp.where(allowed, scores, -1e30)
    row_max = jnp.max(masked, axis=-1, keepdims=True)
    weights = jnp.where(allowed, jnp.exp(masked - row_max), 0.0)
    probs = weights / jnp.sum(weights, axis=-1, keepdims=True)
    probs_b = probs.astype(jnp.bfloat16)
    attended = jnp.einsum(
        "hqk,khd->qhd", probs_b, value_heads, preferred_element_type=jnp.float32
    ).astype(jnp.bfloat16)
    grad_probs = jnp.einsum(
        "qhd,khd->hqk", grad_heads, value_heads, preferred_element_type=jnp.float32
    )
    row_term = jnp.sum(probs * grad_probs, axis=-1, keepdims=True)
    grad_scores = (probs * (grad_probs - row_term) * score_scale).astype(jnp.bfloat16)
    grad_query = jnp.einsum(
        "hqk,khd->qhd", grad_scores, key_heads, preferred_element_type=jnp.float32
    )
    grad_key = jnp.einsum(
        "hqk,qhd->khd", grad_scores, query_heads, preferred_element_type=jnp.float32
    )
    grad_value = jnp.einsum("hqk,qhd->khd", probs_b, grad_heads, preferred_element_type=jnp.float32)
    return (attended, grad_query, grad_key, grad_value)


def general_device(token_ids, cotangent, table, w_query, w_key, w_value, w_out, window):
    local_ids = token_ids[0]
    grad_out = cotangent[0]
    length = local_ids.shape[0]
    features = table.shape[1]
    tail_rows = min(length, WINDOW)
    reach_devs = -(-WINDOW // length)
    halo_rows = reach_devs * tail_rows
    offset = lax.axis_index("seq") * length
    own_pos = offset + jnp.arange(length, dtype=jnp.int32)
    halo_pos = offset - halo_rows + jnp.arange(halo_rows, dtype=jnp.int32)
    score_scale = HEAD_DIM ** (-0.5)
    embedded = embed_rows(local_ids, table)
    widened, inv_rms, normed = normalize(embedded)
    query = rotate(jnp.dot(normed, w_query, preferred_element_type=jnp.float32), own_pos).astype(
        jnp.bfloat16
    )
    key_own, value_own = keys_values(normed, own_pos, w_key, w_value)
    key_pieces = []
    value_pieces = []
    for hop_index in range(reach_devs):
        far_keys, far_values = shifted((key_own, value_own), "seq", hop_index + 1)
        key_pieces.insert(0, far_keys)
        value_pieces.insert(0, far_values)
    key_halo = jnp.concatenate(key_pieces, axis=0)
    value_halo = jnp.concatenate(value_pieces, axis=0)
    span_rows = halo_rows + length
    key_all = jnp.concatenate([key_halo, key_own], axis=0)
    value_all = jnp.concatenate([value_halo, value_own], axis=0)
    key_pos = jnp.concatenate([halo_pos, own_pos], axis=0)
    query_heads = query.reshape(length, HEADS, HEAD_DIM)
    key_heads = key_all.reshape(span_rows, HEADS, HEAD_DIM)
    value_heads = value_all.reshape(span_rows, HEADS, HEAD_DIM)
    grad_att = ndot(grad_out, w_out).astype(jnp.bfloat16)
    grad_heads = grad_att.reshape(length, HEADS, HEAD_DIM)
    group_size = 4
    attended_parts = []
    query_parts = []
    key_parts = []
    value_parts = []
    for group_index in range(HEADS // group_size):
        lower = group_index * group_size
        upper = lower + group_size
        outputs = head_group(
            query_heads[:, lower:upper],
            key_heads[:, lower:upper],
            value_heads[:, lower:upper],
            grad_heads[:, lower:upper],
            window[lower:upper],
            own_pos,
            key_pos,
            score_scale,
        )
        attended_parts.append(outputs[0])
        query_parts.append(outputs[1])
        key_parts.append(outputs[2])
        value_parts.append(outputs[3])
    attended = jnp.concatenate(attended_parts, axis=1).reshape(length, features)
    grad_query = jnp.concatenate(query_parts, axis=1).reshape(length, features)
    grad_key = jnp.concatenate(key_parts, axis=1).reshape(span_rows, features)
    grad_value = jnp.concatenate(value_parts, axis=1).reshape(span_rows, features)
    tail_keys = grad_key[:halo_rows].reshape(reach_devs, tail_rows, features)
    tail_values = grad_value[:halo_rows].reshape(reach_devs, tail_rows, features)
    back_keys = jnp.zeros((tail_rows, features), jnp.float32)
    back_values = jnp.zeros((tail_rows, features), jnp.float32)
    for hop_index in range(reach_devs):
        got_keys, got_values = shifted(
            (tail_keys[reach_devs - 1 - hop_index], tail_values[reach_devs - 1 - hop_index]),
            "seq",
            -(hop_index + 1),
        )
        back_keys = back_keys + got_keys
        back_values = back_values + got_values
    own_keys = grad_key[halo_rows:]
    own_values = grad_value[halo_rows:]
    own_keys = jnp.concatenate([own_keys[: length - tail_rows], own_keys + back_keys], axis=0)
    own_values = jnp.concatenate(
        [own_values[: length - tail_rows], own_values + back_values], axis=0
    )
    grad_q_lin = unrotate(grad_query, own_pos).astype(jnp.bfloat16)
    grad_k_lin = unrotate(own_keys, own_pos).astype(jnp.bfloat16)
    grad_v_lin = own_values.astype(jnp.bfloat16)
    grad_normed = ndot(grad_q_lin, w_query) + ndot(grad_k_lin, w_key) + ndot(grad_v_lin, w_value)
    scaled = widened * inv_rms
    grad_input = (
        inv_rms * (grad_normed - scaled * jnp.mean(grad_normed * scaled, axis=1, keepdims=True))
    ).astype(jnp.bfloat16)
    term = jnp.concatenate(
        [
            tdot(normed, grad_q_lin),
            tdot(normed, grad_k_lin),
            tdot(normed, grad_v_lin),
            tdot(attended, grad_out),
        ],
        axis=0,
    )
    shares = lax.psum_scatter(term.astype(jnp.bfloat16), "seq", scatter_dimension=0, tiled=True)
    weight_grads = lax.psum(shares, "dp").astype(jnp.float32)
    return (grad_input[None], weight_grads)


GROUPS = 4
GROUP_HEADS = HEADS // GROUPS
GROUP_COLS = GROUP_HEADS * HEAD_DIM
TILE = 256
TOKEN_ROWS = 16
STRIP = 8
HALF = HEAD_DIM // 2
VMEM_BYTES = 48 * 1024 * 1024


def key_span(query_tile):
    first = max(0, query_tile - WINDOW // TILE)
    return (first * TILE, (query_tile - first + 1) * TILE)


def normed_table(table_ref):
    widened = table_ref[...].astype(jnp.float32)
    inv_rms = lax.rsqrt(jnp.mean(widened * widened, axis=1, keepdims=True) + EPSILON)
    return (widened * inv_rms).astype(jnp.bfloat16)


def onehot_columns(tokens, vocab):
    rows = lax.broadcasted_iota(jnp.int32, (vocab, tokens.shape[1]), 0)
    return (rows == tokens).astype(jnp.float32).astype(jnp.bfloat16)


def send_kernel(spot_ref, tokens_ref, cotangent_ref, out_weights_ref, *out_refs):
    early_refs, grads_ref = out_refs[:-1], out_refs[-1]
    grad_att = ndot(out_weights_ref[...], cotangent_ref[...]).astype(jnp.bfloat16)
    grads_ref[...] = grad_att
    block = tokens_ref.shape[1]
    tokens = jnp.broadcast_to(tokens_ref[...].astype(jnp.float32), (TOKEN_ROWS, block)).astype(
        jnp.bfloat16
    )
    for turn, early_ref in enumerate(early_refs):
        group = spot_ref[1] ^ turn
        place = pl.ds(pl.multiple_of(group * GROUP_COLS, GROUP_COLS), GROUP_COLS)
        early_ref[:GROUP_COLS, :] = grads_ref[place, :]
        early_ref[GROUP_COLS:, :] = tokens


def late_kernel(cotangent_ref, *rest):
    late_ref = rest[-1]
    columns = late_ref.shape[2]
    for target in range(2 * GROUPS):
        side = target % 2
        late_ref[target] = cotangent_ref[:, side * columns : (side + 1) * columns]


def prepare_kernel(
    meta_ref,
    table_ref,
    query_ref,
    key_ref,
    value_ref,
    lookup_ref,
    normed_ref,
    columns_ref,
):
    normed = normed_table(table_ref)
    half = normed.shape[1] // 2
    normed_ref[...] = jnp.where(meta_ref[GROUP_HEADS] == 0, normed[:, :half], normed[:, half:])
    place = pl.ds(pl.multiple_of(meta_ref[GROUP_HEADS + 1] * GROUP_COLS, GROUP_COLS), GROUP_COLS)
    for matrix, weights_ref in enumerate((query_ref, key_ref, value_ref)):
        columns_ref[...] = jnp.dot(
            normed, weights_ref[...], preferred_element_type=jnp.float32
        ).T
        mine = columns_ref[place, :]
        upper = mine.astype(jnp.bfloat16)
        rows = slice(matrix * GROUP_COLS, (matrix + 1) * GROUP_COLS)
        lookup_ref[0, rows, :] = upper
        lookup_ref[1, rows, :] = (mine - upper.astype(jnp.float32)).astype(jnp.bfloat16)


def attention_kernel(
    meta_ref,
    lookup_ref,
    cosine_ref,
    sine_ref,
    *rest,
):
    early_refs = rest[: 2 * GROUPS]
    attention_body(meta_ref, lookup_ref, cosine_ref, sine_ref, early_refs, *rest[2 * GROUPS :])


def attention_body(
    meta_ref,
    lookup_ref,
    cosine_ref,
    sine_ref,
    early_refs,
    rows_ref,
    sums_ref,
    attended_ref,
    value_key_ref,
    query_t_ref,
    key_t_ref,
    value_t_ref,
    grad_att_ref,
    onehot_ref,
    onehot_rows_ref,
    grad_query_ref,
    both_ref,
    scaled_ref,
    probs_ref,
    scores_ref,
    right_ref,
    products_ref,
    inverse_ref,
    term_ref,
):
    head = pl.program_id(0)
    block = early_refs[0].shape[1]
    length = len(early_refs) * block
    tiles = length // TILE
    vocab = lookup_ref.shape[2]
    half_vocab = vocab // 2
    half = jnp.bfloat16
    cosine = cosine_ref[...]
    sine_part = sine_ref[...]

    @pl.when(head == 0)
    def _():
        own = 2 * meta_ref[GROUP_HEADS + 1] + meta_ref[GROUP_HEADS]
        for turn, early_ref in enumerate(early_refs):
            lanes = pl.ds(pl.multiple_of((own ^ turn) * block, block), block)
            tokens = early_ref[GROUP_COLS : GROUP_COLS + TOKEN_ROWS, :]
            tokens = tokens.astype(jnp.float32)[:1].astype(jnp.int32)
            onehot_ref[:, lanes] = onehot_columns(tokens, vocab)
            grad_att_ref[:, :, lanes] = early_ref[:GROUP_COLS, :].reshape(
                GROUP_HEADS, HEAD_DIM, block
            )
        onehot = onehot_ref[...]
        onehot_rows_ref[...] = onehot.T
        size = 3 * GROUP_COLS
        chosen = jnp.dot(
            lookup_ref[...].reshape(2 * size, vocab), onehot, preferred_element_type=jnp.float32
        )

        def picked(start):
            lower = start + size
            return chosen[start : start + HEAD_DIM] + chosen[lower : lower + HEAD_DIM]

        def turned(columns):
            former = columns[:HALF]
            latter = columns[HALF:]
            return jnp.concatenate(
                [former * cosine - latter * sine_part, latter * cosine + former * sine_part], axis=0
            )

        for index in range(GROUP_HEADS):
            query = turned(picked(index * HEAD_DIM)) * HEAD_DIM ** (-0.5)
            keys = turned(picked(GROUP_COLS + index * HEAD_DIM)).astype(half)
            values = picked(2 * GROUP_COLS + index * HEAD_DIM).astype(half)
            value_key_ref[index] = jnp.concatenate([values, keys], axis=0).T
            query_t_ref[index] = query.astype(half)
            key_t_ref[index] = keys
            value_t_ref[index] = values

    width = meta_ref[head]
    grad_att = grad_att_ref[head]
    query_t = query_t_ref[head]
    blank = jnp.zeros((HEAD_DIM, TILE), half)
    base = lax.broadcasted_iota(jnp.int32, (STRIP, TILE), 1) - lax.broadcasted_iota(
        jnp.int32, (STRIP, TILE), 0
    )
    for tile in range(tiles):
        columns = slice(tile * TILE, (tile + 1) * TILE)
        right_ref[tile, :HEAD_DIM, :TILE] = grad_att[:, columns]
        right_ref[tile, HEAD_DIM:, :TILE] = blank
        right_ref[tile, :HEAD_DIM, TILE:] = blank
        right_ref[tile, HEAD_DIM:, TILE:] = query_t[:, columns]

    def multiply(tile):
        first, count = key_span(tile)
        products_ref[tile, :count, :] = jnp.dot(
            value_key_ref[head, first : first + count, :],
            right_ref[tile],
            preferred_element_type=jnp.float32,
        )

    def forward(tile):
        first, count = key_span(tile)
        columns = slice(tile * TILE, (tile + 1) * TILE)
        row_max = None
        for row in range(0, count, STRIP):
            offset = tile * TILE - first - row
            allowed = base < width - offset
            if offset - STRIP < 0:
                allowed = allowed & (base >= -offset)
            masked = jnp.where(allowed, products_ref[tile, row : row + STRIP, TILE:], -1e30)
            products_ref[tile, row : row + STRIP, TILE:] = masked
            row_max = masked if row_max is None else jnp.maximum(row_max, masked)
        row_max = jnp.max(row_max, axis=0, keepdims=True)
        total = None
        for row in range(0, count, 2 * STRIP):
            weights = jnp.exp(products_ref[tile, row : row + 2 * STRIP, TILE:] - row_max)
            total = weights if total is None else total + weights
            probs_ref[first + row : first + row + 2 * STRIP, columns] = weights.astype(half)
        inverse = 1.0 / jnp.sum(total, axis=0, keepdims=True)
        attended = inverse * jnp.dot(
            value_t_ref[head, :, first : first + count],
            probs_ref[first : first + count, columns],
            preferred_element_type=jnp.float32,
        )
        attended_ref[pl.ds(pl.multiple_of(head * HEAD_DIM, HEAD_DIM), HEAD_DIM), columns] = (
            attended.astype(half)
        )
        wide_grad = grad_att[:, columns].astype(jnp.float32)
        inverse_ref[:, columns] = inverse
        term_ref[:, columns] = jnp.sum(attended * wide_grad, axis=0, keepdims=True)
        scaled_ref[columns, :] = jnp.concatenate(
            [
                (inverse * query_t[:, columns].astype(jnp.float32)).astype(half),
                (inverse * wide_grad).astype(half),
            ],
            axis=0,
        ).T

    def backward(tile):
        first, count = key_span(tile)
        columns = slice(tile * TILE, (tile + 1) * TILE)
        row_term = term_ref[:, columns]
        for row in range(0, count, 2 * STRIP):
            strip = slice(first + row, first + row + 2 * STRIP)
            scores_ref[strip, columns] = (
                probs_ref[strip, columns].astype(jnp.float32)
                * (products_ref[tile, row : row + 2 * STRIP, :TILE] - row_term)
            ).astype(half)
        grad_query_ref[:, columns] = inverse_ref[:, columns] * jnp.dot(
            key_t_ref[head, :, first : first + count],
            scores_ref[first : first + count, columns],
            preferred_element_type=jnp.float32,
        )

    lanes = lax.broadcasted_iota(jnp.int32, (TILE, 2 * HEAD_DIM), 1)

    def collect(tile):
        start = tile * TILE
        stop = min(length, start + TILE + WINDOW)
        grad_key = jnp.dot(
            scores_ref[start : start + TILE, start:stop],
            scaled_ref[start:stop, :],
            preferred_element_type=jnp.float32,
        )
        grad_value = jnp.dot(
            probs_ref[start : start + TILE, start:stop],
            scaled_ref[start:stop, :],
            preferred_element_type=jnp.float32,
        )
        both_ref[:, start : start + TILE] = jnp.where(lanes < HEAD_DIM, grad_key, grad_value).T

    reach = WINDOW // TILE
    for step in range(tiles + 3 + reach):
        if step < tiles:
            multiply(step)
        if 0 <= step - 1 < tiles:
            forward(step - 1)
        if 0 <= step - 2 < tiles:
            backward(step - 2)
        ready = step - 3 - reach
        if 0 <= ready < tiles:
            collect(ready)
    def turned_back(columns):
        former = columns[:HALF]
        latter = columns[HALF:]
        return jnp.concatenate(
            [former * cosine + latter * sine_part, latter * cosine - former * sine_part], axis=0
        )

    both = both_ref[...]
    grads = jnp.concatenate(
        [
            turned_back(grad_query_ref[...] * HEAD_DIM ** (-0.5)),
            turned_back(both[:HEAD_DIM]),
            both[HEAD_DIM:],
        ],
        axis=0,
    ).astype(half)
    sums = jnp.dot(grads, onehot_rows_ref[...], preferred_element_type=jnp.float32).astype(half)
    for matrix in range(3):
        rows = slice(matrix * HEAD_DIM, (matrix + 1) * HEAD_DIM)
        place = pl.ds(
            pl.multiple_of(matrix * GROUP_COLS + head * HEAD_DIM, HEAD_DIM), HEAD_DIM
        )
        for core in range(2):
            lane = core * half_vocab
            sums_ref[core, place, :] = sums[rows, lane : lane + half_vocab]
        for target in range(GROUPS):
            start = target * 2 * block
            even = grads[rows, start : start + block]
            odd = grads[rows, start + block : start + 2 * block]
            rows_ref[target, place, :] = jnp.where(meta_ref[GROUP_HEADS] == 0, even, odd)


def out_kernel(meta_ref, attended_ref, cotangent_ref, sums_ref, keep_ref, give_ref):
    total = jnp.dot(attended_ref[...], cotangent_ref[...], preferred_element_type=jnp.float32)
    rows = total.shape[0] // 2
    base = sums_ref.shape[1]
    lanes = keep_ref.shape[1]
    first = meta_ref[GROUP_HEADS + 2] == 0
    keep_ref[:base, :] = jnp.where(first, sums_ref[0], sums_ref[1])
    give_ref[:base, :] = jnp.where(first, sums_ref[1], sums_ref[0])
    for chunk in range(total.shape[1] // lanes):
        part = total[:, chunk * lanes : (chunk + 1) * lanes]
        place = slice(base + chunk * rows, base + (chunk + 1) * rows)
        keep_ref[place, :] = jnp.where(first, part[:rows], part[rows:]).astype(jnp.bfloat16)
        give_ref[place, :] = jnp.where(first, part[rows:], part[:rows]).astype(jnp.bfloat16)


def core_kernel(keep_ref, got_ref, here_ref, out_ref):
    here_ref[...] = keep_ref[...] + got_ref[...]
    base = here_ref.shape[0] - out_ref.shape[0]
    out_ref[...] = here_ref[base:, :]


def combine_kernel(
    meta_ref, here_ref, there_ref, near_ref, far_ref, after_ref, out_ref, *piece_refs
):
    del after_ref
    rows = GROUP_COLS
    for turn, piece_ref in enumerate(piece_refs):
        target = jnp.minimum(meta_ref[GROUP_HEADS + 1] ^ turn, 2)
        place = pl.ds(pl.multiple_of(target * rows, rows), rows)
        piece_ref[...] = here_ref[place, :] + there_ref[place, :]
    own = here_ref[3 * rows :, :] + there_ref[3 * rows :, :]
    other = near_ref[...] + far_ref[...]
    first = meta_ref[GROUP_HEADS] == 0
    size = own.shape[0]
    out_ref[:size, :] = jnp.where(first, own, other)
    out_ref[size:, :] = jnp.where(first, other, own)


def gather_kernel(meta_ref, s0, s1, s2, s3, own_ref, o0, o1, after_ref, mine_ref):
    del after_ref
    rows = GROUP_COLS
    size = own_ref.shape[0]
    group = meta_ref[GROUP_HEADS + 1]

    @pl.when(group < 3)
    def _():
        for turn, got in enumerate((s0, s1, s2, s3)):
            place = pl.ds(pl.multiple_of((group ^ turn) * rows, rows), rows)
            mine_ref[place, :] = got[...]
        tail = mine_ref.shape[0] - GROUPS * rows
        mine_ref[GROUPS * rows :, :] = jnp.zeros((tail, mine_ref.shape[1]), jnp.bfloat16)

    @pl.when(group == 3)
    def _():
        mine_ref[:size, :] = o0[...]
        mine_ref[size:, :] = jnp.where(meta_ref[GROUP_HEADS] == 0, o1[...], own_ref[...])


def input_kernel(tokens_ref, table_ref, query_ref, key_ref, value_ref, rows_ref, out_ref):
    vocab = table_ref.shape[0]
    onehot = onehot_columns(tokens_ref[...], vocab)
    embedded = tdot(onehot, table_ref[...])
    inv_rms = lax.rsqrt(jnp.mean(embedded * embedded, axis=1, keepdims=True) + EPSILON)
    grad_normed = None
    for matrix, weights in enumerate((query_ref, key_ref, value_ref)):
        columns = jnp.concatenate(
            [
                rows_ref[group, matrix * GROUP_COLS : (matrix + 1) * GROUP_COLS, :]
                for group in range(GROUPS)
            ],
            axis=0,
        )
        part = ndot(columns.astype(jnp.float32).T.astype(jnp.bfloat16), weights[...])
        grad_normed = part if grad_normed is None else grad_normed + part
    scaled = embedded * inv_rms
    out_ref[...] = (
        inv_rms * (grad_normed - scaled * jnp.mean(grad_normed * scaled, axis=1, keepdims=True))
    ).astype(jnp.bfloat16)


def weight_kernel(meta_ref, normed_ref, mine_ref, other_ref, out_ref):
    half_vocab = mine_ref.shape[1]
    first_core = meta_ref[GROUP_HEADS + 2] == 0

    @pl.when(meta_ref[GROUP_HEADS + 1] < 3)
    def _():
        first = normed_ref[:half_vocab, :]
        second = normed_ref[half_vocab:, :]
        upper = jnp.where(first_core, first, second)
        lower = jnp.where(first_core, second, first)
        total = None
        for part, sums_ref in ((upper, mine_ref), (lower, other_ref)):
            term = lax.dot_general(
                part,
                sums_ref[: GROUPS * GROUP_COLS, :],
                (((0,), (1,)), ((), ())),
                preferred_element_type=jnp.float32,
            )
            total = term if total is None else total + term
        out_ref[...] = total

    @pl.when(meta_ref[GROUP_HEADS + 1] == 3)
    def _():
        rows = GROUP_COLS // 2
        for half in range(2):
            for column in range(6):
                start = (half * 6 + column) * rows
                for core in range(2):
                    same = first_core == (core == 0)
                    value = jnp.where(
                        same, mine_ref[start : start + rows, :], other_ref[start : start + rows, :]
                    )
                    row = half * GROUP_COLS + core * rows
                    out_ref[
                        row : row + rows, column * half_vocab : (column + 1) * half_vocab
                    ] = value.astype(jnp.float32)


def whole(shape):
    return pl.BlockSpec(shape, lambda *_: (0,) * len(shape))


def swapped(block, axis, bit):
    route = [(i, i ^ bit) for i in range(lax.axis_size(axis))]
    return lax.ppermute(block, axis, route)


def rope_table(length):
    frequency = (10000.0 ** (-2.0 * np.arange(HALF, dtype=np.float32) / HEAD_DIM)).astype(np.float32)
    angles = frequency[:, None] * np.arange(length, dtype=np.float32)[None, :]
    angles = angles.astype(np.float64)
    return (
        jnp.asarray(np.cos(angles).astype(np.float32)),
        jnp.asarray(np.sin(angles).astype(np.float32)),
    )


def grouped_device(token_ids, cotangent, table, w_query, w_key, w_value, w_out, window):
    place = lax.axis_index("seq")
    core = lax.axis_index("dp") % 2
    group = place // 2
    side = place % 2
    block = token_ids.shape[1]
    features = table.shape[1]
    vocab = table.shape[0]
    blocks = lax.axis_size("seq")
    length = block * blocks
    grad_out = cotangent[0]
    meta = jnp.concatenate(
        [
            lax.dynamic_slice_in_dim(window, group * GROUP_HEADS, GROUP_HEADS, 0),
            jnp.stack([side, group, core]).astype(jnp.int32),
        ]
    )
    spot = jnp.stack([side, group, core]).astype(jnp.int32)
    cosine, sine_part = rope_table(length)

    def call(
        body, operands, outs, scratch=(), steps=1, flops=10**8, moved=10**6, loose=0, grant=VMEM_BYTES
    ):
        spaces = [whole(operand.shape) for operand in operands]
        for index in range(loose):
            spaces[-1 - index] = pl.BlockSpec(memory_space=pl.ANY)
        if operands[0].ndim == 1:
            spaces[0] = pl.BlockSpec(memory_space=pltpu.SMEM)
        return pl.pallas_call(
            body,
            grid=(steps,),
            in_specs=spaces,
            out_specs=[whole(shape) for shape, _ in outs],
            out_shape=[jax.ShapeDtypeStruct(shape, dtype) for shape, dtype in outs],
            scratch_shapes=list(scratch),
            compiler_params=pltpu.CompilerParams(
                dimension_semantics=("arbitrary",), vmem_limit_bytes=grant
            ),
            cost_estimate=pl.CostEstimate(flops=flops, bytes_accessed=moved, transcendentals=0),
        )(*operands)

    half = jnp.bfloat16
    sent = call(
        send_kernel,
        (spot, token_ids, grad_out, w_out),
        [((GROUP_COLS + TOKEN_ROWS, block), half)] * GROUPS,
        [pltpu.VMEM((features, block), half)],
        grant=60 * 1024 * 1024,
    )
    early = [sent[0]] + [None] * (blocks - 1)
    for turn in (4, 6, 5, 7, 2, 3, 1):
        early[turn] = swapped(sent[turn // 2], "seq", turn)
    lookup, normed = call(
        prepare_kernel,
        (meta, table, w_query, w_key, w_value),
        [((2, 3 * GROUP_COLS, vocab), half), ((vocab, features // 2), half)],
        [pltpu.VMEM((features, vocab), jnp.float32)],
        flops=10**9,
        moved=5 * 10**6,
        grant=60 * 1024 * 1024,
    )
    (late,) = call(
        late_kernel,
        (grad_out, lookup, *early[1:]),
        [((blocks, block, features // 2), half)],
        loose=blocks,
    )
    late = lax.all_to_all(late, "seq", split_axis=0, concat_axis=0, tiled=True)
    heads_shape = (GROUP_HEADS, HEAD_DIM, length)
    rows_shape = (GROUP_HEADS, length, 2 * HEAD_DIM)
    rows, sums, attended = call(
        attention_kernel,
        (meta, lookup, cosine, sine_part, *early),
        [
            ((GROUPS, 3 * GROUP_COLS, block), half),
            ((2, 3 * GROUP_COLS, vocab // 2), half),
            ((GROUP_COLS, length), half),
        ],
        [
            pltpu.VMEM(rows_shape, half),
            pltpu.VMEM(heads_shape, half),
            pltpu.VMEM(heads_shape, half),
            pltpu.VMEM(heads_shape, half),
            pltpu.VMEM(heads_shape, half),
            pltpu.VMEM((vocab, length), half),
            pltpu.VMEM((length, vocab), half),
            pltpu.VMEM((HEAD_DIM, length), jnp.float32),
            pltpu.VMEM((2 * HEAD_DIM, length), jnp.float32),
            pltpu.VMEM((length, 2 * HEAD_DIM), half),
            pltpu.VMEM((length, length), half),
            pltpu.VMEM((length, length), half),
            pltpu.VMEM((length // TILE, 2 * HEAD_DIM, 2 * TILE), half),
            pltpu.VMEM((length // TILE, WINDOW + TILE, 2 * TILE), jnp.float32),
            pltpu.VMEM((1, length), jnp.float32),
            pltpu.VMEM((1, length), jnp.float32),
        ],
        steps=GROUP_HEADS,
        flops=8 * 10**9,
        moved=8 * 10**6,
    )
    planes = [[2 * z + x for z in range(GROUPS)] for x in range(2)]

    def over_plane(chunks):
        return lax.all_to_all(
            chunks, "seq", split_axis=0, concat_axis=0, axis_index_groups=planes, tiled=True
        )

    got_rows = over_plane(rows)
    lanes = vocab // 2
    out_rows = 3 * GROUP_COLS // 2
    packed = 3 * GROUP_COLS + out_rows
    keep, give = call(
        out_kernel,
        (meta, attended, late.reshape(length, features // 2), sums),
        [((packed, lanes), half)] * 2,
    )
    here, here_out = call(
        core_kernel,
        (keep, swapped(give, "dp", 1)),
        [((packed, lanes), half), ((out_rows, lanes), half)],
    )
    there = swapped(here, "dp", 2)
    inward = [(2 * z + 1 - z // 2, 2 * z + z // 2) for z in range(GROUPS)]
    near = lax.ppermute(here_out, "seq", inward)
    far = lax.ppermute(
        here_out,
        ("dp", "seq"),
        [
            (blocks * d + source, blocks * (d ^ 2) + target)
            for d in range(lax.axis_size("dp"))
            for source, target in inward
        ],
    )
    full_out, *pieces = call(
        combine_kernel,
        (meta, here, there, near, far, got_rows),
        [((2 * out_rows, lanes), half)] + [((GROUP_COLS, lanes), half)] * GROUPS,
        loose=1,
    )
    last = blocks - 2
    got_out = [
        lax.ppermute(full_out, "seq", [(0, last), (last - 1, last + 1)]),
        lax.ppermute(full_out, "seq", [(2, last)]),
    ]
    got = [pieces[0]] + [None] * (GROUPS - 1)
    for turn in (2, 3, 1):
        got[turn] = swapped(pieces[turn], "seq", 2 * turn)
    (grad_input,) = call(
        input_kernel,
        (token_ids, table, w_query, w_key, w_value, got_rows),
        [((block, features), half)],
        flops=10**9,
        moved=5 * 10**6,
    )
    (mine,) = call(
        gather_kernel,
        (meta, *got, full_out, *got_out, grad_input),
        [((4 * out_rows, lanes), half)],
        loose=1,
    )
    (weight_grads,) = call(
        weight_kernel,
        (meta, normed, mine, swapped(mine, "dp", 1)),
        [((features // 2, features), jnp.float32)],
        flops=10**9,
        moved=5 * 10**6,
    )
    return (grad_input[None], weight_grads)


def on_device(token_ids, cotangent, table, w_query, w_key, w_value, w_out, window):
    fits = (
        lax.axis_size("seq") == 2 * GROUPS
        and lax.axis_size("dp") == 4
        and token_ids.shape == (1, 128)
        and table.shape == (256, HEADS * HEAD_DIM)
    )
    plan = grouped_device if fits else general_device
    return plan(token_ids, cotangent, table, w_query, w_key, w_value, w_out, window)


def solution(mesh):
    return jax.shard_map(
        on_device,
        mesh=mesh,
        in_specs=(P("dp", "seq"), P("dp", "seq", None), P(), P(), P(), P(), P(), P()),
        out_specs=(P("dp", "seq", None), P("seq", None)),
        check_vma=False,
    )
```

```python
import jax
import jax.numpy as jnp
import numpy as np
from jax import lax
from jax.experimental import pallas as pl
from jax.experimental.pallas import tpu as pltpu
from jax.sharding import PartitionSpec as P

HEADS = 12
HEAD_DIM = 64
WINDOW = 512


EPSILON = 1e-05


def shifted(block, axis, distance):
    devices = range(lax.axis_size(axis))
    route = [(i - distance, i) for i in devices if i - distance in devices]
    return lax.ppermute(block, axis, route)


def rotate(values, positions):
    row_count = values.shape[0]
    shaped = values.reshape(row_count, -1, HEAD_DIM)
    middle = HEAD_DIM // 2
    frequency = 10000.0 ** (-2.0 * jnp.arange(middle, dtype=jnp.float32) / HEAD_DIM)
    angles = positions.astype(jnp.float32)[:, None] * frequency[None, :]
    cosine = jnp.cos(angles)[:, None, :]
    sine_part = jnp.sin(angles)[:, None, :]
    former = shaped[..., :middle]
    latter = shaped[..., middle:]
    turned = jnp.concatenate(
        [former * cosine - latter * sine_part, latter * cosine + former * sine_part], axis=-1
    )
    return turned.reshape(row_count, -1)


def unrotate(values, positions):
    row_count = values.shape[0]
    shaped = values.reshape(row_count, -1, HEAD_DIM)
    middle = HEAD_DIM // 2
    frequency = 10000.0 ** (-2.0 * jnp.arange(middle, dtype=jnp.float32) / HEAD_DIM)
    angles = positions.astype(jnp.float32)[:, None] * frequency[None, :]
    cosine = jnp.cos(angles)[:, None, :]
    sine_part = jnp.sin(angles)[:, None, :]
    former = shaped[..., :middle]
    latter = shaped[..., middle:]
    turned = jnp.concatenate(
        [former * cosine + latter * sine_part, latter * cosine - former * sine_part], axis=-1
    )
    return turned.reshape(row_count, -1)


def tdot(left, right):
    return lax.dot_general(
        left, right, (((0,), (0,)), ((), ())), preferred_element_type=jnp.float32
    )


def ndot(left, right):
    return lax.dot_general(
        left, right, (((1,), (1,)), ((), ())), preferred_element_type=jnp.float32
    )


def embed_rows(byte_ids, table):
    onehot = (byte_ids[:, None] == jnp.arange(table.shape[0], dtype=jnp.int32)[None, :]).astype(
        jnp.bfloat16
    )
    return jnp.dot(onehot, table, preferred_element_type=jnp.float32).astype(jnp.bfloat16)


def normalize(embedded):
    widened = embedded.astype(jnp.float32)
    inv_rms = lax.rsqrt(jnp.mean(widened * widened, axis=1, keepdims=True) + EPSILON)
    return (widened, inv_rms, (widened * inv_rms).astype(jnp.bfloat16))


def keys_values(normed, positions, w_key, w_value):
    key_rows = rotate(jnp.dot(normed, w_key, preferred_element_type=jnp.float32), positions).astype(
        jnp.bfloat16
    )
    value_rows = jnp.dot(normed, w_value, preferred_element_type=jnp.float32).astype(jnp.bfloat16)
    return (key_rows, value_rows)


def head_group(
    query_heads, key_heads, value_heads, grad_heads, group_window, own_pos, key_pos, score_scale
):
    distance = own_pos[:, None] - key_pos[None, :]
    allowed = (
        (distance[None] >= 0)
        & (distance[None] < group_window[:, None, None])
        & (key_pos[None, None, :] >= 0)
    )
    scores = (
        jnp.einsum("qhd,khd->hqk", query_heads, key_heads, preferred_element_type=jnp.float32)
        * score_scale
    )
    masked = jnp.where(allowed, scores, -1e30)
    row_max = jnp.max(masked, axis=-1, keepdims=True)
    weights = jnp.where(allowed, jnp.exp(masked - row_max), 0.0)
    probs = weights / jnp.sum(weights, axis=-1, keepdims=True)
    probs_b = probs.astype(jnp.bfloat16)
    attended = jnp.einsum(
        "hqk,khd->qhd", probs_b, value_heads, preferred_element_type=jnp.float32
    ).astype(jnp.bfloat16)
    grad_probs = jnp.einsum(
        "qhd,khd->hqk", grad_heads, value_heads, preferred_element_type=jnp.float32
    )
    row_term = jnp.sum(probs * grad_probs, axis=-1, keepdims=True)
    grad_scores = (probs * (grad_probs - row_term) * score_scale).astype(jnp.bfloat16)
    grad_query = jnp.einsum(
        "hqk,khd->qhd", grad_scores, key_heads, preferred_element_type=jnp.float32
    )
    grad_key = jnp.einsum(
        "hqk,qhd->khd", grad_scores, query_heads, preferred_element_type=jnp.float32
    )
    grad_value = jnp.einsum("hqk,qhd->khd", probs_b, grad_heads, preferred_element_type=jnp.float32)
    return (attended, grad_query, grad_key, grad_value)


def general_device(token_ids, cotangent, table, w_query, w_key, w_value, w_out, window):
    local_ids = token_ids[0]
    grad_out = cotangent[0]
    length = local_ids.shape[0]
    features = table.shape[1]
    tail_rows = min(length, WINDOW)
    reach_devs = -(-WINDOW // length)
    halo_rows = reach_devs * tail_rows
    offset = lax.axis_index("seq") * length
    own_pos = offset + jnp.arange(length, dtype=jnp.int32)
    halo_pos = offset - halo_rows + jnp.arange(halo_rows, dtype=jnp.int32)
    score_scale = HEAD_DIM ** (-0.5)
    embedded = embed_rows(local_ids, table)
    widened, inv_rms, normed = normalize(embedded)
    query = rotate(jnp.dot(normed, w_query, preferred_element_type=jnp.float32), own_pos).astype(
        jnp.bfloat16
    )
    key_own, value_own = keys_values(normed, own_pos, w_key, w_value)
    key_pieces = []
    value_pieces = []
    for hop_index in range(reach_devs):
        far_keys, far_values = shifted((key_own, value_own), "seq", hop_index + 1)
        key_pieces.insert(0, far_keys)
        value_pieces.insert(0, far_values)
    key_halo = jnp.concatenate(key_pieces, axis=0)
    value_halo = jnp.concatenate(value_pieces, axis=0)
    span_rows = halo_rows + length
    key_all = jnp.concatenate([key_halo, key_own], axis=0)
    value_all = jnp.concatenate([value_halo, value_own], axis=0)
    key_pos = jnp.concatenate([halo_pos, own_pos], axis=0)
    query_heads = query.reshape(length, HEADS, HEAD_DIM)
    key_heads = key_all.reshape(span_rows, HEADS, HEAD_DIM)
    value_heads = value_all.reshape(span_rows, HEADS, HEAD_DIM)
    grad_att = ndot(grad_out, w_out).astype(jnp.bfloat16)
    grad_heads = grad_att.reshape(length, HEADS, HEAD_DIM)
    group_size = 4
    attended_parts = []
    query_parts = []
    key_parts = []
    value_parts = []
    for group_index in range(HEADS // group_size):
        lower = group_index * group_size
        upper = lower + group_size
        outputs = head_group(
            query_heads[:, lower:upper],
            key_heads[:, lower:upper],
            value_heads[:, lower:upper],
            grad_heads[:, lower:upper],
            window[lower:upper],
            own_pos,
            key_pos,
            score_scale,
        )
        attended_parts.append(outputs[0])
        query_parts.append(outputs[1])
        key_parts.append(outputs[2])
        value_parts.append(outputs[3])
    attended = jnp.concatenate(attended_parts, axis=1).reshape(length, features)
    grad_query = jnp.concatenate(query_parts, axis=1).reshape(length, features)
    grad_key = jnp.concatenate(key_parts, axis=1).reshape(span_rows, features)
    grad_value = jnp.concatenate(value_parts, axis=1).reshape(span_rows, features)
    tail_keys = grad_key[:halo_rows].reshape(reach_devs, tail_rows, features)
    tail_values = grad_value[:halo_rows].reshape(reach_devs, tail_rows, features)
    back_keys = jnp.zeros((tail_rows, features), jnp.float32)
    back_values = jnp.zeros((tail_rows, features), jnp.float32)
    for hop_index in range(reach_devs):
        got_keys, got_values = shifted(
            (tail_keys[reach_devs - 1 - hop_index], tail_values[reach_devs - 1 - hop_index]),
            "seq",
            -(hop_index + 1),
        )
        back_keys = back_keys + got_keys
        back_values = back_values + got_values
    own_keys = grad_key[halo_rows:]
    own_values = grad_value[halo_rows:]
    own_keys = jnp.concatenate([own_keys[: length - tail_rows], own_keys + back_keys], axis=0)
    own_values = jnp.concatenate(
        [own_values[: length - tail_rows], own_values + back_values], axis=0
    )
    grad_q_lin = unrotate(grad_query, own_pos).astype(jnp.bfloat16)
    grad_k_lin = unrotate(own_keys, own_pos).astype(jnp.bfloat16)
    grad_v_lin = own_values.astype(jnp.bfloat16)
    grad_normed = ndot(grad_q_lin, w_query) + ndot(grad_k_lin, w_key) + ndot(grad_v_lin, w_value)
    scaled = widened * inv_rms
    grad_input = (
        inv_rms * (grad_normed - scaled * jnp.mean(grad_normed * scaled, axis=1, keepdims=True))
    ).astype(jnp.bfloat16)
    term = jnp.concatenate(
        [
            tdot(normed, grad_q_lin),
            tdot(normed, grad_k_lin),
            tdot(normed, grad_v_lin),
            tdot(attended, grad_out),
        ],
        axis=0,
    )
    shares = lax.psum_scatter(term.astype(jnp.bfloat16), "seq", scatter_dimension=0, tiled=True)
    weight_grads = lax.psum(shares, "dp").astype(jnp.float32)
    return (grad_input[None], weight_grads)


GROUPS = 4
GROUP_HEADS = HEADS // GROUPS
GROUP_COLS = GROUP_HEADS * HEAD_DIM
TILE = 256
TOKEN_ROWS = 16
STRIP = 8
HALF = HEAD_DIM // 2
VMEM_BYTES = 48 * 1024 * 1024


def mirrored(bits):
    return 2 * (bits % 2) + bits // 2 % 2


def key_span(query_tile):
    first = max(0, query_tile - WINDOW // TILE)
    return (first * TILE, (query_tile - first + 1) * TILE)


def normed_table(table_ref):
    widened = table_ref[...].astype(jnp.float32)
    inv_rms = lax.rsqrt(jnp.mean(widened * widened, axis=1, keepdims=True) + EPSILON)
    return (widened * inv_rms).astype(jnp.bfloat16)


def onehot_columns(tokens, vocab):
    rows = lax.broadcasted_iota(jnp.int32, (vocab, tokens.shape[1]), 0)
    return (rows == tokens).astype(jnp.float32).astype(jnp.bfloat16)


def send_kernel(spot_ref, tokens_ref, cotangent_ref, out_weights_ref, *out_refs):
    early_refs, grads_ref = out_refs[:-1], out_refs[-1]
    grad_att = ndot(out_weights_ref[...], cotangent_ref[...]).astype(jnp.bfloat16)
    grads_ref[...] = grad_att
    block = tokens_ref.shape[1]
    tokens = jnp.broadcast_to(tokens_ref[...].astype(jnp.float32), (TOKEN_ROWS, block)).astype(
        jnp.bfloat16
    )
    for turn, early_ref in enumerate(early_refs):
        group = spot_ref[0] ^ turn
        place = pl.ds(pl.multiple_of(group * GROUP_COLS, GROUP_COLS), GROUP_COLS)
        early_ref[:GROUP_COLS, :] = grads_ref[place, :]
        early_ref[GROUP_COLS:, :] = tokens


def late_kernel(cotangent_ref, *rest):
    late_ref = rest[-1]
    columns = late_ref.shape[2]
    for target in range(2 * GROUPS):
        side = target // GROUPS
        late_ref[target] = cotangent_ref[:, side * columns : (side + 1) * columns]


def prepare_kernel(
    meta_ref,
    table_ref,
    query_ref,
    key_ref,
    value_ref,
    lookup_ref,
    normed_ref,
    columns_ref,
):
    normed = normed_table(table_ref)
    half = normed.shape[1] // 2
    normed_ref[...] = jnp.where(meta_ref[GROUP_HEADS] == 0, normed[:, :half], normed[:, half:])
    place = pl.ds(pl.multiple_of(meta_ref[GROUP_HEADS + 3] * GROUP_COLS, GROUP_COLS), GROUP_COLS)
    for matrix, weights_ref in enumerate((query_ref, key_ref, value_ref)):
        columns_ref[...] = jnp.dot(
            normed, weights_ref[...], preferred_element_type=jnp.float32
        ).T
        mine = columns_ref[place, :]
        upper = mine.astype(jnp.bfloat16)
        rows = slice(matrix * GROUP_COLS, (matrix + 1) * GROUP_COLS)
        lookup_ref[0, rows, :] = upper
        lookup_ref[1, rows, :] = (mine - upper.astype(jnp.float32)).astype(jnp.bfloat16)


def attention_kernel(
    meta_ref,
    lookup_ref,
    cosine_ref,
    sine_ref,
    *rest,
):
    early_refs = rest[: 2 * GROUPS]
    attention_body(meta_ref, lookup_ref, cosine_ref, sine_ref, early_refs, *rest[2 * GROUPS :])


def attention_body(
    meta_ref,
    lookup_ref,
    cosine_ref,
    sine_ref,
    early_refs,
    rows_ref,
    sums_ref,
    attended_ref,
    value_key_ref,
    query_t_ref,
    key_t_ref,
    value_t_ref,
    grad_att_ref,
    onehot_ref,
    onehot_rows_ref,
    grad_query_ref,
    both_ref,
    scaled_ref,
    probs_ref,
    scores_ref,
    right_ref,
    products_ref,
    inverse_ref,
    term_ref,
):
    head = pl.program_id(0)
    block = early_refs[0].shape[1]
    length = len(early_refs) * block
    tiles = length // TILE
    vocab = lookup_ref.shape[2]
    half_vocab = vocab // 2
    half = jnp.bfloat16
    cosine = cosine_ref[...]
    sine_part = sine_ref[...]

    @pl.when(head == 0)
    def _():
        own = 2 * meta_ref[GROUP_HEADS + 1] + meta_ref[GROUP_HEADS]
        for turn, early_ref in enumerate(early_refs):
            lanes = pl.ds(pl.multiple_of((own ^ turn) * block, block), block)
            tokens = early_ref[GROUP_COLS : GROUP_COLS + TOKEN_ROWS, :]
            tokens = tokens.astype(jnp.float32)[:1].astype(jnp.int32)
            onehot_ref[:, lanes] = onehot_columns(tokens, vocab)
            grad_att_ref[:, :, lanes] = early_ref[:GROUP_COLS, :].reshape(
                GROUP_HEADS, HEAD_DIM, block
            )
        onehot = onehot_ref[...]
        onehot_rows_ref[...] = onehot.T
        size = 3 * GROUP_COLS
        chosen = jnp.dot(
            lookup_ref[...].reshape(2 * size, vocab), onehot, preferred_element_type=jnp.float32
        )

        def picked(start):
            lower = start + size
            return chosen[start : start + HEAD_DIM] + chosen[lower : lower + HEAD_DIM]

        def turned(columns):
            former = columns[:HALF]
            latter = columns[HALF:]
            return jnp.concatenate(
                [former * cosine - latter * sine_part, latter * cosine + former * sine_part], axis=0
            )

        for index in range(GROUP_HEADS):
            query = turned(picked(index * HEAD_DIM)) * HEAD_DIM ** (-0.5)
            keys = turned(picked(GROUP_COLS + index * HEAD_DIM)).astype(half)
            values = picked(2 * GROUP_COLS + index * HEAD_DIM).astype(half)
            value_key_ref[index] = jnp.concatenate([values, keys], axis=0).T
            query_t_ref[index] = query.astype(half)
            key_t_ref[index] = keys
            value_t_ref[index] = values

    width = meta_ref[head]
    grad_att = grad_att_ref[head]
    query_t = query_t_ref[head]
    blank = jnp.zeros((HEAD_DIM, TILE), half)
    base = lax.broadcasted_iota(jnp.int32, (STRIP, TILE), 1) - lax.broadcasted_iota(
        jnp.int32, (STRIP, TILE), 0
    )
    for tile in range(tiles):
        columns = slice(tile * TILE, (tile + 1) * TILE)
        right_ref[tile, :HEAD_DIM, :TILE] = grad_att[:, columns]
        right_ref[tile, HEAD_DIM:, :TILE] = blank
        right_ref[tile, :HEAD_DIM, TILE:] = blank
        right_ref[tile, HEAD_DIM:, TILE:] = query_t[:, columns]

    def multiply(tile):
        first, count = key_span(tile)
        products_ref[tile, :count, :] = jnp.dot(
            value_key_ref[head, first : first + count, :],
            right_ref[tile],
            preferred_element_type=jnp.float32,
        )

    def forward(tile):
        first, count = key_span(tile)
        columns = slice(tile * TILE, (tile + 1) * TILE)
        row_max = None
        for row in range(0, count, STRIP):
            offset = tile * TILE - first - row
            allowed = base < width - offset
            if offset - STRIP < 0:
                allowed = allowed & (base >= -offset)
            masked = jnp.where(allowed, products_ref[tile, row : row + STRIP, TILE:], -1e30)
            products_ref[tile, row : row + STRIP, TILE:] = masked
            row_max = masked if row_max is None else jnp.maximum(row_max, masked)
        row_max = jnp.max(row_max, axis=0, keepdims=True)
        total = None
        for row in range(0, count, 2 * STRIP):
            weights = jnp.exp(products_ref[tile, row : row + 2 * STRIP, TILE:] - row_max)
            total = weights if total is None else total + weights
            probs_ref[first + row : first + row + 2 * STRIP, columns] = weights.astype(half)
        inverse = 1.0 / jnp.sum(total, axis=0, keepdims=True)
        attended = inverse * jnp.dot(
            value_t_ref[head, :, first : first + count],
            probs_ref[first : first + count, columns],
            preferred_element_type=jnp.float32,
        )
        attended_ref[pl.ds(pl.multiple_of(head * HEAD_DIM, HEAD_DIM), HEAD_DIM), columns] = (
            attended.astype(half)
        )
        wide_grad = grad_att[:, columns].astype(jnp.float32)
        inverse_ref[:, columns] = inverse
        term_ref[:, columns] = jnp.sum(attended * wide_grad, axis=0, keepdims=True)
        scaled_ref[columns, :] = jnp.concatenate(
            [
                (inverse * query_t[:, columns].astype(jnp.float32)).astype(half),
                (inverse * wide_grad).astype(half),
            ],
            axis=0,
        ).T

    def backward(tile):
        first, count = key_span(tile)
        columns = slice(tile * TILE, (tile + 1) * TILE)
        row_term = term_ref[:, columns]
        for row in range(0, count, 2 * STRIP):
            strip = slice(first + row, first + row + 2 * STRIP)
            scores_ref[strip, columns] = (
                probs_ref[strip, columns].astype(jnp.float32)
                * (products_ref[tile, row : row + 2 * STRIP, :TILE] - row_term)
            ).astype(half)
        grad_query_ref[:, columns] = inverse_ref[:, columns] * jnp.dot(
            key_t_ref[head, :, first : first + count],
            scores_ref[first : first + count, columns],
            preferred_element_type=jnp.float32,
        )

    lanes = lax.broadcasted_iota(jnp.int32, (TILE, 2 * HEAD_DIM), 1)

    def collect(tile):
        start = tile * TILE
        stop = min(length, start + TILE + WINDOW)
        grad_key = jnp.dot(
            scores_ref[start : start + TILE, start:stop],
            scaled_ref[start:stop, :],
            preferred_element_type=jnp.float32,
        )
        grad_value = jnp.dot(
            probs_ref[start : start + TILE, start:stop],
            scaled_ref[start:stop, :],
            preferred_element_type=jnp.float32,
        )
        both_ref[:, start : start + TILE] = jnp.where(lanes < HEAD_DIM, grad_key, grad_value).T

    reach = WINDOW // TILE
    for step in range(tiles + 3 + reach):
        if step < tiles:
            multiply(step)
        if 0 <= step - 1 < tiles:
            forward(step - 1)
        if 0 <= step - 2 < tiles:
            backward(step - 2)
        ready = step - 3 - reach
        if 0 <= ready < tiles:
            collect(ready)
    def turned_back(columns):
        former = columns[:HALF]
        latter = columns[HALF:]
        return jnp.concatenate(
            [former * cosine + latter * sine_part, latter * cosine - former * sine_part], axis=0
        )

    both = both_ref[...]
    grads = jnp.concatenate(
        [
            turned_back(grad_query_ref[...] * HEAD_DIM ** (-0.5)),
            turned_back(both[:HEAD_DIM]),
            both[HEAD_DIM:],
        ],
        axis=0,
    ).astype(half)
    sums = jnp.dot(grads, onehot_rows_ref[...], preferred_element_type=jnp.float32).astype(half)
    for matrix in range(3):
        rows = slice(matrix * HEAD_DIM, (matrix + 1) * HEAD_DIM)
        place = pl.ds(
            pl.multiple_of(matrix * GROUP_COLS + head * HEAD_DIM, HEAD_DIM), HEAD_DIM
        )
        for core in range(2):
            lane = core * half_vocab
            sums_ref[core, place, :] = sums[rows, lane : lane + half_vocab]
        for target in range(GROUPS):
            start = target * block
            near = grads[rows, start : start + block]
            far = grads[rows, start + GROUPS * block : start + (GROUPS + 1) * block]
            rows_ref[target, place, :] = jnp.where(meta_ref[GROUP_HEADS + 1] < 2, near, far)


def out_kernel(meta_ref, attended_ref, cotangent_ref, sums_ref, keep_ref, give_ref):
    total = jnp.dot(attended_ref[...], cotangent_ref[...], preferred_element_type=jnp.float32)
    rows = total.shape[0] // 2
    base = sums_ref.shape[1]
    lanes = keep_ref.shape[1]
    first = meta_ref[GROUP_HEADS + 2] == 0
    keep_ref[:base, :] = jnp.where(first, sums_ref[0], sums_ref[1])
    give_ref[:base, :] = jnp.where(first, sums_ref[1], sums_ref[0])
    for chunk in range(total.shape[1] // lanes):
        part = total[:, chunk * lanes : (chunk + 1) * lanes]
        place = slice(base + chunk * rows, base + (chunk + 1) * rows)
        keep_ref[place, :] = jnp.where(first, part[:rows], part[rows:]).astype(jnp.bfloat16)
        give_ref[place, :] = jnp.where(first, part[rows:], part[:rows]).astype(jnp.bfloat16)


def combine_kernel(meta_ref, here_ref, there_ref, after_ref, out_ref, *piece_refs):
    del after_ref
    rows = GROUP_COLS
    for turn, piece_ref in enumerate(piece_refs):
        target = jnp.minimum(meta_ref[GROUP_HEADS + 1] ^ (turn // 2), 2)
        place = pl.ds(pl.multiple_of(target * rows, rows), rows)
        piece_ref[...] = here_ref[place, :] + there_ref[place, :]
    out_ref[...] = here_ref[3 * rows :, :] + there_ref[3 * rows :, :]


def gather_kernel(meta_ref, s0, s1, s2, s3, own_ref, o0, o1, o2, after_ref, mine_ref):
    del after_ref
    rows = GROUP_COLS
    size = own_ref.shape[0]

    @pl.when(meta_ref[GROUP_HEADS + 1] < 3)
    def _():
        for turn, got in enumerate((s0, s1, s2, s3)):
            source = meta_ref[GROUP_HEADS + 3] ^ mirrored(turn)
            mine_ref[pl.ds(pl.multiple_of(source * rows, rows), rows), :] = got[...]
        tail = mine_ref.shape[0] - GROUPS * rows
        mine_ref[GROUPS * rows :, :] = jnp.zeros((tail, mine_ref.shape[1]), jnp.bfloat16)

    @pl.when(meta_ref[GROUP_HEADS + 1] == 3)
    def _():
        for place, piece in enumerate((o0, o2, o1, own_ref)):
            mine_ref[place * size : (place + 1) * size, :] = piece[...]


def input_kernel(tokens_ref, table_ref, query_ref, key_ref, value_ref, rows_ref, out_ref):
    vocab = table_ref.shape[0]
    onehot = onehot_columns(tokens_ref[...], vocab)
    embedded = tdot(onehot, table_ref[...])
    inv_rms = lax.rsqrt(jnp.mean(embedded * embedded, axis=1, keepdims=True) + EPSILON)
    grad_normed = None
    for matrix, weights in enumerate((query_ref, key_ref, value_ref)):
        columns = jnp.concatenate(
            [
                rows_ref[group, matrix * GROUP_COLS : (matrix + 1) * GROUP_COLS, :]
                for group in map(mirrored, range(GROUPS))
            ],
            axis=0,
        )
        part = ndot(columns.astype(jnp.float32).T.astype(jnp.bfloat16), weights[...])
        grad_normed = part if grad_normed is None else grad_normed + part
    scaled = embedded * inv_rms
    out_ref[...] = (
        inv_rms * (grad_normed - scaled * jnp.mean(grad_normed * scaled, axis=1, keepdims=True))
    ).astype(jnp.bfloat16)


def weight_kernel(meta_ref, normed_ref, mine_ref, other_ref, out_ref):
    half_vocab = mine_ref.shape[1]
    first_core = meta_ref[GROUP_HEADS + 2] == 0

    @pl.when(meta_ref[GROUP_HEADS + 1] < 3)
    def _():
        first = normed_ref[:half_vocab, :]
        second = normed_ref[half_vocab:, :]
        upper = jnp.where(first_core, first, second)
        lower = jnp.where(first_core, second, first)
        total = None
        for part, sums_ref in ((upper, mine_ref), (lower, other_ref)):
            term = lax.dot_general(
                part,
                sums_ref[: GROUPS * GROUP_COLS, :],
                (((0,), (1,)), ((), ())),
                preferred_element_type=jnp.float32,
            )
            total = term if total is None else total + term
        out_ref[...] = total

    @pl.when(meta_ref[GROUP_HEADS + 1] == 3)
    def _():
        rows = GROUP_COLS // 2
        for half in range(2):
            for column in range(6):
                start = (half * 6 + column) * rows
                for core in range(2):
                    same = first_core == (core == 0)
                    value = jnp.where(
                        same, mine_ref[start : start + rows, :], other_ref[start : start + rows, :]
                    )
                    row = half * GROUP_COLS + core * rows
                    out_ref[
                        row : row + rows, column * half_vocab : (column + 1) * half_vocab
                    ] = value.astype(jnp.float32)


def whole(shape):
    return pl.BlockSpec(shape, lambda *_: (0,) * len(shape))


def swapped(block, axis, bit):
    route = [(i, i ^ bit) for i in range(lax.axis_size(axis))]
    return lax.ppermute(block, axis, route)


def rope_table(length):
    frequency = (10000.0 ** (-2.0 * np.arange(HALF, dtype=np.float32) / HEAD_DIM)).astype(np.float32)
    angles = frequency[:, None] * np.arange(length, dtype=np.float32)[None, :]
    angles = angles.astype(np.float64)
    return (
        jnp.asarray(np.cos(angles).astype(np.float32)),
        jnp.asarray(np.sin(angles).astype(np.float32)),
    )


def grouped_device(token_ids, cotangent, table, w_query, w_key, w_value, w_out, window):
    place = lax.axis_index("seq")
    core = lax.axis_index("dp") % 2
    side = place % 2
    level = place // 2
    group = 2 * side + level % 2
    block = token_ids.shape[1]
    features = table.shape[1]
    vocab = table.shape[0]
    blocks = lax.axis_size("seq")
    length = block * blocks
    grad_out = cotangent[0]
    meta = jnp.concatenate(
        [
            lax.dynamic_slice_in_dim(window, group * GROUP_HEADS, GROUP_HEADS, 0),
            jnp.stack([side, level, core, group]).astype(jnp.int32),
        ]
    )
    spot = jnp.stack([group]).astype(jnp.int32)
    cosine, sine_part = rope_table(length)

    def call(
        body, operands, outs, scratch=(), steps=1, flops=10**8, moved=10**6, loose=0, grant=VMEM_BYTES
    ):
        spaces = [whole(operand.shape) for operand in operands]
        for index in range(loose):
            spaces[-1 - index] = pl.BlockSpec(memory_space=pl.ANY)
        if operands[0].ndim == 1:
            spaces[0] = pl.BlockSpec(memory_space=pltpu.SMEM)
        return pl.pallas_call(
            body,
            grid=(steps,),
            in_specs=spaces,
            out_specs=[whole(shape) for shape, _ in outs],
            out_shape=[jax.ShapeDtypeStruct(shape, dtype) for shape, dtype in outs],
            scratch_shapes=list(scratch),
            compiler_params=pltpu.CompilerParams(
                dimension_semantics=("arbitrary",), vmem_limit_bytes=grant
            ),
            cost_estimate=pl.CostEstimate(flops=flops, bytes_accessed=moved, transcendentals=0),
        )(*operands)

    half = jnp.bfloat16
    sent = call(
        send_kernel,
        (spot, token_ids, grad_out, w_out),
        [((GROUP_COLS + TOKEN_ROWS, block), half)] * GROUPS,
        [pltpu.VMEM((features, block), half)],
        grant=60 * 1024 * 1024,
    )
    early = [sent[0]] + [None] * (blocks - 1)
    for turn in (4, 6, 5, 7, 2, 3, 1):
        early[turn] = swapped(sent[mirrored(turn)], "seq", turn)
    lookup, normed = call(
        prepare_kernel,
        (meta, table, w_query, w_key, w_value),
        [((2, 3 * GROUP_COLS, vocab), half), ((vocab, features // 2), half)],
        [pltpu.VMEM((features, vocab), jnp.float32)],
        flops=10**9,
        moved=5 * 10**6,
        grant=60 * 1024 * 1024,
    )
    (late,) = call(
        late_kernel,
        (grad_out, lookup, *early[1:]),
        [((blocks, block, features // 2), half)],
        loose=blocks,
    )
    late = lax.all_to_all(late, "seq", split_axis=0, concat_axis=0, tiled=True)
    heads_shape = (GROUP_HEADS, HEAD_DIM, length)
    rows_shape = (GROUP_HEADS, length, 2 * HEAD_DIM)
    rows, sums, attended = call(
        attention_kernel,
        (meta, lookup, cosine, sine_part, *early),
        [
            ((GROUPS, 3 * GROUP_COLS, block), half),
            ((2, 3 * GROUP_COLS, vocab // 2), half),
            ((GROUP_COLS, length), half),
        ],
        [
            pltpu.VMEM(rows_shape, half),
            pltpu.VMEM(heads_shape, half),
            pltpu.VMEM(heads_shape, half),
            pltpu.VMEM(heads_shape, half),
            pltpu.VMEM(heads_shape, half),
            pltpu.VMEM((vocab, length), half),
            pltpu.VMEM((length, vocab), half),
            pltpu.VMEM((HEAD_DIM, length), jnp.float32),
            pltpu.VMEM((2 * HEAD_DIM, length), jnp.float32),
            pltpu.VMEM((length, 2 * HEAD_DIM), half),
            pltpu.VMEM((length, length), half),
            pltpu.VMEM((length, length), half),
            pltpu.VMEM((length // TILE, 2 * HEAD_DIM, 2 * TILE), half),
            pltpu.VMEM((length // TILE, WINDOW + TILE, 2 * TILE), jnp.float32),
            pltpu.VMEM((1, length), jnp.float32),
            pltpu.VMEM((1, length), jnp.float32),
        ],
        steps=GROUP_HEADS,
        flops=8 * 10**9,
        moved=8 * 10**6,
    )
    planes = [[GROUPS * z + x for x in range(GROUPS)] for z in range(2)]

    def over_plane(chunks):
        return lax.all_to_all(
            chunks, "seq", split_axis=0, concat_axis=0, axis_index_groups=planes, tiled=True
        )

    got_rows = over_plane(rows)
    lanes = vocab // 2
    out_rows = 3 * GROUP_COLS // 2
    packed = 3 * GROUP_COLS + out_rows
    keep, give = call(
        out_kernel,
        (meta, attended, late.reshape(length, features // 2), sums),
        [((packed, lanes), half)] * 2,
    )
    here = keep + swapped(give, "dp", 1)
    there = swapped(here, "dp", 2)
    kept_out, *pieces = call(
        combine_kernel,
        (meta, here, there, got_rows),
        [((out_rows, lanes), half)] + [((GROUP_COLS, lanes), half)] * GROUPS,
        loose=1,
    )
    last = blocks - 2
    got = [pieces[0]] + [swapped(pieces[turn], "seq", turn) for turn in (1, 2, 3)]
    got_out = [
        lax.ppermute(kept_out, "seq", [(2 * z, last), (2 * z + 1, last + 1)]) for z in range(3)
    ]
    (grad_input,) = call(
        input_kernel,
        (token_ids, table, w_query, w_key, w_value, got_rows),
        [((block, features), half)],
        flops=10**9,
        moved=5 * 10**6,
    )
    (mine,) = call(
        gather_kernel,
        (meta, *got, kept_out, *got_out, grad_input),
        [((4 * out_rows, lanes), half)],
        loose=1,
    )
    (weight_grads,) = call(
        weight_kernel,
        (meta, normed, mine, swapped(mine, "dp", 1)),
        [((features // 2, features), jnp.float32)],
        flops=10**9,
        moved=5 * 10**6,
    )
    return (grad_input[None], weight_grads)


def on_device(token_ids, cotangent, table, w_query, w_key, w_value, w_out, window):
    fits = (
        lax.axis_size("seq") == 2 * GROUPS
        and lax.axis_size("dp") == 4
        and token_ids.shape == (1, 128)
        and table.shape == (256, HEADS * HEAD_DIM)
    )
    plan = grouped_device if fits else general_device
    return plan(token_ids, cotangent, table, w_query, w_key, w_value, w_out, window)


def solution(mesh):
    return jax.shard_map(
        on_device,
        mesh=mesh,
        in_specs=(P("dp", "seq"), P("dp", "seq", None), P(), P(), P(), P(), P(), P()),
        out_specs=(P("dp", "seq", None), P("seq", None)),
        check_vma=False,
    )
```

```python
import jax
import jax.numpy as jnp
import numpy as np
from jax import lax
from jax.experimental import pallas as pl
from jax.experimental.pallas import tpu as pltpu
from jax.sharding import PartitionSpec as P

HEADS = 12
HEAD_DIM = 64
WINDOW = 512


EPSILON = 1e-05


def shifted(block, axis, distance):
    devices = range(lax.axis_size(axis))
    route = [(i - distance, i) for i in devices if i - distance in devices]
    return lax.ppermute(block, axis, route)


def rotate(values, positions):
    row_count = values.shape[0]
    shaped = values.reshape(row_count, -1, HEAD_DIM)
    middle = HEAD_DIM // 2
    frequency = 10000.0 ** (-2.0 * jnp.arange(middle, dtype=jnp.float32) / HEAD_DIM)
    angles = positions.astype(jnp.float32)[:, None] * frequency[None, :]
    cosine = jnp.cos(angles)[:, None, :]
    sine_part = jnp.sin(angles)[:, None, :]
    former = shaped[..., :middle]
    latter = shaped[..., middle:]
    turned = jnp.concatenate(
        [former * cosine - latter * sine_part, latter * cosine + former * sine_part], axis=-1
    )
    return turned.reshape(row_count, -1)


def unrotate(values, positions):
    row_count = values.shape[0]
    shaped = values.reshape(row_count, -1, HEAD_DIM)
    middle = HEAD_DIM // 2
    frequency = 10000.0 ** (-2.0 * jnp.arange(middle, dtype=jnp.float32) / HEAD_DIM)
    angles = positions.astype(jnp.float32)[:, None] * frequency[None, :]
    cosine = jnp.cos(angles)[:, None, :]
    sine_part = jnp.sin(angles)[:, None, :]
    former = shaped[..., :middle]
    latter = shaped[..., middle:]
    turned = jnp.concatenate(
        [former * cosine + latter * sine_part, latter * cosine - former * sine_part], axis=-1
    )
    return turned.reshape(row_count, -1)


def tdot(left, right):
    return lax.dot_general(
        left, right, (((0,), (0,)), ((), ())), preferred_element_type=jnp.float32
    )


def ndot(left, right):
    return lax.dot_general(
        left, right, (((1,), (1,)), ((), ())), preferred_element_type=jnp.float32
    )


def embed_rows(byte_ids, table):
    onehot = (byte_ids[:, None] == jnp.arange(table.shape[0], dtype=jnp.int32)[None, :]).astype(
        jnp.bfloat16
    )
    return jnp.dot(onehot, table, preferred_element_type=jnp.float32).astype(jnp.bfloat16)


def normalize(embedded):
    widened = embedded.astype(jnp.float32)
    inv_rms = lax.rsqrt(jnp.mean(widened * widened, axis=1, keepdims=True) + EPSILON)
    return (widened, inv_rms, (widened * inv_rms).astype(jnp.bfloat16))


def keys_values(normed, positions, w_key, w_value):
    key_rows = rotate(jnp.dot(normed, w_key, preferred_element_type=jnp.float32), positions).astype(
        jnp.bfloat16
    )
    value_rows = jnp.dot(normed, w_value, preferred_element_type=jnp.float32).astype(jnp.bfloat16)
    return (key_rows, value_rows)


def head_group(
    query_heads, key_heads, value_heads, grad_heads, group_window, own_pos, key_pos, score_scale
):
    distance = own_pos[:, None] - key_pos[None, :]
    allowed = (
        (distance[None] >= 0)
        & (distance[None] < group_window[:, None, None])
        & (key_pos[None, None, :] >= 0)
    )
    scores = (
        jnp.einsum("qhd,khd->hqk", query_heads, key_heads, preferred_element_type=jnp.float32)
        * score_scale
    )
    masked = jnp.where(allowed, scores, -1e30)
    row_max = jnp.max(masked, axis=-1, keepdims=True)
    weights = jnp.where(allowed, jnp.exp(masked - row_max), 0.0)
    probs = weights / jnp.sum(weights, axis=-1, keepdims=True)
    probs_b = probs.astype(jnp.bfloat16)
    attended = jnp.einsum(
        "hqk,khd->qhd", probs_b, value_heads, preferred_element_type=jnp.float32
    ).astype(jnp.bfloat16)
    grad_probs = jnp.einsum(
        "qhd,khd->hqk", grad_heads, value_heads, preferred_element_type=jnp.float32
    )
    row_term = jnp.sum(probs * grad_probs, axis=-1, keepdims=True)
    grad_scores = (probs * (grad_probs - row_term) * score_scale).astype(jnp.bfloat16)
    grad_query = jnp.einsum(
        "hqk,khd->qhd", grad_scores, key_heads, preferred_element_type=jnp.float32
    )
    grad_key = jnp.einsum(
        "hqk,qhd->khd", grad_scores, query_heads, preferred_element_type=jnp.float32
    )
    grad_value = jnp.einsum("hqk,qhd->khd", probs_b, grad_heads, preferred_element_type=jnp.float32)
    return (attended, grad_query, grad_key, grad_value)


def general_device(token_ids, cotangent, table, w_query, w_key, w_value, w_out, window):
    local_ids = token_ids[0]
    grad_out = cotangent[0]
    length = local_ids.shape[0]
    features = table.shape[1]
    tail_rows = min(length, WINDOW)
    reach_devs = -(-WINDOW // length)
    halo_rows = reach_devs * tail_rows
    offset = lax.axis_index("seq") * length
    own_pos = offset + jnp.arange(length, dtype=jnp.int32)
    halo_pos = offset - halo_rows + jnp.arange(halo_rows, dtype=jnp.int32)
    score_scale = HEAD_DIM ** (-0.5)
    embedded = embed_rows(local_ids, table)
    widened, inv_rms, normed = normalize(embedded)
    query = rotate(jnp.dot(normed, w_query, preferred_element_type=jnp.float32), own_pos).astype(
        jnp.bfloat16
    )
    key_own, value_own = keys_values(normed, own_pos, w_key, w_value)
    key_pieces = []
    value_pieces = []
    for hop_index in range(reach_devs):
        far_keys, far_values = shifted((key_own, value_own), "seq", hop_index + 1)
        key_pieces.insert(0, far_keys)
        value_pieces.insert(0, far_values)
    key_halo = jnp.concatenate(key_pieces, axis=0)
    value_halo = jnp.concatenate(value_pieces, axis=0)
    span_rows = halo_rows + length
    key_all = jnp.concatenate([key_halo, key_own], axis=0)
    value_all = jnp.concatenate([value_halo, value_own], axis=0)
    key_pos = jnp.concatenate([halo_pos, own_pos], axis=0)
    query_heads = query.reshape(length, HEADS, HEAD_DIM)
    key_heads = key_all.reshape(span_rows, HEADS, HEAD_DIM)
    value_heads = value_all.reshape(span_rows, HEADS, HEAD_DIM)
    grad_att = ndot(grad_out, w_out).astype(jnp.bfloat16)
    grad_heads = grad_att.reshape(length, HEADS, HEAD_DIM)
    group_size = 4
    attended_parts = []
    query_parts = []
    key_parts = []
    value_parts = []
    for group_index in range(HEADS // group_size):
        lower = group_index * group_size
        upper = lower + group_size
        outputs = head_group(
            query_heads[:, lower:upper],
            key_heads[:, lower:upper],
            value_heads[:, lower:upper],
            grad_heads[:, lower:upper],
            window[lower:upper],
            own_pos,
            key_pos,
            score_scale,
        )
        attended_parts.append(outputs[0])
        query_parts.append(outputs[1])
        key_parts.append(outputs[2])
        value_parts.append(outputs[3])
    attended = jnp.concatenate(attended_parts, axis=1).reshape(length, features)
    grad_query = jnp.concatenate(query_parts, axis=1).reshape(length, features)
    grad_key = jnp.concatenate(key_parts, axis=1).reshape(span_rows, features)
    grad_value = jnp.concatenate(value_parts, axis=1).reshape(span_rows, features)
    tail_keys = grad_key[:halo_rows].reshape(reach_devs, tail_rows, features)
    tail_values = grad_value[:halo_rows].reshape(reach_devs, tail_rows, features)
    back_keys = jnp.zeros((tail_rows, features), jnp.float32)
    back_values = jnp.zeros((tail_rows, features), jnp.float32)
    for hop_index in range(reach_devs):
        got_keys, got_values = shifted(
            (tail_keys[reach_devs - 1 - hop_index], tail_values[reach_devs - 1 - hop_index]),
            "seq",
            -(hop_index + 1),
        )
        back_keys = back_keys + got_keys
        back_values = back_values + got_values
    own_keys = grad_key[halo_rows:]
    own_values = grad_value[halo_rows:]
    own_keys = jnp.concatenate([own_keys[: length - tail_rows], own_keys + back_keys], axis=0)
    own_values = jnp.concatenate(
        [own_values[: length - tail_rows], own_values + back_values], axis=0
    )
    grad_q_lin = unrotate(grad_query, own_pos).astype(jnp.bfloat16)
    grad_k_lin = unrotate(own_keys, own_pos).astype(jnp.bfloat16)
    grad_v_lin = own_values.astype(jnp.bfloat16)
    grad_normed = ndot(grad_q_lin, w_query) + ndot(grad_k_lin, w_key) + ndot(grad_v_lin, w_value)
    scaled = widened * inv_rms
    grad_input = (
        inv_rms * (grad_normed - scaled * jnp.mean(grad_normed * scaled, axis=1, keepdims=True))
    ).astype(jnp.bfloat16)
    term = jnp.concatenate(
        [
            tdot(normed, grad_q_lin),
            tdot(normed, grad_k_lin),
            tdot(normed, grad_v_lin),
            tdot(attended, grad_out),
        ],
        axis=0,
    )
    shares = lax.psum_scatter(term.astype(jnp.bfloat16), "seq", scatter_dimension=0, tiled=True)
    weight_grads = lax.psum(shares, "dp").astype(jnp.float32)
    return (grad_input[None], weight_grads)


GROUPS = 4
GROUP_HEADS = HEADS // GROUPS
GROUP_COLS = GROUP_HEADS * HEAD_DIM
TILE = 256
TOKEN_ROWS = 16
STRIP = 8
HALF = HEAD_DIM // 2
VMEM_BYTES = 48 * 1024 * 1024


def mirrored(bits):
    return 2 * (bits % 2) + bits // 2 % 2


def key_span(query_tile):
    first = max(0, query_tile - WINDOW // TILE)
    return (first * TILE, (query_tile - first + 1) * TILE)


def normed_table(table_ref):
    widened = table_ref[...].astype(jnp.float32)
    inv_rms = lax.rsqrt(jnp.mean(widened * widened, axis=1, keepdims=True) + EPSILON)
    return (widened * inv_rms).astype(jnp.bfloat16)


def onehot_columns(tokens, vocab):
    rows = lax.broadcasted_iota(jnp.int32, (vocab, tokens.shape[1]), 0)
    return (rows == tokens).astype(jnp.float32).astype(jnp.bfloat16)


def send_kernel(spot_ref, tokens_ref, cotangent_ref, out_weights_ref, *out_refs):
    early_refs, grads_ref = out_refs[:-1], out_refs[-1]
    grad_att = ndot(out_weights_ref[...], cotangent_ref[...]).astype(jnp.bfloat16)
    grads_ref[...] = grad_att
    block = tokens_ref.shape[1]
    tokens = jnp.broadcast_to(tokens_ref[...].astype(jnp.float32), (TOKEN_ROWS, block)).astype(
        jnp.bfloat16
    )
    for turn, early_ref in enumerate(early_refs):
        group = spot_ref[0] ^ turn
        place = pl.ds(pl.multiple_of(group * GROUP_COLS, GROUP_COLS), GROUP_COLS)
        early_ref[:GROUP_COLS, :] = grads_ref[place, :]
        early_ref[GROUP_COLS:, :] = tokens


def late_kernel(cotangent_ref, *rest):
    late_ref = rest[-1]
    columns = late_ref.shape[2]
    for target in range(2 * GROUPS):
        side = target // GROUPS
        late_ref[target] = cotangent_ref[:, side * columns : (side + 1) * columns]


def prepare_kernel(
    meta_ref,
    table_ref,
    query_ref,
    key_ref,
    value_ref,
    lookup_ref,
    normed_ref,
    columns_ref,
):
    normed = normed_table(table_ref)
    half = normed.shape[1] // 2
    normed_ref[...] = jnp.where(meta_ref[GROUP_HEADS] == 0, normed[:, :half], normed[:, half:])
    place = pl.ds(pl.multiple_of(meta_ref[GROUP_HEADS + 3] * GROUP_COLS, GROUP_COLS), GROUP_COLS)
    for matrix, weights_ref in enumerate((query_ref, key_ref, value_ref)):
        columns_ref[...] = jnp.dot(
            normed, weights_ref[...], preferred_element_type=jnp.float32
        ).T
        mine = columns_ref[place, :]
        upper = mine.astype(jnp.bfloat16)
        rows = slice(matrix * GROUP_COLS, (matrix + 1) * GROUP_COLS)
        lookup_ref[0, rows, :] = upper
        lookup_ref[1, rows, :] = (mine - upper.astype(jnp.float32)).astype(jnp.bfloat16)


def attention_kernel(
    meta_ref,
    lookup_ref,
    cosine_ref,
    sine_ref,
    *rest,
):
    early_refs = rest[: 2 * GROUPS]
    attention_body(meta_ref, lookup_ref, cosine_ref, sine_ref, early_refs, *rest[2 * GROUPS :])


def attention_body(
    meta_ref,
    lookup_ref,
    cosine_ref,
    sine_ref,
    early_refs,
    rows_ref,
    keep_ref,
    give_ref,
    attended_ref,
    value_key_ref,
    query_t_ref,
    key_t_ref,
    value_t_ref,
    grad_att_ref,
    onehot_ref,
    onehot_rows_ref,
    grad_query_ref,
    both_ref,
    scaled_ref,
    probs_ref,
    scores_ref,
    right_ref,
    products_ref,
    inverse_ref,
    term_ref,
):
    head = pl.program_id(0)
    block = early_refs[0].shape[1]
    length = len(early_refs) * block
    tiles = length // TILE
    vocab = lookup_ref.shape[2]
    half_vocab = vocab // 2
    half = jnp.bfloat16
    cosine = cosine_ref[...]
    sine_part = sine_ref[...]

    @pl.when(head == 0)
    def _():
        own = 2 * meta_ref[GROUP_HEADS + 1] + meta_ref[GROUP_HEADS]
        for turn, early_ref in enumerate(early_refs):
            lanes = pl.ds(pl.multiple_of((own ^ turn) * block, block), block)
            tokens = early_ref[GROUP_COLS : GROUP_COLS + TOKEN_ROWS, :]
            tokens = tokens.astype(jnp.float32)[:1].astype(jnp.int32)
            onehot_ref[:, lanes] = onehot_columns(tokens, vocab)
            grad_att_ref[:, :, lanes] = early_ref[:GROUP_COLS, :].reshape(
                GROUP_HEADS, HEAD_DIM, block
            )
        onehot = onehot_ref[...]
        onehot_rows_ref[...] = onehot.T
        size = 3 * GROUP_COLS
        chosen = jnp.dot(
            lookup_ref[...].reshape(2 * size, vocab), onehot, preferred_element_type=jnp.float32
        )

        def picked(start):
            lower = start + size
            return chosen[start : start + HEAD_DIM] + chosen[lower : lower + HEAD_DIM]

        def turned(columns):
            former = columns[:HALF]
            latter = columns[HALF:]
            return jnp.concatenate(
                [former * cosine - latter * sine_part, latter * cosine + former * sine_part], axis=0
            )

        for index in range(GROUP_HEADS):
            query = turned(picked(index * HEAD_DIM)) * HEAD_DIM ** (-0.5)
            keys = turned(picked(GROUP_COLS + index * HEAD_DIM)).astype(half)
            values = picked(2 * GROUP_COLS + index * HEAD_DIM).astype(half)
            value_key_ref[index] = jnp.concatenate([values, keys], axis=0).T
            query_t_ref[index] = query.astype(half)
            key_t_ref[index] = keys
            value_t_ref[index] = values

    width = meta_ref[head]
    grad_att = grad_att_ref[head]
    query_t = query_t_ref[head]
    blank = jnp.zeros((HEAD_DIM, TILE), half)
    base = lax.broadcasted_iota(jnp.int32, (STRIP, TILE), 1) - lax.broadcasted_iota(
        jnp.int32, (STRIP, TILE), 0
    )
    for tile in range(tiles):
        columns = slice(tile * TILE, (tile + 1) * TILE)
        right_ref[tile, :HEAD_DIM, :TILE] = grad_att[:, columns]
        right_ref[tile, HEAD_DIM:, :TILE] = blank
        right_ref[tile, :HEAD_DIM, TILE:] = blank
        right_ref[tile, HEAD_DIM:, TILE:] = query_t[:, columns]

    def multiply(tile):
        first, count = key_span(tile)
        products_ref[tile, :count, :] = jnp.dot(
            value_key_ref[head, first : first + count, :],
            right_ref[tile],
            preferred_element_type=jnp.float32,
        )

    def forward(tile):
        first, count = key_span(tile)
        columns = slice(tile * TILE, (tile + 1) * TILE)
        row_max = None
        for row in range(0, count, STRIP):
            offset = tile * TILE - first - row
            allowed = base < width - offset
            if offset - STRIP < 0:
                allowed = allowed & (base >= -offset)
            masked = jnp.where(allowed, products_ref[tile, row : row + STRIP, TILE:], -1e30)
            products_ref[tile, row : row + STRIP, TILE:] = masked
            row_max = masked if row_max is None else jnp.maximum(row_max, masked)
        row_max = jnp.max(row_max, axis=0, keepdims=True)
        total = None
        for row in range(0, count, 2 * STRIP):
            weights = jnp.exp(products_ref[tile, row : row + 2 * STRIP, TILE:] - row_max)
            total = weights if total is None else total + weights
            probs_ref[first + row : first + row + 2 * STRIP, columns] = weights.astype(half)
        inverse = 1.0 / jnp.sum(total, axis=0, keepdims=True)
        attended = inverse * jnp.dot(
            value_t_ref[head, :, first : first + count],
            probs_ref[first : first + count, columns],
            preferred_element_type=jnp.float32,
        )
        attended_ref[pl.ds(pl.multiple_of(head * HEAD_DIM, HEAD_DIM), HEAD_DIM), columns] = (
            attended.astype(half)
        )
        wide_grad = grad_att[:, columns].astype(jnp.float32)
        inverse_ref[:, columns] = inverse
        term_ref[:, columns] = jnp.sum(attended * wide_grad, axis=0, keepdims=True)
        scaled_ref[columns, :] = jnp.concatenate(
            [
                (inverse * query_t[:, columns].astype(jnp.float32)).astype(half),
                (inverse * wide_grad).astype(half),
            ],
            axis=0,
        ).T

    def backward(tile):
        first, count = key_span(tile)
        columns = slice(tile * TILE, (tile + 1) * TILE)
        row_term = term_ref[:, columns]
        for row in range(0, count, 2 * STRIP):
            strip = slice(first + row, first + row + 2 * STRIP)
            scores_ref[strip, columns] = (
                probs_ref[strip, columns].astype(jnp.float32)
                * (products_ref[tile, row : row + 2 * STRIP, :TILE] - row_term)
            ).astype(half)
        grad_query_ref[:, columns] = inverse_ref[:, columns] * jnp.dot(
            key_t_ref[head, :, first : first + count],
            scores_ref[first : first + count, columns],
            preferred_element_type=jnp.float32,
        )

    lanes = lax.broadcasted_iota(jnp.int32, (TILE, 2 * HEAD_DIM), 1)

    def collect(tile):
        start = tile * TILE
        stop = min(length, start + TILE + WINDOW)
        grad_key = jnp.dot(
            scores_ref[start : start + TILE, start:stop],
            scaled_ref[start:stop, :],
            preferred_element_type=jnp.float32,
        )
        grad_value = jnp.dot(
            probs_ref[start : start + TILE, start:stop],
            scaled_ref[start:stop, :],
            preferred_element_type=jnp.float32,
        )
        both_ref[:, start : start + TILE] = jnp.where(lanes < HEAD_DIM, grad_key, grad_value).T

    reach = WINDOW // TILE
    for step in range(tiles + 3 + reach):
        if step < tiles:
            multiply(step)
        if 0 <= step - 1 < tiles:
            forward(step - 1)
        if 0 <= step - 2 < tiles:
            backward(step - 2)
        ready = step - 3 - reach
        if 0 <= ready < tiles:
            collect(ready)
    def turned_back(columns):
        former = columns[:HALF]
        latter = columns[HALF:]
        return jnp.concatenate(
            [former * cosine + latter * sine_part, latter * cosine - former * sine_part], axis=0
        )

    both = both_ref[...]
    grads = jnp.concatenate(
        [
            turned_back(grad_query_ref[...] * HEAD_DIM ** (-0.5)),
            turned_back(both[:HEAD_DIM]),
            both[HEAD_DIM:],
        ],
        axis=0,
    ).astype(half)
    sums = jnp.dot(grads, onehot_rows_ref[...], preferred_element_type=jnp.float32).astype(half)
    for matrix in range(3):
        rows = slice(matrix * HEAD_DIM, (matrix + 1) * HEAD_DIM)
        place = pl.ds(
            pl.multiple_of(matrix * GROUP_COLS + head * HEAD_DIM, HEAD_DIM), HEAD_DIM
        )
        low = sums[rows, :half_vocab]
        high = sums[rows, half_vocab:]
        first = meta_ref[GROUP_HEADS + 2] == 0
        keep_ref[place, :] = jnp.where(first, low, high)
        give_ref[place, :] = jnp.where(first, high, low)
        for target in range(GROUPS):
            start = target * block
            near = grads[rows, start : start + block]
            far = grads[rows, start + GROUPS * block : start + (GROUPS + 1) * block]
            rows_ref[target, place, :] = jnp.where(meta_ref[GROUP_HEADS + 1] < 2, near, far)


def out_kernel(meta_ref, attended_ref, cotangent_ref, after_ref, keep_ref, give_ref):
    del after_ref
    total = jnp.dot(attended_ref[...], cotangent_ref[...], preferred_element_type=jnp.float32)
    rows = total.shape[0] // 2
    lanes = keep_ref.shape[1]
    first = meta_ref[GROUP_HEADS + 2] == 0
    for chunk in range(total.shape[1] // lanes):
        part = total[:, chunk * lanes : (chunk + 1) * lanes]
        place = slice(chunk * rows, (chunk + 1) * rows)
        keep_ref[place, :] = jnp.where(first, part[:rows], part[rows:]).astype(jnp.bfloat16)
        give_ref[place, :] = jnp.where(first, part[rows:], part[:rows]).astype(jnp.bfloat16)


def combine_kernel(meta_ref, here_ref, there_ref, rows_ref, *rest):
    del rows_ref
    rows = GROUP_COLS
    for turn, piece_ref in enumerate(rest[:GROUPS]):
        target = jnp.minimum(meta_ref[GROUP_HEADS + 1] ^ (turn // 2), 2)
        place = pl.ds(pl.multiple_of(target * rows, rows), rows)
        piece_ref[...] = here_ref[place, :] + there_ref[place, :]


def gather_kernel(meta_ref, s0, s1, s2, s3, own_ref, o0, o1, o2, after_ref, mine_ref):
    del after_ref
    rows = GROUP_COLS
    size = own_ref.shape[0]

    @pl.when(meta_ref[GROUP_HEADS + 1] < 3)
    def _():
        for turn, got in enumerate((s0, s1, s2, s3)):
            source = meta_ref[GROUP_HEADS + 3] ^ mirrored(turn)
            mine_ref[pl.ds(pl.multiple_of(source * rows, rows), rows), :] = got[...]
        tail = mine_ref.shape[0] - GROUPS * rows
        mine_ref[GROUPS * rows :, :] = jnp.zeros((tail, mine_ref.shape[1]), jnp.bfloat16)

    @pl.when(meta_ref[GROUP_HEADS + 1] == 3)
    def _():
        for place, piece in enumerate((o0, o2, o1, own_ref)):
            mine_ref[place * size : (place + 1) * size, :] = piece[...]


def input_kernel(tokens_ref, table_ref, query_ref, key_ref, value_ref, rows_ref, out_ref):
    vocab = table_ref.shape[0]
    onehot = onehot_columns(tokens_ref[...], vocab)
    embedded = tdot(onehot, table_ref[...])
    inv_rms = lax.rsqrt(jnp.mean(embedded * embedded, axis=1, keepdims=True) + EPSILON)
    grad_normed = None
    for matrix, weights in enumerate((query_ref, key_ref, value_ref)):
        columns = jnp.concatenate(
            [
                rows_ref[group, matrix * GROUP_COLS : (matrix + 1) * GROUP_COLS, :]
                for group in map(mirrored, range(GROUPS))
            ],
            axis=0,
        )
        part = ndot(columns.astype(jnp.float32).T.astype(jnp.bfloat16), weights[...])
        grad_normed = part if grad_normed is None else grad_normed + part
    scaled = embedded * inv_rms
    out_ref[...] = (
        inv_rms * (grad_normed - scaled * jnp.mean(grad_normed * scaled, axis=1, keepdims=True))
    ).astype(jnp.bfloat16)


def weight_kernel(meta_ref, normed_ref, mine_ref, other_ref, out_ref):
    half_vocab = mine_ref.shape[1]
    first_core = meta_ref[GROUP_HEADS + 2] == 0

    @pl.when(meta_ref[GROUP_HEADS + 1] < 3)
    def _():
        first = normed_ref[:half_vocab, :]
        second = normed_ref[half_vocab:, :]
        upper = jnp.where(first_core, first, second)
        lower = jnp.where(first_core, second, first)
        total = None
        for part, sums_ref in ((upper, mine_ref), (lower, other_ref)):
            term = lax.dot_general(
                part,
                sums_ref[: GROUPS * GROUP_COLS, :],
                (((0,), (1,)), ((), ())),
                preferred_element_type=jnp.float32,
            )
            total = term if total is None else total + term
        out_ref[...] = total

    @pl.when(meta_ref[GROUP_HEADS + 1] == 3)
    def _():
        rows = GROUP_COLS // 2
        for half in range(2):
            for column in range(6):
                start = (half * 6 + column) * rows
                for core in range(2):
                    same = first_core == (core == 0)
                    value = jnp.where(
                        same, mine_ref[start : start + rows, :], other_ref[start : start + rows, :]
                    )
                    row = half * GROUP_COLS + core * rows
                    out_ref[
                        row : row + rows, column * half_vocab : (column + 1) * half_vocab
                    ] = value.astype(jnp.float32)


def whole(shape):
    return pl.BlockSpec(shape, lambda *_: (0,) * len(shape))


def swapped(block, axis, bit):
    route = [(i, i ^ bit) for i in range(lax.axis_size(axis))]
    return lax.ppermute(block, axis, route)


def rope_table(length):
    frequency = (10000.0 ** (-2.0 * np.arange(HALF, dtype=np.float32) / HEAD_DIM)).astype(np.float32)
    angles = frequency[:, None] * np.arange(length, dtype=np.float32)[None, :]
    angles = angles.astype(np.float64)
    return (
        jnp.asarray(np.cos(angles).astype(np.float32)),
        jnp.asarray(np.sin(angles).astype(np.float32)),
    )


def grouped_device(token_ids, cotangent, table, w_query, w_key, w_value, w_out, window):
    place = lax.axis_index("seq")
    core = lax.axis_index("dp") % 2
    side = place % 2
    level = place // 2
    group = 2 * side + level % 2
    block = token_ids.shape[1]
    features = table.shape[1]
    vocab = table.shape[0]
    blocks = lax.axis_size("seq")
    length = block * blocks
    grad_out = cotangent[0]
    meta = jnp.concatenate(
        [
            lax.dynamic_slice_in_dim(window, group * GROUP_HEADS, GROUP_HEADS, 0),
            jnp.stack([side, level, core, group]).astype(jnp.int32),
        ]
    )
    spot = jnp.stack([group]).astype(jnp.int32)
    cosine, sine_part = rope_table(length)

    def call(
        body, operands, outs, scratch=(), steps=1, flops=10**8, moved=10**6, loose=0, passed=False, grant=VMEM_BYTES
    ):
        spaces = [whole(operand.shape) for operand in operands]
        for index in range(loose):
            spaces[-1 - index] = pl.BlockSpec(memory_space=pl.ANY)
        if operands[0].ndim == 1:
            spaces[0] = pl.BlockSpec(memory_space=pltpu.SMEM)
        results = [whole(shape) for shape, _ in outs]
        aliases = {}
        if passed:
            results[-1] = pl.BlockSpec(memory_space=pl.ANY)
            aliases = {len(operands) - 1: len(outs) - 1}
        return pl.pallas_call(
            body,
            grid=(steps,),
            in_specs=spaces,
            out_specs=results,
            input_output_aliases=aliases,
            out_shape=[jax.ShapeDtypeStruct(shape, dtype) for shape, dtype in outs],
            scratch_shapes=list(scratch),
            compiler_params=pltpu.CompilerParams(
                dimension_semantics=("arbitrary",), vmem_limit_bytes=grant
            ),
            cost_estimate=pl.CostEstimate(flops=flops, bytes_accessed=moved, transcendentals=0),
        )(*operands)

    half = jnp.bfloat16
    sent = call(
        send_kernel,
        (spot, token_ids, grad_out, w_out),
        [((GROUP_COLS + TOKEN_ROWS, block), half)] * GROUPS,
        [pltpu.VMEM((features, block), half)],
        grant=60 * 1024 * 1024,
    )
    early = [sent[0]] + [None] * (blocks - 1)
    for turn in (4, 6, 5, 7, 2, 3, 1):
        early[turn] = swapped(sent[mirrored(turn)], "seq", turn)
    lookup, normed = call(
        prepare_kernel,
        (meta, table, w_query, w_key, w_value),
        [((2, 3 * GROUP_COLS, vocab), half), ((vocab, features // 2), half)],
        [pltpu.VMEM((features, vocab), jnp.float32)],
        flops=10**9,
        moved=5 * 10**6,
        grant=60 * 1024 * 1024,
    )
    (late,) = call(
        late_kernel,
        (grad_out, lookup, *early[1:]),
        [((blocks, block, features // 2), half)],
        loose=blocks,
    )
    late = lax.all_to_all(late, "seq", split_axis=0, concat_axis=0, tiled=True)
    heads_shape = (GROUP_HEADS, HEAD_DIM, length)
    rows_shape = (GROUP_HEADS, length, 2 * HEAD_DIM)
    rows, keep, give, attended = call(
        attention_kernel,
        (meta, lookup, cosine, sine_part, *early),
        [
            ((GROUPS, 3 * GROUP_COLS, block), half),
            *[((3 * GROUP_COLS, vocab // 2), half)] * 2,
            ((GROUP_COLS, length), half),
        ],
        [
            pltpu.VMEM(rows_shape, half),
            pltpu.VMEM(heads_shape, half),
            pltpu.VMEM(heads_shape, half),
            pltpu.VMEM(heads_shape, half),
            pltpu.VMEM(heads_shape, half),
            pltpu.VMEM((vocab, length), half),
            pltpu.VMEM((length, vocab), half),
            pltpu.VMEM((HEAD_DIM, length), jnp.float32),
            pltpu.VMEM((2 * HEAD_DIM, length), jnp.float32),
            pltpu.VMEM((length, 2 * HEAD_DIM), half),
            pltpu.VMEM((length, length), half),
            pltpu.VMEM((length, length), half),
            pltpu.VMEM((length // TILE, 2 * HEAD_DIM, 2 * TILE), half),
            pltpu.VMEM((length // TILE, WINDOW + TILE, 2 * TILE), jnp.float32),
            pltpu.VMEM((1, length), jnp.float32),
            pltpu.VMEM((1, length), jnp.float32),
        ],
        steps=GROUP_HEADS,
        flops=8 * 10**9,
        moved=8 * 10**6,
    )
    planes = [[GROUPS * z + x for x in range(GROUPS)] for z in range(2)]

    def over_plane(chunks):
        return lax.all_to_all(
            chunks, "seq", split_axis=0, concat_axis=0, axis_index_groups=planes, tiled=True
        )

    lanes = vocab // 2
    out_rows = 3 * GROUP_COLS // 2
    here = keep + swapped(give, "dp", 1)
    there = swapped(here, "dp", 2)
    *pieces, rows = call(
        combine_kernel,
        (meta, here, there, rows),
        [((GROUP_COLS, lanes), half)] * GROUPS + [(rows.shape, half)],
        loose=1,
        passed=True,
    )
    got_rows = over_plane(rows)
    keep, give = call(
        out_kernel,
        (meta, attended, late.reshape(length, features // 2), pieces[0]),
        [((out_rows, lanes), half)] * 2,
        loose=1,
    )
    here = keep + swapped(give, "dp", 1)
    kept_out = here + swapped(here, "dp", 2)
    last = blocks - 2
    got = [pieces[0]] + [swapped(pieces[turn], "seq", turn) for turn in (1, 2, 3)]
    got_out = [
        lax.ppermute(kept_out, "seq", [(2 * z, last), (2 * z + 1, last + 1)]) for z in range(3)
    ]
    (grad_input,) = call(
        input_kernel,
        (token_ids, table, w_query, w_key, w_value, got_rows),
        [((block, features), half)],
        flops=10**9,
        moved=5 * 10**6,
    )
    (mine,) = call(
        gather_kernel,
        (meta, *got, kept_out, *got_out, grad_input),
        [((4 * out_rows, lanes), half)],
        loose=1,
    )
    (weight_grads,) = call(
        weight_kernel,
        (meta, normed, mine, swapped(mine, "dp", 1)),
        [((features // 2, features), jnp.float32)],
        flops=10**9,
        moved=5 * 10**6,
    )
    return (grad_input[None], weight_grads)


def on_device(token_ids, cotangent, table, w_query, w_key, w_value, w_out, window):
    fits = (
        lax.axis_size("seq") == 2 * GROUPS
        and lax.axis_size("dp") == 4
        and token_ids.shape == (1, 128)
        and table.shape == (256, HEADS * HEAD_DIM)
    )
    plan = grouped_device if fits else general_device
    return plan(token_ids, cotangent, table, w_query, w_key, w_value, w_out, window)


def solution(mesh):
    return jax.shard_map(
        on_device,
        mesh=mesh,
        in_specs=(P("dp", "seq"), P("dp", "seq", None), P(), P(), P(), P(), P(), P()),
        out_specs=(P("dp", "seq", None), P("seq", None)),
        check_vma=False,
    )
```

```python
import jax
import jax.numpy as jnp
import numpy as np
from jax import lax
from jax.experimental import pallas as pl
from jax.experimental.pallas import tpu as pltpu
from jax.sharding import PartitionSpec as P

HEADS = 12
HEAD_DIM = 64
WINDOW = 512


EPSILON = 1e-05


def shifted(block, axis, distance):
    devices = range(lax.axis_size(axis))
    route = [(i - distance, i) for i in devices if i - distance in devices]
    return lax.ppermute(block, axis, route)


def rotate(values, positions):
    row_count = values.shape[0]
    shaped = values.reshape(row_count, -1, HEAD_DIM)
    middle = HEAD_DIM // 2
    frequency = 10000.0 ** (-2.0 * jnp.arange(middle, dtype=jnp.float32) / HEAD_DIM)
    angles = positions.astype(jnp.float32)[:, None] * frequency[None, :]
    cosine = jnp.cos(angles)[:, None, :]
    sine_part = jnp.sin(angles)[:, None, :]
    former = shaped[..., :middle]
    latter = shaped[..., middle:]
    turned = jnp.concatenate(
        [former * cosine - latter * sine_part, latter * cosine + former * sine_part], axis=-1
    )
    return turned.reshape(row_count, -1)


def unrotate(values, positions):
    row_count = values.shape[0]
    shaped = values.reshape(row_count, -1, HEAD_DIM)
    middle = HEAD_DIM // 2
    frequency = 10000.0 ** (-2.0 * jnp.arange(middle, dtype=jnp.float32) / HEAD_DIM)
    angles = positions.astype(jnp.float32)[:, None] * frequency[None, :]
    cosine = jnp.cos(angles)[:, None, :]
    sine_part = jnp.sin(angles)[:, None, :]
    former = shaped[..., :middle]
    latter = shaped[..., middle:]
    turned = jnp.concatenate(
        [former * cosine + latter * sine_part, latter * cosine - former * sine_part], axis=-1
    )
    return turned.reshape(row_count, -1)


def tdot(left, right):
    return lax.dot_general(
        left, right, (((0,), (0,)), ((), ())), preferred_element_type=jnp.float32
    )


def ndot(left, right):
    return lax.dot_general(
        left, right, (((1,), (1,)), ((), ())), preferred_element_type=jnp.float32
    )


def embed_rows(byte_ids, table):
    onehot = (byte_ids[:, None] == jnp.arange(table.shape[0], dtype=jnp.int32)[None, :]).astype(
        jnp.bfloat16
    )
    return jnp.dot(onehot, table, preferred_element_type=jnp.float32).astype(jnp.bfloat16)


def normalize(embedded):
    widened = embedded.astype(jnp.float32)
    inv_rms = lax.rsqrt(jnp.mean(widened * widened, axis=1, keepdims=True) + EPSILON)
    return (widened, inv_rms, (widened * inv_rms).astype(jnp.bfloat16))


def keys_values(normed, positions, w_key, w_value):
    key_rows = rotate(jnp.dot(normed, w_key, preferred_element_type=jnp.float32), positions).astype(
        jnp.bfloat16
    )
    value_rows = jnp.dot(normed, w_value, preferred_element_type=jnp.float32).astype(jnp.bfloat16)
    return (key_rows, value_rows)


def head_group(
    query_heads, key_heads, value_heads, grad_heads, group_window, own_pos, key_pos, score_scale
):
    distance = own_pos[:, None] - key_pos[None, :]
    allowed = (
        (distance[None] >= 0)
        & (distance[None] < group_window[:, None, None])
        & (key_pos[None, None, :] >= 0)
    )
    scores = (
        jnp.einsum("qhd,khd->hqk", query_heads, key_heads, preferred_element_type=jnp.float32)
        * score_scale
    )
    masked = jnp.where(allowed, scores, -1e30)
    row_max = jnp.max(masked, axis=-1, keepdims=True)
    weights = jnp.where(allowed, jnp.exp(masked - row_max), 0.0)
    probs = weights / jnp.sum(weights, axis=-1, keepdims=True)
    probs_b = probs.astype(jnp.bfloat16)
    attended = jnp.einsum(
        "hqk,khd->qhd", probs_b, value_heads, preferred_element_type=jnp.float32
    ).astype(jnp.bfloat16)
    grad_probs = jnp.einsum(
        "qhd,khd->hqk", grad_heads, value_heads, preferred_element_type=jnp.float32
    )
    row_term = jnp.sum(probs * grad_probs, axis=-1, keepdims=True)
    grad_scores = (probs * (grad_probs - row_term) * score_scale).astype(jnp.bfloat16)
    grad_query = jnp.einsum(
        "hqk,khd->qhd", grad_scores, key_heads, preferred_element_type=jnp.float32
    )
    grad_key = jnp.einsum(
        "hqk,qhd->khd", grad_scores, query_heads, preferred_element_type=jnp.float32
    )
    grad_value = jnp.einsum("hqk,qhd->khd", probs_b, grad_heads, preferred_element_type=jnp.float32)
    return (attended, grad_query, grad_key, grad_value)


def general_device(token_ids, cotangent, table, w_query, w_key, w_value, w_out, window):
    local_ids = token_ids[0]
    grad_out = cotangent[0]
    length = local_ids.shape[0]
    features = table.shape[1]
    tail_rows = min(length, WINDOW)
    reach_devs = -(-WINDOW // length)
    halo_rows = reach_devs * tail_rows
    offset = lax.axis_index("seq") * length
    own_pos = offset + jnp.arange(length, dtype=jnp.int32)
    halo_pos = offset - halo_rows + jnp.arange(halo_rows, dtype=jnp.int32)
    score_scale = HEAD_DIM ** (-0.5)
    embedded = embed_rows(local_ids, table)
    widened, inv_rms, normed = normalize(embedded)
    query = rotate(jnp.dot(normed, w_query, preferred_element_type=jnp.float32), own_pos).astype(
        jnp.bfloat16
    )
    key_own, value_own = keys_values(normed, own_pos, w_key, w_value)
    key_pieces = []
    value_pieces = []
    for hop_index in range(reach_devs):
        far_keys, far_values = shifted((key_own, value_own), "seq", hop_index + 1)
        key_pieces.insert(0, far_keys)
        value_pieces.insert(0, far_values)
    key_halo = jnp.concatenate(key_pieces, axis=0)
    value_halo = jnp.concatenate(value_pieces, axis=0)
    span_rows = halo_rows + length
    key_all = jnp.concatenate([key_halo, key_own], axis=0)
    value_all = jnp.concatenate([value_halo, value_own], axis=0)
    key_pos = jnp.concatenate([halo_pos, own_pos], axis=0)
    query_heads = query.reshape(length, HEADS, HEAD_DIM)
    key_heads = key_all.reshape(span_rows, HEADS, HEAD_DIM)
    value_heads = value_all.reshape(span_rows, HEADS, HEAD_DIM)
    grad_att = ndot(grad_out, w_out).astype(jnp.bfloat16)
    grad_heads = grad_att.reshape(length, HEADS, HEAD_DIM)
    group_size = 4
    attended_parts = []
    query_parts = []
    key_parts = []
    value_parts = []
    for group_index in range(HEADS // group_size):
        lower = group_index * group_size
        upper = lower + group_size
        outputs = head_group(
            query_heads[:, lower:upper],
            key_heads[:, lower:upper],
            value_heads[:, lower:upper],
            grad_heads[:, lower:upper],
            window[lower:upper],
            own_pos,
            key_pos,
            score_scale,
        )
        attended_parts.append(outputs[0])
        query_parts.append(outputs[1])
        key_parts.append(outputs[2])
        value_parts.append(outputs[3])
    attended = jnp.concatenate(attended_parts, axis=1).reshape(length, features)
    grad_query = jnp.concatenate(query_parts, axis=1).reshape(length, features)
    grad_key = jnp.concatenate(key_parts, axis=1).reshape(span_rows, features)
    grad_value = jnp.concatenate(value_parts, axis=1).reshape(span_rows, features)
    tail_keys = grad_key[:halo_rows].reshape(reach_devs, tail_rows, features)
    tail_values = grad_value[:halo_rows].reshape(reach_devs, tail_rows, features)
    back_keys = jnp.zeros((tail_rows, features), jnp.float32)
    back_values = jnp.zeros((tail_rows, features), jnp.float32)
    for hop_index in range(reach_devs):
        got_keys, got_values = shifted(
            (tail_keys[reach_devs - 1 - hop_index], tail_values[reach_devs - 1 - hop_index]),
            "seq",
            -(hop_index + 1),
        )
        back_keys = back_keys + got_keys
        back_values = back_values + got_values
    own_keys = grad_key[halo_rows:]
    own_values = grad_value[halo_rows:]
    own_keys = jnp.concatenate([own_keys[: length - tail_rows], own_keys + back_keys], axis=0)
    own_values = jnp.concatenate(
        [own_values[: length - tail_rows], own_values + back_values], axis=0
    )
    grad_q_lin = unrotate(grad_query, own_pos).astype(jnp.bfloat16)
    grad_k_lin = unrotate(own_keys, own_pos).astype(jnp.bfloat16)
    grad_v_lin = own_values.astype(jnp.bfloat16)
    grad_normed = ndot(grad_q_lin, w_query) + ndot(grad_k_lin, w_key) + ndot(grad_v_lin, w_value)
    scaled = widened * inv_rms
    grad_input = (
        inv_rms * (grad_normed - scaled * jnp.mean(grad_normed * scaled, axis=1, keepdims=True))
    ).astype(jnp.bfloat16)
    term = jnp.concatenate(
        [
            tdot(normed, grad_q_lin),
            tdot(normed, grad_k_lin),
            tdot(normed, grad_v_lin),
            tdot(attended, grad_out),
        ],
        axis=0,
    )
    shares = lax.psum_scatter(term.astype(jnp.bfloat16), "seq", scatter_dimension=0, tiled=True)
    weight_grads = lax.psum(shares, "dp").astype(jnp.float32)
    return (grad_input[None], weight_grads)


GROUPS = 4
GROUP_HEADS = HEADS // GROUPS
GROUP_COLS = GROUP_HEADS * HEAD_DIM
TILE = 256
TOKEN_ROWS = 16
STRIP = 8
HALF = HEAD_DIM // 2
VMEM_BYTES = 48 * 1024 * 1024


def mirrored(bits):
    return 2 * (bits % 2) + bits // 2 % 2


def key_span(query_tile):
    first = max(0, query_tile - WINDOW // TILE)
    return (first * TILE, (query_tile - first + 1) * TILE)


def normed_table(table_ref):
    widened = table_ref[...].astype(jnp.float32)
    inv_rms = lax.rsqrt(jnp.mean(widened * widened, axis=1, keepdims=True) + EPSILON)
    return (widened * inv_rms).astype(jnp.bfloat16)


def onehot_columns(tokens, vocab):
    rows = lax.broadcasted_iota(jnp.int32, (vocab, tokens.shape[1]), 0)
    return (rows == tokens).astype(jnp.float32).astype(jnp.bfloat16)


def send_kernel(spot_ref, tokens_ref, cotangent_ref, out_weights_ref, *out_refs):
    early_refs, grads_ref = out_refs[:-1], out_refs[-1]
    grad_att = ndot(out_weights_ref[...], cotangent_ref[...]).astype(jnp.bfloat16)
    grads_ref[...] = grad_att
    block = tokens_ref.shape[1]
    tokens = jnp.broadcast_to(tokens_ref[...].astype(jnp.float32), (TOKEN_ROWS, block)).astype(
        jnp.bfloat16
    )
    for turn, early_ref in enumerate(early_refs):
        group = spot_ref[0] ^ turn
        place = pl.ds(pl.multiple_of(group * GROUP_COLS, GROUP_COLS), GROUP_COLS)
        early_ref[:GROUP_COLS, :] = grads_ref[place, :]
        early_ref[GROUP_COLS:, :] = tokens


def late_kernel(cotangent_ref, *rest):
    late_ref = rest[-1]
    columns = late_ref.shape[2]
    for target in range(2 * GROUPS):
        side = target // GROUPS
        late_ref[target] = cotangent_ref[:, side * columns : (side + 1) * columns]


def prepare_kernel(
    meta_ref,
    table_ref,
    query_ref,
    key_ref,
    value_ref,
    lookup_ref,
    normed_ref,
    columns_ref,
):
    normed = normed_table(table_ref)
    half = normed.shape[1] // 2
    normed_ref[...] = jnp.where(meta_ref[GROUP_HEADS] == 0, normed[:, :half], normed[:, half:])
    place = pl.ds(pl.multiple_of(meta_ref[GROUP_HEADS + 3] * GROUP_COLS, GROUP_COLS), GROUP_COLS)
    for matrix, weights_ref in enumerate((query_ref, key_ref, value_ref)):
        columns_ref[...] = jnp.dot(
            normed, weights_ref[...], preferred_element_type=jnp.float32
        ).T
        mine = columns_ref[place, :]
        upper = mine.astype(jnp.bfloat16)
        rows = slice(matrix * GROUP_COLS, (matrix + 1) * GROUP_COLS)
        lookup_ref[0, rows, :] = upper
        lookup_ref[1, rows, :] = (mine - upper.astype(jnp.float32)).astype(jnp.bfloat16)


def attention_kernel(
    meta_ref,
    lookup_ref,
    cosine_ref,
    sine_ref,
    *rest,
):
    early_refs = rest[: 2 * GROUPS]
    attention_body(meta_ref, lookup_ref, cosine_ref, sine_ref, early_refs, *rest[2 * GROUPS :])


def attention_body(
    meta_ref,
    lookup_ref,
    cosine_ref,
    sine_ref,
    early_refs,
    rows_ref,
    sums_ref,
    attended_ref,
    value_key_ref,
    query_t_ref,
    key_t_ref,
    value_t_ref,
    grad_att_ref,
    onehot_ref,
    onehot_rows_ref,
    grad_query_ref,
    both_ref,
    scaled_ref,
    probs_ref,
    scores_ref,
    right_ref,
    products_ref,
    inverse_ref,
    term_ref,
):
    head = pl.program_id(0)
    block = early_refs[0].shape[1]
    length = len(early_refs) * block
    tiles = length // TILE
    vocab = lookup_ref.shape[2]
    half_vocab = vocab // 2
    half = jnp.bfloat16
    cosine = cosine_ref[...]
    sine_part = sine_ref[...]

    @pl.when(head == 0)
    def _():
        own = 2 * meta_ref[GROUP_HEADS + 1] + meta_ref[GROUP_HEADS]
        for turn, early_ref in enumerate(early_refs):
            lanes = pl.ds(pl.multiple_of((own ^ turn) * block, block), block)
            tokens = early_ref[GROUP_COLS : GROUP_COLS + TOKEN_ROWS, :]
            tokens = tokens.astype(jnp.float32)[:1].astype(jnp.int32)
            onehot_ref[:, lanes] = onehot_columns(tokens, vocab)
            grad_att_ref[:, :, lanes] = early_ref[:GROUP_COLS, :].reshape(
                GROUP_HEADS, HEAD_DIM, block
            )
        onehot = onehot_ref[...]
        onehot_rows_ref[...] = onehot.T
        size = 3 * GROUP_COLS
        chosen = jnp.dot(
            lookup_ref[...].reshape(2 * size, vocab), onehot, preferred_element_type=jnp.float32
        )

        def picked(start):
            lower = start + size
            return chosen[start : start + HEAD_DIM] + chosen[lower : lower + HEAD_DIM]

        def turned(columns):
            former = columns[:HALF]
            latter = columns[HALF:]
            return jnp.concatenate(
                [former * cosine - latter * sine_part, latter * cosine + former * sine_part], axis=0
            )

        for index in range(GROUP_HEADS):
            query = turned(picked(index * HEAD_DIM)) * HEAD_DIM ** (-0.5)
            keys = turned(picked(GROUP_COLS + index * HEAD_DIM)).astype(half)
            values = picked(2 * GROUP_COLS + index * HEAD_DIM).astype(half)
            value_key_ref[index] = jnp.concatenate([values, keys], axis=0).T
            query_t_ref[index] = query.astype(half)
            key_t_ref[index] = keys
            value_t_ref[index] = values

    width = meta_ref[head]
    grad_att = grad_att_ref[head]
    query_t = query_t_ref[head]
    blank = jnp.zeros((HEAD_DIM, TILE), half)
    base = lax.broadcasted_iota(jnp.int32, (STRIP, TILE), 1) - lax.broadcasted_iota(
        jnp.int32, (STRIP, TILE), 0
    )
    for tile in range(tiles):
        columns = slice(tile * TILE, (tile + 1) * TILE)
        right_ref[tile, :HEAD_DIM, :TILE] = grad_att[:, columns]
        right_ref[tile, HEAD_DIM:, :TILE] = blank
        right_ref[tile, :HEAD_DIM, TILE:] = blank
        right_ref[tile, HEAD_DIM:, TILE:] = query_t[:, columns]

    def multiply(tile):
        first, count = key_span(tile)
        products_ref[tile, :count, :] = jnp.dot(
            value_key_ref[head, first : first + count, :],
            right_ref[tile],
            preferred_element_type=jnp.float32,
        )

    def forward(tile):
        first, count = key_span(tile)
        columns = slice(tile * TILE, (tile + 1) * TILE)
        row_max = None
        for row in range(0, count, STRIP):
            offset = tile * TILE - first - row
            allowed = base < width - offset
            if offset - STRIP < 0:
                allowed = allowed & (base >= -offset)
            masked = jnp.where(allowed, products_ref[tile, row : row + STRIP, TILE:], -1e30)
            products_ref[tile, row : row + STRIP, TILE:] = masked
            row_max = masked if row_max is None else jnp.maximum(row_max, masked)
        row_max = jnp.max(row_max, axis=0, keepdims=True)
        total = None
        for row in range(0, count, 2 * STRIP):
            weights = jnp.exp(products_ref[tile, row : row + 2 * STRIP, TILE:] - row_max)
            total = weights if total is None else total + weights
            probs_ref[first + row : first + row + 2 * STRIP, columns] = weights.astype(half)
        inverse = 1.0 / jnp.sum(total, axis=0, keepdims=True)
        attended = inverse * jnp.dot(
            value_t_ref[head, :, first : first + count],
            probs_ref[first : first + count, columns],
            preferred_element_type=jnp.float32,
        )
        attended_ref[pl.ds(pl.multiple_of(head * HEAD_DIM, HEAD_DIM), HEAD_DIM), columns] = (
            attended.astype(half)
        )
        wide_grad = grad_att[:, columns].astype(jnp.float32)
        inverse_ref[:, columns] = inverse
        term_ref[:, columns] = jnp.sum(attended * wide_grad, axis=0, keepdims=True)
        scaled_ref[columns, :] = jnp.concatenate(
            [
                (inverse * query_t[:, columns].astype(jnp.float32)).astype(half),
                (inverse * wide_grad).astype(half),
            ],
            axis=0,
        ).T

    def backward(tile):
        first, count = key_span(tile)
        columns = slice(tile * TILE, (tile + 1) * TILE)
        row_term = term_ref[:, columns]
        for row in range(0, count, 2 * STRIP):
            strip = slice(first + row, first + row + 2 * STRIP)
            scores_ref[strip, columns] = (
                probs_ref[strip, columns].astype(jnp.float32)
                * (products_ref[tile, row : row + 2 * STRIP, :TILE] - row_term)
            ).astype(half)
        grad_query_ref[:, columns] = inverse_ref[:, columns] * jnp.dot(
            key_t_ref[head, :, first : first + count],
            scores_ref[first : first + count, columns],
            preferred_element_type=jnp.float32,
        )

    lanes = lax.broadcasted_iota(jnp.int32, (TILE, 2 * HEAD_DIM), 1)

    def collect(tile):
        start = tile * TILE
        stop = min(length, start + TILE + WINDOW)
        grad_key = jnp.dot(
            scores_ref[start : start + TILE, start:stop],
            scaled_ref[start:stop, :],
            preferred_element_type=jnp.float32,
        )
        grad_value = jnp.dot(
            probs_ref[start : start + TILE, start:stop],
            scaled_ref[start:stop, :],
            preferred_element_type=jnp.float32,
        )
        both_ref[:, start : start + TILE] = jnp.where(lanes < HEAD_DIM, grad_key, grad_value).T

    reach = WINDOW // TILE
    for step in range(tiles + 3 + reach):
        if step < tiles:
            multiply(step)
        if 0 <= step - 1 < tiles:
            forward(step - 1)
        if 0 <= step - 2 < tiles:
            backward(step - 2)
        ready = step - 3 - reach
        if 0 <= ready < tiles:
            collect(ready)
    def turned_back(columns):
        former = columns[:HALF]
        latter = columns[HALF:]
        return jnp.concatenate(
            [former * cosine + latter * sine_part, latter * cosine - former * sine_part], axis=0
        )

    both = both_ref[...]
    grads = jnp.concatenate(
        [
            turned_back(grad_query_ref[...] * HEAD_DIM ** (-0.5)),
            turned_back(both[:HEAD_DIM]),
            both[HEAD_DIM:],
        ],
        axis=0,
    ).astype(half)
    sums = jnp.dot(grads, onehot_rows_ref[...], preferred_element_type=jnp.float32).astype(half)
    for matrix in range(3):
        rows = slice(matrix * HEAD_DIM, (matrix + 1) * HEAD_DIM)
        place = pl.ds(
            pl.multiple_of(matrix * GROUP_COLS + head * HEAD_DIM, HEAD_DIM), HEAD_DIM
        )
        for core in range(2):
            lane = core * half_vocab
            sums_ref[core, place, :] = sums[rows, lane : lane + half_vocab]
        for target in range(GROUPS):
            start = target * block
            near = grads[rows, start : start + block]
            far = grads[rows, start + GROUPS * block : start + (GROUPS + 1) * block]
            rows_ref[target, place, :] = jnp.where(meta_ref[GROUP_HEADS + 1] < 2, near, far)


def out_kernel(meta_ref, attended_ref, cotangent_ref, sums_ref, keep_ref, give_ref):
    total = jnp.dot(attended_ref[...], cotangent_ref[...], preferred_element_type=jnp.float32)
    rows = total.shape[0] // 2
    base = sums_ref.shape[1]
    lanes = keep_ref.shape[1]
    first = meta_ref[GROUP_HEADS + 2] == 0
    keep_ref[:base, :] = jnp.where(first, sums_ref[0], sums_ref[1])
    give_ref[:base, :] = jnp.where(first, sums_ref[1], sums_ref[0])
    for chunk in range(total.shape[1] // lanes):
        part = total[:, chunk * lanes : (chunk + 1) * lanes]
        place = slice(base + chunk * rows, base + (chunk + 1) * rows)
        keep_ref[place, :] = jnp.where(first, part[:rows], part[rows:]).astype(jnp.bfloat16)
        give_ref[place, :] = jnp.where(first, part[rows:], part[:rows]).astype(jnp.bfloat16)


def combine_kernel(meta_ref, here_ref, there_ref, after_ref, out_ref, *piece_refs):
    del after_ref
    rows = GROUP_COLS
    for turn, piece_ref in enumerate(piece_refs):
        target = jnp.minimum(meta_ref[GROUP_HEADS + 1] ^ (turn // 2), 2)
        place = pl.ds(pl.multiple_of(target * rows, rows), rows)
        piece_ref[...] = here_ref[place, :] + there_ref[place, :]
    out_ref[...] = here_ref[3 * rows :, :] + there_ref[3 * rows :, :]


def gather_kernel(meta_ref, s0, s1, s2, s3, own_ref, o0, o1, o2, mine_ref):
    rows = GROUP_COLS
    size = own_ref.shape[0]

    @pl.when(meta_ref[GROUP_HEADS + 1] < 3)
    def _():
        for turn, got in enumerate((s0, s1, s2, s3)):
            source = meta_ref[GROUP_HEADS + 3] ^ mirrored(turn)
            mine_ref[pl.ds(pl.multiple_of(source * rows, rows), rows), :] = got[...]
        tail = mine_ref.shape[0] - GROUPS * rows
        mine_ref[GROUPS * rows :, :] = jnp.zeros((tail, mine_ref.shape[1]), jnp.bfloat16)

    @pl.when(meta_ref[GROUP_HEADS + 1] == 3)
    def _():
        for place, piece in enumerate((o0, o2, o1, own_ref)):
            mine_ref[place * size : (place + 1) * size, :] = piece[...]


def input_kernel(tokens_ref, table_ref, query_ref, key_ref, value_ref, rows_ref, out_ref):
    vocab = table_ref.shape[0]
    onehot = onehot_columns(tokens_ref[...], vocab)
    embedded = tdot(onehot, table_ref[...])
    inv_rms = lax.rsqrt(jnp.mean(embedded * embedded, axis=1, keepdims=True) + EPSILON)
    grad_normed = None
    for matrix, weights in enumerate((query_ref, key_ref, value_ref)):
        columns = jnp.concatenate(
            [
                rows_ref[group, matrix * GROUP_COLS : (matrix + 1) * GROUP_COLS, :]
                for group in map(mirrored, range(GROUPS))
            ],
            axis=0,
        )
        part = ndot(columns.astype(jnp.float32).T.astype(jnp.bfloat16), weights[...])
        grad_normed = part if grad_normed is None else grad_normed + part
    scaled = embedded * inv_rms
    out_ref[...] = (
        inv_rms * (grad_normed - scaled * jnp.mean(grad_normed * scaled, axis=1, keepdims=True))
    ).astype(jnp.bfloat16)


def weight_kernel(meta_ref, normed_ref, mine_ref, other_ref, out_ref):
    half_vocab = mine_ref.shape[1]
    first_core = meta_ref[GROUP_HEADS + 2] == 0

    @pl.when(meta_ref[GROUP_HEADS + 1] < 3)
    def _():
        first = normed_ref[:half_vocab, :]
        second = normed_ref[half_vocab:, :]
        upper = jnp.where(first_core, first, second)
        lower = jnp.where(first_core, second, first)
        total = None
        for part, sums_ref in ((upper, mine_ref), (lower, other_ref)):
            term = lax.dot_general(
                part,
                sums_ref[: GROUPS * GROUP_COLS, :],
                (((0,), (1,)), ((), ())),
                preferred_element_type=jnp.float32,
            )
            total = term if total is None else total + term
        out_ref[...] = total

    @pl.when(meta_ref[GROUP_HEADS + 1] == 3)
    def _():
        rows = GROUP_COLS // 2
        for half in range(2):
            for column in range(6):
                start = (half * 6 + column) * rows
                for core in range(2):
                    same = first_core == (core == 0)
                    value = jnp.where(
                        same, mine_ref[start : start + rows, :], other_ref[start : start + rows, :]
                    )
                    row = half * GROUP_COLS + core * rows
                    out_ref[
                        row : row + rows, column * half_vocab : (column + 1) * half_vocab
                    ] = value.astype(jnp.float32)


def whole(shape):
    return pl.BlockSpec(shape, lambda *_: (0,) * len(shape))


def swapped(block, axis, bit):
    route = [(i, i ^ bit) for i in range(lax.axis_size(axis))]
    return lax.ppermute(block, axis, route)


def rope_table(length):
    frequency = (10000.0 ** (-2.0 * np.arange(HALF, dtype=np.float32) / HEAD_DIM)).astype(np.float32)
    angles = frequency[:, None] * np.arange(length, dtype=np.float32)[None, :]
    angles = angles.astype(np.float64)
    return (
        jnp.asarray(np.cos(angles).astype(np.float32)),
        jnp.asarray(np.sin(angles).astype(np.float32)),
    )


def grouped_device(token_ids, cotangent, table, w_query, w_key, w_value, w_out, window):
    place = lax.axis_index("seq")
    core = lax.axis_index("dp") % 2
    side = place % 2
    level = place // 2
    group = 2 * side + level % 2
    block = token_ids.shape[1]
    features = table.shape[1]
    vocab = table.shape[0]
    blocks = lax.axis_size("seq")
    length = block * blocks
    grad_out = cotangent[0]
    meta = jnp.concatenate(
        [
            lax.dynamic_slice_in_dim(window, group * GROUP_HEADS, GROUP_HEADS, 0),
            jnp.stack([side, level, core, group]).astype(jnp.int32),
        ]
    )
    spot = jnp.stack([group]).astype(jnp.int32)
    cosine, sine_part = rope_table(length)

    def call(
        body, operands, outs, scratch=(), steps=1, flops=10**8, moved=10**6, loose=0, grant=VMEM_BYTES
    ):
        spaces = [whole(operand.shape) for operand in operands]
        for index in range(loose):
            spaces[-1 - index] = pl.BlockSpec(memory_space=pl.ANY)
        if operands[0].ndim == 1:
            spaces[0] = pl.BlockSpec(memory_space=pltpu.SMEM)
        return pl.pallas_call(
            body,
            grid=(steps,),
            in_specs=spaces,
            out_specs=[whole(shape) for shape, _ in outs],
            out_shape=[jax.ShapeDtypeStruct(shape, dtype) for shape, dtype in outs],
            scratch_shapes=list(scratch),
            compiler_params=pltpu.CompilerParams(
                dimension_semantics=("arbitrary",), vmem_limit_bytes=grant
            ),
            cost_estimate=pl.CostEstimate(flops=flops, bytes_accessed=moved, transcendentals=0),
        )(*operands)

    half = jnp.bfloat16
    sent = call(
        send_kernel,
        (spot, token_ids, grad_out, w_out),
        [((GROUP_COLS + TOKEN_ROWS, block), half)] * GROUPS,
        [pltpu.VMEM((features, block), half)],
        grant=60 * 1024 * 1024,
    )
    early = [sent[0]] + [None] * (blocks - 1)
    for turn in (4, 6, 5, 7, 2, 3, 1):
        early[turn] = swapped(sent[mirrored(turn)], "seq", turn)
    lookup, normed = call(
        prepare_kernel,
        (meta, table, w_query, w_key, w_value),
        [((2, 3 * GROUP_COLS, vocab), half), ((vocab, features // 2), half)],
        [pltpu.VMEM((features, vocab), jnp.float32)],
        flops=10**9,
        moved=5 * 10**6,
        grant=60 * 1024 * 1024,
    )
    (late,) = call(
        late_kernel,
        (grad_out, lookup, *early[1:]),
        [((blocks, block, features // 2), half)],
        loose=blocks,
    )
    late = lax.all_to_all(late, "seq", split_axis=0, concat_axis=0, tiled=True)
    heads_shape = (GROUP_HEADS, HEAD_DIM, length)
    rows_shape = (GROUP_HEADS, length, 2 * HEAD_DIM)
    rows, sums, attended = call(
        attention_kernel,
        (meta, lookup, cosine, sine_part, *early),
        [
            ((GROUPS, 3 * GROUP_COLS, block), half),
            ((2, 3 * GROUP_COLS, vocab // 2), half),
            ((GROUP_COLS, length), half),
        ],
        [
            pltpu.VMEM(rows_shape, half),
            pltpu.VMEM(heads_shape, half),
            pltpu.VMEM(heads_shape, half),
            pltpu.VMEM(heads_shape, half),
            pltpu.VMEM(heads_shape, half),
            pltpu.VMEM((vocab, length), half),
            pltpu.VMEM((length, vocab), half),
            pltpu.VMEM((HEAD_DIM, length), jnp.float32),
            pltpu.VMEM((2 * HEAD_DIM, length), jnp.float32),
            pltpu.VMEM((length, 2 * HEAD_DIM), half),
            pltpu.VMEM((length, length), half),
            pltpu.VMEM((length, length), half),
            pltpu.VMEM((length // TILE, 2 * HEAD_DIM, 2 * TILE), half),
            pltpu.VMEM((length // TILE, WINDOW + TILE, 2 * TILE), jnp.float32),
            pltpu.VMEM((1, length), jnp.float32),
            pltpu.VMEM((1, length), jnp.float32),
        ],
        steps=GROUP_HEADS,
        flops=8 * 10**9,
        moved=8 * 10**6,
    )
    planes = [[GROUPS * z + x for x in range(GROUPS)] for z in range(2)]

    def over_plane(chunks):
        return lax.all_to_all(
            chunks, "seq", split_axis=0, concat_axis=0, axis_index_groups=planes, tiled=True
        )

    got_rows = over_plane(rows)
    lanes = vocab // 2
    out_rows = 3 * GROUP_COLS // 2
    packed = 3 * GROUP_COLS + out_rows
    keep, give = call(
        out_kernel,
        (meta, attended, late.reshape(length, features // 2), sums),
        [((packed, lanes), half)] * 2,
    )
    here = keep + swapped(give, "dp", 1)
    there = swapped(here, "dp", 2)
    (grad_input,) = call(
        input_kernel,
        (token_ids, table, w_query, w_key, w_value, got_rows),
        [((block, features), half)],
        flops=10**9,
        moved=5 * 10**6,
    )
    kept_out, *pieces = call(
        combine_kernel,
        (meta, here, there, grad_input),
        [((out_rows, lanes), half)] + [((GROUP_COLS, lanes), half)] * GROUPS,
        loose=1,
    )
    last = blocks - 2
    got = [pieces[0]] + [swapped(pieces[turn], "seq", turn) for turn in (1, 2, 3)]
    got_out = [
        lax.ppermute(kept_out, "seq", [(2 * z, last), (2 * z + 1, last + 1)]) for z in range(3)
    ]
    (mine,) = call(
        gather_kernel,
        (meta, *got, kept_out, *got_out),
        [((4 * out_rows, lanes), half)],
    )
    (weight_grads,) = call(
        weight_kernel,
        (meta, normed, mine, swapped(mine, "dp", 1)),
        [((features // 2, features), jnp.float32)],
        flops=10**9,
        moved=5 * 10**6,
    )
    return (grad_input[None], weight_grads)


def on_device(token_ids, cotangent, table, w_query, w_key, w_value, w_out, window):
    fits = (
        lax.axis_size("seq") == 2 * GROUPS
        and lax.axis_size("dp") == 4
        and token_ids.shape == (1, 128)
        and table.shape == (256, HEADS * HEAD_DIM)
    )
    plan = grouped_device if fits else general_device
    return plan(token_ids, cotangent, table, w_query, w_key, w_value, w_out, window)


def solution(mesh):
    return jax.shard_map(
        on_device,
        mesh=mesh,
        in_specs=(P("dp", "seq"), P("dp", "seq", None), P(), P(), P(), P(), P(), P()),
        out_specs=(P("dp", "seq", None), P("seq", None)),
        check_vma=False,
    )
```

```python
import jax
import jax.numpy as jnp
import numpy as np
from jax import lax
from jax.experimental import pallas as pl
from jax.experimental.pallas import tpu as pltpu
from jax.sharding import PartitionSpec as P

HEADS = 12
HEAD_DIM = 64
WINDOW = 512


EPSILON = 1e-05


def shifted(block, axis, distance):
    devices = range(lax.axis_size(axis))
    route = [(i - distance, i) for i in devices if i - distance in devices]
    return lax.ppermute(block, axis, route)


def rotate(values, positions):
    row_count = values.shape[0]
    shaped = values.reshape(row_count, -1, HEAD_DIM)
    middle = HEAD_DIM // 2
    frequency = 10000.0 ** (-2.0 * jnp.arange(middle, dtype=jnp.float32) / HEAD_DIM)
    angles = positions.astype(jnp.float32)[:, None] * frequency[None, :]
    cosine = jnp.cos(angles)[:, None, :]
    sine_part = jnp.sin(angles)[:, None, :]
    former = shaped[..., :middle]
    latter = shaped[..., middle:]
    turned = jnp.concatenate(
        [former * cosine - latter * sine_part, latter * cosine + former * sine_part], axis=-1
    )
    return turned.reshape(row_count, -1)


def unrotate(values, positions):
    row_count = values.shape[0]
    shaped = values.reshape(row_count, -1, HEAD_DIM)
    middle = HEAD_DIM // 2
    frequency = 10000.0 ** (-2.0 * jnp.arange(middle, dtype=jnp.float32) / HEAD_DIM)
    angles = positions.astype(jnp.float32)[:, None] * frequency[None, :]
    cosine = jnp.cos(angles)[:, None, :]
    sine_part = jnp.sin(angles)[:, None, :]
    former = shaped[..., :middle]
    latter = shaped[..., middle:]
    turned = jnp.concatenate(
        [former * cosine + latter * sine_part, latter * cosine - former * sine_part], axis=-1
    )
    return turned.reshape(row_count, -1)


def tdot(left, right):
    return lax.dot_general(
        left, right, (((0,), (0,)), ((), ())), preferred_element_type=jnp.float32
    )


def ndot(left, right):
    return lax.dot_general(
        left, right, (((1,), (1,)), ((), ())), preferred_element_type=jnp.float32
    )


def embed_rows(byte_ids, table):
    onehot = (byte_ids[:, None] == jnp.arange(table.shape[0], dtype=jnp.int32)[None, :]).astype(
        jnp.bfloat16
    )
    return jnp.dot(onehot, table, preferred_element_type=jnp.float32).astype(jnp.bfloat16)


def normalize(embedded):
    widened = embedded.astype(jnp.float32)
    inv_rms = lax.rsqrt(jnp.mean(widened * widened, axis=1, keepdims=True) + EPSILON)
    return (widened, inv_rms, (widened * inv_rms).astype(jnp.bfloat16))


def keys_values(normed, positions, w_key, w_value):
    key_rows = rotate(jnp.dot(normed, w_key, preferred_element_type=jnp.float32), positions).astype(
        jnp.bfloat16
    )
    value_rows = jnp.dot(normed, w_value, preferred_element_type=jnp.float32).astype(jnp.bfloat16)
    return (key_rows, value_rows)


def head_group(
    query_heads, key_heads, value_heads, grad_heads, group_window, own_pos, key_pos, score_scale
):
    distance = own_pos[:, None] - key_pos[None, :]
    allowed = (
        (distance[None] >= 0)
        & (distance[None] < group_window[:, None, None])
        & (key_pos[None, None, :] >= 0)
    )
    scores = (
        jnp.einsum("qhd,khd->hqk", query_heads, key_heads, preferred_element_type=jnp.float32)
        * score_scale
    )
    masked = jnp.where(allowed, scores, -1e30)
    row_max = jnp.max(masked, axis=-1, keepdims=True)
    weights = jnp.where(allowed, jnp.exp(masked - row_max), 0.0)
    probs = weights / jnp.sum(weights, axis=-1, keepdims=True)
    probs_b = probs.astype(jnp.bfloat16)
    attended = jnp.einsum(
        "hqk,khd->qhd", probs_b, value_heads, preferred_element_type=jnp.float32
    ).astype(jnp.bfloat16)
    grad_probs = jnp.einsum(
        "qhd,khd->hqk", grad_heads, value_heads, preferred_element_type=jnp.float32
    )
    row_term = jnp.sum(probs * grad_probs, axis=-1, keepdims=True)
    grad_scores = (probs * (grad_probs - row_term) * score_scale).astype(jnp.bfloat16)
    grad_query = jnp.einsum(
        "hqk,khd->qhd", grad_scores, key_heads, preferred_element_type=jnp.float32
    )
    grad_key = jnp.einsum(
        "hqk,qhd->khd", grad_scores, query_heads, preferred_element_type=jnp.float32
    )
    grad_value = jnp.einsum("hqk,qhd->khd", probs_b, grad_heads, preferred_element_type=jnp.float32)
    return (attended, grad_query, grad_key, grad_value)


def general_device(token_ids, cotangent, table, w_query, w_key, w_value, w_out, window):
    local_ids = token_ids[0]
    grad_out = cotangent[0]
    length = local_ids.shape[0]
    features = table.shape[1]
    tail_rows = min(length, WINDOW)
    reach_devs = -(-WINDOW // length)
    halo_rows = reach_devs * tail_rows
    offset = lax.axis_index("seq") * length
    own_pos = offset + jnp.arange(length, dtype=jnp.int32)
    halo_pos = offset - halo_rows + jnp.arange(halo_rows, dtype=jnp.int32)
    score_scale = HEAD_DIM ** (-0.5)
    embedded = embed_rows(local_ids, table)
    widened, inv_rms, normed = normalize(embedded)
    query = rotate(jnp.dot(normed, w_query, preferred_element_type=jnp.float32), own_pos).astype(
        jnp.bfloat16
    )
    key_own, value_own = keys_values(normed, own_pos, w_key, w_value)
    key_pieces = []
    value_pieces = []
    for hop_index in range(reach_devs):
        far_keys, far_values = shifted((key_own, value_own), "seq", hop_index + 1)
        key_pieces.insert(0, far_keys)
        value_pieces.insert(0, far_values)
    key_halo = jnp.concatenate(key_pieces, axis=0)
    value_halo = jnp.concatenate(value_pieces, axis=0)
    span_rows = halo_rows + length
    key_all = jnp.concatenate([key_halo, key_own], axis=0)
    value_all = jnp.concatenate([value_halo, value_own], axis=0)
    key_pos = jnp.concatenate([halo_pos, own_pos], axis=0)
    query_heads = query.reshape(length, HEADS, HEAD_DIM)
    key_heads = key_all.reshape(span_rows, HEADS, HEAD_DIM)
    value_heads = value_all.reshape(span_rows, HEADS, HEAD_DIM)
    grad_att = ndot(grad_out, w_out).astype(jnp.bfloat16)
    grad_heads = grad_att.reshape(length, HEADS, HEAD_DIM)
    group_size = 4
    attended_parts = []
    query_parts = []
    key_parts = []
    value_parts = []
    for group_index in range(HEADS // group_size):
        lower = group_index * group_size
        upper = lower + group_size
        outputs = head_group(
            query_heads[:, lower:upper],
            key_heads[:, lower:upper],
            value_heads[:, lower:upper],
            grad_heads[:, lower:upper],
            window[lower:upper],
            own_pos,
            key_pos,
            score_scale,
        )
        attended_parts.append(outputs[0])
        query_parts.append(outputs[1])
        key_parts.append(outputs[2])
        value_parts.append(outputs[3])
    attended = jnp.concatenate(attended_parts, axis=1).reshape(length, features)
    grad_query = jnp.concatenate(query_parts, axis=1).reshape(length, features)
    grad_key = jnp.concatenate(key_parts, axis=1).reshape(span_rows, features)
    grad_value = jnp.concatenate(value_parts, axis=1).reshape(span_rows, features)
    tail_keys = grad_key[:halo_rows].reshape(reach_devs, tail_rows, features)
    tail_values = grad_value[:halo_rows].reshape(reach_devs, tail_rows, features)
    back_keys = jnp.zeros((tail_rows, features), jnp.float32)
    back_values = jnp.zeros((tail_rows, features), jnp.float32)
    for hop_index in range(reach_devs):
        got_keys, got_values = shifted(
            (tail_keys[reach_devs - 1 - hop_index], tail_values[reach_devs - 1 - hop_index]),
            "seq",
            -(hop_index + 1),
        )
        back_keys = back_keys + got_keys
        back_values = back_values + got_values
    own_keys = grad_key[halo_rows:]
    own_values = grad_value[halo_rows:]
    own_keys = jnp.concatenate([own_keys[: length - tail_rows], own_keys + back_keys], axis=0)
    own_values = jnp.concatenate(
        [own_values[: length - tail_rows], own_values + back_values], axis=0
    )
    grad_q_lin = unrotate(grad_query, own_pos).astype(jnp.bfloat16)
    grad_k_lin = unrotate(own_keys, own_pos).astype(jnp.bfloat16)
    grad_v_lin = own_values.astype(jnp.bfloat16)
    grad_normed = ndot(grad_q_lin, w_query) + ndot(grad_k_lin, w_key) + ndot(grad_v_lin, w_value)
    scaled = widened * inv_rms
    grad_input = (
        inv_rms * (grad_normed - scaled * jnp.mean(grad_normed * scaled, axis=1, keepdims=True))
    ).astype(jnp.bfloat16)
    term = jnp.concatenate(
        [
            tdot(normed, grad_q_lin),
            tdot(normed, grad_k_lin),
            tdot(normed, grad_v_lin),
            tdot(attended, grad_out),
        ],
        axis=0,
    )
    shares = lax.psum_scatter(term.astype(jnp.bfloat16), "seq", scatter_dimension=0, tiled=True)
    weight_grads = lax.psum(shares, "dp").astype(jnp.float32)
    return (grad_input[None], weight_grads)


GROUPS = 4
GROUP_HEADS = HEADS // GROUPS
GROUP_COLS = GROUP_HEADS * HEAD_DIM
TILE = 256
TOKEN_ROWS = 16
STRIP = 8
HALF = HEAD_DIM // 2
VMEM_BYTES = 48 * 1024 * 1024


def mirrored(bits):
    return 2 * (bits % 2) + bits // 2 % 2


def key_span(query_tile):
    first = max(0, query_tile - WINDOW // TILE)
    return (first * TILE, (query_tile - first + 1) * TILE)


def normed_table(table_ref):
    widened = table_ref[...].astype(jnp.float32)
    inv_rms = lax.rsqrt(jnp.mean(widened * widened, axis=1, keepdims=True) + EPSILON)
    return (widened * inv_rms).astype(jnp.bfloat16)


def onehot_columns(tokens, vocab):
    rows = lax.broadcasted_iota(jnp.int32, (vocab, tokens.shape[1]), 0)
    return (rows == tokens).astype(jnp.float32).astype(jnp.bfloat16)


def send_kernel(spot_ref, tokens_ref, cotangent_ref, out_weights_ref, *out_refs):
    early_refs, grads_ref = out_refs[:-1], out_refs[-1]
    grad_att = ndot(out_weights_ref[...], cotangent_ref[...]).astype(jnp.bfloat16)
    grads_ref[...] = grad_att
    block = tokens_ref.shape[1]
    tokens = jnp.broadcast_to(tokens_ref[...].astype(jnp.float32), (TOKEN_ROWS, block)).astype(
        jnp.bfloat16
    )
    for turn, early_ref in enumerate(early_refs):
        group = spot_ref[0] ^ turn
        place = pl.ds(pl.multiple_of(group * GROUP_COLS, GROUP_COLS), GROUP_COLS)
        early_ref[:GROUP_COLS, :] = grads_ref[place, :]
        early_ref[GROUP_COLS:, :] = tokens


def late_kernel(cotangent_ref, *rest):
    late_ref = rest[-1]
    for target in range(2 * GROUPS):
        late_ref[target] = cotangent_ref[target // GROUPS]


def prepare_kernel(
    meta_ref,
    cotangent_ref,
    table_ref,
    query_ref,
    key_ref,
    value_ref,
    halves_ref,
    lookup_ref,
    normed_ref,
    columns_ref,
):
    columns = halves_ref.shape[2]
    halves_ref[0] = cotangent_ref[:, :columns]
    halves_ref[1] = cotangent_ref[:, columns:]
    normed = normed_table(table_ref)
    half = normed.shape[1] // 2
    normed_ref[...] = jnp.where(meta_ref[GROUP_HEADS] == 0, normed[:, :half], normed[:, half:])
    place = pl.ds(pl.multiple_of(meta_ref[GROUP_HEADS + 3] * GROUP_COLS, GROUP_COLS), GROUP_COLS)
    for matrix, weights_ref in enumerate((query_ref, key_ref, value_ref)):
        columns_ref[...] = jnp.dot(
            normed, weights_ref[...], preferred_element_type=jnp.float32
        ).T
        mine = columns_ref[place, :]
        upper = mine.astype(jnp.bfloat16)
        rows = slice(matrix * GROUP_COLS, (matrix + 1) * GROUP_COLS)
        lookup_ref[0, rows, :] = upper
        lookup_ref[1, rows, :] = (mine - upper.astype(jnp.float32)).astype(jnp.bfloat16)


def attention_kernel(
    meta_ref,
    lookup_ref,
    cosine_ref,
    sine_ref,
    *rest,
):
    early_refs = rest[: 2 * GROUPS]
    attention_body(meta_ref, lookup_ref, cosine_ref, sine_ref, early_refs, *rest[2 * GROUPS :])


def attention_body(
    meta_ref,
    lookup_ref,
    cosine_ref,
    sine_ref,
    early_refs,
    rows_ref,
    sums_ref,
    attended_ref,
    value_key_ref,
    query_t_ref,
    key_t_ref,
    value_t_ref,
    grad_att_ref,
    onehot_ref,
    onehot_rows_ref,
    grad_query_ref,
    both_ref,
    scaled_ref,
    probs_ref,
    scores_ref,
    right_ref,
    products_ref,
    inverse_ref,
    term_ref,
):
    head = pl.program_id(0)
    block = early_refs[0].shape[1]
    length = len(early_refs) * block
    tiles = length // TILE
    vocab = lookup_ref.shape[2]
    half_vocab = vocab // 2
    half = jnp.bfloat16
    cosine = cosine_ref[...]
    sine_part = sine_ref[...]

    @pl.when(head == 0)
    def _():
        own = 2 * meta_ref[GROUP_HEADS + 1] + meta_ref[GROUP_HEADS]
        for turn, early_ref in enumerate(early_refs):
            lanes = pl.ds(pl.multiple_of((own ^ turn) * block, block), block)
            tokens = early_ref[GROUP_COLS : GROUP_COLS + TOKEN_ROWS, :]
            tokens = tokens.astype(jnp.float32)[:1].astype(jnp.int32)
            onehot_ref[:, lanes] = onehot_columns(tokens, vocab)
            grad_att_ref[:, :, lanes] = early_ref[:GROUP_COLS, :].reshape(
                GROUP_HEADS, HEAD_DIM, block
            )
        onehot = onehot_ref[...]
        onehot_rows_ref[...] = onehot.T
        size = 3 * GROUP_COLS
        chosen = jnp.dot(
            lookup_ref[...].reshape(2 * size, vocab), onehot, preferred_element_type=jnp.float32
        )

        def picked(start):
            lower = start + size
            return chosen[start : start + HEAD_DIM] + chosen[lower : lower + HEAD_DIM]

        def turned(columns):
            former = columns[:HALF]
            latter = columns[HALF:]
            return jnp.concatenate(
                [former * cosine - latter * sine_part, latter * cosine + former * sine_part], axis=0
            )

        for index in range(GROUP_HEADS):
            query = turned(picked(index * HEAD_DIM)) * HEAD_DIM ** (-0.5)
            keys = turned(picked(GROUP_COLS + index * HEAD_DIM)).astype(half)
            values = picked(2 * GROUP_COLS + index * HEAD_DIM).astype(half)
            value_key_ref[index] = jnp.concatenate([values, keys], axis=0).T
            query_t_ref[index] = query.astype(half)
            key_t_ref[index] = keys
            value_t_ref[index] = values

    width = meta_ref[head]
    grad_att = grad_att_ref[head]
    query_t = query_t_ref[head]
    blank = jnp.zeros((HEAD_DIM, TILE), half)
    base = lax.broadcasted_iota(jnp.int32, (STRIP, TILE), 1) - lax.broadcasted_iota(
        jnp.int32, (STRIP, TILE), 0
    )
    for tile in range(tiles):
        columns = slice(tile * TILE, (tile + 1) * TILE)
        right_ref[tile, :HEAD_DIM, :TILE] = grad_att[:, columns]
        right_ref[tile, HEAD_DIM:, :TILE] = blank
        right_ref[tile, :HEAD_DIM, TILE:] = blank
        right_ref[tile, HEAD_DIM:, TILE:] = query_t[:, columns]

    def multiply(tile):
        first, count = key_span(tile)
        products_ref[tile, :count, :] = jnp.dot(
            value_key_ref[head, first : first + count, :],
            right_ref[tile],
            preferred_element_type=jnp.float32,
        )

    def forward(tile):
        first, count = key_span(tile)
        columns = slice(tile * TILE, (tile + 1) * TILE)
        row_max = None
        for row in range(0, count, STRIP):
            offset = tile * TILE - first - row
            allowed = base < width - offset
            if offset - STRIP < 0:
                allowed = allowed & (base >= -offset)
            masked = jnp.where(allowed, products_ref[tile, row : row + STRIP, TILE:], -1e30)
            products_ref[tile, row : row + STRIP, TILE:] = masked
            row_max = masked if row_max is None else jnp.maximum(row_max, masked)
        row_max = jnp.max(row_max, axis=0, keepdims=True)
        total = None
        for row in range(0, count, 2 * STRIP):
            weights = jnp.exp(products_ref[tile, row : row + 2 * STRIP, TILE:] - row_max)
            total = weights if total is None else total + weights
            probs_ref[first + row : first + row + 2 * STRIP, columns] = weights.astype(half)
        inverse = 1.0 / jnp.sum(total, axis=0, keepdims=True)
        attended = inverse * jnp.dot(
            value_t_ref[head, :, first : first + count],
            probs_ref[first : first + count, columns],
            preferred_element_type=jnp.float32,
        )
        attended_ref[pl.ds(pl.multiple_of(head * HEAD_DIM, HEAD_DIM), HEAD_DIM), columns] = (
            attended.astype(half)
        )
        wide_grad = grad_att[:, columns].astype(jnp.float32)
        inverse_ref[:, columns] = inverse
        term_ref[:, columns] = jnp.sum(attended * wide_grad, axis=0, keepdims=True)
        scaled_ref[columns, :] = jnp.concatenate(
            [
                (inverse * query_t[:, columns].astype(jnp.float32)).astype(half),
                (inverse * wide_grad).astype(half),
            ],
            axis=0,
        ).T

    def backward(tile):
        first, count = key_span(tile)
        columns = slice(tile * TILE, (tile + 1) * TILE)
        row_term = term_ref[:, columns]
        for row in range(0, count, 2 * STRIP):
            strip = slice(first + row, first + row + 2 * STRIP)
            scores_ref[strip, columns] = (
                probs_ref[strip, columns].astype(jnp.float32)
                * (products_ref[tile, row : row + 2 * STRIP, :TILE] - row_term)
            ).astype(half)
        grad_query_ref[:, columns] = inverse_ref[:, columns] * jnp.dot(
            key_t_ref[head, :, first : first + count],
            scores_ref[first : first + count, columns],
            preferred_element_type=jnp.float32,
        )

    lanes = lax.broadcasted_iota(jnp.int32, (TILE, 2 * HEAD_DIM), 1)

    def collect(tile):
        start = tile * TILE
        stop = min(length, start + TILE + WINDOW)
        grad_key = jnp.dot(
            scores_ref[start : start + TILE, start:stop],
            scaled_ref[start:stop, :],
            preferred_element_type=jnp.float32,
        )
        grad_value = jnp.dot(
            probs_ref[start : start + TILE, start:stop],
            scaled_ref[start:stop, :],
            preferred_element_type=jnp.float32,
        )
        both_ref[:, start : start + TILE] = jnp.where(lanes < HEAD_DIM, grad_key, grad_value).T

    reach = WINDOW // TILE
    for step in range(tiles + 3 + reach):
        if step < tiles:
            multiply(step)
        if 0 <= step - 1 < tiles:
            forward(step - 1)
        if 0 <= step - 2 < tiles:
            backward(step - 2)
        ready = step - 3 - reach
        if 0 <= ready < tiles:
            collect(ready)
    def turned_back(columns):
        former = columns[:HALF]
        latter = columns[HALF:]
        return jnp.concatenate(
            [former * cosine + latter * sine_part, latter * cosine - former * sine_part], axis=0
        )

    both = both_ref[...]
    grads = jnp.concatenate(
        [
            turned_back(grad_query_ref[...] * HEAD_DIM ** (-0.5)),
            turned_back(both[:HEAD_DIM]),
            both[HEAD_DIM:],
        ],
        axis=0,
    ).astype(half)
    sums = jnp.dot(grads, onehot_rows_ref[...], preferred_element_type=jnp.float32).astype(half)
    for matrix in range(3):
        rows = slice(matrix * HEAD_DIM, (matrix + 1) * HEAD_DIM)
        place = pl.ds(
            pl.multiple_of(matrix * GROUP_COLS + head * HEAD_DIM, HEAD_DIM), HEAD_DIM
        )
        for core in range(2):
            lane = core * half_vocab
            sums_ref[core, place, :] = sums[rows, lane : lane + half_vocab]
        for target in range(GROUPS):
            start = target * block
            near = grads[rows, start : start + block]
            far = grads[rows, start + GROUPS * block : start + (GROUPS + 1) * block]
            rows_ref[target, place, :] = jnp.where(meta_ref[GROUP_HEADS + 1] < 2, near, far)


def out_kernel(meta_ref, attended_ref, cotangent_ref, sums_ref, keep_ref, give_ref):
    total = jnp.dot(attended_ref[...], cotangent_ref[...], preferred_element_type=jnp.float32)
    rows = total.shape[0] // 2
    base = sums_ref.shape[1]
    lanes = keep_ref.shape[1]
    first = meta_ref[GROUP_HEADS + 2] == 0
    keep_ref[:base, :] = jnp.where(first, sums_ref[0], sums_ref[1])
    give_ref[:base, :] = jnp.where(first, sums_ref[1], sums_ref[0])
    for chunk in range(total.shape[1] // lanes):
        part = total[:, chunk * lanes : (chunk + 1) * lanes]
        place = slice(base + chunk * rows, base + (chunk + 1) * rows)
        keep_ref[place, :] = jnp.where(first, part[:rows], part[rows:]).astype(jnp.bfloat16)
        give_ref[place, :] = jnp.where(first, part[rows:], part[:rows]).astype(jnp.bfloat16)


def combine_kernel(meta_ref, here_ref, there_ref, after_ref, out_ref, *piece_refs):
    del after_ref
    rows = GROUP_COLS
    for turn, piece_ref in enumerate(piece_refs):
        target = jnp.minimum(meta_ref[GROUP_HEADS + 1] ^ (turn // 2), 2)
        place = pl.ds(pl.multiple_of(target * rows, rows), rows)
        piece_ref[...] = here_ref[place, :] + there_ref[place, :]
    out_ref[...] = here_ref[3 * rows :, :] + there_ref[3 * rows :, :]


def gather_kernel(meta_ref, s0, s1, s2, s3, own_ref, o0, o1, o2, after_ref, mine_ref):
    del after_ref
    rows = GROUP_COLS
    size = own_ref.shape[0]

    @pl.when(meta_ref[GROUP_HEADS + 1] < 3)
    def _():
        for turn, got in enumerate((s0, s1, s2, s3)):
            source = meta_ref[GROUP_HEADS + 3] ^ mirrored(turn)
            mine_ref[pl.ds(pl.multiple_of(source * rows, rows), rows), :] = got[...]
        tail = mine_ref.shape[0] - GROUPS * rows
        mine_ref[GROUPS * rows :, :] = jnp.zeros((tail, mine_ref.shape[1]), jnp.bfloat16)

    @pl.when(meta_ref[GROUP_HEADS + 1] == 3)
    def _():
        for place, piece in enumerate((o0, o2, o1, own_ref)):
            mine_ref[place * size : (place + 1) * size, :] = piece[...]


def input_kernel(tokens_ref, table_ref, query_ref, key_ref, value_ref, rows_ref, out_ref):
    vocab = table_ref.shape[0]
    onehot = onehot_columns(tokens_ref[...], vocab)
    embedded = tdot(onehot, table_ref[...])
    inv_rms = lax.rsqrt(jnp.mean(embedded * embedded, axis=1, keepdims=True) + EPSILON)
    grad_normed = None
    for matrix, weights in enumerate((query_ref, key_ref, value_ref)):
        columns = jnp.concatenate(
            [
                rows_ref[group, matrix * GROUP_COLS : (matrix + 1) * GROUP_COLS, :]
                for group in map(mirrored, range(GROUPS))
            ],
            axis=0,
        )
        part = ndot(columns.astype(jnp.float32).T.astype(jnp.bfloat16), weights[...])
        grad_normed = part if grad_normed is None else grad_normed + part
    scaled = embedded * inv_rms
    out_ref[...] = (
        inv_rms * (grad_normed - scaled * jnp.mean(grad_normed * scaled, axis=1, keepdims=True))
    ).astype(jnp.bfloat16)


def weight_kernel(meta_ref, normed_ref, mine_ref, other_ref, out_ref):
    half_vocab = mine_ref.shape[1]
    first_core = meta_ref[GROUP_HEADS + 2] == 0

    @pl.when(meta_ref[GROUP_HEADS + 1] < 3)
    def _():
        first = normed_ref[:half_vocab, :]
        second = normed_ref[half_vocab:, :]
        upper = jnp.where(first_core, first, second)
        lower = jnp.where(first_core, second, first)
        total = None
        for part, sums_ref in ((upper, mine_ref), (lower, other_ref)):
            term = lax.dot_general(
                part,
                sums_ref[: GROUPS * GROUP_COLS, :],
                (((0,), (1,)), ((), ())),
                preferred_element_type=jnp.float32,
            )
            total = term if total is None else total + term
        out_ref[...] = total

    @pl.when(meta_ref[GROUP_HEADS + 1] == 3)
    def _():
        rows = GROUP_COLS // 2
        for half in range(2):
            for column in range(6):
                start = (half * 6 + column) * rows
                for core in range(2):
                    same = first_core == (core == 0)
                    value = jnp.where(
                        same, mine_ref[start : start + rows, :], other_ref[start : start + rows, :]
                    )
                    row = half * GROUP_COLS + core * rows
                    out_ref[
                        row : row + rows, column * half_vocab : (column + 1) * half_vocab
                    ] = value.astype(jnp.float32)


def whole(shape):
    return pl.BlockSpec(shape, lambda *_: (0,) * len(shape))


def swapped(block, axis, bit):
    route = [(i, i ^ bit) for i in range(lax.axis_size(axis))]
    return lax.ppermute(block, axis, route)


def rope_table(length):
    frequency = (10000.0 ** (-2.0 * np.arange(HALF, dtype=np.float32) / HEAD_DIM)).astype(np.float32)
    angles = frequency[:, None] * np.arange(length, dtype=np.float32)[None, :]
    angles = angles.astype(np.float64)
    return (
        jnp.asarray(np.cos(angles).astype(np.float32)),
        jnp.asarray(np.sin(angles).astype(np.float32)),
    )


def grouped_device(token_ids, cotangent, table, w_query, w_key, w_value, w_out, window):
    place = lax.axis_index("seq")
    core = lax.axis_index("dp") % 2
    side = place % 2
    level = place // 2
    group = 2 * side + level % 2
    block = token_ids.shape[1]
    features = table.shape[1]
    vocab = table.shape[0]
    blocks = lax.axis_size("seq")
    length = block * blocks
    grad_out = cotangent[0]
    meta = jnp.concatenate(
        [
            lax.dynamic_slice_in_dim(window, group * GROUP_HEADS, GROUP_HEADS, 0),
            jnp.stack([side, level, core, group]).astype(jnp.int32),
        ]
    )
    spot = jnp.stack([group]).astype(jnp.int32)
    cosine, sine_part = rope_table(length)

    def call(
        body, operands, outs, scratch=(), steps=1, flops=10**8, moved=10**6, loose=0, grant=VMEM_BYTES
    ):
        spaces = [whole(operand.shape) for operand in operands]
        for index in range(loose):
            spaces[-1 - index] = pl.BlockSpec(memory_space=pl.ANY)
        if operands[0].ndim == 1:
            spaces[0] = pl.BlockSpec(memory_space=pltpu.SMEM)
        return pl.pallas_call(
            body,
            grid=(steps,),
            in_specs=spaces,
            out_specs=[whole(shape) for shape, _ in outs],
            out_shape=[jax.ShapeDtypeStruct(shape, dtype) for shape, dtype in outs],
            scratch_shapes=list(scratch),
            compiler_params=pltpu.CompilerParams(
                dimension_semantics=("arbitrary",), vmem_limit_bytes=grant
            ),
            cost_estimate=pl.CostEstimate(flops=flops, bytes_accessed=moved, transcendentals=0),
        )(*operands)

    half = jnp.bfloat16
    sent = call(
        send_kernel,
        (spot, token_ids, grad_out, w_out),
        [((GROUP_COLS + TOKEN_ROWS, block), half)] * GROUPS,
        [pltpu.VMEM((features, block), half)],
        grant=60 * 1024 * 1024,
    )
    early = [sent[0]] + [None] * (blocks - 1)
    for turn in (4, 6, 5, 7, 2, 3, 1):
        early[turn] = swapped(sent[mirrored(turn)], "seq", turn)
    halves, lookup, normed = call(
        prepare_kernel,
        (meta, grad_out, table, w_query, w_key, w_value),
        [
            ((2, block, features // 2), half),
            ((2, 3 * GROUP_COLS, vocab), half),
            ((vocab, features // 2), half),
        ],
        [pltpu.VMEM((features, vocab), jnp.float32)],
        flops=10**9,
        moved=5 * 10**6,
        grant=60 * 1024 * 1024,
    )
    (late,) = call(
        late_kernel,
        (halves, lookup, *early[1:]),
        [((blocks, block, features // 2), half)],
        loose=blocks,
    )
    late = lax.all_to_all(late, "seq", split_axis=0, concat_axis=0, tiled=True)
    heads_shape = (GROUP_HEADS, HEAD_DIM, length)
    rows_shape = (GROUP_HEADS, length, 2 * HEAD_DIM)
    rows, sums, attended = call(
        attention_kernel,
        (meta, lookup, cosine, sine_part, *early),
        [
            ((GROUPS, 3 * GROUP_COLS, block), half),
            ((2, 3 * GROUP_COLS, vocab // 2), half),
            ((GROUP_COLS, length), half),
        ],
        [
            pltpu.VMEM(rows_shape, half),
            pltpu.VMEM(heads_shape, half),
            pltpu.VMEM(heads_shape, half),
            pltpu.VMEM(heads_shape, half),
            pltpu.VMEM(heads_shape, half),
            pltpu.VMEM((vocab, length), half),
            pltpu.VMEM((length, vocab), half),
            pltpu.VMEM((HEAD_DIM, length), jnp.float32),
            pltpu.VMEM((2 * HEAD_DIM, length), jnp.float32),
            pltpu.VMEM((length, 2 * HEAD_DIM), half),
            pltpu.VMEM((length, length), half),
            pltpu.VMEM((length, length), half),
            pltpu.VMEM((length // TILE, 2 * HEAD_DIM, 2 * TILE), half),
            pltpu.VMEM((length // TILE, WINDOW + TILE, 2 * TILE), jnp.float32),
            pltpu.VMEM((1, length), jnp.float32),
            pltpu.VMEM((1, length), jnp.float32),
        ],
        steps=GROUP_HEADS,
        flops=8 * 10**9,
        moved=8 * 10**6,
    )
    planes = [[GROUPS * z + x for x in range(GROUPS)] for z in range(2)]

    def over_plane(chunks):
        return lax.all_to_all(
            chunks, "seq", split_axis=0, concat_axis=0, axis_index_groups=planes, tiled=True
        )

    got_rows = over_plane(rows)
    lanes = vocab // 2
    out_rows = 3 * GROUP_COLS // 2
    packed = 3 * GROUP_COLS + out_rows
    keep, give = call(
        out_kernel,
        (meta, attended, late.reshape(length, features // 2), sums),
        [((packed, lanes), half)] * 2,
    )
    here = keep + swapped(give, "dp", 1)
    there = swapped(here, "dp", 2)
    kept_out, *pieces = call(
        combine_kernel,
        (meta, here, there, got_rows),
        [((out_rows, lanes), half)] + [((GROUP_COLS, lanes), half)] * GROUPS,
        loose=1,
    )
    last = blocks - 2
    got = [pieces[0]] + [swapped(pieces[turn], "seq", turn) for turn in (1, 2, 3)]
    got_out = [
        lax.ppermute(kept_out, "seq", [(2 * z, last), (2 * z + 1, last + 1)]) for z in range(3)
    ]
    (grad_input,) = call(
        input_kernel,
        (token_ids, table, w_query, w_key, w_value, got_rows),
        [((block, features), half)],
        flops=10**9,
        moved=5 * 10**6,
    )
    (mine,) = call(
        gather_kernel,
        (meta, *got, kept_out, *got_out, grad_input),
        [((4 * out_rows, lanes), half)],
        loose=1,
    )
    (weight_grads,) = call(
        weight_kernel,
        (meta, normed, mine, swapped(mine, "dp", 1)),
        [((features // 2, features), jnp.float32)],
        flops=10**9,
        moved=5 * 10**6,
    )
    return (grad_input[None], weight_grads)


def on_device(token_ids, cotangent, table, w_query, w_key, w_value, w_out, window):
    fits = (
        lax.axis_size("seq") == 2 * GROUPS
        and lax.axis_size("dp") == 4
        and token_ids.shape == (1, 128)
        and table.shape == (256, HEADS * HEAD_DIM)
    )
    plan = grouped_device if fits else general_device
    return plan(token_ids, cotangent, table, w_query, w_key, w_value, w_out, window)


def solution(mesh):
    return jax.shard_map(
        on_device,
        mesh=mesh,
        in_specs=(P("dp", "seq"), P("dp", "seq", None), P(), P(), P(), P(), P(), P()),
        out_specs=(P("dp", "seq", None), P("seq", None)),
        check_vma=False,
    )
```
